32 devices in a mesh: stream: 2 (over x), batch: 16 (over z, y, core).
Axes of the slice: x: 2, y: 2, z: 4, core: 2. Of those that a mesh axis runs over, the one named last changes fastest.
Arguments:
- tokens: bfloat16 [2, 256, 64, 768], P('stream', 'batch'), may hold values from -6 to 6
- out_grad: bfloat16 [2, 256, 64, 768], P('stream', 'batch'), may hold values from -6 to 6
- master: float32 [128, 80, 768], P(None, 'batch'), may hold values from -2 to 2, as said below
- first_moment: float32 [128, 80, 768], P(None, 'batch'), may hold values from -32768 to 32768
- second_moment: float32 [128, 80, 768], P(None, 'batch'), may hold values from 0 to 32768, as said below
- small_params: float32 [12, 768], replicated, may hold values from -2 to 2
- small_first: float32 [12, 768], replicated, may hold values from -32768 to 32768
- small_second: float32 [12, 768], replicated, may hold values from 0 to 32768, as said below
- logit_scale: float32 [1], replicated, may hold values from 30 to 60
- scale_first: float32 [1], replicated, may hold values from -16.896 to 16.896
- scale_second: float32 [1], replicated, may hold values from 11.79648 to 190.0544
- pair_lang: int32 [256], replicated, may hold values from 0 to 108
- unit_owner: int32 [72], replicated, may hold values from 0 to 15, as said below
Outputs:
- block_out: bfloat16 [2, 256, 64, 768], P('stream', 'batch')
- input_grad: bfloat16 [2, 256, 64, 768], P('stream', 'batch')
- new_master: float32 [128, 80, 768], P(None, 'batch')
- new_first: float32 [128, 80, 768], P(None, 'batch')
- new_second: float32 [128, 80, 768], P(None, 'batch')
- new_copy: bfloat16 [128, 80, 768], P(None, 'batch')
- new_small: float32 [12, 768], replicated
- new_small_first: float32 [12, 768], replicated
- new_small_second: float32 [12, 768], replicated
- scale_new: float32 [1], replicated
- scale_first_new: float32 [1], replicated
- scale_second_new: float32 [1], replicated
- loss: float32 [1], replicated
The draws below stay inside these ranges and needn't reach their ends.
Inputs may be any that keep to these rules, and one draw needn't show every extreme that they name: `unit_owner`: each entry names the device of the batch axis that owns weight block u; no device owns more than 5 blocks, and one owns exactly 5. `master`: slots that no block uses hold values of the same kind. `second_moment`: Positive. `small_second`: Positive.
All inputs are finite; a program needn't handle non-finite values.
Results may differ from the reference program's by a relative error of at most 0.012.
Values may be sent and summed in bfloat16 or wider, within the bound.
A program may use at most 320 MiB of HBM per device.

```python
import math
import jax
import jax.numpy as jnp
import numpy as np
from jax import lax

D = 768
H = 12
HD = 64
FF = 3072
LEN = 64
UR = 128
SLOTS = 5
LANGS = 109
STEP = 10
OWNERS = 16
PAIRS = 256
TOKENS = 32768
UNITS = 72
MROWS = 80
SMALL_ROWS = 12


def owner_table(key):
    heavy_key, spread_key, order_key = jax.random.split(jax.random.fold_in(key, 11), 3)
    heavy = jax.random.randint(heavy_key, (), 0, OWNERS)
    spots = jax.random.permutation(spread_key, (OWNERS - 1) * SLOTS)[:UNITS - SLOTS]
    lighter = (spots // SLOTS).astype(jnp.int32)
    lighter = lighter + (lighter >= heavy).astype(jnp.int32)
    listed = jnp.concatenate([jnp.full((SLOTS,), heavy, dtype=jnp.int32), lighter])
    return listed[jax.random.permutation(order_key, UNITS)].astype(jnp.int32)


def slot_table(key):
    owners_list = owner_table(key)
    same_owner = owners_list[:, None] == owners_list[None, :]
    ordinal = jnp.arange(UNITS, dtype=jnp.int32)
    earlier = ordinal[None, :] < ordinal[:, None]
    slot_number = jnp.sum(jnp.where(same_owner & earlier, 1, 0), axis=1).astype(jnp.int32)
    positions = owners_list * SLOTS + slot_number
    return jnp.arange(MROWS, dtype=jnp.int32)[:, None] == positions[None, :]


def kind_values(values_six):
    query_blocks = D // UR
    inner_blocks = FF // UR
    ends = [query_blocks, 2 * query_blocks, 3 * query_blocks, 4 * query_blocks, 4 * query_blocks + inner_blocks]
    ordinal = jnp.arange(UNITS)
    result = jnp.full((UNITS,), values_six[5], dtype=jnp.float32)
    for member in range(4, -1, -1):
        result = jnp.where(ordinal < ends[member], jnp.float32(values_six[member]), result)
    return result


def per_slot(key, values_six, empty_value):
    table = slot_table(key)
    per_unit = kind_values(values_six)
    taken = jnp.any(table, axis=1)
    return jnp.sum(jnp.where(table, per_unit[None, :], 0.0), axis=1) + jnp.where(taken, 0.0, empty_value)


def grad_kinds():
    return (0.5, 0.5, 0.5, 0.16, 0.4, 0.4)


def small_factors():
    inner_rows = FF // D
    return jnp.array([0.5, 0.5, 0.8] + [0.4] * inner_rows + [0.7, 1.0, 1.0, 1.0, 1.0], dtype=jnp.float32)


def signed_noise(key, shape):
    return jnp.clip(jax.random.normal(key, shape, jnp.float32), -4.0, 4.0)


def square_factor(key, shape):
    return jnp.exp(jax.random.uniform(key, shape, jnp.float32, math.log(0.5), math.log(8.0)))


def draw_unit_owner(key, part):
    return owner_table(key)


def draw_master(key, part):
    stds = per_slot(key, (D ** (-0.5), D ** (-0.5), D ** (-0.5), (D // 16) ** (-0.5), D ** (-0.5), FF ** (-0.5)), D ** (-0.5))
    noise = signed_noise(jax.random.fold_in(key, 21), (UR, MROWS, D))
    return noise * stds[None, :, None]


def draw_first_moment(key, part):
    root = math.sqrt(TOKENS)
    kinds = tuple((0.111 * factor * root for factor in grad_kinds()))
    scales = per_slot(key, kinds, 0.111 * 0.4 * root)
    noise = signed_noise(jax.random.fold_in(key, 22), (UR, MROWS, D))
    return noise * scales[None, :, None]


def draw_second_moment(key, part):
    kinds = tuple((0.001 * factor * factor * TOKENS for factor in grad_kinds()))
    scales = per_slot(key, kinds, 0.001 * 0.16 * TOKENS)
    factor_draw = square_factor(jax.random.fold_in(key, 23), (UR, MROWS, D))
    return factor_draw * scales[None, :, None]


def draw_small_params(key, part):
    inner_rows = FF // D
    noise = signed_noise(jax.random.fold_in(key, 31), (SMALL_ROWS, D))
    rows_ids = jnp.arange(SMALL_ROWS)
    gain_rows = (rows_ids == 4 + inner_rows) | (rows_ids == 6 + inner_rows)
    return jnp.where(gain_rows[:, None], 1.0 + 0.1 * noise, 0.1 * noise)


def draw_small_first(key, part):
    root = math.sqrt(TOKENS)
    noise = signed_noise(jax.random.fold_in(key, 32), (SMALL_ROWS, D))
    return noise * (0.111 * root * small_factors())[:, None]


def draw_small_second(key, part):
    factors = small_factors()
    factor_draw = square_factor(jax.random.fold_in(key, 33), (SMALL_ROWS, D))
    return factor_draw * (0.001 * TOKENS * factors * factors)[:, None]


def set_ends(drawn, key, smallest, high):
    dims = drawn.shape
    index_at = [jax.random.randint(jax.random.fold_in(key, axis), (), 0, dims[axis]) for axis in range(len(dims))]
    drawn = drawn.at[tuple(index_at)].set(smallest)
    longest = dims.index(max(dims))
    index_at[longest] = (index_at[longest] + 1) % dims[longest]
    return drawn.at[tuple(index_at)].set(high)


def levels(key, shape, pieces, smallest, largest):
    level = 1.0
    for dim, shards_of in pieces:
        draws = jax.random.uniform(jax.random.fold_in(jax.random.fold_in(key, 6), dim), (shards_of,), jnp.float32, smallest / len(pieces), largest / len(pieces))
        level = level * jnp.repeat(jnp.exp(draws), shape[dim] // shards_of).reshape((-1,) + (1,) * (len(shape) - 1 - dim))
    return level


def cumulative_ranks(amount, slope):
    portions = [(1 << 20) // math.isqrt(rank ** slope) + 1 for rank in range(1, amount + 1)]
    scale = 1 + sum(portions) // (1 << 30)
    return np.cumsum(np.array([max(1, weight // scale) for weight in portions]))


def ranked_ids(stream_key, shape, number_of, lean):
    table = cumulative_ranks(number_of, lean)
    ticket = jax.random.randint(jax.random.fold_in(stream_key, 1), shape, 0, int(table[number_of - 1]))
    rank = jnp.searchsorted(jnp.asarray(table, jnp.int32), ticket, side="right")
    return jax.random.permutation(jax.random.fold_in(stream_key, 2), number_of)[rank].astype(jnp.int32)


def bell_draw(stream_key, dims, scale, most, cuts=(), kind=jnp.bfloat16):
    drawn = scale * jax.random.normal(stream_key, dims, jnp.float32)
    if cuts:
        drawn = drawn * levels(stream_key, dims, cuts, -0.22, 0.18)
    return jnp.clip(drawn, -most, most).astype(kind)


def setup_inputs(seed: int = 0) -> dict:
    streams_of = jax.random.split(jax.random.key(seed), 14)
    return {
        "tokens": bell_draw(streams_of[0], (2, PAIRS, LEN, D), 1.0, 6.0, ((0, 2), (1, 16))),
        "out_grad": bell_draw(streams_of[1], (2, PAIRS, LEN, D), 1.0, 6.0, ((0, 2), (1, 16))),
        "master": draw_master(jax.random.fold_in(streams_of[13], 71), 0),
        "first_moment": draw_first_moment(jax.random.fold_in(streams_of[13], 71), 0),
        "second_moment": draw_second_moment(jax.random.fold_in(streams_of[13], 71), 0),
        "small_params": draw_small_params(jax.random.fold_in(streams_of[13], 71), 0),
        "small_first": draw_small_first(jax.random.fold_in(streams_of[13], 71), 0),
        "small_second": draw_small_second(jax.random.fold_in(streams_of[13], 71), 0),
        "logit_scale": jnp.clip(jax.random.uniform(streams_of[8], (1,), jnp.float32, 30.0, 60.0), 30.0, 60.0),
        "scale_first": jnp.clip(jax.random.uniform(streams_of[9], (1,), jnp.float32, -16.896, 16.896), -16.896, 16.896),
        "scale_second": jnp.clip(jnp.exp(jax.random.uniform(streams_of[10], (1,), jnp.float32, math.log(11.79648), math.log(190.0544))), 11.79648, 190.0544),
        "pair_lang": set_ends(ranked_ids(streams_of[11], (PAIRS,), LANGS, 2), jax.random.fold_in(streams_of[11], 3), 0, LANGS - 1).astype(jnp.int32),
        "unit_owner": draw_unit_owner(jax.random.fold_in(streams_of[13], 71), 0),
    }


HIGHEST = lax.Precision.HIGHEST
BETA_ONE = 0.9
BETA_TWO = 0.999
ADAM_EPS = 1e-06
RATE_UNITS = 0.02
RATE_SMALL = 0.1
RATE_SCALE = 2.0
DECAY = 0.01
MARGIN = 0.3
NORM_EPS = 1e-06

@jax.custom_vjp
def low(v):
    return lax.optimization_barrier(v.astype(jnp.bfloat16)).astype(jnp.float32)

@jax.custom_vjp
def low_back(v):
    return v

def low_keep(v):
    return (low(v), None)

def low_pass(kept, grad):
    return (grad,)

def back_keep(v):
    return (v, None)

def back_low(kept, grad):
    return (low(grad),)
low.defvjp(low_keep, low_pass)
low_back.defvjp(back_keep, back_low)

def unit_positions(owner_list, slot_count):
    unit_total = owner_list.shape[0]
    same_owner = owner_list[:, None] == owner_list[None, :]
    ordinal = jnp.arange(unit_total, dtype=jnp.int32)
    earlier = ordinal[None, :] < ordinal[:, None]
    slot_number = lax.optimization_barrier(jnp.sum(jnp.where(same_owner & earlier, 1, 0), axis=1)).astype(jnp.int32)
    return (owner_list.astype(jnp.int32) * slot_count + slot_number).astype(jnp.int32)

def layer_norm(resid, gain, shift):
    centre = lax.optimization_barrier(jnp.mean(resid, axis=-1, keepdims=True))
    centred = resid - centre
    variance = lax.optimization_barrier(jnp.mean(centred * centred, axis=-1, keepdims=True))
    return centred * lax.rsqrt(variance + NORM_EPS) * gain + shift

def gelu_exact(values):
    return jax.nn.gelu(values, approximate=False)

def normalize(vectors):
    return vectors * lax.rsqrt(lax.optimization_barrier(jnp.sum(vectors * vectors, axis=-1, keepdims=True)) + NORM_EPS)

def to_matrix(unit_block):
    return jnp.transpose(unit_block, (1, 0, 2)).reshape(-1, unit_block.shape[2])

def from_matrix(matrix, unit_rows):
    return jnp.transpose(matrix.reshape(-1, unit_rows, matrix.shape[1]), (1, 0, 2))

def unpack_small(small_set):
    inner_rows = FF // D
    return (small_set[0], small_set[1], small_set[2], small_set[3:3 + inner_rows].reshape(FF), small_set[3 + inner_rows], small_set[4 + inner_rows], small_set[5 + inner_rows], small_set[6 + inner_rows], small_set[7 + inner_rows])

def adamw(weight_in, gradient, moment_one, moment_two, rate_value, decay_value, fix_one, fix_two):
    new_one = BETA_ONE * moment_one + (1.0 - BETA_ONE) * gradient
    new_two = BETA_TWO * moment_two + (1.0 - BETA_TWO) * gradient * gradient
    stepped = new_one / fix_one / (jnp.sqrt(new_two / fix_two) + ADAM_EPS)
    return (weight_in - rate_value * (stepped + decay_value * weight_in), new_one, new_two)

def encode(block_rows, matrices, small_set):
    w_query, w_key, w_value, w_out, w_inner, w_outer = matrices
    bias_query, bias_value, bias_out, bias_inner, bias_outer, gain_one, shift_one, gain_two, shift_two = unpack_small(small_set)
    sentences, length, model_width = block_rows.shape
    flat_rows = block_rows.reshape(sentences * length, model_width)
    shape_heads = (sentences, length, H, HD)
    queries = low_back(low(jnp.dot(flat_rows, w_query, precision=HIGHEST) + bias_query))
    keys_rows = low_back(low(jnp.dot(flat_rows, w_key, precision=HIGHEST)))
    values_rows = low_back(low(jnp.dot(flat_rows, w_value, precision=HIGHEST) + bias_value))
    scores = low_back(jnp.einsum('slhe,smhe->shlm', queries.reshape(shape_heads), keys_rows.reshape(shape_heads), precision=HIGHEST) * HD ** (-0.5))
    softmax_rows = low(jax.nn.softmax(scores, axis=-1))
    context = jnp.einsum('shlm,smhe->slhe', softmax_rows, values_rows.reshape(shape_heads), precision=HIGHEST)
    context = low_back(low(context.reshape(sentences * length, model_width)))
    attended = low_back(jnp.dot(context, w_out, precision=HIGHEST) + bias_out)
    hidden_one = layer_norm(flat_rows + attended, gain_one, shift_one)
    inner_act = low_back(jnp.dot(low(hidden_one), w_inner.T, precision=HIGHEST) + bias_inner)
    active = low(gelu_exact(inner_act))
    outer_out = low_back(jnp.dot(active, w_outer, precision=HIGHEST) + bias_outer)
    output = layer_norm(hidden_one + outer_out, gain_two, shift_two)
    return output.reshape(sentences, length, model_width)

def direction_loss(row_vecs, col_vecs, languages, scale_value):
    cosines = jnp.dot(row_vecs, col_vecs.T, precision=HIGHEST)
    diagonal = jnp.eye(row_vecs.shape[0], dtype=cosines.dtype)
    logits = scale_value * (cosines - MARGIN * diagonal)
    same_group = languages[:, None] == languages[None, :]
    masked = jnp.where(same_group, logits, -1e+30)
    row_top = lax.optimization_barrier(jnp.max(masked, axis=1, keepdims=True))
    exp_total = lax.optimization_barrier(jnp.sum(jnp.where(same_group, jnp.exp(masked - row_top), 0.0), axis=1))
    return jnp.sum(jnp.log(exp_total) + row_top[:, 0] - jnp.diagonal(logits))

def objective(matrices, small_set, scale_value, token_rows, grad_rows, languages):
    block_size = math.gcd(64, 2 * PAIRS)
    token_blocks = token_rows.reshape(-1, block_size, LEN, D)
    grad_blocks = grad_rows.reshape(-1, block_size, LEN, D)

    def one_block(pair_of):
        block_in, block_grad = pair_of
        result = encode(block_in, matrices, small_set)
        return (jnp.sum(result * block_grad), result[:, 0, :])
    partial_sums, heads_out = lax.map(jax.checkpoint(one_block), (token_blocks, grad_blocks))
    pooled = normalize(heads_out.reshape(2, PAIRS, D))
    loss_sum = direction_loss(pooled[0], pooled[1], languages, scale_value) + direction_loss(pooled[1], pooled[0], languages, scale_value)
    return (jnp.sum(partial_sums) + loss_sum, loss_sum)

def reference(tokens, out_grad, master, first_moment, second_moment, small_params, small_first, small_second, logit_scale, scale_first, scale_second, pair_lang, unit_owner):
    positions = unit_positions(unit_owner, SLOTS)
    query_blocks = D // UR
    inner_blocks = FF // UR
    edges = [0, query_blocks, 2 * query_blocks, 3 * query_blocks, 4 * query_blocks, 4 * query_blocks + inner_blocks, 4 * query_blocks + 2 * inner_blocks]
    old_units = master[:, positions, :]
    working = low(old_units)
    matrices = tuple((to_matrix(working[:, edges[member]:edges[member + 1], :]) for member in range(6)))
    token_rows = tokens.astype(jnp.float32)
    grad_rows = out_grad.astype(jnp.float32)

    def wrapped(matrices_in, small_in, scale_in, tokens_in):
        return objective(matrices_in, small_in, scale_in, tokens_in, grad_rows, pair_lang)
    total, pullback, loss_sum = jax.vjp(wrapped, matrices, small_params, logit_scale[0], token_rows, has_aux=True)
    grad_mats, grad_small, grad_scale, grad_tokens = pullback(jnp.ones_like(total))
    block_size = math.gcd(64, 2 * PAIRS)

    def forward_block(block_in):
        return encode(block_in, matrices, small_params).astype(jnp.bfloat16)
    block_out = lax.map(forward_block, token_rows.reshape(-1, block_size, LEN, D)).reshape(2, PAIRS, LEN, D)
    grad_units = jnp.concatenate([from_matrix(grad_matrix, UR) for grad_matrix in grad_mats], axis=1)
    step_value = jnp.float32(STEP)
    fix_one = 1.0 - BETA_ONE ** step_value
    fix_two = 1.0 - BETA_TWO ** step_value
    new_units, new_one_units, new_two_units = adamw(old_units, grad_units, first_moment[:, positions, :], second_moment[:, positions, :], RATE_UNITS, DECAY, fix_one, fix_two)
    new_master = master.at[:, positions, :].set(new_units)
    new_first = first_moment.at[:, positions, :].set(new_one_units)
    new_second = second_moment.at[:, positions, :].set(new_two_units)
    new_copy = new_master.astype(jnp.bfloat16)
    new_small, new_small_first, new_small_second = adamw(small_params, grad_small, small_first, small_second, RATE_SMALL, 0.0, fix_one, fix_two)
    scale_new, scale_one, scale_two = adamw(logit_scale, grad_scale.reshape(1), scale_first, scale_second, RATE_SCALE, 0.0, fix_one, fix_two)
    loss_out = (loss_sum / (2 * PAIRS)).reshape(1)
    return (block_out, grad_tokens.astype(jnp.bfloat16), new_master, new_first, new_second, new_copy, new_small, new_small_first, new_small_second, scale_new, scale_one, scale_two, loss_out)
```

```python
import functools

import jax
import jax.numpy as jnp
from jax import lax
from jax.experimental import pallas as pl
from jax.experimental.pallas import tpu as pltpu
from jax.sharding import PartitionSpec as P

H = 12
HD = 64
FF = 3072
STEP = 10
ZS = 4
UR_ROWS = 128
LEN_ROWS = 64
VMEM_MOST = 60 << 20
MESH = pl.DeviceIdType.MESH

HIGHEST = lax.Precision.HIGHEST
BETA_ONE = 0.9
BETA_TWO = 0.999
ADAM_EPS = 1e-06
RATE_UNITS = 0.02
RATE_SMALL = 0.1
RATE_SCALE = 2.0
DECAY = 0.01
MARGIN = 0.3
NORM_EPS = 1e-06


def place():
    s = lax.axis_index("stream")
    b = lax.axis_index("batch")
    return s, b // 4, (b // 2) % 2, b % 2


def batch_of(z, y, c):
    return (z * 2 + y) * 2 + c


def greet(s, z, y, c, others):
    barrier = pltpu.get_barrier_semaphore()

    def hello(target):
        pl.semaphore_signal(barrier, inc=1, device_id=target, device_id_type=MESH)

    hello((s, batch_of(z, y, 1 - c)))
    hello((s, batch_of(z, 1 - y, c)))
    hello((1 - s, batch_of(z, y, c)))
    if others == "line":
        for far in range(1, ZS):

            @pl.when(z >= far)
            def _():
                hello((s, batch_of(z - far, y, c)))

            @pl.when(z + far < ZS)
            def _():
                hello((s, batch_of(z + far, y, c)))

        pl.semaphore_wait(barrier, 3 + ZS - 1)
    else:

        @pl.when(z >= 1)
        def _():
            hello((s, batch_of(z - 1, y, c)))

        @pl.when(z + 1 < ZS)
        def _():
            hello((s, batch_of(z + 1, y, c)))

        pl.semaphore_wait(barrier, 3 + (z + 2) // 3 + (5 - z) // 3)


GR = 80
GX = UR_ROWS - GR


def gather_kernel(own_ref, out_ref, low, stage_sem, zl_s, zl_r, zr_s, zr_r, y_s, y_r, x_s, x_r, ca_s, ca_r, cb_s, cb_r):
    s, z, y, c = place()
    slots = own_ref.shape[0]
    steps = ZS * slots
    base = pl.multiple_of(s * GX, 16)
    only = pl.multiple_of(s * GR, 16)
    theirs = pl.multiple_of((1 - s) * GR, 16)

    def at(zz, yy, cc, j):
        return batch_of(zz, yy, cc) * slots + j

    greet(s, z, y, c, "next")

    def push(src, row, start, size, send, recv, target):
        return pltpu.make_async_remote_copy(
            src_ref=src,
            dst_ref=out_ref.at[row, pl.ds(start, size)],
            send_sem=send,
            recv_sem=recv,
            device_id=target,
            device_id_type=MESH,
        )

    left = (s, batch_of(z - 1, y, c))
    right = (s, batch_of(z + 1, y, c))
    across = (s, batch_of(z, 1 - y, c))
    other = (1 - s, batch_of(z, y, c))
    sibling = (s, batch_of(z, y, 1 - c))

    def to_left(src, zz, j):
        row = at(zz, y, c, j)
        return push(src(row), row, base, GR, zl_s.at[zz, j], zl_r.at[zz, j], left)

    def to_right(src, zz, j):
        row = at(zz, y, c, j)
        return push(src(row), row, base, GR, zr_s.at[zz, j], zr_r.at[zz, j], right)

    def to_across(src, zz, j):
        row = at(zz, y, c, j)
        return push(src(row), row, base, GR, y_s.at[zz, j], y_r.at[zz, j], across)

    def to_other(zz, yy, j):
        row = at(zz, yy, c, j)
        return push(out_ref.at[row, pl.ds(only, GX)], row, only, GX, x_s.at[zz, yy, j], x_r.at[zz, yy, j], other)

    def to_sibling(zz, yy, j):
        row = at(zz, yy, c, j)
        return push(out_ref.at[row, pl.ds(base, GR)], row, base, GR, ca_s.at[zz, yy, j], ca_r.at[zz, yy, j], sibling)

    def rest_to_sibling(zz, yy, j):
        row = at(zz, yy, c, j)
        return push(out_ref.at[row, pl.ds(theirs, GX)], row, theirs, GX, cb_s.at[zz, yy, j], cb_r.at[zz, yy, j], sibling)

    def landed(row):
        return out_ref.at[row, pl.ds(base, GR)]

    def from_left(zz, j):
        row = at(zz, y, c, j)
        return push(landed(row), row, base, GR, zr_s.at[zz, j], zr_r.at[zz, j], right)

    def arrived_line(zz, j, onward):
        onward.start()
        to_across(landed, zz, j).start()
        to_other(zz, y, j).start()
        to_sibling(zz, y, j).start()

    def stage(j):
        return pltpu.make_async_copy(low.at[j], out_ref.at[at(z, y, c, j)], stage_sem.at[j])

    for j in range(slots):
        low[j] = own_ref[j].astype(jnp.bfloat16)
        mine = lambda row: low.at[j, pl.ds(base, GR)]

        @pl.when(z > 0)
        def _():
            to_left(mine, z, j).start()

        @pl.when(z < ZS - 1)
        def _():
            to_right(mine, z, j).start()

        to_across(mine, z, j).start()
        row = at(z, y, c, j)
        push(low.at[j, pl.ds(base, GR)], row, base, GR, ca_s.at[z, y, j], ca_r.at[z, y, j], sibling).start()
        push(low.at[j, pl.ds(theirs, GX)], row, theirs, GX, cb_s.at[z, y, j], cb_r.at[z, y, j], sibling).start()
        stage(j).start()

    def line_step(t):
        d = t // slots
        j = t % slots

        @pl.when((d >= 1) & (z - d >= 0))
        def _():
            zz = z - d
            to_right(landed, zz, j).wait_recv()

            @pl.when(z < ZS - 1)
            def _():
                to_right(landed, zz, j).start()

            to_across(landed, zz, j).start()
            to_other(zz, y, j).start()
            to_sibling(zz, y, j).start()

        @pl.when((d >= 1) & (z + d < ZS))
        def _():
            zz = z + d
            to_left(landed, zz, j).wait_recv()

            @pl.when(z > 0)
            def _():
                to_left(landed, zz, j).start()

            to_across(landed, zz, j).start()
            to_other(zz, y, j).start()
            to_sibling(zz, y, j).start()

    def across_one(zz, j):
        row = at(zz, 1 - y, c, j)
        push(landed(row), row, base, GR, y_s.at[zz, j], y_r.at[zz, j], across).wait_recv()
        to_other(zz, 1 - y, j).start()
        to_sibling(zz, 1 - y, j).start()

    def across_step(t):
        d = t // slots
        j = t % slots

        @pl.when(z - d >= 0)
        def _():
            across_one(z - d, j)

        @pl.when((d >= 1) & (z + d < ZS))
        def _():
            across_one(z + d, j)

    def other_one(zz, yy, j):
        row = at(zz, yy, c, j)
        push(
            out_ref.at[row, pl.ds(theirs, GX)], row, theirs, GX, x_s.at[zz, yy, j], x_r.at[zz, yy, j], other
        ).wait_recv()
        rest_to_sibling(zz, yy, j).start()

    def other_step(t, yy, first):
        d = t // slots
        j = t % slots

        @pl.when((d >= first) & (z - d >= 0))
        def _():
            other_one(z - d, yy, j)

        @pl.when((d >= 1) & (z + d < ZS))
        def _():
            other_one(z + d, yy, j)

    @pl.loop(0, steps + 3)
    def _(t):
        @pl.when(t < steps)
        def _():
            line_step(t)

        @pl.when((t >= 1) & (t < steps + 1))
        def _():
            across_step(t - 1)

        @pl.when((t >= 2) & (t < steps + 2))
        def _():
            other_step(t - 2, y, 1)

        @pl.when(t >= 3)
        def _():
            other_step(t - 3, 1 - y, 0)

    for j in range(slots):
        stage(j).wait()

    @pl.loop(0, steps)
    def _(t):
        zz = t // slots
        j = t % slots

        @pl.when((z > 0) & (zz >= z))
        def _():
            to_left(landed, zz, j).wait_send()

        @pl.when((z < ZS - 1) & (zz <= z))
        def _():
            to_right(landed, zz, j).wait_send()

        to_across(landed, zz, j).wait_send()

        @pl.when(zz != z)
        def _():
            to_other(zz, y, j).wait_send()

        to_other(zz, 1 - y, j).wait_send()
        for yy in range(2):
            to_sibling(zz, yy, j).wait_send()
            rest_to_sibling(zz, yy, j).wait_send()
            row = at(zz, yy, 1 - c, j)
            push(landed(row), row, base, GR, ca_s.at[zz, yy, j], ca_r.at[zz, yy, j], sibling).wait_recv()
            push(
                out_ref.at[row, pl.ds(theirs, GX)], row, theirs, GX, cb_s.at[zz, yy, j], cb_r.at[zz, yy, j], sibling
            ).wait_recv()


def gather_units(own):
    slots, rows, width = own.shape
    owners = lax.axis_size("batch")
    line = [pltpu.SemaphoreType.DMA((ZS, slots))] * 6
    plane = [pltpu.SemaphoreType.DMA((ZS, 2, slots))] * 6
    return pl.pallas_call(
        gather_kernel,
        name="gather_units",
        out_shape=jax.ShapeDtypeStruct((owners * slots, rows, width), jnp.bfloat16),
        in_specs=[pl.BlockSpec(memory_space=pltpu.VMEM)],
        out_specs=pl.BlockSpec(memory_space=pl.ANY),
        scratch_shapes=[pltpu.VMEM((slots, rows, width), jnp.bfloat16), pltpu.SemaphoreType.DMA((slots,))] + line + plane,
        compiler_params=pltpu.CompilerParams(collective_id=0, has_side_effects=True, vmem_limit_bytes=24 << 20),
    )(own)


RX = 32
RY = UR_ROWS - RX


def reduce_kernel(g_ref, small_ref, out_ref, small_out, held, c_in, x_in, y_in, z_in, f_in, t_acc, t_in,
                  p_sem, c_s, c_r, x_s, x_r, y_s, y_r, zl_s, zl_r, zr_s, zr_r, f_s, f_r, t_s, t_r):
    s, z, y, c = place()
    slots = out_ref.shape[0]
    steps = ZS * slots
    base = pl.multiple_of(s * RX, 16)
    only = pl.multiple_of(s * RY, 16)
    theirs = pl.multiple_of((1 - s) * RY, 16)
    left = (s, batch_of(z - 1, y, c))
    right = (s, batch_of(z + 1, y, c))
    across = (s, batch_of(z, 1 - y, c))
    other = (1 - s, batch_of(z, y, c))
    sibling = (s, batch_of(z, y, 1 - c))
    round_to = (sibling, across, other, (s, batch_of(z + 1 - 2 * (z % 2), y, c)), (s, batch_of((z + 2) % ZS, y, c)))
    greet(s, z, y, c, "line")

    def remote(src, dst, send, recv, target):
        return pltpu.make_async_remote_copy(
            src_ref=src, dst_ref=dst, send_sem=send, recv_sem=recv, device_id=target, device_id_type=MESH
        )

    def where_of(t):
        return (3 * (t // slots)) % ZS, t % slots

    def to_sibling(zz, yy, j):
        row = batch_of(zz, yy, 1 - c) * slots + j
        return remote(g_ref.at[row], c_in.at[zz, yy, j], c_s.at[zz, yy, j], c_r.at[zz, yy, j], sibling)

    def fetch(zz, yy, j):
        row = batch_of(zz, yy, c) * slots + j
        return pltpu.make_async_copy(g_ref.at[row], held.at[zz, yy, j], p_sem.at[zz, yy, j])

    def to_other(zz, yy, j):
        return remote(held.at[zz, yy, j, pl.ds(theirs, RX)], x_in.at[zz, yy, j], x_s.at[zz, yy, j], x_r.at[zz, yy, j], other)

    def to_across(zz, j):
        return remote(held.at[zz, 1 - y, j, pl.ds(base, RY)], y_in.at[zz, j], y_s.at[zz, j], y_r.at[zz, j], across)

    def to_left(zz, j):
        return remote(held.at[zz, y, j, pl.ds(base, RY)], z_in.at[1, zz, j], zl_s.at[zz, j], zl_r.at[zz, j], left)

    def to_right(zz, j):
        return remote(held.at[zz, y, j, pl.ds(base, RY)], z_in.at[0, zz, j], zr_s.at[zz, j], zr_r.at[zz, j], right)

    def final(j):
        return remote(held.at[z, y, j, pl.ds(base, RY)], f_in.at[j], f_s.at[j], f_r.at[j], other)

    def turn(r):
        return remote(t_acc.at[r], t_in.at[r], t_s.at[r], t_r.at[r], round_to[r])

    def add(zz, yy, j, start, size, got):
        mine = held.at[zz, yy, j, pl.ds(start, size)]
        mine[...] = (mine[...].astype(jnp.float32) + got[...].astype(jnp.float32)).astype(jnp.bfloat16)

    @pl.loop(0, steps)
    def _(t):
        zz, j = where_of(t)
        for yy in (1 - y, y):
            to_sibling(zz, yy, j).start()
            fetch(zz, yy, j).start()

    t_acc[0] = small_ref[...]

    def core_stage(t):
        zz, j = where_of(t)
        for yy in (1 - y, y):
            fetch(zz, yy, j).wait()
            to_sibling(zz, yy, j).wait_recv()
            add(zz, yy, j, 0, UR_ROWS, c_in.at[zz, yy, j])
            to_other(zz, yy, j).start()

    def other_stage(t):
        zz, j = where_of(t)
        for yy in (1 - y, y):
            to_other(zz, yy, j).wait_recv()
            add(zz, yy, j, only, RX, x_in.at[zz, yy, j])
        to_across(zz, j).start()

    def across_stage(t):
        zz, j = where_of(t)
        to_across(zz, j).wait_recv()
        add(zz, y, j, base, RY, y_in.at[zz, j])

    def from_left(zz, j):
        to_right(zz, j).wait_recv()
        add(zz, y, j, base, RY, z_in.at[0, zz, j])

    def from_right(zz, j):
        to_left(zz, j).wait_recv()
        add(zz, y, j, base, RY, z_in.at[1, zz, j])

    def line_stage(t, hops):
        zz, j = where_of(t)

        @pl.when((zz > z) & (z == hops))
        def _():
            if hops > 0:
                from_left(zz, j)
            to_right(zz, j).start()

        @pl.when((zz < z) & (ZS - 1 - z == hops))
        def _():
            if hops > 0:
                from_right(zz, j)
            to_left(zz, j).start()

        @pl.when((zz == z) & (3 - ((z + 2) // 3) * ((5 - z) // 3) == hops))
        def _():
            @pl.when(z > 0)
            def _():
                from_left(zz, j)

            @pl.when(z < ZS - 1)
            def _():
                from_right(zz, j)

            final(j).start()

    def final_stage(t):
        zz, j = where_of(t)

        @pl.when(zz == z)
        def _():
            final(j).wait_recv()
            f32 = jnp.float32
            out_ref[j, pl.ds(only, RX)] = held[z, y, j, pl.ds(only, RX)].astype(f32)
            shared = f_in[j, pl.ds(pl.multiple_of(s * RX, 16), RY - RX)].astype(f32)
            out_ref[j, pl.ds(RX, RY - RX)] = held[z, y, j, pl.ds(RX, RY - RX)].astype(f32) + shared
            out_ref[j, pl.ds(theirs, RX)] = f_in[j, pl.ds(pl.multiple_of((1 - s) * (RY - RX), 16), RX)].astype(f32)

    @pl.loop(0, steps + 6)
    def _(i):
        @pl.when(i < steps)
        def _():
            core_stage(i)

        @pl.when((i >= 1) & (i < steps + 1))
        def _():
            other_stage(i - 1)

        @pl.when((i >= 2) & (i < steps + 2))
        def _():
            across_stage(i - 2)

        for hops in range(ZS):

            @pl.when((i >= 2 + hops) & (i < steps + 2 + hops))
            def _():
                line_stage(i - 2 - hops, hops)

        @pl.when(i >= 6)
        def _():
            final_stage(i - 6)

        for r in range(5):

            @pl.when(i == 3 * r)
            def _():
                turn(r).start()

            @pl.when(i == 3 * r + 2)
            def _():
                turn(r).wait()
                t_acc[r + 1] = t_acc[r] + t_in[r]

    small_out[...] = t_acc[5]

    @pl.loop(0, steps)
    def _(t):
        zz, j = where_of(t)
        for yy in range(2):
            to_sibling(zz, yy, j).wait_send()
            to_other(zz, yy, j).wait_send()
        to_across(zz, j).wait_send()

        @pl.when(zz > z)
        def _():
            to_right(zz, j).wait_send()

        @pl.when(zz < z)
        def _():
            to_left(zz, j).wait_send()

        @pl.when(zz == z)
        def _():
            final(j).wait_send()


def reduce_units(grads, small, slots):
    owners = lax.axis_size("batch")
    _, rows, width = grads.shape
    bf, f32 = jnp.bfloat16, jnp.float32
    dma = pltpu.SemaphoreType.DMA
    return pl.pallas_call(
        reduce_kernel,
        name="reduce_units",
        out_shape=[jax.ShapeDtypeStruct((slots, rows, width), f32), jax.ShapeDtypeStruct(small.shape, f32)],
        in_specs=[pl.BlockSpec(memory_space=pl.ANY), pl.BlockSpec(memory_space=pltpu.VMEM)],
        out_specs=[pl.BlockSpec(memory_space=pltpu.VMEM)] * 2,
        scratch_shapes=[
            pltpu.VMEM((ZS, 2, slots, rows, width), bf),
            pltpu.VMEM((ZS, 2, slots, rows, width), bf),
            pltpu.VMEM((ZS, 2, slots, RX, width), bf),
            pltpu.VMEM((ZS, slots, RY, width), bf),
            pltpu.VMEM((2, ZS, slots, RY, width), bf),
            pltpu.VMEM((slots, RY, width), bf),
            pltpu.VMEM((6,) + small.shape, f32),
            pltpu.VMEM((5,) + small.shape, f32),
        ]
        + [dma((ZS, 2, slots))] * 5
        + [dma((ZS, slots))] * 6
        + [dma((slots,))] * 2
        + [dma((5,))] * 2,
        compiler_params=pltpu.CompilerParams(collective_id=2, has_side_effects=True, vmem_limit_bytes=VMEM_MOST),
    )(grads, small)


def rank_kernel(scale_ref, cls_ref, lang_row, lang_col, dc_ref, stats_ref, every, weights, z_s, z_r, pair_s, pair_r):
    s, z, y, c = place()
    sents, width = cls_ref.shape
    pairs = lang_row.shape[1]
    greet(s, z, y, c, "line")
    cls = cls_ref[...]
    root = lax.rsqrt(jnp.sum(cls * cls, axis=-1, keepdims=True) + NORM_EPS)
    unit = cls * root
    every[s, z, y, c] = unit.astype(jnp.bfloat16)

    def along(to, frm):
        return pltpu.make_async_remote_copy(
            src_ref=every.at[s, frm, y, c], dst_ref=every.at[s, frm, y, c], send_sem=z_s.at[to], recv_sem=z_r.at[frm],
            device_id=(s, batch_of(to, y, c)), device_id_type=MESH,
        )

    for to in range(ZS):

        @pl.when(z != to)
        def _():
            along(to, z).start()

    for frm in range(ZS):

        @pl.when(z != frm)
        def _():
            along(frm, frm).wait_recv()

    def swap(view, n, target):
        copy = pltpu.make_async_remote_copy(
            src_ref=view, dst_ref=view, send_sem=pair_s.at[n], recv_sem=pair_r.at[n], device_id=target,
            device_id_type=MESH,
        )
        copy.start()
        return copy

    first = swap(every.at[s, :, y, c], 0, (s, batch_of(z, 1 - y, c)))
    first.wait_recv()
    then = swap(every.at[s, :, :, c], 1, (1 - s, batch_of(z, y, c)))
    then.wait_recv()
    last = swap(every.at[:, :, :, c], 2, (s, batch_of(z, y, 1 - c)))
    last.wait_recv()
    scale = scale_ref[0]
    e_zero = every[0].reshape(pairs, width)
    e_one = every[1].reshape(pairs, width)
    cosines = lax.dot_general(e_zero, e_one, (((1,), (1,)), ((), ())), preferred_element_type=jnp.float32)
    own = lax.broadcasted_iota(jnp.int32, (pairs, pairs), 0) == lax.broadcasted_iota(jnp.int32, (pairs, pairs), 1)
    same = lang_col[...] == lang_row[...]
    diagonal = jnp.where(own, 1.0, 0.0)
    shifted = cosines - MARGIN * diagonal
    logits = scale * shifted
    masked = jnp.where(same, logits, -1e30)
    both = -2.0 * diagonal
    total = -2.0 * jnp.sum(logits * diagonal)
    for axis in range(2):
        top = jnp.max(masked, axis=axis, keepdims=True)
        grown = jnp.where(same, jnp.exp(masked - top), 0.0)
        summed = jnp.sum(grown, axis=axis, keepdims=True)
        both += grown / summed
        total += jnp.sum(jnp.log(summed) + top)
    line = lax.broadcasted_iota(jnp.int32, stats_ref.shape, 0)
    stats_ref[...] = jnp.where(line == 0, total, jnp.sum(both * shifted))
    weights[0] = both
    weights[1] = both.T
    rows = weights[s, pl.ds(pl.multiple_of(batch_of(z, y, c) * sents, 16), sents), :]
    partners = every[1 - s].reshape(pairs, width)
    high = rows.astype(jnp.bfloat16)
    rest = (rows - high.astype(jnp.float32)).astype(jnp.bfloat16)
    mix = (((1,), (0,)), ((), ()))
    de = lax.dot_general(high, partners, mix, preferred_element_type=jnp.float32)
    de += lax.dot_general(rest, partners, mix, preferred_element_type=jnp.float32)
    de = scale * de
    dc_ref[...] = (de - unit * jnp.sum(unit * de, axis=-1, keepdims=True)) * root
    for to in range(ZS):

        @pl.when(z != to)
        def _():
            along(to, z).wait_send()

    first.wait_send()
    then.wait_send()
    last.wait_send()


def rank_loss(cls, scale, langs):
    sents, width = cls.shape
    pairs = langs.shape[0]
    dma = pltpu.SemaphoreType.DMA
    vmem = pl.BlockSpec(memory_space=pltpu.VMEM)
    return pl.pallas_call(
        rank_kernel,
        name="rank_loss",
        out_shape=[jax.ShapeDtypeStruct((sents, width), jnp.float32), jax.ShapeDtypeStruct((8, 128), jnp.float32)],
        in_specs=[pl.BlockSpec(memory_space=pltpu.SMEM), vmem, vmem, vmem],
        out_specs=[vmem, vmem],
        scratch_shapes=[
            pltpu.VMEM((2, ZS, 2, 2, sents, width), jnp.bfloat16),
            pltpu.VMEM((2, pairs, pairs), jnp.float32),
            dma((ZS,)), dma((ZS,)), dma((3,)), dma((3,)),
        ],
        compiler_params=pltpu.CompilerParams(collective_id=1, has_side_effects=True, vmem_limit_bytes=24 << 20),
    )(scale, cls, langs.reshape(1, pairs), langs.reshape(pairs, 1))


TILE = 256
GROUP = LEN_ROWS


def dot_nn(a, b):
    return lax.dot_general(a, b, (((1,), (0,)), ((), ())), preferred_element_type=jnp.float32)


def dot_nt(a, b):
    return lax.dot_general(a, b, (((1,), (1,)), ((), ())), preferred_element_type=jnp.float32)


def dot_tn(a, b):
    return lax.dot_general(a, b, (((0,), (0,)), ((), ())), preferred_element_type=jnp.float32)


def gelu_parts(u):
    t = 1.0 / (1.0 + (0.3275911 * 0.7071067811865476) * jnp.abs(u))
    bell = jnp.exp(-0.5 * u * u)
    tail = t * (
        0.127414796 + t * (-0.142248368 + t * (0.7107068705 + t * (-0.7265760135 + t * 0.5307027145)))
    ) * bell
    phi_sum = jnp.where(u >= 0.0, 1.0 - tail, tail)
    return u * phi_sum, phi_sum + u * (0.3989422804014327 * bell)


def norm_parts(resid):
    centre = jnp.mean(resid, axis=-1, keepdims=True)
    centred = resid - centre
    rs = lax.rsqrt(jnp.mean(centred * centred, axis=-1, keepdims=True) + NORM_EPS)
    return centred * rs, rs


def norm_back(dy, unit, rs, gain):
    gd = gain * dy
    return rs * (gd - jnp.mean(gd, axis=-1, keepdims=True) - unit * jnp.mean(gd * unit, axis=-1, keepdims=True))


def lane_halves():
    lane = lax.broadcasted_iota(jnp.int32, (1, 2 * HD), 1)
    first = jnp.where(lane < HD, 1.0, 0.0)
    return first.astype(jnp.bfloat16), (1.0 - first).astype(jnp.bfloat16), lane < HD


def both_heads(rows, first, second):
    return jnp.concatenate([rows * first, rows * second], axis=0)


def fetch_all(pos_ref, units_hbm, held, sems, edges, order):
    for m in order:
        for u in range(edges[m], edges[m + 1]):
            pltpu.make_async_copy(units_hbm.at[pos_ref[u]], held.at[u], sems.at[m]).start()


def fetch_wait(units_hbm, held, sems, edges, m):
    lo, hi = edges[m], edges[m + 1]
    pltpu.make_async_copy(units_hbm.at[pl.ds(0, hi - lo)], held.at[pl.ds(lo, hi - lo)], sems.at[m]).wait()


def matrix_of(held, lo, hi):
    block = held[lo:hi]
    return block.reshape((hi - lo) * block.shape[1], block.shape[2])


def forward_kernel(
    edges, pos_ref, x_ref, small_ref, units_hbm,
    out_ref, q_ref, k_ref, v_ref, probs_ref, ctx_ref, n1_ref, rs1_ref, hb_ref, act_ref, slope_ref, n2_ref, rs2_ref,
    cls_ref, held, sems,
):
    first_tile = pl.program_id(0) == 0
    width = x_ref.shape[1]

    def need(m):
        @pl.when(first_tile)
        def _():
            fetch_wait(units_hbm, held, sems, edges, m)

    @pl.when(first_tile)
    def _():
        fetch_all(pos_ref, units_hbm, held, sems, edges, range(6))

    inner_rows = FF // width
    row = lambda r: small_ref[r : r + 1, :]
    x = x_ref[...]
    need(0)
    q = (dot_nn(x, matrix_of(held, edges[0], edges[1])) + row(0)).astype(jnp.bfloat16)
    q_ref[...] = q
    need(1)
    k = dot_nn(x, matrix_of(held, edges[1], edges[2])).astype(jnp.bfloat16)
    k_ref[...] = k
    need(2)
    v = (dot_nn(x, matrix_of(held, edges[2], edges[3])) + row(1)).astype(jnp.bfloat16)
    v_ref[...] = v
    first, second, is_first = lane_halves()
    for sent in range(TILE // GROUP):
        rows = slice(sent * GROUP, (sent + 1) * GROUP)
        for pair in range(H // 2):
            lanes = slice(pair * 2 * HD, (pair + 1) * 2 * HD)
            qq = both_heads(q[rows, lanes], first, second)
            scores = dot_nt(k[rows, lanes], qq) * HD ** (-0.5)
            scores = scores - jnp.max(scores, axis=0, keepdims=True)
            grown = jnp.exp(scores)
            probs = (grown * (1.0 / jnp.sum(grown, axis=0, keepdims=True))).astype(jnp.bfloat16)
            probs_ref[sent, pair] = probs
            mixed = dot_tn(probs, v[rows, lanes])
            ctx_ref[rows, lanes] = jnp.where(is_first, mixed[:GROUP], mixed[GROUP:]).astype(jnp.bfloat16)
    need(3)
    attended = dot_nn(ctx_ref[...], matrix_of(held, edges[3], edges[4])) + row(2)
    n1, rs1 = norm_parts(x.astype(jnp.float32) + attended)
    n1_ref[...] = n1
    rs1_ref[...] = rs1
    h1 = n1 * row(4 + inner_rows) + row(5 + inner_rows)
    hb = h1.astype(jnp.bfloat16)
    hb_ref[...] = hb
    need(4)
    need(5)
    per = (edges[5] - edges[4]) // inner_rows
    total = h1 + row(3 + inner_rows)
    for part in range(inner_rows):
        cols = slice(part * width, (part + 1) * width)
        w_in = matrix_of(held, edges[4] + part * per, edges[4] + (part + 1) * per)
        u = dot_nt(hb, w_in) + row(3 + part)
        value, slope = gelu_parts(u)
        act = value.astype(jnp.bfloat16)
        act_ref[:, cols] = act
        slope_ref[:, cols] = slope.astype(jnp.bfloat16)
        total += dot_nn(act, matrix_of(held, edges[5] + part * per, edges[5] + (part + 1) * per))
    n2, rs2 = norm_parts(total)
    n2_ref[...] = n2
    rs2_ref[...] = rs2
    y = n2 * row(6 + inner_rows) + row(7 + inner_rows)
    out_ref[...] = y.astype(jnp.bfloat16)
    for sent in range(TILE // GROUP):
        cls_ref[0, sent : sent + 1, :] = y[sent * GROUP : sent * GROUP + 1, :]


def tiles(shape):
    rest = len(shape) - 1
    return pl.BlockSpec((TILE,) + tuple(shape[1:]), lambda i, *_: (i,) + (0,) * rest)


def whole(shape):
    return pl.BlockSpec(tuple(shape), lambda i, *_: (0,) * len(shape))


def run_forward(x, small, units, positions, edges):
    rows, width = x.shape
    count = rows // TILE
    sents = TILE // GROUP
    bf, f32 = jnp.bfloat16, jnp.float32
    probs_shape = (rows // GROUP, H // 2, GROUP, 2 * HD)
    outs = [
        ((rows, width), bf), ((rows, width), bf), ((rows, width), bf), ((rows, width), bf), (probs_shape, bf),
        ((rows, width), bf), ((rows, width), f32), ((rows, 1), f32), ((rows, width), bf), ((rows, FF), bf),
        ((rows, FF), bf), ((rows, width), f32), ((rows, 1), f32), ((count, sents, width), f32),
    ]
    specs = [tiles(shape) for shape, _ in outs]
    specs[4] = pl.BlockSpec((sents,) + probs_shape[1:], lambda i, *_: (i, 0, 0, 0))
    specs[13] = pl.BlockSpec((1, sents, width), lambda i, *_: (i, 0, 0))
    return pl.pallas_call(
        functools.partial(forward_kernel, edges),
        name="layer_forward",
        grid_spec=pltpu.PrefetchScalarGridSpec(
            num_scalar_prefetch=1,
            grid=(count,),
            in_specs=[tiles(x.shape), whole(small.shape), pl.BlockSpec(memory_space=pl.ANY)],
            out_specs=specs,
            scratch_shapes=[pltpu.VMEM((edges[6],) + units.shape[1:], bf), pltpu.SemaphoreType.DMA((6,))],
        ),
        out_shape=[jax.ShapeDtypeStruct(shape, kind) for shape, kind in outs],
        compiler_params=pltpu.CompilerParams(vmem_limit_bytes=VMEM_MOST),
    )(positions, x, small, units)


def backward_kernel(
    edges, pos_ref, og_ref, dc_ref, small_ref, q_ref, k_ref, v_ref, probs_ref, n1_ref, rs1_ref, slope_ref, n2_ref,
    rs2_ref, units_hbm,
    dx_ref, df_ref, du_ref, da_ref, dq_ref, dk_ref, dv_ref, gsmall_ref, dy_ref, dctx_ref, held, sems,
):
    first_tile = pl.program_id(0) == 0
    width = og_ref.shape[1]
    inner_rows = FF // width

    def need(m):
        @pl.when(first_tile)
        def _():
            fetch_wait(units_hbm, held, sems, edges, m)

    @pl.when(first_tile)
    def _():
        fetch_all(pos_ref, units_hbm, held, sems, edges, (5, 4, 3, 0, 1, 2))
        gsmall_ref[...] = jnp.zeros_like(gsmall_ref)

    row = lambda r: small_ref[r : r + 1, :]

    def add_small(r, values):
        gsmall_ref[r : r + 1, :] += jnp.sum(values.astype(jnp.float32), axis=0, keepdims=True)

    dy_ref[...] = og_ref[...].astype(jnp.float32)
    for sent in range(TILE // GROUP):
        dy_ref[sent * GROUP : sent * GROUP + 1, :] += dc_ref[0, sent : sent + 1, :]
    dy = dy_ref[...]
    n2 = n2_ref[...]
    add_small(6 + inner_rows, dy * n2)
    add_small(7 + inner_rows, dy)
    dr2 = norm_back(dy, n2, rs2_ref[...], row(6 + inner_rows))
    df = dr2.astype(jnp.bfloat16)
    df_ref[...] = df
    add_small(3 + inner_rows, df)
    need(5)
    need(4)
    per = (edges[5] - edges[4]) // inner_rows
    dh1 = dr2
    for part in range(inner_rows):
        cols = slice(part * width, (part + 1) * width)
        da = dot_nt(df, matrix_of(held, edges[5] + part * per, edges[5] + (part + 1) * per))
        du = (da * slope_ref[:, cols].astype(jnp.float32)).astype(jnp.bfloat16)
        du_ref[:, cols] = du
        add_small(3 + part, du)
        dh1 += dot_nn(du, matrix_of(held, edges[4] + part * per, edges[4] + (part + 1) * per))
    n1 = n1_ref[...]
    add_small(4 + inner_rows, dh1 * n1)
    add_small(5 + inner_rows, dh1)
    dr1 = norm_back(dh1, n1, rs1_ref[...], row(4 + inner_rows))
    dattn = dr1.astype(jnp.bfloat16)
    da_ref[...] = dattn
    add_small(2, dattn)
    need(3)
    dctx_ref[...] = dot_nt(dattn, matrix_of(held, edges[3], edges[4])).astype(jnp.bfloat16)
    first, second, is_first = lane_halves()
    for sent in range(TILE // GROUP):
        rows = slice(sent * GROUP, (sent + 1) * GROUP)
        for pair in range(H // 2):
            lanes = slice(pair * 2 * HD, (pair + 1) * 2 * HD)
            dcc = both_heads(dctx_ref[rows, lanes], first, second)
            qq = both_heads(q_ref[rows, lanes], first, second)
            low = probs_ref[sent, pair]
            probs = low.astype(jnp.float32)
            dprobs = dot_nt(v_ref[rows, lanes], dcc)
            dscores = probs * (dprobs - jnp.sum(dprobs * probs, axis=0, keepdims=True))
            dscores = dscores.astype(jnp.bfloat16)
            dv_ref[rows, lanes] = dot_nn(low, dcc).astype(jnp.bfloat16)
            dk_ref[rows, lanes] = (dot_nn(dscores, qq) * HD ** (-0.5)).astype(jnp.bfloat16)
            mixed = dot_tn(dscores, k_ref[rows, lanes]) * HD ** (-0.5)
            dq_ref[rows, lanes] = jnp.where(is_first, mixed[:GROUP], mixed[GROUP:]).astype(jnp.bfloat16)
    dx = dr1
    for m, (ref, r) in enumerate(((dq_ref, 0), (dk_ref, None), (dv_ref, 1))):
        need(m)
        rows = ref[...]
        if r is not None:
            add_small(r, rows)
        dx += dot_nt(rows, matrix_of(held, edges[m], edges[m + 1]))
    dx_ref[...] = dx.astype(jnp.bfloat16)


def run_backward(og, dc, small, saved, units, positions, edges):
    rows, width = og.shape
    count = rows // TILE
    sents = TILE // GROUP
    bf, f32 = jnp.bfloat16, jnp.float32
    _, q, k, v, probs, _, n1, rs1, _, _, slope, n2, rs2, _ = saved
    ins = [og, dc, small, q, k, v, probs, n1, rs1, slope, n2, rs2]
    in_specs = [tiles(a.shape) for a in ins]
    in_specs[1] = pl.BlockSpec((1, sents, width), lambda i, *_: (i, 0, 0))
    in_specs[2] = whole(small.shape)
    in_specs[6] = pl.BlockSpec((sents,) + probs.shape[1:], lambda i, *_: (i, 0, 0, 0))
    outs = [((rows, width), bf)] * 2 + [((rows, FF), bf)] + [((rows, width), bf)] * 4 + [(small.shape, f32)]
    specs = [tiles(shape) for shape, _ in outs]
    specs[7] = whole(small.shape)
    return pl.pallas_call(
        functools.partial(backward_kernel, edges),
        name="layer_backward",
        grid_spec=pltpu.PrefetchScalarGridSpec(
            num_scalar_prefetch=1,
            grid=(count,),
            in_specs=in_specs + [pl.BlockSpec(memory_space=pl.ANY)],
            out_specs=specs,
            scratch_shapes=[
                pltpu.VMEM((TILE, width), f32),
                pltpu.VMEM((TILE, width), bf),
                pltpu.VMEM((edges[6],) + units.shape[1:], bf),
                pltpu.SemaphoreType.DMA((6,)),
            ],
        ),
        out_shape=[jax.ShapeDtypeStruct(shape, kind) for shape, kind in outs],
        compiler_params=pltpu.CompilerParams(vmem_limit_bytes=VMEM_MOST),
    )(positions, *ins, units)


def weight_grad_kernel(
    edges, pos_ref, x_hbm, ctx_hbm, du_hbm, act_hbm, dq_hbm, dk_hbm, dv_hbm, da_hbm, hb_hbm, df_hbm, out_hbm,
    x_v, ctx_v, du_v, act_v, right, staged, sems, out_sems,
):
    width = x_v.shape[1]
    unit_rows = out_hbm.shape[1]
    inner_rows = FF // width
    loads = [(act_hbm, act_v), (df_hbm, right.at[5]), (du_hbm, du_v), (hb_hbm, right.at[4]), (ctx_hbm, ctx_v),
             (da_hbm, right.at[3]), (x_hbm, x_v), (dq_hbm, right.at[0]), (dk_hbm, right.at[1]), (dv_hbm, right.at[2])]
    copies = [pltpu.make_async_copy(src, dst, sems.at[i]) for i, (src, dst) in enumerate(loads)]
    for copy in copies:
        copy.start()
    waited = set()
    per = width // unit_rows
    work = []
    for part in range(inner_rows):
        work.append((act_v, part, 5, edges[5] + part * per, (0, 1)))
    for part in range(inner_rows):
        work.append((du_v, part, 4, edges[4] + part * per, (2, 3)))
    work.append((ctx_v, 0, 3, edges[3], (4, 5)))
    work.append((x_v, 0, 0, edges[0], (6, 7)))
    work.append((x_v, 0, 1, edges[1], (6, 8)))
    work.append((x_v, 0, 2, edges[2], (6, 9)))
    for step, (left, part, m, unit, needs) in enumerate(work):
        slot = step % 2
        for n in needs:
            if n not in waited:
                copies[n].wait()
                waited.add(n)
        if step >= 2:
            pltpu.make_async_copy(out_hbm.at[pl.ds(0, per)], staged.at[slot], out_sems.at[slot]).wait()
        half = per // 2
        for piece in range(2):
            cols = slice(part * width + piece * half * unit_rows, part * width + (piece + 1) * half * unit_rows)
            block = dot_tn(left[:, cols], right[m]).astype(jnp.bfloat16)
            staged[slot, piece * half : (piece + 1) * half] = block.reshape(half, unit_rows, width)
        for n in range(per):
            pltpu.make_async_copy(staged.at[slot, n], out_hbm.at[pos_ref[unit + n]], out_sems.at[slot]).start()
    for slot in range(2):
        pltpu.make_async_copy(out_hbm.at[pl.ds(0, per)], staged.at[slot], out_sems.at[slot]).wait()


def run_weight_grads(x, saved, back, positions, edges, places, unit_rows):
    rows, width = x.shape
    bf = jnp.bfloat16
    ctx, hb, act = saved[5], saved[8], saved[9]
    _, df, du, da, dq, dk, dv, _ = back
    per = width // unit_rows
    anyw = pl.BlockSpec(memory_space=pl.ANY)
    return pl.pallas_call(
        functools.partial(weight_grad_kernel, edges),
        name="weight_grads",
        in_specs=[pl.BlockSpec(memory_space=pltpu.SMEM)] + [anyw] * 10,
        out_specs=anyw,
        scratch_shapes=[
            pltpu.VMEM((rows, width), bf), pltpu.VMEM((rows, width), bf), pltpu.VMEM((rows, FF), bf),
            pltpu.VMEM((rows, FF), bf), pltpu.VMEM((6, rows, width), bf),
            pltpu.VMEM((2, per, unit_rows, width), bf),
            pltpu.SemaphoreType.DMA((10,)), pltpu.SemaphoreType.DMA((2,)),
        ],
        out_shape=jax.ShapeDtypeStruct((places, unit_rows, width), bf),
        compiler_params=pltpu.CompilerParams(vmem_limit_bytes=VMEM_MOST),
    )(positions, x, ctx, du, act, dq, dk, dv, da, hb, df)


def unit_positions(owner_list, slot_count):
    unit_total = owner_list.shape[0]
    same_owner = owner_list[:, None] == owner_list[None, :]
    ordinal = jnp.arange(unit_total, dtype=jnp.int32)
    earlier = ordinal[None, :] < ordinal[:, None]
    slot_number = jnp.sum(jnp.where(same_owner & earlier, 1, 0), axis=1).astype(jnp.int32)
    return owner_list * slot_count + slot_number


def adamw(weight_in, gradient, moment_one, moment_two, rate_value, decay_value, fix_one, fix_two):
    new_one = BETA_ONE * moment_one + (1.0 - BETA_ONE) * gradient
    new_two = BETA_TWO * moment_two + (1.0 - BETA_TWO) * gradient * gradient
    stepped = new_one / fix_one / (jnp.sqrt(new_two / fix_two) + ADAM_EPS)
    return (weight_in - rate_value * (stepped + decay_value * weight_in), new_one, new_two)


def any_size_units(own, positions, owners):
    slots, rows, width = own.shape
    table = jnp.arange(owners * slots, dtype=jnp.int32)[:, None] == positions[None, :]
    bands = lax.all_to_all(
        own.transpose(1, 0, 2).astype(jnp.bfloat16), "batch", split_axis=0, concat_axis=1, tiled=True
    )
    ordered = jnp.einsum(
        "rpd,pu->rud", bands, table.astype(jnp.bfloat16), preferred_element_type=jnp.float32
    ).astype(jnp.bfloat16)
    return lax.all_gather(ordered, "batch", axis=0, tiled=True).transpose(1, 0, 2)


def any_size_sums(grads, positions, owners, slots):
    table = jnp.arange(owners * slots, dtype=jnp.int32)[:, None] == positions[None, :]
    pieces = lax.psum_scatter(grads.transpose(1, 0, 2).astype(jnp.float32), "batch", scatter_dimension=0, tiled=True)
    summed = lax.psum(pieces.astype(jnp.bfloat16), "stream").astype(jnp.float32)
    send_rows = jnp.einsum("rud,pu->rpd", summed, table.astype(jnp.float32), precision=HIGHEST)
    owned = lax.all_to_all(send_rows.astype(jnp.bfloat16), "batch", split_axis=1, concat_axis=0, tiled=True)
    return owned.astype(jnp.float32).transpose(1, 0, 2)


def any_size_rank(cls, scale, langs, owners):
    sents, width = cls.shape
    root = lax.rsqrt(jnp.sum(cls * cls, axis=-1, keepdims=True) + NORM_EPS)
    unit = cls * root
    every = lax.all_gather(unit.astype(jnp.bfloat16), "batch", axis=0, tiled=True)
    every = lax.all_gather(every, "stream", axis=0)
    cosines = jnp.dot(every[0], every[1].T, preferred_element_type=jnp.float32)
    diagonal = jnp.eye(cosines.shape[0], dtype=jnp.float32)
    same = langs[:, None] == langs[None, :]
    shifted = cosines - MARGIN * diagonal
    logits = scale[0] * shifted
    masked = jnp.where(same, logits, -1e30)
    both = -2.0 * diagonal
    total = -2.0 * jnp.sum(logits * diagonal)
    for axis in range(2):
        top = jnp.max(masked, axis=axis, keepdims=True)
        grown = jnp.where(same, jnp.exp(masked - top), 0.0)
        summed = jnp.sum(grown, axis=axis, keepdims=True)
        both += grown / summed
        total += jnp.sum(jnp.log(summed) + top)
    s = lax.axis_index("stream")
    turned = jnp.where(s == 0, both, both.T)
    rows = lax.dynamic_slice_in_dim(turned, lax.axis_index("batch") * sents, sents)
    partners = lax.dynamic_index_in_dim(every, 1 - s, keepdims=False).astype(jnp.float32)
    de = scale[0] * jnp.dot(rows, partners, precision=HIGHEST)
    dc = (de - unit * jnp.sum(unit * de, axis=-1, keepdims=True)) * root
    return dc, total, jnp.sum(both * shifted)


def per_device(
    tokens, out_grad, master, first_moment, second_moment, small_params, small_first, small_second, logit_scale,
    scale_first, scale_second, pair_lang, unit_owner,
):
    owners = lax.axis_size("batch")
    here_batch = lax.axis_index("batch")
    unit_rows, slot_count, width = master.shape
    query_blocks = width // unit_rows
    inner_blocks = FF // unit_rows
    edges = [query_blocks * n for n in range(5)]
    edges += [edges[4] + inner_blocks, edges[4] + 2 * inner_blocks]
    units_total = unit_owner.shape[0]
    positions = unit_positions(unit_owner, slot_count)
    on_block = owners == 4 * ZS
    own = master.transpose(1, 0, 2)
    if on_block:
        units, where, places = gather_units(own), positions, owners * slot_count
    else:
        units = any_size_units(own, positions, owners)
        where, places = jnp.arange(units_total, dtype=jnp.int32), units_total
    sentences, length = tokens.shape[1], tokens.shape[2]
    flat = tokens.reshape(sentences * length, width)
    saved = run_forward(flat, small_params, units, where, edges)
    cls = saved[13]
    if on_block:
        dc, stats = rank_loss(cls.reshape(sentences, width), logit_scale, pair_lang)
        loss_total, grad_scale = stats[0, :1], stats[1, :1]
    else:
        dc, loss_total, grad_scale = any_size_rank(cls.reshape(sentences, width), logit_scale, pair_lang, owners)
        loss_total, grad_scale = loss_total.reshape(1), grad_scale.reshape(1)
    back = run_backward(
        out_grad.reshape(sentences * length, width), dc.reshape(cls.shape), small_params, saved, units, where, edges
    )
    grads = run_weight_grads(flat, saved, back, where, edges, places, unit_rows)
    if on_block:
        owned_grad, small_total = reduce_units(grads, back[7], slot_count)
    else:
        owned_grad = any_size_sums(grads, positions, owners, slot_count)
        small_total = lax.psum(back[7], ("stream", "batch"))
    step_value = float(STEP)
    fix_one = 1.0 - BETA_ONE**step_value
    fix_two = 1.0 - BETA_TWO**step_value
    my_places = here_batch * slot_count + jnp.arange(slot_count, dtype=jnp.int32)
    filled = jnp.any(my_places[:, None] == positions[None, :], axis=1)[:, None, None]
    first_in, second_in = first_moment.transpose(1, 0, 2), second_moment.transpose(1, 0, 2)
    moved = adamw(own, owned_grad, first_in, second_in, RATE_UNITS, DECAY, fix_one, fix_two)
    new_master, new_first, new_second = (
        jnp.where(filled, new, old) for new, old in zip(moved, (own, first_in, second_in))
    )
    new_copy = new_master.astype(jnp.bfloat16)
    new_small, new_small_first, new_small_second = adamw(
        small_params, small_total, small_first, small_second, RATE_SMALL, 0.0, fix_one, fix_two
    )
    scale_new, scale_one, scale_two = adamw(
        logit_scale, grad_scale, scale_first, scale_second, RATE_SCALE, 0.0, fix_one, fix_two
    )
    loss_out = loss_total / (2 * owners * sentences)
    back_order = lambda a: a.transpose(1, 0, 2)
    return (
        saved[0].reshape(tokens.shape),
        back[0].reshape(tokens.shape),
        back_order(new_master),
        back_order(new_first),
        back_order(new_second),
        back_order(new_copy),
        new_small,
        new_small_first,
        new_small_second,
        scale_new,
        scale_one,
        scale_two,
        loss_out,
    )


def solution(mesh):
    rows = P("stream", "batch", None, None)
    blocks = P(None, "batch", None)
    return jax.shard_map(
        per_device,
        mesh=mesh,
        in_specs=(rows, rows, blocks, blocks, blocks) + (P(),) * 8,
        out_specs=(rows, rows, blocks, blocks, blocks, blocks) + (P(),) * 7,
        check_vma=False,
    )
```

```python
import functools

import jax
import jax.numpy as jnp
from jax import lax
from jax.experimental import pallas as pl
from jax.experimental.pallas import tpu as pltpu
from jax.sharding import PartitionSpec as P

H = 12
HD = 64
FF = 3072
STEP = 10
ZS = 4
UR_ROWS = 128
LEN_ROWS = 64
VMEM_MOST = 60 << 20
MESH = pl.DeviceIdType.MESH

HIGHEST = lax.Precision.HIGHEST
BETA_ONE = 0.9
BETA_TWO = 0.999
ADAM_EPS = 1e-06
RATE_UNITS = 0.02
RATE_SMALL = 0.1
RATE_SCALE = 2.0
DECAY = 0.01
MARGIN = 0.3
NORM_EPS = 1e-06


def place():
    s = lax.axis_index("stream")
    b = lax.axis_index("batch")
    return s, b // 4, (b // 2) % 2, b % 2


def batch_of(z, y, c):
    return (z * 2 + y) * 2 + c


def greet(s, z, y, c, others):
    barrier = pltpu.get_barrier_semaphore()

    def hello(target):
        pl.semaphore_signal(barrier, inc=1, device_id=target, device_id_type=MESH)

    hello((s, batch_of(z, y, 1 - c)))
    hello((s, batch_of(z, 1 - y, c)))
    hello((1 - s, batch_of(z, y, c)))
    if others == "line":
        for far in range(1, ZS):

            @pl.when(z >= far)
            def _():
                hello((s, batch_of(z - far, y, c)))

            @pl.when(z + far < ZS)
            def _():
                hello((s, batch_of(z + far, y, c)))

        pl.semaphore_wait(barrier, 3 + ZS - 1)
    else:

        @pl.when(z >= 1)
        def _():
            hello((s, batch_of(z - 1, y, c)))

        @pl.when(z + 1 < ZS)
        def _():
            hello((s, batch_of(z + 1, y, c)))

        pl.semaphore_wait(barrier, 3 + (z + 2) // 3 + (5 - z) // 3)


GR = 80
GX = UR_ROWS - GR


def gather_kernel(own_ref, out_ref, low, stage_sem, zl_s, zl_r, zr_s, zr_r, y_s, y_r, x_s, x_r, ca_s, ca_r, cb_s, cb_r):
    s, z, y, c = place()
    slots = own_ref.shape[0]
    steps = ZS * slots
    base = pl.multiple_of(s * GX, 16)
    only = pl.multiple_of(s * GR, 16)
    theirs = pl.multiple_of((1 - s) * GR, 16)

    def at(zz, yy, cc, j):
        return batch_of(zz, yy, cc) * slots + j

    greet(s, z, y, c, "next")

    def push(src, row, start, size, send, recv, target):
        return pltpu.make_async_remote_copy(
            src_ref=src,
            dst_ref=out_ref.at[row, pl.ds(start, size)],
            send_sem=send,
            recv_sem=recv,
            device_id=target,
            device_id_type=MESH,
        )

    left = (s, batch_of(z - 1, y, c))
    right = (s, batch_of(z + 1, y, c))
    across = (s, batch_of(z, 1 - y, c))
    other = (1 - s, batch_of(z, y, c))
    sibling = (s, batch_of(z, y, 1 - c))

    def to_left(src, zz, j):
        row = at(zz, y, c, j)
        return push(src(row), row, base, GR, zl_s.at[zz, j], zl_r.at[zz, j], left)

    def to_right(src, zz, j):
        row = at(zz, y, c, j)
        return push(src(row), row, base, GR, zr_s.at[zz, j], zr_r.at[zz, j], right)

    def to_across(src, zz, j):
        row = at(zz, y, c, j)
        return push(src(row), row, base, GR, y_s.at[zz, j], y_r.at[zz, j], across)

    def to_other(zz, yy, j):
        row = at(zz, yy, c, j)
        return push(out_ref.at[row, pl.ds(only, GX)], row, only, GX, x_s.at[zz, yy, j], x_r.at[zz, yy, j], other)

    def to_sibling(zz, yy, j):
        row = at(zz, yy, c, j)
        return push(out_ref.at[row, pl.ds(base, GR)], row, base, GR, ca_s.at[zz, yy, j], ca_r.at[zz, yy, j], sibling)

    def rest_to_sibling(zz, yy, j):
        row = at(zz, yy, c, j)
        return push(out_ref.at[row, pl.ds(theirs, GX)], row, theirs, GX, cb_s.at[zz, yy, j], cb_r.at[zz, yy, j], sibling)

    def landed(row):
        return out_ref.at[row, pl.ds(base, GR)]

    def from_left(zz, j):
        row = at(zz, y, c, j)
        return push(landed(row), row, base, GR, zr_s.at[zz, j], zr_r.at[zz, j], right)

    def arrived_line(zz, j, onward):
        onward.start()
        to_across(landed, zz, j).start()
        to_other(zz, y, j).start()
        to_sibling(zz, y, j).start()

    def stage(j):
        return pltpu.make_async_copy(low.at[j], out_ref.at[at(z, y, c, j)], stage_sem.at[j])

    for j in range(slots):
        low[j] = own_ref[j].astype(jnp.bfloat16)
        mine = lambda row: low.at[j, pl.ds(base, GR)]

        @pl.when(z > 0)
        def _():
            to_left(mine, z, j).start()

        @pl.when(z < ZS - 1)
        def _():
            to_right(mine, z, j).start()

        to_across(mine, z, j).start()
        row = at(z, y, c, j)
        push(low.at[j, pl.ds(base, GR)], row, base, GR, ca_s.at[z, y, j], ca_r.at[z, y, j], sibling).start()
        push(low.at[j, pl.ds(theirs, GX)], row, theirs, GX, cb_s.at[z, y, j], cb_r.at[z, y, j], sibling).start()
        stage(j).start()

    def line_step(t):
        d = t // slots
        j = t % slots

        @pl.when((d >= 1) & (z - d >= 0))
        def _():
            zz = z - d
            to_right(landed, zz, j).wait_recv()

            @pl.when(z < ZS - 1)
            def _():
                to_right(landed, zz, j).start()

            to_across(landed, zz, j).start()
            to_other(zz, y, j).start()
            to_sibling(zz, y, j).start()

        @pl.when((d >= 1) & (z + d < ZS))
        def _():
            zz = z + d
            to_left(landed, zz, j).wait_recv()

            @pl.when(z > 0)
            def _():
                to_left(landed, zz, j).start()

            to_across(landed, zz, j).start()
            to_other(zz, y, j).start()
            to_sibling(zz, y, j).start()

    def across_one(zz, j):
        row = at(zz, 1 - y, c, j)
        push(landed(row), row, base, GR, y_s.at[zz, j], y_r.at[zz, j], across).wait_recv()
        to_other(zz, 1 - y, j).start()
        to_sibling(zz, 1 - y, j).start()

    def across_step(t):
        d = t // slots
        j = t % slots

        @pl.when(z - d >= 0)
        def _():
            across_one(z - d, j)

        @pl.when((d >= 1) & (z + d < ZS))
        def _():
            across_one(z + d, j)

    def other_one(zz, yy, j):
        row = at(zz, yy, c, j)
        push(
            out_ref.at[row, pl.ds(theirs, GX)], row, theirs, GX, x_s.at[zz, yy, j], x_r.at[zz, yy, j], other
        ).wait_recv()
        rest_to_sibling(zz, yy, j).start()

    def other_step(t, yy, first):
        d = t // slots
        j = t % slots

        @pl.when((d >= first) & (z - d >= 0))
        def _():
            other_one(z - d, yy, j)

        @pl.when((d >= 1) & (z + d < ZS))
        def _():
            other_one(z + d, yy, j)

    @pl.loop(0, steps + 3)
    def _(t):
        @pl.when(t < steps)
        def _():
            line_step(t)

        @pl.when((t >= 1) & (t < steps + 1))
        def _():
            across_step(t - 1)

        @pl.when((t >= 2) & (t < steps + 2))
        def _():
            other_step(t - 2, y, 1)

        @pl.when(t >= 3)
        def _():
            other_step(t - 3, 1 - y, 0)

    for j in range(slots):
        stage(j).wait()

    @pl.loop(0, steps)
    def _(t):
        zz = t // slots
        j = t % slots

        @pl.when((z > 0) & (zz >= z))
        def _():
            to_left(landed, zz, j).wait_send()

        @pl.when((z < ZS - 1) & (zz <= z))
        def _():
            to_right(landed, zz, j).wait_send()

        to_across(landed, zz, j).wait_send()

        @pl.when(zz != z)
        def _():
            to_other(zz, y, j).wait_send()

        to_other(zz, 1 - y, j).wait_send()
        for yy in range(2):
            to_sibling(zz, yy, j).wait_send()
            rest_to_sibling(zz, yy, j).wait_send()
            row = at(zz, yy, 1 - c, j)
            push(landed(row), row, base, GR, ca_s.at[zz, yy, j], ca_r.at[zz, yy, j], sibling).wait_recv()
            push(
                out_ref.at[row, pl.ds(theirs, GX)], row, theirs, GX, cb_s.at[zz, yy, j], cb_r.at[zz, yy, j], sibling
            ).wait_recv()


def gather_units(own):
    slots, rows, width = own.shape
    owners = lax.axis_size("batch")
    line = [pltpu.SemaphoreType.DMA((ZS, slots))] * 6
    plane = [pltpu.SemaphoreType.DMA((ZS, 2, slots))] * 6
    return pl.pallas_call(
        gather_kernel,
        name="gather_units",
        out_shape=jax.ShapeDtypeStruct((owners * slots, rows, width), jnp.bfloat16),
        in_specs=[pl.BlockSpec(memory_space=pltpu.VMEM)],
        out_specs=pl.BlockSpec(memory_space=pl.ANY),
        scratch_shapes=[pltpu.VMEM((slots, rows, width), jnp.bfloat16), pltpu.SemaphoreType.DMA((slots,))] + line + plane,
        compiler_params=pltpu.CompilerParams(collective_id=0, has_side_effects=True, vmem_limit_bytes=VMEM_MOST),
    )(own)


RX = 32
RY = UR_ROWS - RX


def reduce_kernel(g_ref, small_ref, out_ref, small_out, held, c_in, x_in, y_in, z_in, f_in, t_acc, t_in,
                  p_sem, c_s, c_r, x_s, x_r, y_s, y_r, zl_s, zl_r, zr_s, zr_r, f_s, f_r, t_s, t_r):
    s, z, y, c = place()
    slots = out_ref.shape[0]
    steps = ZS * slots
    base = pl.multiple_of(s * RX, 16)
    only = pl.multiple_of(s * RY, 16)
    theirs = pl.multiple_of((1 - s) * RY, 16)
    left = (s, batch_of(z - 1, y, c))
    right = (s, batch_of(z + 1, y, c))
    across = (s, batch_of(z, 1 - y, c))
    other = (1 - s, batch_of(z, y, c))
    sibling = (s, batch_of(z, y, 1 - c))
    round_to = (sibling, across, other, (s, batch_of(z + 1 - 2 * (z % 2), y, c)), (s, batch_of((z + 2) % ZS, y, c)))
    greet(s, z, y, c, "line")

    def remote(src, dst, send, recv, target):
        return pltpu.make_async_remote_copy(
            src_ref=src, dst_ref=dst, send_sem=send, recv_sem=recv, device_id=target, device_id_type=MESH
        )

    def where_of(t):
        return (3 * (t // slots)) % ZS, t % slots

    def to_sibling(zz, yy, j):
        row = batch_of(zz, yy, 1 - c) * slots + j
        return remote(g_ref.at[row], c_in.at[zz, yy, j], c_s.at[zz, yy, j], c_r.at[zz, yy, j], sibling)

    def fetch(zz, yy, j):
        row = batch_of(zz, yy, c) * slots + j
        return pltpu.make_async_copy(g_ref.at[row], held.at[zz, yy, j], p_sem.at[zz, yy, j])

    def to_other(zz, yy, j):
        return remote(held.at[zz, yy, j, pl.ds(theirs, RX)], x_in.at[zz, yy, j], x_s.at[zz, yy, j], x_r.at[zz, yy, j], other)

    def to_across(zz, j):
        return remote(held.at[zz, 1 - y, j, pl.ds(base, RY)], y_in.at[zz, j], y_s.at[zz, j], y_r.at[zz, j], across)

    def to_left(zz, j):
        return remote(held.at[zz, y, j, pl.ds(base, RY)], z_in.at[1, zz, j], zl_s.at[zz, j], zl_r.at[zz, j], left)

    def to_right(zz, j):
        return remote(held.at[zz, y, j, pl.ds(base, RY)], z_in.at[0, zz, j], zr_s.at[zz, j], zr_r.at[zz, j], right)

    def final(j):
        return remote(held.at[z, y, j, pl.ds(base, RY)], f_in.at[j], f_s.at[j], f_r.at[j], other)

    def turn(r):
        return remote(t_acc.at[r], t_in.at[r], t_s.at[r], t_r.at[r], round_to[r])

    def add(zz, yy, j, start, size, got):
        mine = held.at[zz, yy, j, pl.ds(start, size)]
        mine[...] = (mine[...].astype(jnp.float32) + got[...].astype(jnp.float32)).astype(jnp.bfloat16)

    @pl.loop(0, steps)
    def _(t):
        zz, j = where_of(t)
        for yy in (1 - y, y):
            to_sibling(zz, yy, j).start()
            fetch(zz, yy, j).start()

    t_acc[0] = small_ref[...]

    def core_stage(t):
        zz, j = where_of(t)
        for yy in (1 - y, y):
            fetch(zz, yy, j).wait()
            to_sibling(zz, yy, j).wait_recv()
            add(zz, yy, j, 0, UR_ROWS, c_in.at[zz, yy, j])
            to_other(zz, yy, j).start()

    def other_stage(t):
        zz, j = where_of(t)
        for yy in (1 - y, y):
            to_other(zz, yy, j).wait_recv()
            add(zz, yy, j, only, RX, x_in.at[zz, yy, j])
        to_across(zz, j).start()

    def across_stage(t):
        zz, j = where_of(t)
        to_across(zz, j).wait_recv()
        add(zz, y, j, base, RY, y_in.at[zz, j])

    def from_left(zz, j):
        to_right(zz, j).wait_recv()
        add(zz, y, j, base, RY, z_in.at[0, zz, j])

    def from_right(zz, j):
        to_left(zz, j).wait_recv()
        add(zz, y, j, base, RY, z_in.at[1, zz, j])

    def line_stage(t, hops):
        zz, j = where_of(t)

        @pl.when((zz > z) & (z == hops))
        def _():
            if hops > 0:
                from_left(zz, j)
            to_right(zz, j).start()

        @pl.when((zz < z) & (ZS - 1 - z == hops))
        def _():
            if hops > 0:
                from_right(zz, j)
            to_left(zz, j).start()

        @pl.when((zz == z) & (3 - ((z + 2) // 3) * ((5 - z) // 3) == hops))
        def _():
            @pl.when(z > 0)
            def _():
                from_left(zz, j)

            @pl.when(z < ZS - 1)
            def _():
                from_right(zz, j)

            final(j).start()

    def final_stage(t):
        zz, j = where_of(t)

        @pl.when(zz == z)
        def _():
            final(j).wait_recv()
            f32 = jnp.float32
            out_ref[j, pl.ds(only, RX)] = held[z, y, j, pl.ds(only, RX)].astype(f32)
            shared = f_in[j, pl.ds(pl.multiple_of(s * RX, 16), RY - RX)].astype(f32)
            out_ref[j, pl.ds(RX, RY - RX)] = held[z, y, j, pl.ds(RX, RY - RX)].astype(f32) + shared
            out_ref[j, pl.ds(theirs, RX)] = f_in[j, pl.ds(pl.multiple_of((1 - s) * (RY - RX), 16), RX)].astype(f32)

    @pl.loop(0, steps + 6)
    def _(i):
        @pl.when(i < steps)
        def _():
            core_stage(i)

        @pl.when((i >= 1) & (i < steps + 1))
        def _():
            other_stage(i - 1)

        @pl.when((i >= 2) & (i < steps + 2))
        def _():
            across_stage(i - 2)

        for hops in range(ZS):

            @pl.when((i >= 2 + hops) & (i < steps + 2 + hops))
            def _():
                line_stage(i - 2 - hops, hops)

        @pl.when(i >= 6)
        def _():
            final_stage(i - 6)

        for r in range(5):

            @pl.when(i == 3 * r)
            def _():
                turn(r).start()

            @pl.when(i == 3 * r + 2)
            def _():
                turn(r).wait()
                t_acc[r + 1] = t_acc[r] + t_in[r]

    small_out[...] = t_acc[5]

    @pl.loop(0, steps)
    def _(t):
        zz, j = where_of(t)
        for yy in range(2):
            to_sibling(zz, yy, j).wait_send()
            to_other(zz, yy, j).wait_send()
        to_across(zz, j).wait_send()

        @pl.when(zz > z)
        def _():
            to_right(zz, j).wait_send()

        @pl.when(zz < z)
        def _():
            to_left(zz, j).wait_send()

        @pl.when(zz == z)
        def _():
            final(j).wait_send()


def reduce_units(grads, small, slots):
    owners = lax.axis_size("batch")
    _, rows, width = grads.shape
    bf, f32 = jnp.bfloat16, jnp.float32
    dma = pltpu.SemaphoreType.DMA
    return pl.pallas_call(
        reduce_kernel,
        name="reduce_units",
        out_shape=[jax.ShapeDtypeStruct((slots, rows, width), f32), jax.ShapeDtypeStruct(small.shape, f32)],
        in_specs=[pl.BlockSpec(memory_space=pl.ANY), pl.BlockSpec(memory_space=pltpu.VMEM)],
        out_specs=[pl.BlockSpec(memory_space=pltpu.VMEM)] * 2,
        scratch_shapes=[
            pltpu.VMEM((ZS, 2, slots, rows, width), bf),
            pltpu.VMEM((ZS, 2, slots, rows, width), bf),
            pltpu.VMEM((ZS, 2, slots, RX, width), bf),
            pltpu.VMEM((ZS, slots, RY, width), bf),
            pltpu.VMEM((2, ZS, slots, RY, width), bf),
            pltpu.VMEM((slots, RY, width), bf),
            pltpu.VMEM((6,) + small.shape, f32),
            pltpu.VMEM((5,) + small.shape, f32),
        ]
        + [dma((ZS, 2, slots))] * 5
        + [dma((ZS, slots))] * 6
        + [dma((slots,))] * 2
        + [dma((5,))] * 2,
        compiler_params=pltpu.CompilerParams(collective_id=2, has_side_effects=True, vmem_limit_bytes=VMEM_MOST),
    )(grads, small)


def rank_kernel(scale_ref, cls_ref, lang_row, lang_col, dc_ref, stats_ref, every, weights, z_s, z_r, pair_s, pair_r):
    s, z, y, c = place()
    sents, width = cls_ref.shape
    pairs = lang_row.shape[1]
    greet(s, z, y, c, "line")
    cls = cls_ref[...]
    root = lax.rsqrt(jnp.sum(cls * cls, axis=-1, keepdims=True) + NORM_EPS)
    unit = cls * root
    every[s, z, y, c] = unit.astype(jnp.bfloat16)

    def along(to, frm):
        return pltpu.make_async_remote_copy(
            src_ref=every.at[s, frm, y, c], dst_ref=every.at[s, frm, y, c], send_sem=z_s.at[to], recv_sem=z_r.at[frm],
            device_id=(s, batch_of(to, y, c)), device_id_type=MESH,
        )

    for to in range(ZS):

        @pl.when(z != to)
        def _():
            along(to, z).start()

    for frm in range(ZS):

        @pl.when(z != frm)
        def _():
            along(frm, frm).wait_recv()

    def swap(view, n, target):
        copy = pltpu.make_async_remote_copy(
            src_ref=view, dst_ref=view, send_sem=pair_s.at[n], recv_sem=pair_r.at[n], device_id=target,
            device_id_type=MESH,
        )
        copy.start()
        return copy

    first = swap(every.at[s, :, y, c], 0, (s, batch_of(z, 1 - y, c)))
    first.wait_recv()
    then = swap(every.at[s, :, :, c], 1, (1 - s, batch_of(z, y, c)))
    then.wait_recv()
    last = swap(every.at[:, :, :, c], 2, (s, batch_of(z, y, 1 - c)))
    last.wait_recv()
    scale = scale_ref[0]
    e_zero = every[0].reshape(pairs, width)
    e_one = every[1].reshape(pairs, width)
    cosines = lax.dot_general(e_zero, e_one, (((1,), (1,)), ((), ())), preferred_element_type=jnp.float32)
    own = lax.broadcasted_iota(jnp.int32, (pairs, pairs), 0) == lax.broadcasted_iota(jnp.int32, (pairs, pairs), 1)
    same = lang_col[...] == lang_row[...]
    diagonal = jnp.where(own, 1.0, 0.0)
    shifted = cosines - MARGIN * diagonal
    logits = scale * shifted
    masked = jnp.where(same, logits, -1e30)
    both = -2.0 * diagonal
    total = -2.0 * jnp.sum(logits * diagonal)
    for axis in range(2):
        top = jnp.max(masked, axis=axis, keepdims=True)
        grown = jnp.where(same, jnp.exp(masked - top), 0.0)
        summed = jnp.sum(grown, axis=axis, keepdims=True)
        both += grown / summed
        total += jnp.sum(jnp.log(summed) + top)
    line = lax.broadcasted_iota(jnp.int32, stats_ref.shape, 0)
    stats_ref[...] = jnp.where(line == 0, total, jnp.sum(both * shifted))
    weights[0] = both
    weights[1] = both.T
    rows = weights[s, pl.ds(pl.multiple_of(batch_of(z, y, c) * sents, 16), sents), :]
    partners = every[1 - s].reshape(pairs, width)
    high = rows.astype(jnp.bfloat16)
    rest = (rows - high.astype(jnp.float32)).astype(jnp.bfloat16)
    mix = (((1,), (0,)), ((), ()))
    de = lax.dot_general(high, partners, mix, preferred_element_type=jnp.float32)
    de += lax.dot_general(rest, partners, mix, preferred_element_type=jnp.float32)
    de = scale * de
    dc_ref[...] = (de - unit * jnp.sum(unit * de, axis=-1, keepdims=True)) * root
    for to in range(ZS):

        @pl.when(z != to)
        def _():
            along(to, z).wait_send()

    first.wait_send()
    then.wait_send()
    last.wait_send()


def rank_loss(cls, scale, langs):
    sents, width = cls.shape
    pairs = langs.shape[0]
    dma = pltpu.SemaphoreType.DMA
    vmem = pl.BlockSpec(memory_space=pltpu.VMEM)
    return pl.pallas_call(
        rank_kernel,
        name="rank_loss",
        out_shape=[jax.ShapeDtypeStruct((sents, width), jnp.float32), jax.ShapeDtypeStruct((8, 128), jnp.float32)],
        in_specs=[pl.BlockSpec(memory_space=pltpu.SMEM), vmem, vmem, vmem],
        out_specs=[vmem, vmem],
        scratch_shapes=[
            pltpu.VMEM((2, ZS, 2, 2, sents, width), jnp.bfloat16),
            pltpu.VMEM((2, pairs, pairs), jnp.float32),
            dma((ZS,)), dma((ZS,)), dma((3,)), dma((3,)),
        ],
        compiler_params=pltpu.CompilerParams(collective_id=1, has_side_effects=True, vmem_limit_bytes=24 << 20),
    )(scale, cls, langs.reshape(1, pairs), langs.reshape(pairs, 1))


TILE = 256
GROUP = LEN_ROWS


def dot_nn(a, b):
    return lax.dot_general(a, b, (((1,), (0,)), ((), ())), preferred_element_type=jnp.float32)


def dot_nt(a, b):
    return lax.dot_general(a, b, (((1,), (1,)), ((), ())), preferred_element_type=jnp.float32)


def dot_tn(a, b):
    return lax.dot_general(a, b, (((0,), (0,)), ((), ())), preferred_element_type=jnp.float32)


def gelu_parts(u):
    t = 1.0 / (1.0 + (0.3275911 * 0.7071067811865476) * jnp.abs(u))
    bell = jnp.exp(-0.5 * u * u)
    tail = t * (
        0.127414796 + t * (-0.142248368 + t * (0.7107068705 + t * (-0.7265760135 + t * 0.5307027145)))
    ) * bell
    phi_sum = jnp.where(u >= 0.0, 1.0 - tail, tail)
    return u * phi_sum, phi_sum + u * (0.3989422804014327 * bell)


def norm_parts(resid):
    centre = jnp.mean(resid, axis=-1, keepdims=True)
    centred = resid - centre
    rs = lax.rsqrt(jnp.mean(centred * centred, axis=-1, keepdims=True) + NORM_EPS)
    return centred * rs, rs


def norm_back(dy, unit, rs, gain):
    gd = gain * dy
    return rs * (gd - jnp.mean(gd, axis=-1, keepdims=True) - unit * jnp.mean(gd * unit, axis=-1, keepdims=True))


def lane_halves():
    lane = lax.broadcasted_iota(jnp.int32, (1, 2 * HD), 1)
    first = jnp.where(lane < HD, 1.0, 0.0)
    return first.astype(jnp.bfloat16), (1.0 - first).astype(jnp.bfloat16), lane < HD


def both_heads(rows, first, second):
    return jnp.concatenate([rows * first, rows * second], axis=0)


def fetch_all(pos_ref, units_hbm, held, sems, edges, order):
    for m in order:
        for u in range(edges[m], edges[m + 1]):
            pltpu.make_async_copy(units_hbm.at[pos_ref[u]], held.at[u], sems.at[m]).start()


def fetch_wait(units_hbm, held, sems, edges, m):
    lo, hi = edges[m], edges[m + 1]
    pltpu.make_async_copy(units_hbm.at[pl.ds(0, hi - lo)], held.at[pl.ds(lo, hi - lo)], sems.at[m]).wait()


def matrix_of(held, lo, hi):
    block = held[lo:hi]
    return block.reshape((hi - lo) * block.shape[1], block.shape[2])


def forward_kernel(
    edges, pos_ref, x_ref, small_ref, units_hbm,
    out_ref, q_ref, k_ref, v_ref, probs_ref, ctx_ref, n1_ref, rs1_ref, hb_ref, act_ref, slope_ref, n2_ref, rs2_ref,
    cls_ref, held, sems,
):
    first_tile = pl.program_id(0) == 0
    width = x_ref.shape[1]

    def need(m):
        @pl.when(first_tile)
        def _():
            fetch_wait(units_hbm, held, sems, edges, m)

    @pl.when(first_tile)
    def _():
        fetch_all(pos_ref, units_hbm, held, sems, edges, range(6))

    inner_rows = FF // width
    row = lambda r: small_ref[r : r + 1, :]
    x = x_ref[...]
    need(0)
    q = (dot_nn(x, matrix_of(held, edges[0], edges[1])) + row(0)).astype(jnp.bfloat16)
    q_ref[...] = q
    need(1)
    k = dot_nn(x, matrix_of(held, edges[1], edges[2])).astype(jnp.bfloat16)
    k_ref[...] = k
    need(2)
    v = (dot_nn(x, matrix_of(held, edges[2], edges[3])) + row(1)).astype(jnp.bfloat16)
    v_ref[...] = v
    first, second, is_first = lane_halves()
    every_pair = [slice(pair * 2 * HD, (pair + 1) * 2 * HD) for pair in range(H // 2)]
    every_sent = [slice(sent * GROUP, (sent + 1) * GROUP) for sent in range(TILE // GROUP)]
    for sent, rows in enumerate(every_sent):
        scores = jnp.concatenate(
            [dot_nt(k[rows, lanes], both_heads(q[rows, lanes], first, second)) for lanes in every_pair], axis=1
        )
        grown = jnp.exp((scores - jnp.max(scores, axis=0, keepdims=True)) * HD ** (-0.5))
        probs = (grown * (1.0 / jnp.sum(grown, axis=0, keepdims=True))).astype(jnp.bfloat16)
        probs_ref[sent] = probs
        mixed = [dot_tn(probs[:, lanes], v[rows, lanes]) for lanes in every_pair]
        ctx_ref[rows, :] = jnp.concatenate(
            [jnp.where(is_first, m[:GROUP], m[GROUP:]) for m in mixed], axis=1
        ).astype(jnp.bfloat16)
    need(3)
    attended = dot_nn(ctx_ref[...], matrix_of(held, edges[3], edges[4])) + row(2)
    n1, rs1 = norm_parts(x.astype(jnp.float32) + attended)
    n1_ref[...] = n1
    rs1_ref[...] = rs1
    h1 = n1 * row(4 + inner_rows) + row(5 + inner_rows)
    hb = h1.astype(jnp.bfloat16)
    hb_ref[...] = hb
    need(4)
    need(5)
    per = (edges[5] - edges[4]) // inner_rows
    total = h1 + row(3 + inner_rows)
    for part in range(inner_rows):
        cols = slice(part * width, (part + 1) * width)
        w_in = matrix_of(held, edges[4] + part * per, edges[4] + (part + 1) * per)
        u = dot_nt(hb, w_in) + row(3 + part)
        value, slope = gelu_parts(u)
        act = value.astype(jnp.bfloat16)
        act_ref[:, cols] = act
        slope_ref[:, cols] = slope.astype(jnp.bfloat16)
        total += dot_nn(act, matrix_of(held, edges[5] + part * per, edges[5] + (part + 1) * per))
    n2, rs2 = norm_parts(total)
    n2_ref[...] = n2
    rs2_ref[...] = rs2
    y = n2 * row(6 + inner_rows) + row(7 + inner_rows)
    out_ref[...] = y.astype(jnp.bfloat16)
    for sent in range(TILE // GROUP):
        cls_ref[0, sent : sent + 1, :] = y[sent * GROUP : sent * GROUP + 1, :]


def tiles(shape):
    rest = len(shape) - 1
    return pl.BlockSpec((TILE,) + tuple(shape[1:]), lambda i, *_: (i,) + (0,) * rest)


def whole(shape):
    return pl.BlockSpec(tuple(shape), lambda i, *_: (0,) * len(shape))


def run_forward(x, small, units, positions, edges):
    rows, width = x.shape
    count = rows // TILE
    sents = TILE // GROUP
    bf, f32 = jnp.bfloat16, jnp.float32
    probs_shape = (rows // GROUP, GROUP, width)
    outs = [
        ((rows, width), bf), ((rows, width), bf), ((rows, width), bf), ((rows, width), bf), (probs_shape, bf),
        ((rows, width), bf), ((rows, width), f32), ((rows, 1), f32), ((rows, width), bf), ((rows, FF), bf),
        ((rows, FF), bf), ((rows, width), f32), ((rows, 1), f32), ((count, sents, width), f32),
    ]
    specs = [tiles(shape) for shape, _ in outs]
    specs[4] = pl.BlockSpec((sents,) + probs_shape[1:], lambda i, *_: (i, 0, 0))
    specs[13] = pl.BlockSpec((1, sents, width), lambda i, *_: (i, 0, 0))
    return pl.pallas_call(
        functools.partial(forward_kernel, edges),
        name="layer_forward",
        grid_spec=pltpu.PrefetchScalarGridSpec(
            num_scalar_prefetch=1,
            grid=(count,),
            in_specs=[tiles(x.shape), whole(small.shape), pl.BlockSpec(memory_space=pl.ANY)],
            out_specs=specs,
            scratch_shapes=[pltpu.VMEM((edges[6],) + units.shape[1:], bf), pltpu.SemaphoreType.DMA((6,))],
        ),
        out_shape=[jax.ShapeDtypeStruct(shape, kind) for shape, kind in outs],
        compiler_params=pltpu.CompilerParams(vmem_limit_bytes=VMEM_MOST),
    )(positions, x, small, units)


def backward_kernel(
    edges, pos_ref, og_ref, dc_ref, small_ref, q_ref, k_ref, v_ref, probs_ref, n1_ref, rs1_ref, slope_ref, n2_ref,
    rs2_ref, units_hbm,
    dx_ref, df_ref, du_ref, da_ref, dq_ref, dk_ref, dv_ref, gsmall_ref, dy_ref, dctx_ref, held, sems,
):
    first_tile = pl.program_id(0) == 0
    width = og_ref.shape[1]
    inner_rows = FF // width

    def need(m):
        @pl.when(first_tile)
        def _():
            fetch_wait(units_hbm, held, sems, edges, m)

    @pl.when(first_tile)
    def _():
        fetch_all(pos_ref, units_hbm, held, sems, edges, (5, 4, 3, 0, 1, 2))
        gsmall_ref[...] = jnp.zeros_like(gsmall_ref)

    row = lambda r: small_ref[r : r + 1, :]

    def add_small(r, values):
        gsmall_ref[r : r + 1, :] += jnp.sum(values.astype(jnp.float32), axis=0, keepdims=True)

    dy_ref[...] = og_ref[...].astype(jnp.float32)
    for sent in range(TILE // GROUP):
        dy_ref[sent * GROUP : sent * GROUP + 1, :] += dc_ref[0, sent : sent + 1, :]
    dy = dy_ref[...]
    n2 = n2_ref[...]
    add_small(6 + inner_rows, dy * n2)
    add_small(7 + inner_rows, dy)
    dr2 = norm_back(dy, n2, rs2_ref[...], row(6 + inner_rows))
    df = dr2.astype(jnp.bfloat16)
    df_ref[...] = df
    add_small(3 + inner_rows, df)
    need(5)
    need(4)
    per = (edges[5] - edges[4]) // inner_rows
    dh1 = dr2
    for part in range(inner_rows):
        cols = slice(part * width, (part + 1) * width)
        da = dot_nt(df, matrix_of(held, edges[5] + part * per, edges[5] + (part + 1) * per))
        du = (da * slope_ref[:, cols].astype(jnp.float32)).astype(jnp.bfloat16)
        du_ref[:, cols] = du
        add_small(3 + part, du)
        dh1 += dot_nn(du, matrix_of(held, edges[4] + part * per, edges[4] + (part + 1) * per))
    n1 = n1_ref[...]
    add_small(4 + inner_rows, dh1 * n1)
    add_small(5 + inner_rows, dh1)
    dr1 = norm_back(dh1, n1, rs1_ref[...], row(4 + inner_rows))
    dattn = dr1.astype(jnp.bfloat16)
    da_ref[...] = dattn
    add_small(2, dattn)
    need(3)
    dctx_ref[...] = dot_nt(dattn, matrix_of(held, edges[3], edges[4])).astype(jnp.bfloat16)
    first, second, is_first = lane_halves()
    every_pair = [slice(pair * 2 * HD, (pair + 1) * 2 * HD) for pair in range(H // 2)]
    for sent in range(TILE // GROUP):
        rows = slice(sent * GROUP, (sent + 1) * GROUP)
        dcc = [both_heads(dctx_ref[rows, lanes], first, second) for lanes in every_pair]
        dprobs = jnp.concatenate(
            [dot_nt(v_ref[rows, lanes], wide) for lanes, wide in zip(every_pair, dcc)], axis=1
        )
        low = probs_ref[sent]
        probs = low.astype(jnp.float32)
        dscores = probs * (dprobs - jnp.sum(dprobs * probs, axis=0, keepdims=True))
        dscores = (dscores * HD ** (-0.5)).astype(jnp.bfloat16)
        dv_ref[rows, :] = jnp.concatenate(
            [dot_nn(low[:, lanes], wide) for lanes, wide in zip(every_pair, dcc)], axis=1
        ).astype(jnp.bfloat16)
        qq = [both_heads(q_ref[rows, lanes], first, second) for lanes in every_pair]
        dk_ref[rows, :] = jnp.concatenate(
            [dot_nn(dscores[:, lanes], wide) for lanes, wide in zip(every_pair, qq)], axis=1
        ).astype(jnp.bfloat16)
        mixed = [dot_tn(dscores[:, lanes], k_ref[rows, lanes]) for lanes in every_pair]
        dq_ref[rows, :] = jnp.concatenate(
            [jnp.where(is_first, m[:GROUP], m[GROUP:]) for m in mixed], axis=1
        ).astype(jnp.bfloat16)
    dx = dr1
    for m, (ref, r) in enumerate(((dq_ref, 0), (dk_ref, None), (dv_ref, 1))):
        need(m)
        rows = ref[...]
        if r is not None:
            add_small(r, rows)
        dx += dot_nt(rows, matrix_of(held, edges[m], edges[m + 1]))
    dx_ref[...] = dx.astype(jnp.bfloat16)


def run_backward(og, dc, small, saved, units, positions, edges):
    rows, width = og.shape
    count = rows // TILE
    sents = TILE // GROUP
    bf, f32 = jnp.bfloat16, jnp.float32
    _, q, k, v, probs, _, n1, rs1, _, _, slope, n2, rs2, _ = saved
    ins = [og, dc, small, q, k, v, probs, n1, rs1, slope, n2, rs2]
    in_specs = [tiles(a.shape) for a in ins]
    in_specs[1] = pl.BlockSpec((1, sents, width), lambda i, *_: (i, 0, 0))
    in_specs[2] = whole(small.shape)
    in_specs[6] = pl.BlockSpec((sents,) + probs.shape[1:], lambda i, *_: (i, 0, 0))
    outs = [((rows, width), bf)] * 2 + [((rows, FF), bf)] + [((rows, width), bf)] * 4 + [(small.shape, f32)]
    specs = [tiles(shape) for shape, _ in outs]
    specs[7] = whole(small.shape)
    return pl.pallas_call(
        functools.partial(backward_kernel, edges),
        name="layer_backward",
        grid_spec=pltpu.PrefetchScalarGridSpec(
            num_scalar_prefetch=1,
            grid=(count,),
            in_specs=in_specs + [pl.BlockSpec(memory_space=pl.ANY)],
            out_specs=specs,
            scratch_shapes=[
                pltpu.VMEM((TILE, width), f32),
                pltpu.VMEM((TILE, width), bf),
                pltpu.VMEM((edges[6],) + units.shape[1:], bf),
                pltpu.SemaphoreType.DMA((6,)),
            ],
        ),
        out_shape=[jax.ShapeDtypeStruct(shape, kind) for shape, kind in outs],
        compiler_params=pltpu.CompilerParams(vmem_limit_bytes=VMEM_MOST),
    )(positions, *ins, units)


def weight_grad_kernel(
    edges, pos_ref, x_hbm, ctx_hbm, du_hbm, act_hbm, dq_hbm, dk_hbm, dv_hbm, da_hbm, hb_hbm, df_hbm, out_hbm,
    x_v, ctx_v, du_v, act_v, right, staged, sems, out_sems,
):
    width = x_v.shape[1]
    unit_rows = out_hbm.shape[1]
    inner_rows = FF // width
    loads = [(act_hbm, act_v), (df_hbm, right.at[5]), (du_hbm, du_v), (hb_hbm, right.at[4]), (ctx_hbm, ctx_v),
             (da_hbm, right.at[3]), (x_hbm, x_v), (dq_hbm, right.at[0]), (dk_hbm, right.at[1]), (dv_hbm, right.at[2])]
    copies = [pltpu.make_async_copy(src, dst, sems.at[i]) for i, (src, dst) in enumerate(loads)]
    for copy in copies:
        copy.start()
    waited = set()
    per = width // unit_rows
    work = []
    for part in range(inner_rows):
        work.append((act_v, part, 5, edges[5] + part * per, (0, 1)))
    for part in range(inner_rows):
        work.append((du_v, part, 4, edges[4] + part * per, (2, 3)))
    work.append((ctx_v, 0, 3, edges[3], (4, 5)))
    work.append((x_v, 0, 0, edges[0], (6, 7)))
    work.append((x_v, 0, 1, edges[1], (6, 8)))
    work.append((x_v, 0, 2, edges[2], (6, 9)))
    for step, (left, part, m, unit, needs) in enumerate(work):
        slot = step % 2
        for n in needs:
            if n not in waited:
                copies[n].wait()
                waited.add(n)
        if step >= 2:
            pltpu.make_async_copy(out_hbm.at[pl.ds(0, per)], staged.at[slot], out_sems.at[slot]).wait()
        half = per // 2
        for piece in range(2):
            cols = slice(part * width + piece * half * unit_rows, part * width + (piece + 1) * half * unit_rows)
            block = dot_tn(left[:, cols], right[m]).astype(jnp.bfloat16)
            staged[slot, piece * half : (piece + 1) * half] = block.reshape(half, unit_rows, width)
        for n in range(per):
            pltpu.make_async_copy(staged.at[slot, n], out_hbm.at[pos_ref[unit + n]], out_sems.at[slot]).start()
    for slot in range(2):
        pltpu.make_async_copy(out_hbm.at[pl.ds(0, per)], staged.at[slot], out_sems.at[slot]).wait()


def run_weight_grads(x, saved, back, positions, edges, places, unit_rows):
    rows, width = x.shape
    bf = jnp.bfloat16
    ctx, hb, act = saved[5], saved[8], saved[9]
    _, df, du, da, dq, dk, dv, _ = back
    per = width // unit_rows
    anyw = pl.BlockSpec(memory_space=pl.ANY)
    return pl.pallas_call(
        functools.partial(weight_grad_kernel, edges),
        name="weight_grads",
        in_specs=[pl.BlockSpec(memory_space=pltpu.SMEM)] + [anyw] * 10,
        out_specs=anyw,
        scratch_shapes=[
            pltpu.VMEM((rows, width), bf), pltpu.VMEM((rows, width), bf), pltpu.VMEM((rows, FF), bf),
            pltpu.VMEM((rows, FF), bf), pltpu.VMEM((6, rows, width), bf),
            pltpu.VMEM((2, per, unit_rows, width), bf),
            pltpu.SemaphoreType.DMA((10,)), pltpu.SemaphoreType.DMA((2,)),
        ],
        out_shape=jax.ShapeDtypeStruct((places, unit_rows, width), bf),
        compiler_params=pltpu.CompilerParams(vmem_limit_bytes=VMEM_MOST),
    )(positions, x, ctx, du, act, dq, dk, dv, da, hb, df)


def unit_positions(owner_list, slot_count):
    unit_total = owner_list.shape[0]
    same_owner = owner_list[:, None] == owner_list[None, :]
    ordinal = jnp.arange(unit_total, dtype=jnp.int32)
    earlier = ordinal[None, :] < ordinal[:, None]
    slot_number = jnp.sum(jnp.where(same_owner & earlier, 1, 0), axis=1).astype(jnp.int32)
    return owner_list * slot_count + slot_number


def adamw(weight_in, gradient, moment_one, moment_two, rate_value, decay_value, fix_one, fix_two):
    new_one = BETA_ONE * moment_one + (1.0 - BETA_ONE) * gradient
    new_two = BETA_TWO * moment_two + (1.0 - BETA_TWO) * gradient * gradient
    stepped = new_one / fix_one / (jnp.sqrt(new_two / fix_two) + ADAM_EPS)
    return (weight_in - rate_value * (stepped + decay_value * weight_in), new_one, new_two)


def any_size_units(own, positions, owners):
    slots, rows, width = own.shape
    table = jnp.arange(owners * slots, dtype=jnp.int32)[:, None] == positions[None, :]
    bands = lax.all_to_all(
        own.transpose(1, 0, 2).astype(jnp.bfloat16), "batch", split_axis=0, concat_axis=1, tiled=True
    )
    ordered = jnp.einsum(
        "rpd,pu->rud", bands, table.astype(jnp.bfloat16), preferred_element_type=jnp.float32
    ).astype(jnp.bfloat16)
    return lax.all_gather(ordered, "batch", axis=0, tiled=True).transpose(1, 0, 2)


def any_size_sums(grads, positions, owners, slots):
    table = jnp.arange(owners * slots, dtype=jnp.int32)[:, None] == positions[None, :]
    pieces = lax.psum_scatter(grads.transpose(1, 0, 2).astype(jnp.float32), "batch", scatter_dimension=0, tiled=True)
    summed = lax.psum(pieces.astype(jnp.bfloat16), "stream").astype(jnp.float32)
    send_rows = jnp.einsum("rud,pu->rpd", summed, table.astype(jnp.float32), precision=HIGHEST)
    owned = lax.all_to_all(send_rows.astype(jnp.bfloat16), "batch", split_axis=1, concat_axis=0, tiled=True)
    return owned.astype(jnp.float32).transpose(1, 0, 2)


def any_size_rank(cls, scale, langs, owners):
    sents, width = cls.shape
    root = lax.rsqrt(jnp.sum(cls * cls, axis=-1, keepdims=True) + NORM_EPS)
    unit = cls * root
    every = lax.all_gather(unit.astype(jnp.bfloat16), "batch", axis=0, tiled=True)
    every = lax.all_gather(every, "stream", axis=0)
    cosines = jnp.dot(every[0], every[1].T, preferred_element_type=jnp.float32)
    diagonal = jnp.eye(cosines.shape[0], dtype=jnp.float32)
    same = langs[:, None] == langs[None, :]
    shifted = cosines - MARGIN * diagonal
    logits = scale[0] * shifted
    masked = jnp.where(same, logits, -1e30)
    both = -2.0 * diagonal
    total = -2.0 * jnp.sum(logits * diagonal)
    for axis in range(2):
        top = jnp.max(masked, axis=axis, keepdims=True)
        grown = jnp.where(same, jnp.exp(masked - top), 0.0)
        summed = jnp.sum(grown, axis=axis, keepdims=True)
        both += grown / summed
        total += jnp.sum(jnp.log(summed) + top)
    s = lax.axis_index("stream")
    turned = jnp.where(s == 0, both, both.T)
    rows = lax.dynamic_slice_in_dim(turned, lax.axis_index("batch") * sents, sents)
    partners = lax.dynamic_index_in_dim(every, 1 - s, keepdims=False).astype(jnp.float32)
    de = scale[0] * jnp.dot(rows, partners, precision=HIGHEST)
    dc = (de - unit * jnp.sum(unit * de, axis=-1, keepdims=True)) * root
    return dc, total, jnp.sum(both * shifted)


def per_device(
    tokens, out_grad, master, first_moment, second_moment, small_params, small_first, small_second, logit_scale,
    scale_first, scale_second, pair_lang, unit_owner,
):
    owners = lax.axis_size("batch")
    here_batch = lax.axis_index("batch")
    unit_rows, slot_count, width = master.shape
    query_blocks = width // unit_rows
    inner_blocks = FF // unit_rows
    edges = [query_blocks * n for n in range(5)]
    edges += [edges[4] + inner_blocks, edges[4] + 2 * inner_blocks]
    units_total = unit_owner.shape[0]
    positions = unit_positions(unit_owner, slot_count)
    on_block = owners == 4 * ZS
    own = master.transpose(1, 0, 2)
    if on_block:
        units, where, places = gather_units(own), positions, owners * slot_count
    else:
        units = any_size_units(own, positions, owners)
        where, places = jnp.arange(units_total, dtype=jnp.int32), units_total
    sentences, length = tokens.shape[1], tokens.shape[2]
    flat = tokens.reshape(sentences * length, width)
    saved = run_forward(flat, small_params, units, where, edges)
    cls = saved[13]
    if on_block:
        dc, stats = rank_loss(cls.reshape(sentences, width), logit_scale, pair_lang)
        loss_total, grad_scale = stats[0, :1], stats[1, :1]
    else:
        dc, loss_total, grad_scale = any_size_rank(cls.reshape(sentences, width), logit_scale, pair_lang, owners)
        loss_total, grad_scale = loss_total.reshape(1), grad_scale.reshape(1)
    back = run_backward(
        out_grad.reshape(sentences * length, width), dc.reshape(cls.shape), small_params, saved, units, where, edges
    )
    grads = run_weight_grads(flat, saved, back, where, edges, places, unit_rows)
    if on_block:
        owned_grad, small_total = reduce_units(grads, back[7], slot_count)
    else:
        owned_grad = any_size_sums(grads, positions, owners, slot_count)
        small_total = lax.psum(back[7], ("stream", "batch"))
    step_value = float(STEP)
    fix_one = 1.0 - BETA_ONE**step_value
    fix_two = 1.0 - BETA_TWO**step_value
    my_places = here_batch * slot_count + jnp.arange(slot_count, dtype=jnp.int32)
    filled = jnp.any(my_places[:, None] == positions[None, :], axis=1)[:, None, None]
    first_in, second_in = first_moment.transpose(1, 0, 2), second_moment.transpose(1, 0, 2)
    moved = adamw(own, owned_grad, first_in, second_in, RATE_UNITS, DECAY, fix_one, fix_two)
    new_master, new_first, new_second = (
        jnp.where(filled, new, old) for new, old in zip(moved, (own, first_in, second_in))
    )
    new_copy = new_master.astype(jnp.bfloat16)
    new_small, new_small_first, new_small_second = adamw(
        small_params, small_total, small_first, small_second, RATE_SMALL, 0.0, fix_one, fix_two
    )
    scale_new, scale_one, scale_two = adamw(
        logit_scale, grad_scale, scale_first, scale_second, RATE_SCALE, 0.0, fix_one, fix_two
    )
    loss_out = loss_total / (2 * owners * sentences)
    back_order = lambda a: a.transpose(1, 0, 2)
    return (
        saved[0].reshape(tokens.shape),
        back[0].reshape(tokens.shape),
        back_order(new_master),
        back_order(new_first),
        back_order(new_second),
        back_order(new_copy),
        new_small,
        new_small_first,
        new_small_second,
        scale_new,
        scale_one,
        scale_two,
        loss_out,
    )


def solution(mesh):
    rows = P("stream", "batch", None, None)
    blocks = P(None, "batch", None)
    return jax.shard_map(
        per_device,
        mesh=mesh,
        in_specs=(rows, rows, blocks, blocks, blocks) + (P(),) * 8,
        out_specs=(rows, rows, blocks, blocks, blocks, blocks) + (P(),) * 7,
        check_vma=False,
    )
```

```python
import functools

import jax
import jax.numpy as jnp
from jax import lax
from jax.experimental import pallas as pl
from jax.experimental.pallas import tpu as pltpu
from jax.sharding import PartitionSpec as P

H = 12
HD = 64
FF = 3072
STEP = 10
ZS = 4
UR_ROWS = 128
LEN_ROWS = 64
VMEM_MOST = 60 << 20
MESH = pl.DeviceIdType.MESH

HIGHEST = lax.Precision.HIGHEST
BETA_ONE = 0.9
BETA_TWO = 0.999
ADAM_EPS = 1e-06
RATE_UNITS = 0.02
RATE_SMALL = 0.1
RATE_SCALE = 2.0
DECAY = 0.01
MARGIN = 0.3
NORM_EPS = 1e-06


def place():
    s = lax.axis_index("stream")
    b = lax.axis_index("batch")
    return s, b // 4, (b // 2) % 2, b % 2


def batch_of(z, y, c):
    return (z * 2 + y) * 2 + c


def greet(s, z, y, c, others):
    barrier = pltpu.get_barrier_semaphore()

    def hello(target):
        pl.semaphore_signal(barrier, inc=1, device_id=target, device_id_type=MESH)

    hello((s, batch_of(z, y, 1 - c)))
    hello((s, batch_of(z, 1 - y, c)))
    hello((1 - s, batch_of(z, y, c)))
    if others == "line":
        for far in range(1, ZS):

            @pl.when(z >= far)
            def _():
                hello((s, batch_of(z - far, y, c)))

            @pl.when(z + far < ZS)
            def _():
                hello((s, batch_of(z + far, y, c)))

        pl.semaphore_wait(barrier, 3 + ZS - 1)
    else:

        @pl.when(z >= 1)
        def _():
            hello((s, batch_of(z - 1, y, c)))

        @pl.when(z + 1 < ZS)
        def _():
            hello((s, batch_of(z + 1, y, c)))

        pl.semaphore_wait(barrier, 3 + (z + 2) // 3 + (5 - z) // 3)


GR = 80
GX = UR_ROWS - GR


def gather_kernel(own_ref, out_ref, low, stage_sem, zl_s, zl_r, zr_s, zr_r, y_s, y_r, x_s, x_r, ca_s, ca_r, cb_s, cb_r):
    s, z, y, c = place()
    slots = own_ref.shape[0]
    steps = ZS * slots
    base = pl.multiple_of(s * GX, 16)
    only = pl.multiple_of(s * GR, 16)
    theirs = pl.multiple_of((1 - s) * GR, 16)

    def at(zz, yy, cc, j):
        return batch_of(zz, yy, cc) * slots + j

    greet(s, z, y, c, "next")

    def push(src, row, start, size, send, recv, target):
        return pltpu.make_async_remote_copy(
            src_ref=src,
            dst_ref=out_ref.at[row, pl.ds(start, size)],
            send_sem=send,
            recv_sem=recv,
            device_id=target,
            device_id_type=MESH,
        )

    left = (s, batch_of(z - 1, y, c))
    right = (s, batch_of(z + 1, y, c))
    across = (s, batch_of(z, 1 - y, c))
    other = (1 - s, batch_of(z, y, c))
    sibling = (s, batch_of(z, y, 1 - c))

    def to_left(src, zz, j):
        row = at(zz, y, c, j)
        return push(src(row), row, base, GR, zl_s.at[zz, j], zl_r.at[zz, j], left)

    def to_right(src, zz, j):
        row = at(zz, y, c, j)
        return push(src(row), row, base, GR, zr_s.at[zz, j], zr_r.at[zz, j], right)

    def to_across(src, zz, j):
        row = at(zz, y, c, j)
        return push(src(row), row, base, GR, y_s.at[zz, j], y_r.at[zz, j], across)

    def to_other(zz, yy, j):
        row = at(zz, yy, c, j)
        return push(out_ref.at[row, pl.ds(only, GX)], row, only, GX, x_s.at[zz, yy, j], x_r.at[zz, yy, j], other)

    def to_sibling(zz, yy, j):
        row = at(zz, yy, c, j)
        return push(out_ref.at[row, pl.ds(base, GR)], row, base, GR, ca_s.at[zz, yy, j], ca_r.at[zz, yy, j], sibling)

    def rest_to_sibling(zz, yy, j):
        row = at(zz, yy, c, j)
        return push(out_ref.at[row, pl.ds(theirs, GX)], row, theirs, GX, cb_s.at[zz, yy, j], cb_r.at[zz, yy, j], sibling)

    def landed(row):
        return out_ref.at[row, pl.ds(base, GR)]

    def from_left(zz, j):
        row = at(zz, y, c, j)
        return push(landed(row), row, base, GR, zr_s.at[zz, j], zr_r.at[zz, j], right)

    def arrived_line(zz, j, onward):
        onward.start()
        to_across(landed, zz, j).start()
        to_other(zz, y, j).start()
        to_sibling(zz, y, j).start()

    def stage(j):
        return pltpu.make_async_copy(low.at[j], out_ref.at[at(z, y, c, j)], stage_sem.at[j])

    for j in range(slots):
        low[j] = own_ref[j].astype(jnp.bfloat16)
        mine = lambda row: low.at[j, pl.ds(base, GR)]

        @pl.when(z > 0)
        def _():
            to_left(mine, z, j).start()

        @pl.when(z < ZS - 1)
        def _():
            to_right(mine, z, j).start()

        to_across(mine, z, j).start()
        row = at(z, y, c, j)
        push(low.at[j, pl.ds(base, GR)], row, base, GR, ca_s.at[z, y, j], ca_r.at[z, y, j], sibling).start()
        push(low.at[j, pl.ds(theirs, GX)], row, theirs, GX, cb_s.at[z, y, j], cb_r.at[z, y, j], sibling).start()
        stage(j).start()

    def line_step(t):
        d = t // slots
        j = t % slots

        @pl.when((d >= 1) & (z - d >= 0))
        def _():
            zz = z - d
            to_right(landed, zz, j).wait_recv()

            @pl.when(z < ZS - 1)
            def _():
                to_right(landed, zz, j).start()

            to_across(landed, zz, j).start()
            to_other(zz, y, j).start()
            to_sibling(zz, y, j).start()

        @pl.when((d >= 1) & (z + d < ZS))
        def _():
            zz = z + d
            to_left(landed, zz, j).wait_recv()

            @pl.when(z > 0)
            def _():
                to_left(landed, zz, j).start()

            to_across(landed, zz, j).start()
            to_other(zz, y, j).start()
            to_sibling(zz, y, j).start()

    def across_one(zz, j):
        row = at(zz, 1 - y, c, j)
        push(landed(row), row, base, GR, y_s.at[zz, j], y_r.at[zz, j], across).wait_recv()
        to_other(zz, 1 - y, j).start()
        to_sibling(zz, 1 - y, j).start()

    def across_step(t):
        d = t // slots
        j = t % slots

        @pl.when(z - d >= 0)
        def _():
            across_one(z - d, j)

        @pl.when((d >= 1) & (z + d < ZS))
        def _():
            across_one(z + d, j)

    def other_one(zz, yy, j):
        row = at(zz, yy, c, j)
        push(
            out_ref.at[row, pl.ds(theirs, GX)], row, theirs, GX, x_s.at[zz, yy, j], x_r.at[zz, yy, j], other
        ).wait_recv()
        rest_to_sibling(zz, yy, j).start()

    def other_step(t, yy, first):
        d = t // slots
        j = t % slots

        @pl.when((d >= first) & (z - d >= 0))
        def _():
            other_one(z - d, yy, j)

        @pl.when((d >= 1) & (z + d < ZS))
        def _():
            other_one(z + d, yy, j)

    @pl.loop(0, steps + 3)
    def _(t):
        @pl.when(t < steps)
        def _():
            line_step(t)

        @pl.when((t >= 1) & (t < steps + 1))
        def _():
            across_step(t - 1)

        @pl.when((t >= 2) & (t < steps + 2))
        def _():
            other_step(t - 2, y, 1)

        @pl.when(t >= 3)
        def _():
            other_step(t - 3, 1 - y, 0)

    for j in range(slots):
        stage(j).wait()

    @pl.loop(0, steps)
    def _(t):
        zz = t // slots
        j = t % slots

        @pl.when((z > 0) & (zz >= z))
        def _():
            to_left(landed, zz, j).wait_send()

        @pl.when((z < ZS - 1) & (zz <= z))
        def _():
            to_right(landed, zz, j).wait_send()

        to_across(landed, zz, j).wait_send()

        @pl.when(zz != z)
        def _():
            to_other(zz, y, j).wait_send()

        to_other(zz, 1 - y, j).wait_send()
        for yy in range(2):
            to_sibling(zz, yy, j).wait_send()
            rest_to_sibling(zz, yy, j).wait_send()
            row = at(zz, yy, 1 - c, j)
            push(landed(row), row, base, GR, ca_s.at[zz, yy, j], ca_r.at[zz, yy, j], sibling).wait_recv()
            push(
                out_ref.at[row, pl.ds(theirs, GX)], row, theirs, GX, cb_s.at[zz, yy, j], cb_r.at[zz, yy, j], sibling
            ).wait_recv()


def gather_units(own):
    slots, rows, width = own.shape
    owners = lax.axis_size("batch")
    line = [pltpu.SemaphoreType.DMA((ZS, slots))] * 6
    plane = [pltpu.SemaphoreType.DMA((ZS, 2, slots))] * 6
    return pl.pallas_call(
        gather_kernel,
        name="gather_units",
        out_shape=jax.ShapeDtypeStruct((owners * slots, rows, width), jnp.bfloat16),
        in_specs=[pl.BlockSpec(memory_space=pltpu.VMEM)],
        out_specs=pl.BlockSpec(memory_space=pl.ANY),
        scratch_shapes=[pltpu.VMEM((slots, rows, width), jnp.bfloat16), pltpu.SemaphoreType.DMA((slots,))] + line + plane,
        compiler_params=pltpu.CompilerParams(collective_id=0, has_side_effects=True, vmem_limit_bytes=VMEM_MOST),
    )(own)


def rank_kernel(scale_ref, cls_ref, lang_row, lang_col, dc_ref, stats_ref, every, weights, z_s, z_r, pair_s, pair_r):
    s, z, y, c = place()
    sents, width = cls_ref.shape
    pairs = lang_row.shape[1]
    greet(s, z, y, c, "line")
    cls = cls_ref[...]
    root = lax.rsqrt(jnp.sum(cls * cls, axis=-1, keepdims=True) + NORM_EPS)
    unit = cls * root
    every[s, z, y, c] = unit.astype(jnp.bfloat16)

    def along(to, frm):
        return pltpu.make_async_remote_copy(
            src_ref=every.at[s, frm, y, c], dst_ref=every.at[s, frm, y, c], send_sem=z_s.at[to], recv_sem=z_r.at[frm],
            device_id=(s, batch_of(to, y, c)), device_id_type=MESH,
        )

    for to in range(ZS):

        @pl.when(z != to)
        def _():
            along(to, z).start()

    for frm in range(ZS):

        @pl.when(z != frm)
        def _():
            along(frm, frm).wait_recv()

    def swap(view, n, target):
        copy = pltpu.make_async_remote_copy(
            src_ref=view, dst_ref=view, send_sem=pair_s.at[n], recv_sem=pair_r.at[n], device_id=target,
            device_id_type=MESH,
        )
        copy.start()
        return copy

    first = swap(every.at[s, :, y, c], 0, (s, batch_of(z, 1 - y, c)))
    first.wait_recv()
    then = swap(every.at[s, :, :, c], 1, (1 - s, batch_of(z, y, c)))
    then.wait_recv()
    last = swap(every.at[:, :, :, c], 2, (s, batch_of(z, y, 1 - c)))
    last.wait_recv()
    scale = scale_ref[0]
    e_zero = every[0].reshape(pairs, width)
    e_one = every[1].reshape(pairs, width)
    cosines = lax.dot_general(e_zero, e_one, (((1,), (1,)), ((), ())), preferred_element_type=jnp.float32)
    own = lax.broadcasted_iota(jnp.int32, (pairs, pairs), 0) == lax.broadcasted_iota(jnp.int32, (pairs, pairs), 1)
    same = lang_col[...] == lang_row[...]
    diagonal = jnp.where(own, 1.0, 0.0)
    shifted = cosines - MARGIN * diagonal
    logits = scale * shifted
    masked = jnp.where(same, logits, -1e30)
    both = -2.0 * diagonal
    total = -2.0 * jnp.sum(logits * diagonal)
    for axis in range(2):
        top = jnp.max(masked, axis=axis, keepdims=True)
        grown = jnp.where(same, jnp.exp(masked - top), 0.0)
        summed = jnp.sum(grown, axis=axis, keepdims=True)
        both += grown / summed
        total += jnp.sum(jnp.log(summed) + top)
    line = lax.broadcasted_iota(jnp.int32, stats_ref.shape, 0)
    stats_ref[...] = jnp.where(line == 0, total, jnp.sum(both * shifted))
    weights[0] = both
    weights[1] = both.T
    rows = weights[s, pl.ds(pl.multiple_of(batch_of(z, y, c) * sents, 16), sents), :]
    partners = every[1 - s].reshape(pairs, width)
    high = rows.astype(jnp.bfloat16)
    rest = (rows - high.astype(jnp.float32)).astype(jnp.bfloat16)
    mix = (((1,), (0,)), ((), ()))
    de = lax.dot_general(high, partners, mix, preferred_element_type=jnp.float32)
    de += lax.dot_general(rest, partners, mix, preferred_element_type=jnp.float32)
    de = scale * de
    dc_ref[...] = (de - unit * jnp.sum(unit * de, axis=-1, keepdims=True)) * root
    for to in range(ZS):

        @pl.when(z != to)
        def _():
            along(to, z).wait_send()

    first.wait_send()
    then.wait_send()
    last.wait_send()


def rank_loss(cls, scale, langs):
    sents, width = cls.shape
    pairs = langs.shape[0]
    dma = pltpu.SemaphoreType.DMA
    vmem = pl.BlockSpec(memory_space=pltpu.VMEM)
    return pl.pallas_call(
        rank_kernel,
        name="rank_loss",
        out_shape=[jax.ShapeDtypeStruct((sents, width), jnp.float32), jax.ShapeDtypeStruct((8, 128), jnp.float32)],
        in_specs=[pl.BlockSpec(memory_space=pltpu.SMEM), vmem, vmem, vmem],
        out_specs=[vmem, vmem],
        scratch_shapes=[
            pltpu.VMEM((2, ZS, 2, 2, sents, width), jnp.bfloat16),
            pltpu.VMEM((2, pairs, pairs), jnp.float32),
            dma((ZS,)), dma((ZS,)), dma((3,)), dma((3,)),
        ],
        compiler_params=pltpu.CompilerParams(collective_id=1, has_side_effects=True, vmem_limit_bytes=24 << 20),
    )(scale, cls, langs.reshape(1, pairs), langs.reshape(pairs, 1))


TILE = 256
GROUP = LEN_ROWS


def dot_nn(a, b):
    return lax.dot_general(a, b, (((1,), (0,)), ((), ())), preferred_element_type=jnp.float32)


def dot_nt(a, b):
    return lax.dot_general(a, b, (((1,), (1,)), ((), ())), preferred_element_type=jnp.float32)


def dot_tn(a, b):
    return lax.dot_general(a, b, (((0,), (0,)), ((), ())), preferred_element_type=jnp.float32)


def gelu_parts(u):
    t = 1.0 / (1.0 + (0.3275911 * 0.7071067811865476) * jnp.abs(u))
    bell = jnp.exp(-0.5 * u * u)
    tail = t * (
        0.127414796 + t * (-0.142248368 + t * (0.7107068705 + t * (-0.7265760135 + t * 0.5307027145)))
    ) * bell
    phi_sum = jnp.where(u >= 0.0, 1.0 - tail, tail)
    return u * phi_sum, phi_sum + u * (0.3989422804014327 * bell)


def norm_parts(resid):
    centre = jnp.mean(resid, axis=-1, keepdims=True)
    centred = resid - centre
    rs = lax.rsqrt(jnp.mean(centred * centred, axis=-1, keepdims=True) + NORM_EPS)
    return centred * rs, rs


def norm_back(dy, unit, rs, gain):
    gd = gain * dy
    return rs * (gd - jnp.mean(gd, axis=-1, keepdims=True) - unit * jnp.mean(gd * unit, axis=-1, keepdims=True))


def lane_halves():
    lane = lax.broadcasted_iota(jnp.int32, (1, 2 * HD), 1)
    first = jnp.where(lane < HD, 1.0, 0.0)
    return first.astype(jnp.bfloat16), (1.0 - first).astype(jnp.bfloat16), lane < HD


def both_heads(rows, first, second):
    return jnp.concatenate([rows * first, rows * second], axis=0)


def fetch_all(pos_ref, units_hbm, held, sems, edges, order):
    for m in order:
        for u in range(edges[m], edges[m + 1]):
            pltpu.make_async_copy(units_hbm.at[pos_ref[u]], held.at[u], sems.at[m]).start()


def fetch_wait(units_hbm, held, sems, edges, m):
    lo, hi = edges[m], edges[m + 1]
    pltpu.make_async_copy(units_hbm.at[pl.ds(0, hi - lo)], held.at[pl.ds(lo, hi - lo)], sems.at[m]).wait()


def matrix_of(held, lo, hi):
    block = held[lo:hi]
    return block.reshape((hi - lo) * block.shape[1], block.shape[2])


def forward_kernel(
    edges, pos_ref, x_ref, small_ref, units_hbm,
    out_ref, q_ref, k_ref, v_ref, probs_ref, ctx_ref, n1_ref, rs1_ref, hb_ref, act_ref, slope_ref, n2_ref, rs2_ref,
    cls_ref, ordered_hbm, held, sems, keep_sem,
):
    first_tile = pl.program_id(0) == 0
    width = x_ref.shape[1]

    def need(m):
        @pl.when(first_tile)
        def _():
            fetch_wait(units_hbm, held, sems, edges, m)

    @pl.when(first_tile)
    def _():
        fetch_all(pos_ref, units_hbm, held, sems, edges, range(6))

    inner_rows = FF // width
    row = lambda r: small_ref[r : r + 1, :]
    x = x_ref[...]
    need(0)
    q = (dot_nn(x, matrix_of(held, edges[0], edges[1])) + row(0)).astype(jnp.bfloat16)
    q_ref[...] = q
    need(1)
    k = dot_nn(x, matrix_of(held, edges[1], edges[2])).astype(jnp.bfloat16)
    k_ref[...] = k
    need(2)
    v = (dot_nn(x, matrix_of(held, edges[2], edges[3])) + row(1)).astype(jnp.bfloat16)
    v_ref[...] = v
    first, second, is_first = lane_halves()
    every_pair = [slice(pair * 2 * HD, (pair + 1) * 2 * HD) for pair in range(H // 2)]
    every_sent = [slice(sent * GROUP, (sent + 1) * GROUP) for sent in range(TILE // GROUP)]
    for sent, rows in enumerate(every_sent):
        scores = jnp.concatenate(
            [dot_nt(k[rows, lanes], both_heads(q[rows, lanes], first, second)) for lanes in every_pair], axis=1
        )
        grown = jnp.exp((scores - jnp.max(scores, axis=0, keepdims=True)) * HD ** (-0.5))
        probs = (grown * (1.0 / jnp.sum(grown, axis=0, keepdims=True))).astype(jnp.bfloat16)
        probs_ref[sent] = probs
        mixed = [dot_tn(probs[:, lanes], v[rows, lanes]) for lanes in every_pair]
        ctx_ref[rows, :] = jnp.concatenate(
            [jnp.where(is_first, m[:GROUP], m[GROUP:]) for m in mixed], axis=1
        ).astype(jnp.bfloat16)
    need(3)
    attended = dot_nn(ctx_ref[...], matrix_of(held, edges[3], edges[4])) + row(2)
    n1, rs1 = norm_parts(x.astype(jnp.float32) + attended)
    n1_ref[...] = n1
    rs1_ref[...] = rs1
    h1 = n1 * row(4 + inner_rows) + row(5 + inner_rows)
    hb = h1.astype(jnp.bfloat16)
    hb_ref[...] = hb
    need(4)
    need(5)
    keep = pltpu.make_async_copy(held, ordered_hbm, keep_sem)

    @pl.when(first_tile)
    def _():
        keep.start()

    per = (edges[5] - edges[4]) // inner_rows
    total = h1 + row(3 + inner_rows)
    for part in range(inner_rows):
        cols = slice(part * width, (part + 1) * width)
        w_in = matrix_of(held, edges[4] + part * per, edges[4] + (part + 1) * per)
        u = dot_nt(hb, w_in) + row(3 + part)
        value, slope = gelu_parts(u)
        act = value.astype(jnp.bfloat16)
        act_ref[:, cols] = act
        slope_ref[:, cols] = slope.astype(jnp.bfloat16)
        total += dot_nn(act, matrix_of(held, edges[5] + part * per, edges[5] + (part + 1) * per))
    n2, rs2 = norm_parts(total)
    n2_ref[...] = n2
    rs2_ref[...] = rs2
    y = n2 * row(6 + inner_rows) + row(7 + inner_rows)
    out_ref[...] = y.astype(jnp.bfloat16)
    for sent in range(TILE // GROUP):
        cls_ref[0, sent : sent + 1, :] = y[sent * GROUP : sent * GROUP + 1, :]

    @pl.when(pl.program_id(0) == pl.num_programs(0) - 1)
    def _():
        keep.wait()


def tiles(shape):
    rest = len(shape) - 1
    return pl.BlockSpec((TILE,) + tuple(shape[1:]), lambda i, *_: (i,) + (0,) * rest)


def whole(shape):
    return pl.BlockSpec(tuple(shape), lambda i, *_: (0,) * len(shape))


def run_forward(x, small, units, positions, edges):
    rows, width = x.shape
    count = rows // TILE
    sents = TILE // GROUP
    bf, f32 = jnp.bfloat16, jnp.float32
    probs_shape = (rows // GROUP, GROUP, width)
    outs = [
        ((rows, width), bf), ((rows, width), bf), ((rows, width), bf), ((rows, width), bf), (probs_shape, bf),
        ((rows, width), bf), ((rows, width), f32), ((rows, 1), f32), ((rows, width), bf), ((rows, FF), bf),
        ((rows, FF), bf), ((rows, width), f32), ((rows, 1), f32), ((count, sents, width), f32),
        ((edges[6],) + units.shape[1:], bf),
    ]
    specs = [tiles(shape) for shape, _ in outs]
    specs[4] = pl.BlockSpec((sents,) + probs_shape[1:], lambda i, *_: (i, 0, 0))
    specs[13] = pl.BlockSpec((1, sents, width), lambda i, *_: (i, 0, 0))
    specs[14] = pl.BlockSpec(memory_space=pl.ANY)
    return pl.pallas_call(
        functools.partial(forward_kernel, edges),
        name="layer_forward",
        grid_spec=pltpu.PrefetchScalarGridSpec(
            num_scalar_prefetch=1,
            grid=(count,),
            in_specs=[tiles(x.shape), whole(small.shape), pl.BlockSpec(memory_space=pl.ANY)],
            out_specs=specs,
            scratch_shapes=[
                pltpu.VMEM((edges[6],) + units.shape[1:], bf), pltpu.SemaphoreType.DMA((6,)), pltpu.SemaphoreType.DMA,
            ],
        ),
        out_shape=[jax.ShapeDtypeStruct(shape, kind) for shape, kind in outs],
        compiler_params=pltpu.CompilerParams(vmem_limit_bytes=VMEM_MOST),
    )(positions, x, small, units)


def backward_kernel(
    edges, pos_ref, og_ref, dc_ref, small_ref, q_ref, k_ref, v_ref, probs_ref, n1_ref, rs1_ref, slope_ref, n2_ref,
    rs2_ref, units_hbm,
    dx_ref, df_ref, du_ref, da_ref, dq_ref, dk_ref, dv_ref, gsmall_ref, dy_ref, dctx_ref, held, sems,
):
    first_tile = pl.program_id(0) == 0
    width = og_ref.shape[1]
    inner_rows = FF // width

    def need(m):
        @pl.when(first_tile)
        def _():
            fetch_wait(units_hbm, held, sems, edges, m)

    @pl.when(first_tile)
    def _():
        fetch_all(pos_ref, units_hbm, held, sems, edges, (5, 4, 3, 0, 1, 2))
        gsmall_ref[...] = jnp.zeros_like(gsmall_ref)

    row = lambda r: small_ref[r : r + 1, :]

    def add_small(r, values):
        gsmall_ref[r : r + 1, :] += jnp.sum(values.astype(jnp.float32), axis=0, keepdims=True)

    dy_ref[...] = og_ref[...].astype(jnp.float32)
    for sent in range(TILE // GROUP):
        dy_ref[sent * GROUP : sent * GROUP + 1, :] += dc_ref[0, sent : sent + 1, :]
    dy = dy_ref[...]
    n2 = n2_ref[...]
    add_small(6 + inner_rows, dy * n2)
    add_small(7 + inner_rows, dy)
    dr2 = norm_back(dy, n2, rs2_ref[...], row(6 + inner_rows))
    df = dr2.astype(jnp.bfloat16)
    df_ref[...] = df
    add_small(3 + inner_rows, df)
    need(5)
    need(4)
    per = (edges[5] - edges[4]) // inner_rows
    dh1 = dr2
    for part in range(inner_rows):
        cols = slice(part * width, (part + 1) * width)
        da = dot_nt(df, matrix_of(held, edges[5] + part * per, edges[5] + (part + 1) * per))
        du = (da * slope_ref[:, cols].astype(jnp.float32)).astype(jnp.bfloat16)
        du_ref[:, cols] = du
        add_small(3 + part, du)
        dh1 += dot_nn(du, matrix_of(held, edges[4] + part * per, edges[4] + (part + 1) * per))
    n1 = n1_ref[...]
    add_small(4 + inner_rows, dh1 * n1)
    add_small(5 + inner_rows, dh1)
    dr1 = norm_back(dh1, n1, rs1_ref[...], row(4 + inner_rows))
    dattn = dr1.astype(jnp.bfloat16)
    da_ref[...] = dattn
    add_small(2, dattn)
    need(3)
    dctx_ref[...] = dot_nt(dattn, matrix_of(held, edges[3], edges[4])).astype(jnp.bfloat16)
    first, second, is_first = lane_halves()
    every_pair = [slice(pair * 2 * HD, (pair + 1) * 2 * HD) for pair in range(H // 2)]
    for sent in range(TILE // GROUP):
        rows = slice(sent * GROUP, (sent + 1) * GROUP)
        dcc = [both_heads(dctx_ref[rows, lanes], first, second) for lanes in every_pair]
        dprobs = jnp.concatenate(
            [dot_nt(v_ref[rows, lanes], wide) for lanes, wide in zip(every_pair, dcc)], axis=1
        )
        low = probs_ref[sent]
        probs = low.astype(jnp.float32)
        dscores = probs * (dprobs - jnp.sum(dprobs * probs, axis=0, keepdims=True))
        dscores = (dscores * HD ** (-0.5)).astype(jnp.bfloat16)
        dv_ref[rows, :] = jnp.concatenate(
            [dot_nn(low[:, lanes], wide) for lanes, wide in zip(every_pair, dcc)], axis=1
        ).astype(jnp.bfloat16)
        qq = [both_heads(q_ref[rows, lanes], first, second) for lanes in every_pair]
        dk_ref[rows, :] = jnp.concatenate(
            [dot_nn(dscores[:, lanes], wide) for lanes, wide in zip(every_pair, qq)], axis=1
        ).astype(jnp.bfloat16)
        mixed = [dot_tn(dscores[:, lanes], k_ref[rows, lanes]) for lanes in every_pair]
        dq_ref[rows, :] = jnp.concatenate(
            [jnp.where(is_first, m[:GROUP], m[GROUP:]) for m in mixed], axis=1
        ).astype(jnp.bfloat16)
    dx = dr1
    for m, (ref, r) in enumerate(((dq_ref, 0), (dk_ref, None), (dv_ref, 1))):
        need(m)
        rows = ref[...]
        if r is not None:
            add_small(r, rows)
        dx += dot_nt(rows, matrix_of(held, edges[m], edges[m + 1]))
    dx_ref[...] = dx.astype(jnp.bfloat16)


def run_backward(og, dc, small, saved, units, positions, edges):
    rows, width = og.shape
    count = rows // TILE
    sents = TILE // GROUP
    bf, f32 = jnp.bfloat16, jnp.float32
    _, q, k, v, probs, _, n1, rs1, _, _, slope, n2, rs2, _ = saved[:14]
    ins = [og, dc, small, q, k, v, probs, n1, rs1, slope, n2, rs2]
    in_specs = [tiles(a.shape) for a in ins]
    in_specs[1] = pl.BlockSpec((1, sents, width), lambda i, *_: (i, 0, 0))
    in_specs[2] = whole(small.shape)
    in_specs[6] = pl.BlockSpec((sents,) + probs.shape[1:], lambda i, *_: (i, 0, 0))
    outs = [((rows, width), bf)] * 2 + [((rows, FF), bf)] + [((rows, width), bf)] * 4 + [(small.shape, f32)]
    specs = [tiles(shape) for shape, _ in outs]
    specs[7] = whole(small.shape)
    return pl.pallas_call(
        functools.partial(backward_kernel, edges),
        name="layer_backward",
        grid_spec=pltpu.PrefetchScalarGridSpec(
            num_scalar_prefetch=1,
            grid=(count,),
            in_specs=in_specs + [pl.BlockSpec(memory_space=pl.ANY)],
            out_specs=specs,
            scratch_shapes=[
                pltpu.VMEM((TILE, width), f32),
                pltpu.VMEM((TILE, width), bf),
                pltpu.VMEM((edges[6],) + units.shape[1:], bf),
                pltpu.SemaphoreType.DMA((6,)),
            ],
        ),
        out_shape=[jax.ShapeDtypeStruct(shape, kind) for shape, kind in outs],
        compiler_params=pltpu.CompilerParams(vmem_limit_bytes=VMEM_MOST),
    )(positions, *ins, units)


def weight_grad_kernel(
    edges, pos_ref, x_hbm, ctx_hbm, du_hbm, act_hbm, dq_hbm, dk_hbm, dv_hbm, da_hbm, hb_hbm, df_hbm, out_hbm,
    x_v, ctx_v, du_v, act_v, right, staged, sems, out_sems,
):
    width = x_v.shape[1]
    unit_rows = out_hbm.shape[1]
    inner_rows = FF // width
    loads = [(act_hbm, act_v), (df_hbm, right.at[5]), (du_hbm, du_v), (hb_hbm, right.at[4]), (ctx_hbm, ctx_v),
             (da_hbm, right.at[3]), (x_hbm, x_v), (dq_hbm, right.at[0]), (dk_hbm, right.at[1]), (dv_hbm, right.at[2])]
    copies = [pltpu.make_async_copy(src, dst, sems.at[i]) for i, (src, dst) in enumerate(loads)]
    for copy in copies:
        copy.start()
    waited = set()
    per = width // unit_rows
    work = []
    for part in range(inner_rows):
        work.append((act_v, part, 5, edges[5] + part * per, (0, 1)))
    for part in range(inner_rows):
        work.append((du_v, part, 4, edges[4] + part * per, (2, 3)))
    work.append((ctx_v, 0, 3, edges[3], (4, 5)))
    work.append((x_v, 0, 0, edges[0], (6, 7)))
    work.append((x_v, 0, 1, edges[1], (6, 8)))
    work.append((x_v, 0, 2, edges[2], (6, 9)))
    for step, (left, part, m, unit, needs) in enumerate(work):
        slot = step % 2
        for n in needs:
            if n not in waited:
                copies[n].wait()
                waited.add(n)
        if step >= 2:
            pltpu.make_async_copy(out_hbm.at[pl.ds(0, per)], staged.at[slot], out_sems.at[slot]).wait()
        half = per // 2
        for piece in range(2):
            cols = slice(part * width + piece * half * unit_rows, part * width + (piece + 1) * half * unit_rows)
            block = dot_tn(left[:, cols], right[m]).astype(jnp.bfloat16)
            staged[slot, piece * half : (piece + 1) * half] = block.reshape(half, unit_rows, width)
        for n in range(per):
            pltpu.make_async_copy(staged.at[slot, n], out_hbm.at[pos_ref[unit + n]], out_sems.at[slot]).start()
    for slot in range(2):
        pltpu.make_async_copy(out_hbm.at[pl.ds(0, per)], staged.at[slot], out_sems.at[slot]).wait()


def run_weight_grads(x, saved, back, positions, edges, places, unit_rows):
    rows, width = x.shape
    bf = jnp.bfloat16
    ctx, hb, act = saved[5], saved[8], saved[9]
    _, df, du, da, dq, dk, dv, _ = back
    per = width // unit_rows
    anyw = pl.BlockSpec(memory_space=pl.ANY)
    return pl.pallas_call(
        functools.partial(weight_grad_kernel, edges),
        name="weight_grads",
        in_specs=[pl.BlockSpec(memory_space=pltpu.SMEM)] + [anyw] * 10,
        out_specs=anyw,
        scratch_shapes=[
            pltpu.VMEM((rows, width), bf), pltpu.VMEM((rows, width), bf), pltpu.VMEM((rows, FF), bf),
            pltpu.VMEM((rows, FF), bf), pltpu.VMEM((6, rows, width), bf),
            pltpu.VMEM((2, per, unit_rows, width), bf),
            pltpu.SemaphoreType.DMA((10,)), pltpu.SemaphoreType.DMA((2,)),
        ],
        out_shape=jax.ShapeDtypeStruct((places, unit_rows, width), bf),
        compiler_params=pltpu.CompilerParams(vmem_limit_bytes=VMEM_MOST),
    )(positions, x, ctx, du, act, dq, dk, dv, da, hb, df)


STEPS = 6
BAND = 16
HALF = 384


def step_units(edges):
    per = edges[1] - edges[0]
    firsts = [(edges[5] + per * t, edges[4] + per * t) for t in range(4)]
    return firsts + [(edges[3], edges[0]), (edges[1], edges[2])]


def sum_places(edges):
    per = edges[1] - edges[0]
    table = [0] * edges[6]
    for t, firsts in enumerate(step_units(edges)):
        for m, first in enumerate(firsts):
            for k in range(per):
                table[first + k] = (k % 2) * (STEPS * per) + t * per + m * (per // 2) + k // 2
    return table


def backward_reduce_kernel(
    edges, tab_ref, small_ref, dc_ref, rs1_ref, rs2_ref, og_hbm, n2_hbm, slope_hbm, act_hbm, hb_hbm, n1_hbm, ctx_hbm,
    q_hbm, k_hbm, v_hbm, x_hbm, probs_hbm, units_hbm,
    dx_hbm, own_out, small_out,
    dh, nbuf, p0, p1, p2, p3, p4, p5, p6, p7, p8, wbuf, gbuf, c_in, xa, yb, ya, xb, z_in, fbuf, a_out, a_in, x_in,
    gsm, t_acc, t_in,
    l_sem, c_s, c_r, xa_s, xa_r, yb_s, yb_r, ya_s, ya_r, xb_s, xb_r, zr_s, zr_r, zl_s, zl_r, f_s, f_r, a_s, a_r, o_s, o_r,
    t_s, t_r, c_free,
):
    s, z, y, c = place()
    bf, f32 = jnp.bfloat16, jnp.float32
    rows_all, width = dh.shape
    count = rows_all // TILE
    inner_rows = FF // width
    per = edges[1] - edges[0]
    unit_rows = gbuf.shape[4]
    slots = own_out.shape[0]
    upper = unit_rows // 2
    sibling = (s, batch_of(z, y, 1 - c))
    across = (s, batch_of(z, 1 - y, c))
    other = (1 - s, batch_of(z, y, c))
    left = (s, batch_of(z - 1, y, c))
    right = (s, batch_of(z + 1, y, c))
    round_to = (sibling, across, other, (s, batch_of(z + 1 - 2 * (z % 2), y, c)), (s, batch_of((z + 2) % ZS, y, c)))

    barrier = pltpu.get_barrier_semaphore()

    def hello(target):
        pl.semaphore_signal(barrier, inc=1, device_id=target, device_id_type=MESH)

    hello(sibling)
    hello(other)
    turns = [(dz, dy) for dz in range(ZS) for dy in range(2) if dz or dy]
    for dz, dy in turns:
        hello((s, batch_of((z + dz) % ZS, (y + dy) % 2, c)))
    pl.semaphore_wait(barrier, 2 + len(turns))

    chunk = lambda ref, p: ref.at[:, pl.ds(p * width, width)]
    matrix = lambda first: units_hbm.at[pl.ds(first, per)]
    firsts = step_units(edges)
    acts, slopes = (p3, p5), (p4, p6)
    loads = {"og": (og_hbm, p0), "n2": (n2_hbm, nbuf), "hb": (hb_hbm, p2), "n1": (n1_hbm, nbuf), "probs": (probs_hbm, p0),
             "ctx": (ctx_hbm, p3), "q": (q_hbm, p4), "k": (k_hbm, p7), "v": (v_hbm, p8), "x": (x_hbm, p3)}
    for p in range(inner_rows):
        loads["act%d" % p] = (chunk(act_hbm, p), acts[p % 2])
        loads["slope%d" % p] = (chunk(slope_hbm, p), slopes[p % 2])
        loads["wo%d" % p] = (matrix(firsts[p][0]), wbuf.at[p % 2, 0])
        loads["wi%d" % p] = (matrix(firsts[p][1]), wbuf.at[p % 2, 1])
    for t in (4, 5):
        for m in range(2):
            loads["w%d%d" % (t, m)] = (matrix(firsts[t][m]), wbuf.at[t % 2, m])
    copies = {
        name: pltpu.make_async_copy(src, dst, l_sem.at[n]) for n, (name, (src, dst)) in enumerate(loads.items())
    }

    def begin(*names):
        for name in names:
            copies[name].start()

    def ready(*names):
        for name in names:
            copies[name].wait()

    begin("og", "n2", "slope0", "wo0", "wi0", "act0", "hb", "slope1", "wo1", "wi1", "act1", "k", "v")

    row = lambda r: small_ref[r : r + 1, :]
    gsm[...] = jnp.zeros_like(gsm)

    def add_small(r, values):
        gsm[r : r + 1, :] += jnp.sum(values.astype(f32), axis=0, keepdims=True)

    def tile_rows(i):
        return pl.ds(pl.multiple_of(i * TILE, TILE), TILE)

    def weight(slot, m):
        return wbuf[slot, m].reshape(per * unit_rows, width)

    def remote(src, dst, send, recv, target):
        return pltpu.make_async_remote_copy(
            src_ref=src, dst_ref=dst, send_sem=send, recv_sem=recv, device_id=target, device_id_type=MESH
        )

    my_rows = pl.ds(pl.multiple_of(s * upper, upper), upper)
    its_rows = pl.ds(pl.multiple_of((1 - s) * upper, upper), upper)
    my_cols = pl.ds(pl.multiple_of(y * HALF, 128), HALF)
    its_cols = pl.ds(pl.multiple_of((1 - y) * HALF, 128), HALF)
    every = pl.ds(0, per // 2)

    def band(zz):
        return pl.ds(pl.multiple_of(s * upper + zz * BAND, BAND), BAND)

    def c_copy(t):
        return remote(gbuf.at[t, :, 1 - c], c_in.at[t % RING], c_s.at[t], c_r.at[t], sibling)

    def xa_copy(t):
        return remote(gbuf.at[t, 0, c, every, its_rows], xa.at[t], xa_s.at[t], xa_r.at[t], other)

    def yb_copy(t):
        return remote(gbuf.at[t, 1, c, every, pl.ds(0, unit_rows), its_cols], yb.at[t], yb_s.at[t], yb_r.at[t], across)

    def ya_copy(t):
        return remote(gbuf.at[t, 0, c, every, my_rows, its_cols], ya.at[t], ya_s.at[t], ya_r.at[t], across)

    def xb_copy(t):
        return remote(gbuf.at[t, 1, c, every, its_rows, my_cols], xb.at[t], xb_s.at[t], xb_r.at[t], other)

    def z_copy(t, zz, way):
        send, recv, target = ((zr_s, zr_r, right), (zl_s, zl_r, left))[way]
        return remote(
            gbuf.at[t, pl.ds(0, 2), c, every, band(zz), my_cols], z_in.at[way, t, zz], send.at[t, zz], recv.at[t, zz], target
        )

    def f_copy(t):
        mine = fbuf.at[pl.ds(c * (STEPS * per) + t * per, per)]
        return remote(mine, mine, f_s.at[t], f_r.at[t], sibling)

    def turn(r):
        return remote(t_acc.at[r], t_in.at[r], t_s.at[r], t_r.at[r], round_to[r])

    def add(view, got):
        @pl.loop(0, per // 2)
        def _(k):
            view.at[k][...] = (view.at[k][...].astype(f32) + got.at[k][...].astype(f32)).astype(bf)

    def ev_c_send(t):
        if t >= RING:
            pl.semaphore_wait(c_free, 1)
        c_copy(t).start()

    def ev_c_wait(t):
        c_copy(t).wait_recv()
        add(gbuf.at[t, 0, c], c_in.at[t % RING, 0])
        xa_copy(t).start()
        add(gbuf.at[t, 1, c], c_in.at[t % RING, 1])
        if t + RING < STEPS:
            pl.semaphore_signal(c_free, inc=1, device_id=sibling, device_id_type=MESH)
        yb_copy(t).start()

    def ev_first(t):
        xa_copy(t).wait_recv()
        add(gbuf.at[t, 0, c, every, my_rows], xa.at[t])
        ya_copy(t).start()
        yb_copy(t).wait_recv()
        add(gbuf.at[t, 1, c, every, pl.ds(0, unit_rows), my_cols], yb.at[t])
        xb_copy(t).start()

    def ev_second(t):
        ya_copy(t).wait_recv()
        add(gbuf.at[t, 0, c, every, my_rows, my_cols], ya.at[t])
        xb_copy(t).wait_recv()
        add(gbuf.at[t, 1, c, every, my_rows, my_cols], xb.at[t])

    def ev_z(t, hop):
        @pl.when(z == hop)
        def _():
            @pl.loop(0, ZS)
            def _(zz):
                @pl.when(zz >= z)
                def _():
                    @pl.when(z > 0)
                    def _():
                        z_copy(t, zz, 0).wait_recv()
                        for m in range(2):
                            add(gbuf.at[t, m, c, every, band(zz), my_cols], z_in.at[0, t, zz, m])

                    @pl.when(zz > z)
                    def _():
                        z_copy(t, zz, 0).start()

        @pl.when(ZS - 1 - z == hop)
        def _():
            @pl.loop(0, ZS)
            def _(zz):
                @pl.when(zz <= z)
                def _():
                    @pl.when(z < ZS - 1)
                    def _():
                        z_copy(t, zz, 1).wait_recv()
                        for m in range(2):
                            add(gbuf.at[t, m, c, every, band(zz), my_cols], z_in.at[1, t, zz, m])

                    @pl.when(zz < z)
                    def _():
                        z_copy(t, zz, 1).start()

    def ev_fin(t):
        for m in range(2):

            @pl.loop(0, per // 2)
            def _(k):
                at = c * (STEPS * per) + t * per + m * (per // 2) + k
                fbuf[at] = gbuf[t, m, c, k, band(z), my_cols]

        f_copy(t).start()

    def ev_turn_start(r):
        if r == 0:
            t_acc[0] = gsm[...]
        turn(r).start()

    def ev_turn_wait(r):
        turn(r).wait()
        t_acc[r + 1] = t_acc[r] + t_in[r]

    def sec_start():
        ready("og", "n2")
        for i in range(count):
            rows = slice(i * TILE, (i + 1) * TILE)
            dh[rows, :] = p0[rows, :].astype(f32)
            for sent in range(TILE // GROUP):
                at = i * TILE + sent * GROUP
                here = i * (TILE // GROUP) + sent
                dh[at : at + 1, :] += dc_ref[here : here + 1, :]
            dy = dh[rows, :]
            n2 = nbuf[rows, :]
            add_small(6 + inner_rows, dy * n2)
            add_small(7 + inner_rows, dy)
            dr2 = norm_back(dy, n2, rs2_ref[rows, :], row(6 + inner_rows))
            dh[rows, :] = dr2
            df = dr2.astype(bf)
            p1[rows, :] = df
            add_small(3 + inner_rows, df)
        begin("n1", "probs")

    def store_grads(t, m, lhs, rhs):
        @pl.loop(0, 2)
        def _(piece):
            half = (per // 2) * unit_rows
            cols = pl.ds(pl.multiple_of(piece * half, 128), half)
            block = dot_tn(lhs[:, cols], rhs[...]).astype(bf)
            for i in range(per // 2):
                part = block[i * unit_rows : (i + 1) * unit_rows]

                @pl.when(piece == 0)
                def _():
                    gbuf[t, m, i % 2, i // 2] = part

                @pl.when(piece == 1)
                def _():
                    k = per // 2 + i
                    gbuf[t, m, k % 2, k // 2] = part

    def sec_inner(p):
        def run():
            ready("slope%d" % p, "wo%d" % p, "wi%d" % p)
            slope = slopes[p % 2]

            @pl.loop(0, count)
            def _(i):
                rows = tile_rows(i)
                da = dot_nt(p1[rows, :], weight(p % 2, 0))
                du = (da * slope[rows, :].astype(f32)).astype(bf)
                slope[rows, :] = du
                add_small(3 + p, du)
                dh[rows, :] += dot_nn(du, weight(p % 2, 1))

            if p == 2:
                begin("w40", "w41")
            if p == 3:
                begin("w50", "w51")
            if p + 2 < inner_rows:
                begin("wo%d" % (p + 2), "wi%d" % (p + 2))

        return run

    def sec_outer_grad(p):
        def run():
            ready("act%d" % p)
            store_grads(p, 0, acts[p % 2], p1)
            if p + 2 < inner_rows:
                begin("act%d" % (p + 2))
            if p == 2:
                begin("ctx")

        return run

    def sec_inner_grad(p):
        def run():
            if p == 0:
                ready("hb")
            store_grads(p, 1, slopes[p % 2], p2)
            if p + 2 < inner_rows:
                begin("slope%d" % (p + 2))
            if p == 2:
                begin("q")

        return run

    def sec_norm():
        ready("n1", "w40", "w41")

        @pl.loop(0, count)
        def _(i):
            rows = tile_rows(i)
            dh1 = dh[rows, :]
            n1 = nbuf[rows, :]
            add_small(4 + inner_rows, dh1 * n1)
            add_small(5 + inner_rows, dh1)
            dr1 = norm_back(dh1, n1, rs1_ref[rows, :], row(4 + inner_rows))
            dh[rows, :] = dr1
            dattn = dr1.astype(bf)
            p1[rows, :] = dattn
            add_small(2, dattn)
            p5[rows, :] = dot_nt(dattn, weight(0, 0)).astype(bf)

    def sec_out_grad():
        ready("ctx")
        store_grads(4, 0, p3, p1)
        begin("x")

    first, second, is_first = lane_halves()
    every_pair = [slice(pair * 2 * HD, (pair + 1) * 2 * HD) for pair in range(H // 2)]

    def sec_heads(part):
        def run():
            if part == 0:
                ready("probs", "q", "k", "v")
            amount = rows_all // GROUP // 2

            @pl.loop(part * amount, (part + 1) * amount)
            def _(sent):
                rows = pl.ds(pl.multiple_of(sent * GROUP, GROUP), GROUP)
                dctx, q, k, v, low = p5[rows, :], p4[rows, :], p7[rows, :], p8[rows, :], p0[rows, :]
                dcc = [both_heads(dctx[:, lanes], first, second) for lanes in every_pair]
                dprobs = jnp.concatenate([dot_nt(v[:, lanes], wide) for lanes, wide in zip(every_pair, dcc)], axis=1)
                probs = low.astype(f32)
                dscores = probs * (dprobs - jnp.sum(dprobs * probs, axis=0, keepdims=True))
                dscores = (dscores * HD ** (-0.5)).astype(bf)
                dv = jnp.concatenate(
                    [dot_nn(low[:, lanes], wide) for lanes, wide in zip(every_pair, dcc)], axis=1
                ).astype(bf)
                p6[rows, :] = dv
                add_small(1, dv)
                qq = [both_heads(q[:, lanes], first, second) for lanes in every_pair]
                p2[rows, :] = jnp.concatenate(
                    [dot_nn(dscores[:, lanes], wide) for lanes, wide in zip(every_pair, qq)], axis=1
                ).astype(bf)
                mixed = [dot_tn(dscores[:, lanes], k[:, lanes]) for lanes in every_pair]
                dq = jnp.concatenate([jnp.where(is_first, m[:GROUP], m[GROUP:]) for m in mixed], axis=1).astype(bf)
                p1[rows, :] = dq
                add_small(0, dq)

        return run

    def sec_query_grad():
        ready("x")
        store_grads(4, 1, p3, p1)

    def sec_key_grad():
        store_grads(5, 0, p3, p2)

    def sec_value_grad():
        store_grads(5, 1, p3, p6)

    def sec_back(part):
        def run():
            if part == 0:
                ready("w50", "w51")

            @pl.loop(part * (count // 2), (part + 1) * (count // 2))
            def _(i):
                rows = tile_rows(i)
                dx = dh[rows, :] + dot_nt(p1[rows, :], weight(0, 1))
                dx += dot_nt(p2[rows, :], weight(1, 0)) + dot_nt(p6[rows, :], weight(1, 1))
                p4[rows, :] = dx.astype(bf)

        return run

    sections = [sec_start]
    for p in range(inner_rows):
        sections += [sec_inner(p), sec_outer_grad(p), sec_inner_grad(p)]
    sections += [sec_norm, sec_out_grad, sec_heads(0), sec_heads(1), sec_query_grad, sec_key_grad, sec_value_grad]
    sections += [sec_back(0), sec_back(1)]
    done = [3, 6, 9, 12, 17, 19]
    events = {}

    def at_tick(tick, order, action):
        events.setdefault(tick, []).append((order, action))

    for t in range(STEPS):
        base = done[t]
        at_tick(base, 0, functools.partial(ev_c_send, t))
        at_tick(base + 1, 1, functools.partial(ev_c_wait, t))
        at_tick(base + 1 + LAG_FIRST, 2, functools.partial(ev_first, t))
        at_tick(base + 1 + LAG_FIRST + LAG_SECOND, 3, functools.partial(ev_second, t))
        for hop in range(ZS):
            at_tick(base + 1 + LAG_FIRST + LAG_SECOND + hop, 4 + hop, functools.partial(ev_z, t, hop))
        at_tick(base + 1 + LAG_FIRST + LAG_SECOND + ZS - 1, 9, functools.partial(ev_fin, t))
    for r in range(5):
        at_tick(17 + 2 * r, 10, functools.partial(ev_turn_start, r))
        at_tick(19 + 2 * r, -1, functools.partial(ev_turn_wait, r))
    for tick in range(max(max(events) + 1, len(sections))):
        if tick < len(sections):
            sections[tick]()
        if tick == len(sections) - 1:
            dx_copy = pltpu.make_async_copy(p4, dx_hbm, l_sem.at[len(loads)])
            dx_copy.start()
        for _, action in sorted(events.get(tick, []), key=lambda item: item[0]):
            action()
    small_out[...] = t_acc[5]
    for t in range(STEPS):
        its = fbuf.at[pl.ds((1 - c) * (STEPS * per) + t * per, per)]
        remote(its, its, f_s.at[t], f_r.at[t], sibling).wait_recv()

    def a_copy(zz, yy):
        return remote(a_out.at[zz, yy], a_in.at[z, y], a_s.at[zz, yy], a_r.at[z, y], (s, batch_of(zz, yy, c)))

    def o_copy(zz, yy):
        return remote(a_in.at[zz, yy], x_in.at[zz, yy], o_s.at[zz, yy], o_r.at[zz, yy], other)

    for dz, dy in turns:
        zz, yy = (z + dz) % ZS, (y + dy) % 2
        for j in range(slots):
            a_out[zz, yy, j] = fbuf[tab_ref[batch_of(zz, yy, c) * slots + j]]
        a_copy(zz, yy).start()
    for j in range(slots):
        a_in[z, y, j] = fbuf[tab_ref[batch_of(z, y, c) * slots + j]]
    o_copy(z, y).start()

    def put(zz, yy, ss, got):
        rows = pl.ds(pl.multiple_of(ss * upper + zz * BAND, BAND), BAND)
        cols = pl.ds(pl.multiple_of(yy * HALF, 128), HALF)
        for j in range(slots):
            own_out[j, rows, cols] = got[zz, yy, j]

    put(z, y, s, a_in)
    for dz, dy in turns:
        zz, yy = (z + dz) % ZS, (y + dy) % 2
        remote(a_in.at[zz, yy], a_in.at[zz, yy], a_s.at[zz, yy], a_r.at[zz, yy], other).wait_recv()
        o_copy(zz, yy).start()
        put(zz, yy, s, a_in)
    for dz, dy in [(0, 0)] + turns:
        zz, yy = (z + dz) % ZS, (y + dy) % 2
        o_copy(zz, yy).wait_recv()
        put(zz, yy, 1 - s, x_in)
    for t in range(STEPS):
        for copy in (c_copy, xa_copy, yb_copy, ya_copy, xb_copy, f_copy):
            copy(t).wait_send()

        @pl.loop(0, ZS)
        def _(zz):
            @pl.when(zz > z)
            def _():
                z_copy(t, zz, 0).wait_send()

            @pl.when(zz < z)
            def _():
                z_copy(t, zz, 1).wait_send()

    for dz, dy in turns:
        a_copy((z + dz) % ZS, (y + dy) % 2).wait_send()
    for dz, dy in [(0, 0)] + turns:
        o_copy((z + dz) % ZS, (y + dy) % 2).wait_send()
    dx_copy.wait()


RING = 3
LAG_FIRST = 3
LAG_SECOND = 2


def run_backward_reduce(og, dc, small, saved, x, units, table, edges, slots):
    rows, width = og.shape
    bf, f32 = jnp.bfloat16, jnp.float32
    _, q, k, v, probs, ctx, n1, rs1, hb, act, slope, n2, rs2, _ = saved[:14]
    unit_rows = units.shape[1]
    per = edges[1] - edges[0]
    half = per // 2
    dma = pltpu.SemaphoreType.DMA
    vm = pltpu.VMEM
    vmem = pl.BlockSpec(memory_space=pltpu.VMEM)
    anyw = pl.BlockSpec(memory_space=pl.ANY)
    upper = unit_rows // 2
    return pl.pallas_call(
        functools.partial(backward_reduce_kernel, edges),
        name="backward_reduce",
        out_shape=[
            jax.ShapeDtypeStruct((rows, width), bf),
            jax.ShapeDtypeStruct((slots, unit_rows, width), bf),
            jax.ShapeDtypeStruct(small.shape, f32),
        ],
        in_specs=[pl.BlockSpec(memory_space=pltpu.SMEM)] + [vmem] * 4 + [anyw] * 13,
        out_specs=[anyw, vmem, vmem],
        scratch_shapes=[vm((rows, width), f32)] * 2
        + [vm((rows, width), bf)] * 9
        + [
            vm((2, 2, per, unit_rows, width), bf),
            vm((STEPS, 2, 2, half, unit_rows, width), bf),
            vm((RING, 2, half, unit_rows, width), bf),
            vm((STEPS, half, upper, width), bf),
            vm((STEPS, half, unit_rows, HALF), bf),
            vm((STEPS, half, upper, HALF), bf),
            vm((STEPS, half, upper, HALF), bf),
            vm((2, STEPS, ZS, 2, half, BAND, HALF), bf),
            vm((2 * STEPS * per, BAND, HALF), bf),
            vm((ZS, 2, slots, BAND, HALF), bf),
            vm((ZS, 2, slots, BAND, HALF), bf),
            vm((ZS, 2, slots, BAND, HALF), bf),
            vm(small.shape, f32),
            vm((6,) + small.shape, f32),
            vm((5,) + small.shape, f32),
        ]
        + [dma((32,))]
        + [dma((STEPS,))] * 10
        + [dma((STEPS, ZS))] * 4
        + [dma((STEPS,))] * 2
        + [dma((ZS, 2))] * 4
        + [dma((5,))] * 2
        + [pltpu.SemaphoreType.REGULAR],
        compiler_params=pltpu.CompilerParams(collective_id=3, has_side_effects=True, vmem_limit_bytes=63 << 20),
    )(table, small, dc, rs1, rs2, og, n2, slope, act, hb, n1, ctx, q, k, v, x, probs.reshape(rows, width), units)


def unit_positions(owner_list, slot_count):
    unit_total = owner_list.shape[0]
    same_owner = owner_list[:, None] == owner_list[None, :]
    ordinal = jnp.arange(unit_total, dtype=jnp.int32)
    earlier = ordinal[None, :] < ordinal[:, None]
    slot_number = jnp.sum(jnp.where(same_owner & earlier, 1, 0), axis=1).astype(jnp.int32)
    return owner_list * slot_count + slot_number


def adamw(weight_in, gradient, moment_one, moment_two, rate_value, decay_value, fix_one, fix_two):
    new_one = BETA_ONE * moment_one + (1.0 - BETA_ONE) * gradient
    new_two = BETA_TWO * moment_two + (1.0 - BETA_TWO) * gradient * gradient
    stepped = new_one / fix_one / (jnp.sqrt(new_two / fix_two) + ADAM_EPS)
    return (weight_in - rate_value * (stepped + decay_value * weight_in), new_one, new_two)


def any_size_units(own, positions, owners):
    slots, rows, width = own.shape
    table = jnp.arange(owners * slots, dtype=jnp.int32)[:, None] == positions[None, :]
    bands = lax.all_to_all(
        own.transpose(1, 0, 2).astype(jnp.bfloat16), "batch", split_axis=0, concat_axis=1, tiled=True
    )
    ordered = jnp.einsum(
        "rpd,pu->rud", bands, table.astype(jnp.bfloat16), preferred_element_type=jnp.float32
    ).astype(jnp.bfloat16)
    return lax.all_gather(ordered, "batch", axis=0, tiled=True).transpose(1, 0, 2)


def any_size_sums(grads, positions, owners, slots):
    table = jnp.arange(owners * slots, dtype=jnp.int32)[:, None] == positions[None, :]
    pieces = lax.psum_scatter(grads.transpose(1, 0, 2).astype(jnp.float32), "batch", scatter_dimension=0, tiled=True)
    summed = lax.psum(pieces.astype(jnp.bfloat16), "stream").astype(jnp.float32)
    send_rows = jnp.einsum("rud,pu->rpd", summed, table.astype(jnp.float32), precision=HIGHEST)
    owned = lax.all_to_all(send_rows.astype(jnp.bfloat16), "batch", split_axis=1, concat_axis=0, tiled=True)
    return owned.astype(jnp.float32).transpose(1, 0, 2)


def any_size_rank(cls, scale, langs, owners):
    sents, width = cls.shape
    root = lax.rsqrt(jnp.sum(cls * cls, axis=-1, keepdims=True) + NORM_EPS)
    unit = cls * root
    every = lax.all_gather(unit.astype(jnp.bfloat16), "batch", axis=0, tiled=True)
    every = lax.all_gather(every, "stream", axis=0)
    cosines = jnp.dot(every[0], every[1].T, preferred_element_type=jnp.float32)
    diagonal = jnp.eye(cosines.shape[0], dtype=jnp.float32)
    same = langs[:, None] == langs[None, :]
    shifted = cosines - MARGIN * diagonal
    logits = scale[0] * shifted
    masked = jnp.where(same, logits, -1e30)
    both = -2.0 * diagonal
    total = -2.0 * jnp.sum(logits * diagonal)
    for axis in range(2):
        top = jnp.max(masked, axis=axis, keepdims=True)
        grown = jnp.where(same, jnp.exp(masked - top), 0.0)
        summed = jnp.sum(grown, axis=axis, keepdims=True)
        both += grown / summed
        total += jnp.sum(jnp.log(summed) + top)
    s = lax.axis_index("stream")
    turned = jnp.where(s == 0, both, both.T)
    rows = lax.dynamic_slice_in_dim(turned, lax.axis_index("batch") * sents, sents)
    partners = lax.dynamic_index_in_dim(every, 1 - s, keepdims=False).astype(jnp.float32)
    de = scale[0] * jnp.dot(rows, partners, precision=HIGHEST)
    dc = (de - unit * jnp.sum(unit * de, axis=-1, keepdims=True)) * root
    return dc, total, jnp.sum(both * shifted)


def per_device(
    tokens, out_grad, master, first_moment, second_moment, small_params, small_first, small_second, logit_scale,
    scale_first, scale_second, pair_lang, unit_owner,
):
    owners = lax.axis_size("batch")
    here_batch = lax.axis_index("batch")
    unit_rows, slot_count, width = master.shape
    query_blocks = width // unit_rows
    inner_blocks = FF // unit_rows
    edges = [query_blocks * n for n in range(5)]
    edges += [edges[4] + inner_blocks, edges[4] + 2 * inner_blocks]
    units_total = unit_owner.shape[0]
    positions = unit_positions(unit_owner, slot_count)
    on_block = owners == 4 * ZS
    own = master.transpose(1, 0, 2)
    if on_block:
        units, where, places = gather_units(own), positions, owners * slot_count
    else:
        units = any_size_units(own, positions, owners)
        where, places = jnp.arange(units_total, dtype=jnp.int32), units_total
    sentences, length = tokens.shape[1], tokens.shape[2]
    flat = tokens.reshape(sentences * length, width)
    saved = run_forward(flat, small_params, units, where, edges)
    cls = saved[13]
    if on_block:
        dc, stats = rank_loss(cls.reshape(sentences, width), logit_scale, pair_lang)
        loss_total, grad_scale = stats[0, :1], stats[1, :1]
    else:
        dc, loss_total, grad_scale = any_size_rank(cls.reshape(sentences, width), logit_scale, pair_lang, owners)
        loss_total, grad_scale = loss_total.reshape(1), grad_scale.reshape(1)
    grad_rows = out_grad.reshape(sentences * length, width)
    if on_block:
        slot_units = jnp.arange(places, dtype=jnp.int32)[:, None] == positions[None, :]
        sum_table = jnp.asarray(sum_places(edges), dtype=jnp.int32)
        table = jnp.sum(jnp.where(slot_units, sum_table[None, :], 0), axis=1, dtype=jnp.int32)
        d_tokens, owned_grad, small_total = run_backward_reduce(
            grad_rows, dc, small_params, saved, flat, saved[14], table, edges, slot_count
        )
        owned_grad = owned_grad.astype(jnp.float32)
    else:
        back = run_backward(grad_rows, dc.reshape(cls.shape), small_params, saved, units, where, edges)
        grads = run_weight_grads(flat, saved, back, where, edges, places, unit_rows)
        d_tokens = back[0]
        owned_grad = any_size_sums(grads, positions, owners, slot_count)
        small_total = lax.psum(back[7], ("stream", "batch"))
    step_value = float(STEP)
    fix_one = 1.0 - BETA_ONE**step_value
    fix_two = 1.0 - BETA_TWO**step_value
    my_places = here_batch * slot_count + jnp.arange(slot_count, dtype=jnp.int32)
    filled = jnp.any(my_places[:, None] == positions[None, :], axis=1)[:, None, None]
    first_in, second_in = first_moment.transpose(1, 0, 2), second_moment.transpose(1, 0, 2)
    moved = adamw(own, owned_grad, first_in, second_in, RATE_UNITS, DECAY, fix_one, fix_two)
    new_master, new_first, new_second = (
        jnp.where(filled, new, old) for new, old in zip(moved, (own, first_in, second_in))
    )
    new_copy = new_master.astype(jnp.bfloat16)
    new_small, new_small_first, new_small_second = adamw(
        small_params, small_total, small_first, small_second, RATE_SMALL, 0.0, fix_one, fix_two
    )
    scale_new, scale_one, scale_two = adamw(
        logit_scale, grad_scale, scale_first, scale_second, RATE_SCALE, 0.0, fix_one, fix_two
    )
    loss_out = loss_total / (2 * owners * sentences)
    back_order = lambda a: a.transpose(1, 0, 2)
    return (
        saved[0].reshape(tokens.shape),
        d_tokens.reshape(tokens.shape),
        back_order(new_master),
        back_order(new_first),
        back_order(new_second),
        back_order(new_copy),
        new_small,
        new_small_first,
        new_small_second,
        scale_new,
        scale_one,
        scale_two,
        loss_out,
    )


def solution(mesh):
    rows = P("stream", "batch", None, None)
    blocks = P(None, "batch", None)
    return jax.shard_map(
        per_device,
        mesh=mesh,
        in_specs=(rows, rows, blocks, blocks, blocks) + (P(),) * 8,
        out_specs=(rows, rows, blocks, blocks, blocks, blocks) + (P(),) * 7,
        check_vma=False,
    )
```

```python
import functools

import jax
import jax.numpy as jnp
from jax import lax
from jax.experimental import pallas as pl
from jax.experimental.pallas import tpu as pltpu
from jax.sharding import PartitionSpec as P

H = 12
HD = 64
FF = 3072
STEP = 10
ZS = 4
UR_ROWS = 128
LEN_ROWS = 64
VMEM_MOST = 60 << 20
MESH = pl.DeviceIdType.MESH

HIGHEST = lax.Precision.HIGHEST
BETA_ONE = 0.9
BETA_TWO = 0.999
ADAM_EPS = 1e-06
RATE_UNITS = 0.02
RATE_SMALL = 0.1
RATE_SCALE = 2.0
DECAY = 0.01
MARGIN = 0.3
NORM_EPS = 1e-06


def place():
    s = lax.axis_index("stream")
    b = lax.axis_index("batch")
    return s, b // 4, (b // 2) % 2, b % 2


def batch_of(z, y, c):
    return (z * 2 + y) * 2 + c


def greet(s, z, y, c, others):
    barrier = pltpu.get_barrier_semaphore()

    def hello(target):
        pl.semaphore_signal(barrier, inc=1, device_id=target, device_id_type=MESH)

    hello((s, batch_of(z, y, 1 - c)))
    hello((s, batch_of(z, 1 - y, c)))
    hello((1 - s, batch_of(z, y, c)))
    if others == "line":
        for far in range(1, ZS):

            @pl.when(z >= far)
            def _():
                hello((s, batch_of(z - far, y, c)))

            @pl.when(z + far < ZS)
            def _():
                hello((s, batch_of(z + far, y, c)))

        pl.semaphore_wait(barrier, 3 + ZS - 1)
    else:

        @pl.when(z >= 1)
        def _():
            hello((s, batch_of(z - 1, y, c)))

        @pl.when(z + 1 < ZS)
        def _():
            hello((s, batch_of(z + 1, y, c)))

        pl.semaphore_wait(barrier, 3 + (z + 2) // 3 + (5 - z) // 3)


GR = 80
GX = UR_ROWS - GR


def gather_kernel(own_ref, out_ref, low, stage_sem, zl_s, zl_r, zr_s, zr_r, y_s, y_r, x_s, x_r, ca_s, ca_r, cb_s, cb_r):
    s, z, y, c = place()
    slots = own_ref.shape[0]
    steps = ZS * slots
    base = pl.multiple_of(s * GX, 16)
    only = pl.multiple_of(s * GR, 16)
    theirs = pl.multiple_of((1 - s) * GR, 16)

    def at(zz, yy, cc, j):
        return batch_of(zz, yy, cc) * slots + j

    greet(s, z, y, c, "next")

    def push(src, row, start, size, send, recv, target):
        return pltpu.make_async_remote_copy(
            src_ref=src,
            dst_ref=out_ref.at[row, pl.ds(start, size)],
            send_sem=send,
            recv_sem=recv,
            device_id=target,
            device_id_type=MESH,
        )

    left = (s, batch_of(z - 1, y, c))
    right = (s, batch_of(z + 1, y, c))
    across = (s, batch_of(z, 1 - y, c))
    other = (1 - s, batch_of(z, y, c))
    sibling = (s, batch_of(z, y, 1 - c))

    def to_left(src, zz, j):
        row = at(zz, y, c, j)
        return push(src(row), row, base, GR, zl_s.at[zz, j], zl_r.at[zz, j], left)

    def to_right(src, zz, j):
        row = at(zz, y, c, j)
        return push(src(row), row, base, GR, zr_s.at[zz, j], zr_r.at[zz, j], right)

    def to_across(src, zz, j):
        row = at(zz, y, c, j)
        return push(src(row), row, base, GR, y_s.at[zz, j], y_r.at[zz, j], across)

    def to_other(zz, yy, j):
        row = at(zz, yy, c, j)
        return push(out_ref.at[row, pl.ds(only, GX)], row, only, GX, x_s.at[zz, yy, j], x_r.at[zz, yy, j], other)

    def to_sibling(zz, yy, j):
        row = at(zz, yy, c, j)
        return push(out_ref.at[row, pl.ds(base, GR)], row, base, GR, ca_s.at[zz, yy, j], ca_r.at[zz, yy, j], sibling)

    def rest_to_sibling(zz, yy, j):
        row = at(zz, yy, c, j)
        return push(out_ref.at[row, pl.ds(theirs, GX)], row, theirs, GX, cb_s.at[zz, yy, j], cb_r.at[zz, yy, j], sibling)

    def landed(row):
        return out_ref.at[row, pl.ds(base, GR)]

    def from_left(zz, j):
        row = at(zz, y, c, j)
        return push(landed(row), row, base, GR, zr_s.at[zz, j], zr_r.at[zz, j], right)

    def arrived_line(zz, j, onward):
        onward.start()
        to_across(landed, zz, j).start()
        to_other(zz, y, j).start()
        to_sibling(zz, y, j).start()

    def stage(j):
        return pltpu.make_async_copy(low.at[j], out_ref.at[at(z, y, c, j)], stage_sem.at[j])

    for j in range(slots):
        low[j] = own_ref[j].astype(jnp.bfloat16)
        mine = lambda row: low.at[j, pl.ds(base, GR)]

        @pl.when(z > 0)
        def _():
            to_left(mine, z, j).start()

        @pl.when(z < ZS - 1)
        def _():
            to_right(mine, z, j).start()

        to_across(mine, z, j).start()
        row = at(z, y, c, j)
        push(low.at[j, pl.ds(base, GR)], row, base, GR, ca_s.at[z, y, j], ca_r.at[z, y, j], sibling).start()
        push(low.at[j, pl.ds(theirs, GX)], row, theirs, GX, cb_s.at[z, y, j], cb_r.at[z, y, j], sibling).start()
        stage(j).start()

    def line_step(t):
        d = t // slots
        j = t % slots

        @pl.when((d >= 1) & (z - d >= 0))
        def _():
            zz = z - d
            to_right(landed, zz, j).wait_recv()

            @pl.when(z < ZS - 1)
            def _():
                to_right(landed, zz, j).start()

            to_across(landed, zz, j).start()
            to_other(zz, y, j).start()
            to_sibling(zz, y, j).start()

        @pl.when((d >= 1) & (z + d < ZS))
        def _():
            zz = z + d
            to_left(landed, zz, j).wait_recv()

            @pl.when(z > 0)
            def _():
                to_left(landed, zz, j).start()

            to_across(landed, zz, j).start()
            to_other(zz, y, j).start()
            to_sibling(zz, y, j).start()

    def across_one(zz, j):
        row = at(zz, 1 - y, c, j)
        push(landed(row), row, base, GR, y_s.at[zz, j], y_r.at[zz, j], across).wait_recv()
        to_other(zz, 1 - y, j).start()
        to_sibling(zz, 1 - y, j).start()

    def across_step(t):
        d = t // slots
        j = t % slots

        @pl.when(z - d >= 0)
        def _():
            across_one(z - d, j)

        @pl.when((d >= 1) & (z + d < ZS))
        def _():
            across_one(z + d, j)

    def other_one(zz, yy, j):
        row = at(zz, yy, c, j)
        push(
            out_ref.at[row, pl.ds(theirs, GX)], row, theirs, GX, x_s.at[zz, yy, j], x_r.at[zz, yy, j], other
        ).wait_recv()
        rest_to_sibling(zz, yy, j).start()

    def other_step(t, yy, first):
        d = t // slots
        j = t % slots

        @pl.when((d >= first) & (z - d >= 0))
        def _():
            other_one(z - d, yy, j)

        @pl.when((d >= 1) & (z + d < ZS))
        def _():
            other_one(z + d, yy, j)

    @pl.loop(0, steps + 3)
    def _(t):
        @pl.when(t < steps)
        def _():
            line_step(t)

        @pl.when((t >= 1) & (t < steps + 1))
        def _():
            across_step(t - 1)

        @pl.when((t >= 2) & (t < steps + 2))
        def _():
            other_step(t - 2, y, 1)

        @pl.when(t >= 3)
        def _():
            other_step(t - 3, 1 - y, 0)

    for j in range(slots):
        stage(j).wait()

    @pl.loop(0, steps)
    def _(t):
        zz = t // slots
        j = t % slots

        @pl.when((z > 0) & (zz >= z))
        def _():
            to_left(landed, zz, j).wait_send()

        @pl.when((z < ZS - 1) & (zz <= z))
        def _():
            to_right(landed, zz, j).wait_send()

        to_across(landed, zz, j).wait_send()

        @pl.when(zz != z)
        def _():
            to_other(zz, y, j).wait_send()

        to_other(zz, 1 - y, j).wait_send()
        for yy in range(2):
            to_sibling(zz, yy, j).wait_send()
            rest_to_sibling(zz, yy, j).wait_send()
            row = at(zz, yy, 1 - c, j)
            push(landed(row), row, base, GR, ca_s.at[zz, yy, j], ca_r.at[zz, yy, j], sibling).wait_recv()
            push(
                out_ref.at[row, pl.ds(theirs, GX)], row, theirs, GX, cb_s.at[zz, yy, j], cb_r.at[zz, yy, j], sibling
            ).wait_recv()


def gather_units(own):
    slots, rows, width = own.shape
    owners = lax.axis_size("batch")
    line = [pltpu.SemaphoreType.DMA((ZS, slots))] * 6
    plane = [pltpu.SemaphoreType.DMA((ZS, 2, slots))] * 6
    return pl.pallas_call(
        gather_kernel,
        name="gather_units",
        out_shape=jax.ShapeDtypeStruct((owners * slots, rows, width), jnp.bfloat16),
        in_specs=[pl.BlockSpec(memory_space=pltpu.VMEM)],
        out_specs=pl.BlockSpec(memory_space=pl.ANY),
        scratch_shapes=[pltpu.VMEM((slots, rows, width), jnp.bfloat16), pltpu.SemaphoreType.DMA((slots,))] + line + plane,
        compiler_params=pltpu.CompilerParams(collective_id=0, has_side_effects=True, vmem_limit_bytes=VMEM_MOST),
    )(own)


def rank_kernel(scale_ref, cls_ref, lang_row, lang_col, dc_ref, stats_ref, every, weights, z_s, z_r, pair_s, pair_r):
    s, z, y, c = place()
    sents, width = cls_ref.shape
    pairs = lang_row.shape[1]
    greet(s, z, y, c, "line")
    cls = cls_ref[...]
    root = lax.rsqrt(jnp.sum(cls * cls, axis=-1, keepdims=True) + NORM_EPS)
    unit = cls * root
    every[s, z, y, c] = unit.astype(jnp.bfloat16)

    def along(to, frm):
        return pltpu.make_async_remote_copy(
            src_ref=every.at[s, frm, y, c], dst_ref=every.at[s, frm, y, c], send_sem=z_s.at[to], recv_sem=z_r.at[frm],
            device_id=(s, batch_of(to, y, c)), device_id_type=MESH,
        )

    for to in range(ZS):

        @pl.when(z != to)
        def _():
            along(to, z).start()

    for frm in range(ZS):

        @pl.when(z != frm)
        def _():
            along(frm, frm).wait_recv()

    def swap(view, n, target):
        copy = pltpu.make_async_remote_copy(
            src_ref=view, dst_ref=view, send_sem=pair_s.at[n], recv_sem=pair_r.at[n], device_id=target,
            device_id_type=MESH,
        )
        copy.start()
        return copy

    first = swap(every.at[s, :, y, c], 0, (s, batch_of(z, 1 - y, c)))
    first.wait_recv()
    then = swap(every.at[s, :, :, c], 1, (1 - s, batch_of(z, y, c)))
    then.wait_recv()
    last = swap(every.at[:, :, :, c], 2, (s, batch_of(z, y, 1 - c)))
    last.wait_recv()
    scale = scale_ref[0]
    e_zero = every[0].reshape(pairs, width)
    e_one = every[1].reshape(pairs, width)
    cosines = lax.dot_general(e_zero, e_one, (((1,), (1,)), ((), ())), preferred_element_type=jnp.float32)
    own = lax.broadcasted_iota(jnp.int32, (pairs, pairs), 0) == lax.broadcasted_iota(jnp.int32, (pairs, pairs), 1)
    same = lang_col[...] == lang_row[...]
    diagonal = jnp.where(own, 1.0, 0.0)
    shifted = cosines - MARGIN * diagonal
    logits = scale * shifted
    masked = jnp.where(same, logits, -1e30)
    both = -2.0 * diagonal
    total = -2.0 * jnp.sum(logits * diagonal)
    for axis in range(2):
        top = jnp.max(masked, axis=axis, keepdims=True)
        grown = jnp.where(same, jnp.exp(masked - top), 0.0)
        summed = jnp.sum(grown, axis=axis, keepdims=True)
        both += grown / summed
        total += jnp.sum(jnp.log(summed) + top)
    line = lax.broadcasted_iota(jnp.int32, stats_ref.shape, 0)
    stats_ref[...] = jnp.where(line == 0, total, jnp.sum(both * shifted))
    weights[0] = both
    weights[1] = both.T
    rows = weights[s, pl.ds(pl.multiple_of(batch_of(z, y, c) * sents, 16), sents), :]
    partners = every[1 - s].reshape(pairs, width)
    high = rows.astype(jnp.bfloat16)
    rest = (rows - high.astype(jnp.float32)).astype(jnp.bfloat16)
    mix = (((1,), (0,)), ((), ()))
    de = lax.dot_general(high, partners, mix, preferred_element_type=jnp.float32)
    de += lax.dot_general(rest, partners, mix, preferred_element_type=jnp.float32)
    de = scale * de
    dc_ref[...] = (de - unit * jnp.sum(unit * de, axis=-1, keepdims=True)) * root
    for to in range(ZS):

        @pl.when(z != to)
        def _():
            along(to, z).wait_send()

    first.wait_send()
    then.wait_send()
    last.wait_send()


def rank_loss(cls, scale, langs):
    sents, width = cls.shape
    pairs = langs.shape[0]
    dma = pltpu.SemaphoreType.DMA
    vmem = pl.BlockSpec(memory_space=pltpu.VMEM)
    return pl.pallas_call(
        rank_kernel,
        name="rank_loss",
        out_shape=[jax.ShapeDtypeStruct((sents, width), jnp.float32), jax.ShapeDtypeStruct((8, 128), jnp.float32)],
        in_specs=[pl.BlockSpec(memory_space=pltpu.SMEM), vmem, vmem, vmem],
        out_specs=[vmem, vmem],
        scratch_shapes=[
            pltpu.VMEM((2, ZS, 2, 2, sents, width), jnp.bfloat16),
            pltpu.VMEM((2, pairs, pairs), jnp.float32),
            dma((ZS,)), dma((ZS,)), dma((3,)), dma((3,)),
        ],
        compiler_params=pltpu.CompilerParams(collective_id=1, has_side_effects=True, vmem_limit_bytes=24 << 20),
    )(scale, cls, langs.reshape(1, pairs), langs.reshape(pairs, 1))


TILE = 256
GROUP = LEN_ROWS


def dot_nn(a, b):
    return lax.dot_general(a, b, (((1,), (0,)), ((), ())), preferred_element_type=jnp.float32)


def dot_nt(a, b):
    return lax.dot_general(a, b, (((1,), (1,)), ((), ())), preferred_element_type=jnp.float32)


def dot_tn(a, b):
    return lax.dot_general(a, b, (((0,), (0,)), ((), ())), preferred_element_type=jnp.float32)


def gelu_parts(u):
    t = 1.0 / (1.0 + (0.3275911 * 0.7071067811865476) * jnp.abs(u))
    bell = jnp.exp(-0.5 * u * u)
    tail = t * (
        0.127414796 + t * (-0.142248368 + t * (0.7107068705 + t * (-0.7265760135 + t * 0.5307027145)))
    ) * bell
    phi_sum = jnp.where(u >= 0.0, 1.0 - tail, tail)
    return u * phi_sum, phi_sum + u * (0.3989422804014327 * bell)


def norm_parts(resid):
    centre = jnp.mean(resid, axis=-1, keepdims=True)
    centred = resid - centre
    rs = lax.rsqrt(jnp.mean(centred * centred, axis=-1, keepdims=True) + NORM_EPS)
    return centred * rs, rs


def norm_back(dy, unit, rs, gain):
    gd = gain * dy
    return rs * (gd - jnp.mean(gd, axis=-1, keepdims=True) - unit * jnp.mean(gd * unit, axis=-1, keepdims=True))


def lane_halves():
    lane = lax.broadcasted_iota(jnp.int32, (1, 2 * HD), 1)
    first = jnp.where(lane < HD, 1.0, 0.0)
    return first.astype(jnp.bfloat16), (1.0 - first).astype(jnp.bfloat16), lane < HD


def both_heads(rows, first, second):
    return jnp.concatenate([rows * first, rows * second], axis=0)


def fetch_all(pos_ref, units_hbm, held, sems, edges, order):
    for m in order:
        for u in range(edges[m], edges[m + 1]):
            pltpu.make_async_copy(units_hbm.at[pos_ref[u]], held.at[u], sems.at[m]).start()


def fetch_wait(units_hbm, held, sems, edges, m):
    lo, hi = edges[m], edges[m + 1]
    pltpu.make_async_copy(units_hbm.at[pl.ds(0, hi - lo)], held.at[pl.ds(lo, hi - lo)], sems.at[m]).wait()


def matrix_of(held, lo, hi):
    block = held[lo:hi]
    return block.reshape((hi - lo) * block.shape[1], block.shape[2])


def forward_kernel(
    edges, pos_ref, x_ref, small_ref, units_hbm,
    out_ref, q_ref, k_ref, v_ref, probs_ref, ctx_ref, n1_ref, rs1_ref, hb_ref, act_ref, slope_ref, n2_ref, rs2_ref,
    cls_ref, ordered_hbm, held, sems, keep_sem,
):
    first_tile = pl.program_id(0) == 0
    width = x_ref.shape[1]

    def need(m):
        @pl.when(first_tile)
        def _():
            fetch_wait(units_hbm, held, sems, edges, m)

    @pl.when(first_tile)
    def _():
        fetch_all(pos_ref, units_hbm, held, sems, edges, range(6))

    inner_rows = FF // width
    row = lambda r: small_ref[r : r + 1, :]
    x = x_ref[...]
    need(0)
    q = (dot_nn(x, matrix_of(held, edges[0], edges[1])) + row(0)).astype(jnp.bfloat16)
    q_ref[...] = q
    need(1)
    k = dot_nn(x, matrix_of(held, edges[1], edges[2])).astype(jnp.bfloat16)
    k_ref[...] = k
    need(2)
    v = (dot_nn(x, matrix_of(held, edges[2], edges[3])) + row(1)).astype(jnp.bfloat16)
    v_ref[...] = v
    first, second, is_first = lane_halves()
    every_pair = [slice(pair * 2 * HD, (pair + 1) * 2 * HD) for pair in range(H // 2)]
    every_sent = [slice(sent * GROUP, (sent + 1) * GROUP) for sent in range(TILE // GROUP)]
    for sent, rows in enumerate(every_sent):
        scores = jnp.concatenate(
            [dot_nt(k[rows, lanes], both_heads(q[rows, lanes], first, second)) for lanes in every_pair], axis=1
        )
        grown = jnp.exp((scores - jnp.max(scores, axis=0, keepdims=True)) * HD ** (-0.5))
        probs = (grown * (1.0 / jnp.sum(grown, axis=0, keepdims=True))).astype(jnp.bfloat16)
        probs_ref[sent] = probs
        mixed = [dot_tn(probs[:, lanes], v[rows, lanes]) for lanes in every_pair]
        ctx_ref[rows, :] = jnp.concatenate(
            [jnp.where(is_first, m[:GROUP], m[GROUP:]) for m in mixed], axis=1
        ).astype(jnp.bfloat16)
    need(3)
    attended = dot_nn(ctx_ref[...], matrix_of(held, edges[3], edges[4])) + row(2)
    n1, rs1 = norm_parts(x.astype(jnp.float32) + attended)
    n1_ref[...] = n1
    rs1_ref[...] = rs1
    h1 = n1 * row(4 + inner_rows) + row(5 + inner_rows)
    hb = h1.astype(jnp.bfloat16)
    hb_ref[...] = hb
    need(4)
    need(5)
    keep = pltpu.make_async_copy(held, ordered_hbm, keep_sem)

    @pl.when(first_tile)
    def _():
        keep.start()

    per = (edges[5] - edges[4]) // inner_rows
    total = h1 + row(3 + inner_rows)
    for part in range(inner_rows):
        cols = slice(part * width, (part + 1) * width)
        w_in = matrix_of(held, edges[4] + part * per, edges[4] + (part + 1) * per)
        u = dot_nt(hb, w_in) + row(3 + part)
        value, slope = gelu_parts(u)
        act = value.astype(jnp.bfloat16)
        act_ref[:, cols] = act
        slope_ref[:, cols] = slope.astype(jnp.bfloat16)
        total += dot_nn(act, matrix_of(held, edges[5] + part * per, edges[5] + (part + 1) * per))
    n2, rs2 = norm_parts(total)
    n2_ref[...] = n2
    rs2_ref[...] = rs2
    y = n2 * row(6 + inner_rows) + row(7 + inner_rows)
    out_ref[...] = y.astype(jnp.bfloat16)
    for sent in range(TILE // GROUP):
        cls_ref[0, sent : sent + 1, :] = y[sent * GROUP : sent * GROUP + 1, :]

    @pl.when(pl.program_id(0) == pl.num_programs(0) - 1)
    def _():
        keep.wait()


def tiles(shape):
    rest = len(shape) - 1
    return pl.BlockSpec((TILE,) + tuple(shape[1:]), lambda i, *_: (i,) + (0,) * rest)


def whole(shape):
    return pl.BlockSpec(tuple(shape), lambda i, *_: (0,) * len(shape))


def run_forward(x, small, units, positions, edges):
    rows, width = x.shape
    count = rows // TILE
    sents = TILE // GROUP
    bf, f32 = jnp.bfloat16, jnp.float32
    probs_shape = (rows // GROUP, GROUP, width)
    outs = [
        ((rows, width), bf), ((rows, width), bf), ((rows, width), bf), ((rows, width), bf), (probs_shape, bf),
        ((rows, width), bf), ((rows, width), f32), ((rows, 1), f32), ((rows, width), bf), ((rows, FF), bf),
        ((rows, FF), bf), ((rows, width), f32), ((rows, 1), f32), ((count, sents, width), f32),
        ((edges[6],) + units.shape[1:], bf),
    ]
    specs = [tiles(shape) for shape, _ in outs]
    specs[4] = pl.BlockSpec((sents,) + probs_shape[1:], lambda i, *_: (i, 0, 0))
    specs[13] = pl.BlockSpec((1, sents, width), lambda i, *_: (i, 0, 0))
    specs[14] = pl.BlockSpec(memory_space=pl.ANY)
    return pl.pallas_call(
        functools.partial(forward_kernel, edges),
        name="layer_forward",
        grid_spec=pltpu.PrefetchScalarGridSpec(
            num_scalar_prefetch=1,
            grid=(count,),
            in_specs=[tiles(x.shape), whole(small.shape), pl.BlockSpec(memory_space=pl.ANY)],
            out_specs=specs,
            scratch_shapes=[
                pltpu.VMEM((edges[6],) + units.shape[1:], bf), pltpu.SemaphoreType.DMA((6,)), pltpu.SemaphoreType.DMA,
            ],
        ),
        out_shape=[jax.ShapeDtypeStruct(shape, kind) for shape, kind in outs],
        compiler_params=pltpu.CompilerParams(vmem_limit_bytes=VMEM_MOST),
    )(positions, x, small, units)


def backward_kernel(
    edges, pos_ref, og_ref, dc_ref, small_ref, q_ref, k_ref, v_ref, probs_ref, n1_ref, rs1_ref, slope_ref, n2_ref,
    rs2_ref, units_hbm,
    dx_ref, df_ref, du_ref, da_ref, dq_ref, dk_ref, dv_ref, gsmall_ref, dy_ref, dctx_ref, held, sems,
):
    first_tile = pl.program_id(0) == 0
    width = og_ref.shape[1]
    inner_rows = FF // width

    def need(m):
        @pl.when(first_tile)
        def _():
            fetch_wait(units_hbm, held, sems, edges, m)

    @pl.when(first_tile)
    def _():
        fetch_all(pos_ref, units_hbm, held, sems, edges, (5, 4, 3, 0, 1, 2))
        gsmall_ref[...] = jnp.zeros_like(gsmall_ref)

    row = lambda r: small_ref[r : r + 1, :]

    def add_small(r, values):
        gsmall_ref[r : r + 1, :] += jnp.sum(values.astype(jnp.float32), axis=0, keepdims=True)

    dy_ref[...] = og_ref[...].astype(jnp.float32)
    for sent in range(TILE // GROUP):
        dy_ref[sent * GROUP : sent * GROUP + 1, :] += dc_ref[0, sent : sent + 1, :]
    dy = dy_ref[...]
    n2 = n2_ref[...]
    add_small(6 + inner_rows, dy * n2)
    add_small(7 + inner_rows, dy)
    dr2 = norm_back(dy, n2, rs2_ref[...], row(6 + inner_rows))
    df = dr2.astype(jnp.bfloat16)
    df_ref[...] = df
    add_small(3 + inner_rows, df)
    need(5)
    need(4)
    per = (edges[5] - edges[4]) // inner_rows
    dh1 = dr2
    for part in range(inner_rows):
        cols = slice(part * width, (part + 1) * width)
        da = dot_nt(df, matrix_of(held, edges[5] + part * per, edges[5] + (part + 1) * per))
        du = (da * slope_ref[:, cols].astype(jnp.float32)).astype(jnp.bfloat16)
        du_ref[:, cols] = du
        add_small(3 + part, du)
        dh1 += dot_nn(du, matrix_of(held, edges[4] + part * per, edges[4] + (part + 1) * per))
    n1 = n1_ref[...]
    add_small(4 + inner_rows, dh1 * n1)
    add_small(5 + inner_rows, dh1)
    dr1 = norm_back(dh1, n1, rs1_ref[...], row(4 + inner_rows))
    dattn = dr1.astype(jnp.bfloat16)
    da_ref[...] = dattn
    add_small(2, dattn)
    need(3)
    dctx_ref[...] = dot_nt(dattn, matrix_of(held, edges[3], edges[4])).astype(jnp.bfloat16)
    first, second, is_first = lane_halves()
    every_pair = [slice(pair * 2 * HD, (pair + 1) * 2 * HD) for pair in range(H // 2)]
    for sent in range(TILE // GROUP):
        rows = slice(sent * GROUP, (sent + 1) * GROUP)
        dcc = [both_heads(dctx_ref[rows, lanes], first, second) for lanes in every_pair]
        dprobs = jnp.concatenate(
            [dot_nt(v_ref[rows, lanes], wide) for lanes, wide in zip(every_pair, dcc)], axis=1
        )
        low = probs_ref[sent]
        probs = low.astype(jnp.float32)
        dscores = probs * (dprobs - jnp.sum(dprobs * probs, axis=0, keepdims=True))
        dscores = (dscores * HD ** (-0.5)).astype(jnp.bfloat16)
        dv_ref[rows, :] = jnp.concatenate(
            [dot_nn(low[:, lanes], wide) for lanes, wide in zip(every_pair, dcc)], axis=1
        ).astype(jnp.bfloat16)
        qq = [both_heads(q_ref[rows, lanes], first, second) for lanes in every_pair]
        dk_ref[rows, :] = jnp.concatenate(
            [dot_nn(dscores[:, lanes], wide) for lanes, wide in zip(every_pair, qq)], axis=1
        ).astype(jnp.bfloat16)
        mixed = [dot_tn(dscores[:, lanes], k_ref[rows, lanes]) for lanes in every_pair]
        dq_ref[rows, :] = jnp.concatenate(
            [jnp.where(is_first, m[:GROUP], m[GROUP:]) for m in mixed], axis=1
        ).astype(jnp.bfloat16)
    dx = dr1
    for m, (ref, r) in enumerate(((dq_ref, 0), (dk_ref, None), (dv_ref, 1))):
        need(m)
        rows = ref[...]
        if r is not None:
            add_small(r, rows)
        dx += dot_nt(rows, matrix_of(held, edges[m], edges[m + 1]))
    dx_ref[...] = dx.astype(jnp.bfloat16)


def run_backward(og, dc, small, saved, units, positions, edges):
    rows, width = og.shape
    count = rows // TILE
    sents = TILE // GROUP
    bf, f32 = jnp.bfloat16, jnp.float32
    _, q, k, v, probs, _, n1, rs1, _, _, slope, n2, rs2, _ = saved[:14]
    ins = [og, dc, small, q, k, v, probs, n1, rs1, slope, n2, rs2]
    in_specs = [tiles(a.shape) for a in ins]
    in_specs[1] = pl.BlockSpec((1, sents, width), lambda i, *_: (i, 0, 0))
    in_specs[2] = whole(small.shape)
    in_specs[6] = pl.BlockSpec((sents,) + probs.shape[1:], lambda i, *_: (i, 0, 0))
    outs = [((rows, width), bf)] * 2 + [((rows, FF), bf)] + [((rows, width), bf)] * 4 + [(small.shape, f32)]
    specs = [tiles(shape) for shape, _ in outs]
    specs[7] = whole(small.shape)
    return pl.pallas_call(
        functools.partial(backward_kernel, edges),
        name="layer_backward",
        grid_spec=pltpu.PrefetchScalarGridSpec(
            num_scalar_prefetch=1,
            grid=(count,),
            in_specs=in_specs + [pl.BlockSpec(memory_space=pl.ANY)],
            out_specs=specs,
            scratch_shapes=[
                pltpu.VMEM((TILE, width), f32),
                pltpu.VMEM((TILE, width), bf),
                pltpu.VMEM((edges[6],) + units.shape[1:], bf),
                pltpu.SemaphoreType.DMA((6,)),
            ],
        ),
        out_shape=[jax.ShapeDtypeStruct(shape, kind) for shape, kind in outs],
        compiler_params=pltpu.CompilerParams(vmem_limit_bytes=VMEM_MOST),
    )(positions, *ins, units)


def weight_grad_kernel(
    edges, pos_ref, x_hbm, ctx_hbm, du_hbm, act_hbm, dq_hbm, dk_hbm, dv_hbm, da_hbm, hb_hbm, df_hbm, out_hbm,
    x_v, ctx_v, du_v, act_v, right, staged, sems, out_sems,
):
    width = x_v.shape[1]
    unit_rows = out_hbm.shape[1]
    inner_rows = FF // width
    loads = [(act_hbm, act_v), (df_hbm, right.at[5]), (du_hbm, du_v), (hb_hbm, right.at[4]), (ctx_hbm, ctx_v),
             (da_hbm, right.at[3]), (x_hbm, x_v), (dq_hbm, right.at[0]), (dk_hbm, right.at[1]), (dv_hbm, right.at[2])]
    copies = [pltpu.make_async_copy(src, dst, sems.at[i]) for i, (src, dst) in enumerate(loads)]
    for copy in copies:
        copy.start()
    waited = set()
    per = width // unit_rows
    work = []
    for part in range(inner_rows):
        work.append((act_v, part, 5, edges[5] + part * per, (0, 1)))
    for part in range(inner_rows):
        work.append((du_v, part, 4, edges[4] + part * per, (2, 3)))
    work.append((ctx_v, 0, 3, edges[3], (4, 5)))
    work.append((x_v, 0, 0, edges[0], (6, 7)))
    work.append((x_v, 0, 1, edges[1], (6, 8)))
    work.append((x_v, 0, 2, edges[2], (6, 9)))
    for step, (left, part, m, unit, needs) in enumerate(work):
        slot = step % 2
        for n in needs:
            if n not in waited:
                copies[n].wait()
                waited.add(n)
        if step >= 2:
            pltpu.make_async_copy(out_hbm.at[pl.ds(0, per)], staged.at[slot], out_sems.at[slot]).wait()
        half = per // 2
        for piece in range(2):
            cols = slice(part * width + piece * half * unit_rows, part * width + (piece + 1) * half * unit_rows)
            block = dot_tn(left[:, cols], right[m]).astype(jnp.bfloat16)
            staged[slot, piece * half : (piece + 1) * half] = block.reshape(half, unit_rows, width)
        for n in range(per):
            pltpu.make_async_copy(staged.at[slot, n], out_hbm.at[pos_ref[unit + n]], out_sems.at[slot]).start()
    for slot in range(2):
        pltpu.make_async_copy(out_hbm.at[pl.ds(0, per)], staged.at[slot], out_sems.at[slot]).wait()


def run_weight_grads(x, saved, back, positions, edges, places, unit_rows):
    rows, width = x.shape
    bf = jnp.bfloat16
    ctx, hb, act = saved[5], saved[8], saved[9]
    _, df, du, da, dq, dk, dv, _ = back
    per = width // unit_rows
    anyw = pl.BlockSpec(memory_space=pl.ANY)
    return pl.pallas_call(
        functools.partial(weight_grad_kernel, edges),
        name="weight_grads",
        in_specs=[pl.BlockSpec(memory_space=pltpu.SMEM)] + [anyw] * 10,
        out_specs=anyw,
        scratch_shapes=[
            pltpu.VMEM((rows, width), bf), pltpu.VMEM((rows, width), bf), pltpu.VMEM((rows, FF), bf),
            pltpu.VMEM((rows, FF), bf), pltpu.VMEM((6, rows, width), bf),
            pltpu.VMEM((2, per, unit_rows, width), bf),
            pltpu.SemaphoreType.DMA((10,)), pltpu.SemaphoreType.DMA((2,)),
        ],
        out_shape=jax.ShapeDtypeStruct((places, unit_rows, width), bf),
        compiler_params=pltpu.CompilerParams(vmem_limit_bytes=VMEM_MOST),
    )(positions, x, ctx, du, act, dq, dk, dv, da, hb, df)


STEPS = 6
EARLY = 2
BAND = 16
HALF = 384


def step_units(edges):
    per = edges[1] - edges[0]
    firsts = [(edge + per * t, edge + per * (t + 1)) for edge in (edges[5], edges[4]) for t in (0, 2)]
    return firsts + [(edges[3], edges[0]), (edges[1], edges[2])]


def sum_places(edges):
    per = edges[1] - edges[0]
    table = [0] * edges[6]
    for t, firsts in enumerate(step_units(edges)):
        for m, first in enumerate(firsts):
            for k in range(per):
                table[first + k] = (k % 2) * (STEPS * per) + t * per + m * (per // 2) + k // 2
    return table


def backward_reduce_kernel(
    edges, tab_ref, small_ref, dc_ref, rs1_ref, rs2_ref, og_hbm, n2_hbm, slope_hbm, act_hbm, hb_hbm, n1_hbm, ctx_hbm,
    q_hbm, k_hbm, v_hbm, x_hbm, probs_hbm, units_hbm,
    dx_hbm, own_out, small_out,
    dh, nbuf, p0, p1, p2, p3, p4, p5, p6, p7, p8, wbuf, gbuf, c_in, xa, yb, ya, xb, ya_low, xb_low, zg, zd, zab, fbuf, a_out, a_in, x_in,
    gsm, t_acc, t_in,
    l_sem, c_s, c_r, xa_s, xa_r, yb_s, yb_r, ya_s, ya_r, xb_s, xb_r, z_s, z_r, f_s, f_r, a_s, a_r, o_s, o_r,
    t_s, t_r, c_free,
):
    s, z, y, c = place()
    bf, f32 = jnp.bfloat16, jnp.float32
    rows_all, width = dh.shape
    count = rows_all // TILE
    inner_rows = FF // width
    per = edges[1] - edges[0]
    upper = gbuf.shape[5]
    unit_rows = 2 * upper
    slots = own_out.shape[0]
    sibling = (s, batch_of(z, y, 1 - c))
    across = (s, batch_of(z, 1 - y, c))
    other = (1 - s, batch_of(z, y, c))
    round_to = (sibling, across, other, (s, batch_of(z + 1 - 2 * (z % 2), y, c)), (s, batch_of((z + 2) % ZS, y, c)))

    barrier = pltpu.get_barrier_semaphore()

    def hello(target):
        pl.semaphore_signal(barrier, inc=1, device_id=target, device_id_type=MESH)

    hello(sibling)
    hello(other)
    turns = [(dz, dy) for dz in range(ZS) for dy in range(2) if dz or dy]
    for dz, dy in turns:
        hello((s, batch_of((z + dz) % ZS, (y + dy) % 2, c)))
    pl.semaphore_wait(barrier, 2 + len(turns))

    chunk = lambda ref, p: ref.at[:, pl.ds(p * width, width)]
    matrix = lambda first: units_hbm.at[pl.ds(first, per)]
    firsts = step_units(edges)
    acts, slopes = (p3, p5), (p4, p6, p3, p5)
    loads = {"og": (og_hbm, p0), "n2": (n2_hbm, nbuf), "hb": (hb_hbm, p2), "n1": (n1_hbm, nbuf), "probs": (probs_hbm, p0),
             "ctx": (ctx_hbm, p4), "q": (q_hbm, p6), "k": (k_hbm, p7), "v": (v_hbm, p8), "x": (x_hbm, p3)}
    for p in range(inner_rows):
        loads["act%d" % p] = (chunk(act_hbm, p), acts[p % 2])
        loads["slope%d" % p] = (chunk(slope_hbm, p), slopes[p])
        loads["wo%d" % p] = (matrix(edges[5] + p * per), wbuf.at[p % 2, 0])
        loads["wi%d" % p] = (matrix(edges[4] + p * per), wbuf.at[p % 2, 1])
    for t in (4, 5):
        for m in range(2):
            loads["w%d%d" % (t, m)] = (matrix(firsts[t][m]), wbuf.at[t % 2, m])
    copies = {
        name: pltpu.make_async_copy(src, dst, l_sem.at[n]) for n, (name, (src, dst)) in enumerate(loads.items())
    }

    def begin(*names):
        for name in names:
            copies[name].start()

    def ready(*names):
        for name in names:
            copies[name].wait()

    begin("og", "n2", "act0", "act1", "slope0", "wo0", "wi0", "hb", "slope1", "wo1", "wi1", "k", "v")

    row = lambda r: small_ref[r : r + 1, :]
    gsm[...] = jnp.zeros_like(gsm)

    def add_small(r, values):
        gsm[r : r + 1, :] += jnp.sum(values.astype(f32), axis=0, keepdims=True)

    def tile_rows(i):
        return pl.ds(pl.multiple_of(i * TILE, TILE), TILE)

    def weight(slot, m):
        return wbuf[slot, m].reshape(per * unit_rows, width)

    def remote(src, dst, send, recv, target):
        return pltpu.make_async_remote_copy(
            src_ref=src, dst_ref=dst, send_sem=send, recv_sem=recv, device_id=target, device_id_type=MESH
        )

    my_cols = pl.ds(pl.multiple_of(y * HALF, 128), HALF)
    its_cols = pl.ds(pl.multiple_of((1 - y) * HALF, 128), HALF)
    blocks = pl.ds(0, per // 2)
    both = pl.ds(0, 2)
    lines = pl.ds(0, upper)

    def band(zz):
        return pl.ds(pl.multiple_of(zz * BAND, BAND), BAND)

    def c_copy(t):
        return remote(gbuf.at[t, :, 1 - c], c_in.at[t % RING], c_s.at[t], c_r.at[t], sibling)

    def xa_copy(t):
        return remote(gbuf.at[t, 0, c, blocks, 1 - s], xa.at[t], xa_s.at[t], xa_r.at[t], other)

    def yb_copy(t):
        return remote(gbuf.at[t, 1, c, blocks, both, lines, its_cols], yb.at[t], yb_s.at[t], yb_r.at[t], across)

    def ya_view(t, cols):
        return gbuf.at[t, 0, c, blocks, s, band(z) if t < EARLY else lines, cols]

    def xb_view(t, ss):
        return gbuf.at[t, 1, c, blocks, ss, band(z) if t < EARLY else lines, my_cols]

    def ya_land(t):
        return ya_low.at[t] if t < EARLY else ya.at[t - EARLY]

    def xb_land(t):
        return xb_low.at[t] if t < EARLY else xb.at[t - EARLY]

    def ya_copy(t):
        return remote(ya_view(t, its_cols), ya_land(t), ya_s.at[t], ya_r.at[t], across)

    def xb_copy(t):
        return remote(xb_view(t, 1 - s), xb_land(t), xb_s.at[t], xb_r.at[t], other)

    def z_views(t, zz, dz):
        if t < EARLY:
            return [
                (gbuf.at[t, 0, c, blocks, s, band(zz)], zg.at[t, dz - 1]),
                (gbuf.at[t, 1, c, blocks, both, band(zz), my_cols], zd.at[t, dz - 1]),
            ]
        return [
            (gbuf.at[t, m, c, blocks, s, band(zz), my_cols], zab.at[t - EARLY, dz - 1, m]) for m in range(2)
        ]

    def z_copies(t, dz):
        zz = (z + dz) % ZS
        return [
            remote(view, land, z_s.at[n, t, dz - 1], z_r.at[n, t, dz - 1], (s, batch_of(zz, y, c)))
            for n, (view, land) in enumerate(z_views(t, zz, dz))
        ]

    def f_copy(t):
        mine = fbuf.at[pl.ds(c * (STEPS * per) + t * per, per)]
        return remote(mine, mine, f_s.at[t], f_r.at[t], sibling)

    def turn(r):
        return remote(t_acc.at[r], t_in.at[r], t_s.at[r], t_r.at[r], round_to[r])

    def add(view, got):
        @pl.loop(0, per // 2)
        def _(k):
            view.at[k][...] = (view.at[k][...].astype(f32) + got.at[k][...].astype(f32)).astype(bf)

    def ev_c_send(t):
        if t >= RING:
            pl.semaphore_wait(c_free, 1)
        c_copy(t).start()

    def ev_c_wait(t):
        c_copy(t).wait_recv()
        add(gbuf.at[t, 0, c], c_in.at[t % RING, 0])
        xa_copy(t).start()
        add(gbuf.at[t, 1, c], c_in.at[t % RING, 1])
        if t + RING < STEPS:
            pl.semaphore_signal(c_free, inc=1, device_id=sibling, device_id_type=MESH)
        yb_copy(t).start()

    def ev_first(t):
        xa_copy(t).wait_recv()
        add(gbuf.at[t, 0, c, blocks, s], xa.at[t])
        if t >= EARLY:
            ya_copy(t).start()
        yb_copy(t).wait_recv()
        add(gbuf.at[t, 1, c, blocks, both, lines, my_cols], yb.at[t])
        if t >= EARLY:
            xb_copy(t).start()

    def ev_second_start(t):
        ya_copy(t).start()
        xb_copy(t).start()

    def ev_second(t):
        ya_copy(t).wait_recv()
        add(ya_view(t, my_cols), ya_land(t))
        xb_copy(t).wait_recv()
        add(xb_view(t, s), xb_land(t))

    def ev_z_send(t):
        for dz in (2, 1, 3):
            for copy in z_copies(t, dz):
                copy.start()

    def ev_z_take(t):
        for dz in (1, 3, 2):
            for copy, (view, land) in zip(z_copies(t, dz), z_views(t, z, dz)):
                copy.wait_recv()
                add(view, land)

    def ev_fin(t):
        for m in range(2):

            @pl.loop(0, per // 2)
            def _(k):
                at = c * (STEPS * per) + t * per + m * (per // 2) + k
                fbuf[at] = gbuf[t, m, c, k, s, band(z), my_cols]

        f_copy(t).start()

    def ev_turn_start(r):
        if r == 0:
            t_acc[0] = gsm[...]
        turn(r).start()

    def ev_turn_wait(r):
        turn(r).wait()
        t_acc[r + 1] = t_acc[r] + t_in[r]

    def sec_start():
        ready("og", "n2")
        for i in range(count):
            rows = slice(i * TILE, (i + 1) * TILE)
            dh[rows, :] = p0[rows, :].astype(f32)
            for sent in range(TILE // GROUP):
                at = i * TILE + sent * GROUP
                here = i * (TILE // GROUP) + sent
                dh[at : at + 1, :] += dc_ref[here : here + 1, :]
            dy = dh[rows, :]
            n2 = nbuf[rows, :]
            add_small(6 + inner_rows, dy * n2)
            add_small(7 + inner_rows, dy)
            dr2 = norm_back(dy, n2, rs2_ref[rows, :], row(6 + inner_rows))
            dh[rows, :] = dr2
            df = dr2.astype(bf)
            p1[rows, :] = df
            add_small(3 + inner_rows, df)
        begin("n1", "probs")

    def store_grads(t, m, lhs, rhs):
        @pl.loop(0, 2)
        def _(piece):
            half = (per // 2) * unit_rows
            cols = pl.ds(pl.multiple_of(piece * half, 128), half)
            block = dot_tn(lhs[:, cols], rhs[...]).astype(bf)
            for i in range(per // 2):
                part = block[i * unit_rows : (i + 1) * unit_rows].reshape(2, upper, width)

                @pl.when(piece == 0)
                def _():
                    gbuf[t, m, i % 2, i // 2] = part

                @pl.when(piece == 1)
                def _():
                    k = per // 2 + i
                    gbuf[t, m, k % 2, k // 2] = part

    def sec_inner(p):
        def run():
            ready("slope%d" % p, "wo%d" % p, "wi%d" % p)
            slope = slopes[p]

            @pl.loop(0, count)
            def _(i):
                rows = tile_rows(i)
                da = dot_nt(p1[rows, :], weight(p % 2, 0))
                du = (da * slope[rows, :].astype(f32)).astype(bf)
                slope[rows, :] = du
                add_small(3 + p, du)
                dh[rows, :] += dot_nn(du, weight(p % 2, 1))

            if p == 2:
                begin("w40", "w41")
            if p == 3:
                begin("w50", "w51")
            if p + 2 < inner_rows:
                begin("wo%d" % (p + 2), "wi%d" % (p + 2))

        return run

    def sec_outer_grad(p):
        def run():
            ready("act%d" % p)
            store_grads(p // 2, p % 2, acts[p % 2], p1)
            if p + 2 < inner_rows:
                begin("act%d" % (p + 2))
            else:
                begin("slope%d" % p)

        return run

    def sec_inner_grad(p):
        def run():
            if p == 0:
                ready("hb")
            store_grads(2 + p // 2, p % 2, slopes[p], p2)
            if p < 3:
                begin(("ctx", "q", "x")[p])

        return run

    def sec_norm():
        ready("n1", "w40", "w41")

        @pl.loop(0, count)
        def _(i):
            rows = tile_rows(i)
            dh1 = dh[rows, :]
            n1 = nbuf[rows, :]
            add_small(4 + inner_rows, dh1 * n1)
            add_small(5 + inner_rows, dh1)
            dr1 = norm_back(dh1, n1, rs1_ref[rows, :], row(4 + inner_rows))
            dh[rows, :] = dr1
            dattn = dr1.astype(bf)
            p1[rows, :] = dattn
            add_small(2, dattn)
            p5[rows, :] = dot_nt(dattn, weight(0, 0)).astype(bf)

    def sec_out_grad():
        ready("ctx")
        store_grads(4, 0, p4, p1)

    first, second, is_first = lane_halves()
    every_pair = [slice(pair * 2 * HD, (pair + 1) * 2 * HD) for pair in range(H // 2)]

    def sec_heads(part):
        def run():
            if part == 0:
                ready("probs", "q", "k", "v")
            amount = rows_all // GROUP // 2

            @pl.loop(part * amount, (part + 1) * amount)
            def _(sent):
                rows = pl.ds(pl.multiple_of(sent * GROUP, GROUP), GROUP)
                dctx, q, k, v, low = p5[rows, :], p6[rows, :], p7[rows, :], p8[rows, :], p0[rows, :]
                dcc = [both_heads(dctx[:, lanes], first, second) for lanes in every_pair]
                dprobs = jnp.concatenate([dot_nt(v[:, lanes], wide) for lanes, wide in zip(every_pair, dcc)], axis=1)
                probs = low.astype(f32)
                dscores = probs * (dprobs - jnp.sum(dprobs * probs, axis=0, keepdims=True))
                dscores = (dscores * HD ** (-0.5)).astype(bf)
                dv = jnp.concatenate(
                    [dot_nn(low[:, lanes], wide) for lanes, wide in zip(every_pair, dcc)], axis=1
                ).astype(bf)
                p4[rows, :] = dv
                add_small(1, dv)
                qq = [both_heads(q[:, lanes], first, second) for lanes in every_pair]
                p2[rows, :] = jnp.concatenate(
                    [dot_nn(dscores[:, lanes], wide) for lanes, wide in zip(every_pair, qq)], axis=1
                ).astype(bf)
                mixed = [dot_tn(dscores[:, lanes], k[:, lanes]) for lanes in every_pair]
                dq = jnp.concatenate([jnp.where(is_first, m[:GROUP], m[GROUP:]) for m in mixed], axis=1).astype(bf)
                p1[rows, :] = dq
                add_small(0, dq)

        return run

    def sec_query_grad():
        ready("x")
        store_grads(4, 1, p3, p1)

    def sec_key_grad():
        store_grads(5, 0, p3, p2)

    def sec_value_grad():
        store_grads(5, 1, p3, p4)

    def sec_back(part):
        def run():
            if part == 0:
                ready("w50", "w51")

            @pl.loop(part * (count // 2), (part + 1) * (count // 2))
            def _(i):
                rows = tile_rows(i)
                dx = dh[rows, :] + dot_nt(p1[rows, :], weight(0, 1))
                dx += dot_nt(p2[rows, :], weight(1, 0)) + dot_nt(p4[rows, :], weight(1, 1))
                p6[rows, :] = dx.astype(bf)

        return run

    sections = [sec_start] + [sec_outer_grad(p) for p in range(inner_rows)]
    for p in range(inner_rows):
        sections += [sec_inner(p), sec_inner_grad(p)]
    sections += [sec_norm, sec_out_grad, sec_heads(0), sec_heads(1), sec_query_grad, sec_key_grad, sec_value_grad]
    sections += [sec_back(0), sec_back(1)]
    done = [2, 4, 8, 12, 17, 19]
    events = {}

    def at_tick(tick, order, action):
        events.setdefault(tick, []).append((order, action))

    for t in range(STEPS):
        at_tick(done[t], 0, functools.partial(ev_c_send, t))
        at_tick(PLACES[t][0], 1, functools.partial(ev_c_wait, t))
        at_tick(PLACES[t][1], 2, functools.partial(ev_first, t))
        if t < EARLY:
            at_tick(PLACES[t][1], 2.5, functools.partial(ev_z_send, t))
            at_tick(PLACES[t][2], 3, functools.partial(ev_z_take, t))
            at_tick(PLACES[t][2], 3.5, functools.partial(ev_second_start, t))
            at_tick(PLACES[t][3], 4, functools.partial(ev_second, t))
        else:
            at_tick(PLACES[t][2], 3, functools.partial(ev_second, t))
            at_tick(PLACES[t][2], 3.5, functools.partial(ev_z_send, t))
            at_tick(PLACES[t][3], 4, functools.partial(ev_z_take, t))
        at_tick(PLACES[t][3], 5, functools.partial(ev_fin, t))
    for r in range(5):
        at_tick(16 + r, 10, functools.partial(ev_turn_start, r))
        at_tick(17 + r, -1, functools.partial(ev_turn_wait, r))
    for tick in range(max(max(events) + 1, len(sections))):
        if tick < len(sections):
            sections[tick]()
        if tick == len(sections) - 1:
            dx_copy = pltpu.make_async_copy(p6, dx_hbm, l_sem.at[len(loads)])
            dx_copy.start()
        for _, action in sorted(events.get(tick, []), key=lambda item: item[0]):
            action()
    small_out[...] = t_acc[5]
    for t in range(STEPS):
        its = fbuf.at[pl.ds((1 - c) * (STEPS * per) + t * per, per)]
        remote(its, its, f_s.at[t], f_r.at[t], sibling).wait_recv()

    def a_copy(zz, yy):
        return remote(a_out.at[zz, yy], a_in.at[z, y], a_s.at[zz, yy], a_r.at[z, y], (s, batch_of(zz, yy, c)))

    def o_copy(zz, yy):
        return remote(a_in.at[zz, yy], x_in.at[zz, yy], o_s.at[zz, yy], o_r.at[zz, yy], other)

    for dz, dy in turns:
        zz, yy = (z + dz) % ZS, (y + dy) % 2
        for j in range(slots):
            a_out[zz, yy, j] = fbuf[tab_ref[batch_of(zz, yy, c) * slots + j]]
        a_copy(zz, yy).start()
    for j in range(slots):
        a_in[z, y, j] = fbuf[tab_ref[batch_of(z, y, c) * slots + j]]
    o_copy(z, y).start()

    def put(zz, yy, ss, got):
        rows = pl.ds(pl.multiple_of(ss * upper + zz * BAND, BAND), BAND)
        cols = pl.ds(pl.multiple_of(yy * HALF, 128), HALF)
        for j in range(slots):
            own_out[j, rows, cols] = got[zz, yy, j]

    put(z, y, s, a_in)
    for dz, dy in turns:
        zz, yy = (z + dz) % ZS, (y + dy) % 2
        remote(a_in.at[zz, yy], a_in.at[zz, yy], a_s.at[zz, yy], a_r.at[zz, yy], other).wait_recv()
        o_copy(zz, yy).start()
        put(zz, yy, s, a_in)
    for dz, dy in [(0, 0)] + turns:
        zz, yy = (z + dz) % ZS, (y + dy) % 2
        o_copy(zz, yy).wait_recv()
        put(zz, yy, 1 - s, x_in)
    for t in range(STEPS):
        for copy in (c_copy, xa_copy, yb_copy, ya_copy, xb_copy, f_copy):
            copy(t).wait_send()

        for dz in range(1, ZS):
            for copy in z_copies(t, dz):
                copy.wait_send()

    for dz, dy in turns:
        a_copy((z + dz) % ZS, (y + dy) % 2).wait_send()
    for dz, dy in [(0, 0)] + turns:
        o_copy((z + dz) % ZS, (y + dy) % 2).wait_send()
    dx_copy.wait()


RING = 3
PLACES = ((5, 9, 36, 43), (8, 12, 22, 78), (10, 15, 19, 41), (13, 17, 21, 27), (18, 21, 35, 43), (20, 24, 41, 47))


def run_backward_reduce(og, dc, small, saved, x, units, table, edges, slots):
    rows, width = og.shape
    bf, f32 = jnp.bfloat16, jnp.float32
    _, q, k, v, probs, ctx, n1, rs1, hb, act, slope, n2, rs2, _ = saved[:14]
    unit_rows = units.shape[1]
    per = edges[1] - edges[0]
    half = per // 2
    dma = pltpu.SemaphoreType.DMA
    vm = pltpu.VMEM
    vmem = pl.BlockSpec(memory_space=pltpu.VMEM)
    anyw = pl.BlockSpec(memory_space=pl.ANY)
    upper = unit_rows // 2
    return pl.pallas_call(
        functools.partial(backward_reduce_kernel, edges),
        name="backward_reduce",
        out_shape=[
            jax.ShapeDtypeStruct((rows, width), bf),
            jax.ShapeDtypeStruct((slots, unit_rows, width), bf),
            jax.ShapeDtypeStruct(small.shape, f32),
        ],
        in_specs=[pl.BlockSpec(memory_space=pltpu.SMEM)] + [vmem] * 4 + [anyw] * 13,
        out_specs=[anyw, vmem, vmem],
        scratch_shapes=[vm((rows, width), f32)] * 2
        + [vm((rows, width), bf)] * 9
        + [
            vm((2, 2, per, unit_rows, width), bf),
            vm((STEPS, 2, 2, half, 2, upper, width), bf),
            vm((RING, 2, half, 2, upper, width), bf),
            vm((STEPS, half, upper, width), bf),
            vm((STEPS, half, 2, upper, HALF), bf),
            vm((STEPS - EARLY, half, upper, HALF), bf),
            vm((STEPS - EARLY, half, upper, HALF), bf),
            vm((EARLY, half, BAND, HALF), bf),
            vm((EARLY, half, BAND, HALF), bf),
            vm((EARLY, ZS - 1, half, BAND, width), bf),
            vm((EARLY, ZS - 1, half, 2, BAND, HALF), bf),
            vm((STEPS - EARLY, ZS - 1, 2, half, BAND, HALF), bf),
            vm((2 * STEPS * per, BAND, HALF), bf),
            vm((ZS, 2, slots, BAND, HALF), bf),
            vm((ZS, 2, slots, BAND, HALF), bf),
            vm((ZS, 2, slots, BAND, HALF), bf),
            vm(small.shape, f32),
            vm((6,) + small.shape, f32),
            vm((5,) + small.shape, f32),
        ]
        + [dma((32,))]
        + [dma((STEPS,))] * 10
        + [dma((2, STEPS, ZS - 1))] * 2
        + [dma((STEPS,))] * 2
        + [dma((ZS, 2))] * 4
        + [dma((5,))] * 2
        + [pltpu.SemaphoreType.REGULAR],
        compiler_params=pltpu.CompilerParams(collective_id=3, has_side_effects=True, vmem_limit_bytes=63 << 20),
    )(table, small, dc, rs1, rs2, og, n2, slope, act, hb, n1, ctx, q, k, v, x, probs.reshape(rows, width), units)


def unit_positions(owner_list, slot_count):
    unit_total = owner_list.shape[0]
    same_owner = owner_list[:, None] == owner_list[None, :]
    ordinal = jnp.arange(unit_total, dtype=jnp.int32)
    earlier = ordinal[None, :] < ordinal[:, None]
    slot_number = jnp.sum(jnp.where(same_owner & earlier, 1, 0), axis=1).astype(jnp.int32)
    return owner_list * slot_count + slot_number


def adamw(weight_in, gradient, moment_one, moment_two, rate_value, decay_value, fix_one, fix_two):
    new_one = BETA_ONE * moment_one + (1.0 - BETA_ONE) * gradient
    new_two = BETA_TWO * moment_two + (1.0 - BETA_TWO) * gradient * gradient
    stepped = new_one / fix_one / (jnp.sqrt(new_two / fix_two) + ADAM_EPS)
    return (weight_in - rate_value * (stepped + decay_value * weight_in), new_one, new_two)


def any_size_units(own, positions, owners):
    slots, rows, width = own.shape
    table = jnp.arange(owners * slots, dtype=jnp.int32)[:, None] == positions[None, :]
    bands = lax.all_to_all(
        own.transpose(1, 0, 2).astype(jnp.bfloat16), "batch", split_axis=0, concat_axis=1, tiled=True
    )
    ordered = jnp.einsum(
        "rpd,pu->rud", bands, table.astype(jnp.bfloat16), preferred_element_type=jnp.float32
    ).astype(jnp.bfloat16)
    return lax.all_gather(ordered, "batch", axis=0, tiled=True).transpose(1, 0, 2)


def any_size_sums(grads, positions, owners, slots):
    table = jnp.arange(owners * slots, dtype=jnp.int32)[:, None] == positions[None, :]
    pieces = lax.psum_scatter(grads.transpose(1, 0, 2).astype(jnp.float32), "batch", scatter_dimension=0, tiled=True)
    summed = lax.psum(pieces.astype(jnp.bfloat16), "stream").astype(jnp.float32)
    send_rows = jnp.einsum("rud,pu->rpd", summed, table.astype(jnp.float32), precision=HIGHEST)
    owned = lax.all_to_all(send_rows.astype(jnp.bfloat16), "batch", split_axis=1, concat_axis=0, tiled=True)
    return owned.astype(jnp.float32).transpose(1, 0, 2)


def any_size_rank(cls, scale, langs, owners):
    sents, width = cls.shape
    root = lax.rsqrt(jnp.sum(cls * cls, axis=-1, keepdims=True) + NORM_EPS)
    unit = cls * root
    every = lax.all_gather(unit.astype(jnp.bfloat16), "batch", axis=0, tiled=True)
    every = lax.all_gather(every, "stream", axis=0)
    cosines = jnp.dot(every[0], every[1].T, preferred_element_type=jnp.float32)
    diagonal = jnp.eye(cosines.shape[0], dtype=jnp.float32)
    same = langs[:, None] == langs[None, :]
    shifted = cosines - MARGIN * diagonal
    logits = scale[0] * shifted
    masked = jnp.where(same, logits, -1e30)
    both = -2.0 * diagonal
    total = -2.0 * jnp.sum(logits * diagonal)
    for axis in range(2):
        top = jnp.max(masked, axis=axis, keepdims=True)
        grown = jnp.where(same, jnp.exp(masked - top), 0.0)
        summed = jnp.sum(grown, axis=axis, keepdims=True)
        both += grown / summed
        total += jnp.sum(jnp.log(summed) + top)
    s = lax.axis_index("stream")
    turned = jnp.where(s == 0, both, both.T)
    rows = lax.dynamic_slice_in_dim(turned, lax.axis_index("batch") * sents, sents)
    partners = lax.dynamic_index_in_dim(every, 1 - s, keepdims=False).astype(jnp.float32)
    de = scale[0] * jnp.dot(rows, partners, precision=HIGHEST)
    dc = (de - unit * jnp.sum(unit * de, axis=-1, keepdims=True)) * root
    return dc, total, jnp.sum(both * shifted)


def per_device(
    tokens, out_grad, master, first_moment, second_moment, small_params, small_first, small_second, logit_scale,
    scale_first, scale_second, pair_lang, unit_owner,
):
    owners = lax.axis_size("batch")
    here_batch = lax.axis_index("batch")
    unit_rows, slot_count, width = master.shape
    query_blocks = width // unit_rows
    inner_blocks = FF // unit_rows
    edges = [query_blocks * n for n in range(5)]
    edges += [edges[4] + inner_blocks, edges[4] + 2 * inner_blocks]
    units_total = unit_owner.shape[0]
    positions = unit_positions(unit_owner, slot_count)
    on_block = owners == 4 * ZS
    own = master.transpose(1, 0, 2)
    if on_block:
        units, where, places = gather_units(own), positions, owners * slot_count
    else:
        units = any_size_units(own, positions, owners)
        where, places = jnp.arange(units_total, dtype=jnp.int32), units_total
    sentences, length = tokens.shape[1], tokens.shape[2]
    flat = tokens.reshape(sentences * length, width)
    saved = run_forward(flat, small_params, units, where, edges)
    cls = saved[13]
    if on_block:
        dc, stats = rank_loss(cls.reshape(sentences, width), logit_scale, pair_lang)
        loss_total, grad_scale = stats[0, :1], stats[1, :1]
    else:
        dc, loss_total, grad_scale = any_size_rank(cls.reshape(sentences, width), logit_scale, pair_lang, owners)
        loss_total, grad_scale = loss_total.reshape(1), grad_scale.reshape(1)
    grad_rows = out_grad.reshape(sentences * length, width)
    if on_block:
        slot_units = jnp.arange(places, dtype=jnp.int32)[:, None] == positions[None, :]
        sum_table = jnp.asarray(sum_places(edges), dtype=jnp.int32)
        table = jnp.sum(jnp.where(slot_units, sum_table[None, :], 0), axis=1, dtype=jnp.int32)
        d_tokens, owned_grad, small_total = run_backward_reduce(
            grad_rows, dc, small_params, saved, flat, saved[14], table, edges, slot_count
        )
        owned_grad = owned_grad.astype(jnp.float32)
    else:
        back = run_backward(grad_rows, dc.reshape(cls.shape), small_params, saved, units, where, edges)
        grads = run_weight_grads(flat, saved, back, where, edges, places, unit_rows)
        d_tokens = back[0]
        owned_grad = any_size_sums(grads, positions, owners, slot_count)
        small_total = lax.psum(back[7], ("stream", "batch"))
    step_value = float(STEP)
    fix_one = 1.0 - BETA_ONE**step_value
    fix_two = 1.0 - BETA_TWO**step_value
    my_places = here_batch * slot_count + jnp.arange(slot_count, dtype=jnp.int32)
    filled = jnp.any(my_places[:, None] == positions[None, :], axis=1)[:, None, None]
    first_in, second_in = first_moment.transpose(1, 0, 2), second_moment.transpose(1, 0, 2)
    moved = adamw(own, owned_grad, first_in, second_in, RATE_UNITS, DECAY, fix_one, fix_two)
    new_master, new_first, new_second = (
        jnp.where(filled, new, old) for new, old in zip(moved, (own, first_in, second_in))
    )
    new_copy = new_master.astype(jnp.bfloat16)
    new_small, new_small_first, new_small_second = adamw(
        small_params, small_total, small_first, small_second, RATE_SMALL, 0.0, fix_one, fix_two
    )
    scale_new, scale_one, scale_two = adamw(
        logit_scale, grad_scale, scale_first, scale_second, RATE_SCALE, 0.0, fix_one, fix_two
    )
    loss_out = loss_total / (2 * owners * sentences)
    back_order = lambda a: a.transpose(1, 0, 2)
    return (
        saved[0].reshape(tokens.shape),
        d_tokens.reshape(tokens.shape),
        back_order(new_master),
        back_order(new_first),
        back_order(new_second),
        back_order(new_copy),
        new_small,
        new_small_first,
        new_small_second,
        scale_new,
        scale_one,
        scale_two,
        loss_out,
    )


def solution(mesh):
    rows = P("stream", "batch", None, None)
    blocks = P(None, "batch", None)
    return jax.shard_map(
        per_device,
        mesh=mesh,
        in_specs=(rows, rows, blocks, blocks, blocks) + (P(),) * 8,
        out_specs=(rows, rows, blocks, blocks, blocks, blocks) + (P(),) * 7,
        check_vma=False,
    )
```

```python
import functools

import jax
import jax.numpy as jnp
from jax import lax
from jax.experimental import pallas as pl
from jax.experimental.pallas import tpu as pltpu
from jax.sharding import PartitionSpec as P

H = 12
HD = 64
FF = 3072
STEP = 10
ZS = 4
UR_ROWS = 128
LEN_ROWS = 64
VMEM_MOST = 60 << 20
MESH = pl.DeviceIdType.MESH

HIGHEST = lax.Precision.HIGHEST
BETA_ONE = 0.9
BETA_TWO = 0.999
ADAM_EPS = 1e-06
RATE_UNITS = 0.02
RATE_SMALL = 0.1
RATE_SCALE = 2.0
DECAY = 0.01
MARGIN = 0.3
NORM_EPS = 1e-06


def place():
    s = lax.axis_index("stream")
    b = lax.axis_index("batch")
    return s, b // 4, (b // 2) % 2, b % 2


def batch_of(z, y, c):
    return (z * 2 + y) * 2 + c


def greet(s, z, y, c, others):
    barrier = pltpu.get_barrier_semaphore()

    def hello(target):
        pl.semaphore_signal(barrier, inc=1, device_id=target, device_id_type=MESH)

    hello((s, batch_of(z, y, 1 - c)))
    hello((s, batch_of(z, 1 - y, c)))
    hello((1 - s, batch_of(z, y, c)))
    if others == "line":
        for far in range(1, ZS):

            @pl.when(z >= far)
            def _():
                hello((s, batch_of(z - far, y, c)))

            @pl.when(z + far < ZS)
            def _():
                hello((s, batch_of(z + far, y, c)))

        pl.semaphore_wait(barrier, 3 + ZS - 1)
    else:

        @pl.when(z >= 1)
        def _():
            hello((s, batch_of(z - 1, y, c)))

        @pl.when(z + 1 < ZS)
        def _():
            hello((s, batch_of(z + 1, y, c)))

        pl.semaphore_wait(barrier, 3 + (z + 2) // 3 + (5 - z) // 3)


GR = 80
GX = UR_ROWS - GR


def gather_kernel(own_ref, out_ref, low, stage_sem, zl_s, zl_r, zr_s, zr_r, y_s, y_r, x_s, x_r, ca_s, ca_r, cb_s, cb_r):
    s, z, y, c = place()
    slots = own_ref.shape[0]
    steps = ZS * slots
    base = pl.multiple_of(s * GX, 16)
    only = pl.multiple_of(s * GR, 16)
    theirs = pl.multiple_of((1 - s) * GR, 16)

    def at(zz, yy, cc, j):
        return batch_of(zz, yy, cc) * slots + j

    greet(s, z, y, c, "next")

    def push(src, row, start, size, send, recv, target):
        return pltpu.make_async_remote_copy(
            src_ref=src,
            dst_ref=out_ref.at[row, pl.ds(start, size)],
            send_sem=send,
            recv_sem=recv,
            device_id=target,
            device_id_type=MESH,
        )

    left = (s, batch_of(z - 1, y, c))
    right = (s, batch_of(z + 1, y, c))
    across = (s, batch_of(z, 1 - y, c))
    other = (1 - s, batch_of(z, y, c))
    sibling = (s, batch_of(z, y, 1 - c))

    def to_left(src, zz, j):
        row = at(zz, y, c, j)
        return push(src(row), row, base, GR, zl_s.at[zz, j], zl_r.at[zz, j], left)

    def to_right(src, zz, j):
        row = at(zz, y, c, j)
        return push(src(row), row, base, GR, zr_s.at[zz, j], zr_r.at[zz, j], right)

    def to_across(src, zz, j):
        row = at(zz, y, c, j)
        return push(src(row), row, base, GR, y_s.at[zz, j], y_r.at[zz, j], across)

    def to_other(zz, yy, j):
        row = at(zz, yy, c, j)
        return push(out_ref.at[row, pl.ds(only, GX)], row, only, GX, x_s.at[zz, yy, j], x_r.at[zz, yy, j], other)

    def to_sibling(zz, yy, j):
        row = at(zz, yy, c, j)
        return push(out_ref.at[row, pl.ds(base, GR)], row, base, GR, ca_s.at[zz, yy, j], ca_r.at[zz, yy, j], sibling)

    def rest_to_sibling(zz, yy, j):
        row = at(zz, yy, c, j)
        return push(out_ref.at[row, pl.ds(theirs, GX)], row, theirs, GX, cb_s.at[zz, yy, j], cb_r.at[zz, yy, j], sibling)

    def landed(row):
        return out_ref.at[row, pl.ds(base, GR)]

    def from_left(zz, j):
        row = at(zz, y, c, j)
        return push(landed(row), row, base, GR, zr_s.at[zz, j], zr_r.at[zz, j], right)

    def arrived_line(zz, j, onward):
        onward.start()
        to_across(landed, zz, j).start()
        to_other(zz, y, j).start()
        to_sibling(zz, y, j).start()

    def stage(j):
        return pltpu.make_async_copy(low.at[j], out_ref.at[at(z, y, c, j)], stage_sem.at[j])

    for j in range(slots):
        low[j] = own_ref[j].astype(jnp.bfloat16)
        mine = lambda row: low.at[j, pl.ds(base, GR)]

        @pl.when(z > 0)
        def _():
            to_left(mine, z, j).start()

        @pl.when(z < ZS - 1)
        def _():
            to_right(mine, z, j).start()

        to_across(mine, z, j).start()
        row = at(z, y, c, j)
        push(low.at[j, pl.ds(base, GR)], row, base, GR, ca_s.at[z, y, j], ca_r.at[z, y, j], sibling).start()
        push(low.at[j, pl.ds(theirs, GX)], row, theirs, GX, cb_s.at[z, y, j], cb_r.at[z, y, j], sibling).start()
        stage(j).start()

    def line_step(t):
        d = t // slots
        j = t % slots

        @pl.when((d >= 1) & (z - d >= 0))
        def _():
            zz = z - d
            to_right(landed, zz, j).wait_recv()

            @pl.when(z < ZS - 1)
            def _():
                to_right(landed, zz, j).start()

            to_across(landed, zz, j).start()
            to_other(zz, y, j).start()
            to_sibling(zz, y, j).start()

        @pl.when((d >= 1) & (z + d < ZS))
        def _():
            zz = z + d
            to_left(landed, zz, j).wait_recv()

            @pl.when(z > 0)
            def _():
                to_left(landed, zz, j).start()

            to_across(landed, zz, j).start()
            to_other(zz, y, j).start()
            to_sibling(zz, y, j).start()

    def across_one(zz, j):
        row = at(zz, 1 - y, c, j)
        push(landed(row), row, base, GR, y_s.at[zz, j], y_r.at[zz, j], across).wait_recv()
        to_other(zz, 1 - y, j).start()
        to_sibling(zz, 1 - y, j).start()

    def across_step(t):
        d = t // slots
        j = t % slots

        @pl.when(z - d >= 0)
        def _():
            across_one(z - d, j)

        @pl.when((d >= 1) & (z + d < ZS))
        def _():
            across_one(z + d, j)

    def other_one(zz, yy, j):
        row = at(zz, yy, c, j)
        push(
            out_ref.at[row, pl.ds(theirs, GX)], row, theirs, GX, x_s.at[zz, yy, j], x_r.at[zz, yy, j], other
        ).wait_recv()
        rest_to_sibling(zz, yy, j).start()

    def other_step(t, yy, first):
        d = t // slots
        j = t % slots

        @pl.when((d >= first) & (z - d >= 0))
        def _():
            other_one(z - d, yy, j)

        @pl.when((d >= 1) & (z + d < ZS))
        def _():
            other_one(z + d, yy, j)

    @pl.loop(0, steps + 3)
    def _(t):
        @pl.when(t < steps)
        def _():
            line_step(t)

        @pl.when((t >= 1) & (t < steps + 1))
        def _():
            across_step(t - 1)

        @pl.when((t >= 2) & (t < steps + 2))
        def _():
            other_step(t - 2, y, 1)

        @pl.when(t >= 3)
        def _():
            other_step(t - 3, 1 - y, 0)

    for j in range(slots):
        stage(j).wait()

    @pl.loop(0, steps)
    def _(t):
        zz = t // slots
        j = t % slots

        @pl.when((z > 0) & (zz >= z))
        def _():
            to_left(landed, zz, j).wait_send()

        @pl.when((z < ZS - 1) & (zz <= z))
        def _():
            to_right(landed, zz, j).wait_send()

        to_across(landed, zz, j).wait_send()

        @pl.when(zz != z)
        def _():
            to_other(zz, y, j).wait_send()

        to_other(zz, 1 - y, j).wait_send()
        for yy in range(2):
            to_sibling(zz, yy, j).wait_send()
            rest_to_sibling(zz, yy, j).wait_send()
            row = at(zz, yy, 1 - c, j)
            push(landed(row), row, base, GR, ca_s.at[zz, yy, j], ca_r.at[zz, yy, j], sibling).wait_recv()
            push(
                out_ref.at[row, pl.ds(theirs, GX)], row, theirs, GX, cb_s.at[zz, yy, j], cb_r.at[zz, yy, j], sibling
            ).wait_recv()


def gather_units(own):
    slots, rows, width = own.shape
    owners = lax.axis_size("batch")
    line = [pltpu.SemaphoreType.DMA((ZS, slots))] * 6
    plane = [pltpu.SemaphoreType.DMA((ZS, 2, slots))] * 6
    return pl.pallas_call(
        gather_kernel,
        name="gather_units",
        out_shape=jax.ShapeDtypeStruct((owners * slots, rows, width), jnp.bfloat16),
        in_specs=[pl.BlockSpec(memory_space=pltpu.VMEM)],
        out_specs=pl.BlockSpec(memory_space=pl.ANY),
        scratch_shapes=[pltpu.VMEM((slots, rows, width), jnp.bfloat16), pltpu.SemaphoreType.DMA((slots,))] + line + plane,
        compiler_params=pltpu.CompilerParams(collective_id=0, has_side_effects=True, vmem_limit_bytes=VMEM_MOST),
    )(own)


TILE = 256
GROUP = LEN_ROWS


def dot_nn(a, b):
    return lax.dot_general(a, b, (((1,), (0,)), ((), ())), preferred_element_type=jnp.float32)


def dot_nt(a, b):
    return lax.dot_general(a, b, (((1,), (1,)), ((), ())), preferred_element_type=jnp.float32)


def dot_tn(a, b):
    return lax.dot_general(a, b, (((0,), (0,)), ((), ())), preferred_element_type=jnp.float32)


def gelu_parts(u):
    t = 1.0 / (1.0 + (0.3275911 * 0.7071067811865476) * jnp.abs(u))
    bell = jnp.exp(-0.5 * u * u)
    tail = t * (
        0.127414796 + t * (-0.142248368 + t * (0.7107068705 + t * (-0.7265760135 + t * 0.5307027145)))
    ) * bell
    phi_sum = jnp.where(u >= 0.0, 1.0 - tail, tail)
    return u * phi_sum, phi_sum + u * (0.3989422804014327 * bell)


def norm_parts(resid):
    centre = jnp.mean(resid, axis=-1, keepdims=True)
    centred = resid - centre
    rs = lax.rsqrt(jnp.mean(centred * centred, axis=-1, keepdims=True) + NORM_EPS)
    return centred * rs, rs


def norm_back(dy, unit, rs, gain):
    gd = gain * dy
    return rs * (gd - jnp.mean(gd, axis=-1, keepdims=True) - unit * jnp.mean(gd * unit, axis=-1, keepdims=True))


def lane_halves():
    lane = lax.broadcasted_iota(jnp.int32, (1, 2 * HD), 1)
    first = jnp.where(lane < HD, 1.0, 0.0)
    return first.astype(jnp.bfloat16), (1.0 - first).astype(jnp.bfloat16), lane < HD


def both_heads(rows, first, second):
    return jnp.concatenate([rows * first, rows * second], axis=0)


def fetch_all(pos_ref, units_hbm, held, sems, edges, order):
    for m in order:
        for u in range(edges[m], edges[m + 1]):
            pltpu.make_async_copy(units_hbm.at[pos_ref[u]], held.at[u], sems.at[m]).start()


def fetch_wait(units_hbm, held, sems, edges, m):
    lo, hi = edges[m], edges[m + 1]
    pltpu.make_async_copy(units_hbm.at[pl.ds(0, hi - lo)], held.at[pl.ds(lo, hi - lo)], sems.at[m]).wait()


def matrix_of(held, lo, hi):
    block = held[lo:hi]
    return block.reshape((hi - lo) * block.shape[1], block.shape[2])


def forward_kernel(
    edges, pos_ref, x_ref, small_ref, units_hbm,
    out_ref, q_ref, k_ref, v_ref, probs_ref, ctx_ref, n1_ref, rs1_ref, hb_ref, act_ref, slope_ref, n2_ref, rs2_ref,
    cls_ref, ordered_hbm, held, sems, keep_sem,
):
    first_tile = pl.program_id(0) == 0
    width = x_ref.shape[1]

    def need(m):
        @pl.when(first_tile)
        def _():
            fetch_wait(units_hbm, held, sems, edges, m)

    @pl.when(first_tile)
    def _():
        fetch_all(pos_ref, units_hbm, held, sems, edges, range(6))

    inner_rows = FF // width
    row = lambda r: small_ref[r : r + 1, :]
    x = x_ref[...]
    need(0)
    q = (dot_nn(x, matrix_of(held, edges[0], edges[1])) + row(0)).astype(jnp.bfloat16)
    q_ref[...] = q
    need(1)
    k = dot_nn(x, matrix_of(held, edges[1], edges[2])).astype(jnp.bfloat16)
    k_ref[...] = k
    need(2)
    v = (dot_nn(x, matrix_of(held, edges[2], edges[3])) + row(1)).astype(jnp.bfloat16)
    v_ref[...] = v
    first, second, is_first = lane_halves()
    every_pair = [slice(pair * 2 * HD, (pair + 1) * 2 * HD) for pair in range(H // 2)]
    every_sent = [slice(sent * GROUP, (sent + 1) * GROUP) for sent in range(TILE // GROUP)]
    for sent, rows in enumerate(every_sent):
        scores = jnp.concatenate(
            [dot_nt(k[rows, lanes], both_heads(q[rows, lanes], first, second)) for lanes in every_pair], axis=1
        )
        grown = jnp.exp((scores - jnp.max(scores, axis=0, keepdims=True)) * HD ** (-0.5))
        probs = (grown * (1.0 / jnp.sum(grown, axis=0, keepdims=True))).astype(jnp.bfloat16)
        probs_ref[sent] = probs
        mixed = [dot_tn(probs[:, lanes], v[rows, lanes]) for lanes in every_pair]
        ctx_ref[rows, :] = jnp.concatenate(
            [jnp.where(is_first, m[:GROUP], m[GROUP:]) for m in mixed], axis=1
        ).astype(jnp.bfloat16)
    need(3)
    attended = dot_nn(ctx_ref[...], matrix_of(held, edges[3], edges[4])) + row(2)
    n1, rs1 = norm_parts(x.astype(jnp.float32) + attended)
    n1_ref[...] = n1
    rs1_ref[...] = rs1
    h1 = n1 * row(4 + inner_rows) + row(5 + inner_rows)
    hb = h1.astype(jnp.bfloat16)
    hb_ref[...] = hb
    need(4)
    need(5)
    keep = pltpu.make_async_copy(held, ordered_hbm, keep_sem)

    @pl.when(first_tile)
    def _():
        keep.start()

    per = (edges[5] - edges[4]) // inner_rows
    total = h1 + row(3 + inner_rows)
    for part in range(inner_rows):
        cols = slice(part * width, (part + 1) * width)
        w_in = matrix_of(held, edges[4] + part * per, edges[4] + (part + 1) * per)
        u = dot_nt(hb, w_in) + row(3 + part)
        value, slope = gelu_parts(u)
        act = value.astype(jnp.bfloat16)
        act_ref[:, cols] = act
        slope_ref[:, cols] = slope.astype(jnp.bfloat16)
        total += dot_nn(act, matrix_of(held, edges[5] + part * per, edges[5] + (part + 1) * per))
    n2, rs2 = norm_parts(total)
    n2_ref[...] = n2
    rs2_ref[...] = rs2
    y = n2 * row(6 + inner_rows) + row(7 + inner_rows)
    out_ref[...] = y.astype(jnp.bfloat16)
    for sent in range(TILE // GROUP):
        cls_ref[0, sent : sent + 1, :] = y[sent * GROUP : sent * GROUP + 1, :]

    @pl.when(pl.program_id(0) == pl.num_programs(0) - 1)
    def _():
        keep.wait()


def tiles(shape):
    rest = len(shape) - 1
    return pl.BlockSpec((TILE,) + tuple(shape[1:]), lambda i, *_: (i,) + (0,) * rest)


def whole(shape):
    return pl.BlockSpec(tuple(shape), lambda i, *_: (0,) * len(shape))


def run_forward(x, small, units, positions, edges):
    rows, width = x.shape
    count = rows // TILE
    sents = TILE // GROUP
    bf, f32 = jnp.bfloat16, jnp.float32
    probs_shape = (rows // GROUP, GROUP, width)
    outs = [
        ((rows, width), bf), ((rows, width), bf), ((rows, width), bf), ((rows, width), bf), (probs_shape, bf),
        ((rows, width), bf), ((rows, width), f32), ((rows, 1), f32), ((rows, width), bf), ((rows, FF), bf),
        ((rows, FF), bf), ((rows, width), f32), ((rows, 1), f32), ((count, sents, width), f32),
        ((edges[6],) + units.shape[1:], bf),
    ]
    specs = [tiles(shape) for shape, _ in outs]
    specs[4] = pl.BlockSpec((sents,) + probs_shape[1:], lambda i, *_: (i, 0, 0))
    specs[13] = pl.BlockSpec((1, sents, width), lambda i, *_: (i, 0, 0))
    specs[14] = pl.BlockSpec(memory_space=pl.ANY)
    return pl.pallas_call(
        functools.partial(forward_kernel, edges),
        name="layer_forward",
        grid_spec=pltpu.PrefetchScalarGridSpec(
            num_scalar_prefetch=1,
            grid=(count,),
            in_specs=[tiles(x.shape), whole(small.shape), pl.BlockSpec(memory_space=pl.ANY)],
            out_specs=specs,
            scratch_shapes=[
                pltpu.VMEM((edges[6],) + units.shape[1:], bf), pltpu.SemaphoreType.DMA((6,)), pltpu.SemaphoreType.DMA,
            ],
        ),
        out_shape=[jax.ShapeDtypeStruct(shape, kind) for shape, kind in outs],
        compiler_params=pltpu.CompilerParams(vmem_limit_bytes=VMEM_MOST),
    )(positions, x, small, units)


def backward_kernel(
    edges, pos_ref, og_ref, dc_ref, small_ref, q_ref, k_ref, v_ref, probs_ref, n1_ref, rs1_ref, slope_ref, n2_ref,
    rs2_ref, units_hbm,
    dx_ref, df_ref, du_ref, da_ref, dq_ref, dk_ref, dv_ref, gsmall_ref, dy_ref, dctx_ref, held, sems,
):
    first_tile = pl.program_id(0) == 0
    width = og_ref.shape[1]
    inner_rows = FF // width

    def need(m):
        @pl.when(first_tile)
        def _():
            fetch_wait(units_hbm, held, sems, edges, m)

    @pl.when(first_tile)
    def _():
        fetch_all(pos_ref, units_hbm, held, sems, edges, (5, 4, 3, 0, 1, 2))
        gsmall_ref[...] = jnp.zeros_like(gsmall_ref)

    row = lambda r: small_ref[r : r + 1, :]

    def add_small(r, values):
        gsmall_ref[r : r + 1, :] += jnp.sum(values.astype(jnp.float32), axis=0, keepdims=True)

    dy_ref[...] = og_ref[...].astype(jnp.float32)
    for sent in range(TILE // GROUP):
        dy_ref[sent * GROUP : sent * GROUP + 1, :] += dc_ref[0, sent : sent + 1, :]
    dy = dy_ref[...]
    n2 = n2_ref[...]
    add_small(6 + inner_rows, dy * n2)
    add_small(7 + inner_rows, dy)
    dr2 = norm_back(dy, n2, rs2_ref[...], row(6 + inner_rows))
    df = dr2.astype(jnp.bfloat16)
    df_ref[...] = df
    add_small(3 + inner_rows, df)
    need(5)
    need(4)
    per = (edges[5] - edges[4]) // inner_rows
    dh1 = dr2
    for part in range(inner_rows):
        cols = slice(part * width, (part + 1) * width)
        da = dot_nt(df, matrix_of(held, edges[5] + part * per, edges[5] + (part + 1) * per))
        du = (da * slope_ref[:, cols].astype(jnp.float32)).astype(jnp.bfloat16)
        du_ref[:, cols] = du
        add_small(3 + part, du)
        dh1 += dot_nn(du, matrix_of(held, edges[4] + part * per, edges[4] + (part + 1) * per))
    n1 = n1_ref[...]
    add_small(4 + inner_rows, dh1 * n1)
    add_small(5 + inner_rows, dh1)
    dr1 = norm_back(dh1, n1, rs1_ref[...], row(4 + inner_rows))
    dattn = dr1.astype(jnp.bfloat16)
    da_ref[...] = dattn
    add_small(2, dattn)
    need(3)
    dctx_ref[...] = dot_nt(dattn, matrix_of(held, edges[3], edges[4])).astype(jnp.bfloat16)
    first, second, is_first = lane_halves()
    every_pair = [slice(pair * 2 * HD, (pair + 1) * 2 * HD) for pair in range(H // 2)]
    for sent in range(TILE // GROUP):
        rows = slice(sent * GROUP, (sent + 1) * GROUP)
        dcc = [both_heads(dctx_ref[rows, lanes], first, second) for lanes in every_pair]
        dprobs = jnp.concatenate(
            [dot_nt(v_ref[rows, lanes], wide) for lanes, wide in zip(every_pair, dcc)], axis=1
        )
        low = probs_ref[sent]
        probs = low.astype(jnp.float32)
        dscores = probs * (dprobs - jnp.sum(dprobs * probs, axis=0, keepdims=True))
        dscores = (dscores * HD ** (-0.5)).astype(jnp.bfloat16)
        dv_ref[rows, :] = jnp.concatenate(
            [dot_nn(low[:, lanes], wide) for lanes, wide in zip(every_pair, dcc)], axis=1
        ).astype(jnp.bfloat16)
        qq = [both_heads(q_ref[rows, lanes], first, second) for lanes in every_pair]
        dk_ref[rows, :] = jnp.concatenate(
            [dot_nn(dscores[:, lanes], wide) for lanes, wide in zip(every_pair, qq)], axis=1
        ).astype(jnp.bfloat16)
        mixed = [dot_tn(dscores[:, lanes], k_ref[rows, lanes]) for lanes in every_pair]
        dq_ref[rows, :] = jnp.concatenate(
            [jnp.where(is_first, m[:GROUP], m[GROUP:]) for m in mixed], axis=1
        ).astype(jnp.bfloat16)
    dx = dr1
    for m, (ref, r) in enumerate(((dq_ref, 0), (dk_ref, None), (dv_ref, 1))):
        need(m)
        rows = ref[...]
        if r is not None:
            add_small(r, rows)
        dx += dot_nt(rows, matrix_of(held, edges[m], edges[m + 1]))
    dx_ref[...] = dx.astype(jnp.bfloat16)


def run_backward(og, dc, small, saved, units, positions, edges):
    rows, width = og.shape
    count = rows // TILE
    sents = TILE // GROUP
    bf, f32 = jnp.bfloat16, jnp.float32
    _, q, k, v, probs, _, n1, rs1, _, _, slope, n2, rs2, _ = saved[:14]
    ins = [og, dc, small, q, k, v, probs, n1, rs1, slope, n2, rs2]
    in_specs = [tiles(a.shape) for a in ins]
    in_specs[1] = pl.BlockSpec((1, sents, width), lambda i, *_: (i, 0, 0))
    in_specs[2] = whole(small.shape)
    in_specs[6] = pl.BlockSpec((sents,) + probs.shape[1:], lambda i, *_: (i, 0, 0))
    outs = [((rows, width), bf)] * 2 + [((rows, FF), bf)] + [((rows, width), bf)] * 4 + [(small.shape, f32)]
    specs = [tiles(shape) for shape, _ in outs]
    specs[7] = whole(small.shape)
    return pl.pallas_call(
        functools.partial(backward_kernel, edges),
        name="layer_backward",
        grid_spec=pltpu.PrefetchScalarGridSpec(
            num_scalar_prefetch=1,
            grid=(count,),
            in_specs=in_specs + [pl.BlockSpec(memory_space=pl.ANY)],
            out_specs=specs,
            scratch_shapes=[
                pltpu.VMEM((TILE, width), f32),
                pltpu.VMEM((TILE, width), bf),
                pltpu.VMEM((edges[6],) + units.shape[1:], bf),
                pltpu.SemaphoreType.DMA((6,)),
            ],
        ),
        out_shape=[jax.ShapeDtypeStruct(shape, kind) for shape, kind in outs],
        compiler_params=pltpu.CompilerParams(vmem_limit_bytes=VMEM_MOST),
    )(positions, *ins, units)


def weight_grad_kernel(
    edges, pos_ref, x_hbm, ctx_hbm, du_hbm, act_hbm, dq_hbm, dk_hbm, dv_hbm, da_hbm, hb_hbm, df_hbm, out_hbm,
    x_v, ctx_v, du_v, act_v, right, staged, sems, out_sems,
):
    width = x_v.shape[1]
    unit_rows = out_hbm.shape[1]
    inner_rows = FF // width
    loads = [(act_hbm, act_v), (df_hbm, right.at[5]), (du_hbm, du_v), (hb_hbm, right.at[4]), (ctx_hbm, ctx_v),
             (da_hbm, right.at[3]), (x_hbm, x_v), (dq_hbm, right.at[0]), (dk_hbm, right.at[1]), (dv_hbm, right.at[2])]
    copies = [pltpu.make_async_copy(src, dst, sems.at[i]) for i, (src, dst) in enumerate(loads)]
    for copy in copies:
        copy.start()
    waited = set()
    per = width // unit_rows
    work = []
    for part in range(inner_rows):
        work.append((act_v, part, 5, edges[5] + part * per, (0, 1)))
    for part in range(inner_rows):
        work.append((du_v, part, 4, edges[4] + part * per, (2, 3)))
    work.append((ctx_v, 0, 3, edges[3], (4, 5)))
    work.append((x_v, 0, 0, edges[0], (6, 7)))
    work.append((x_v, 0, 1, edges[1], (6, 8)))
    work.append((x_v, 0, 2, edges[2], (6, 9)))
    for step, (left, part, m, unit, needs) in enumerate(work):
        slot = step % 2
        for n in needs:
            if n not in waited:
                copies[n].wait()
                waited.add(n)
        if step >= 2:
            pltpu.make_async_copy(out_hbm.at[pl.ds(0, per)], staged.at[slot], out_sems.at[slot]).wait()
        half = per // 2
        for piece in range(2):
            cols = slice(part * width + piece * half * unit_rows, part * width + (piece + 1) * half * unit_rows)
            block = dot_tn(left[:, cols], right[m]).astype(jnp.bfloat16)
            staged[slot, piece * half : (piece + 1) * half] = block.reshape(half, unit_rows, width)
        for n in range(per):
            pltpu.make_async_copy(staged.at[slot, n], out_hbm.at[pos_ref[unit + n]], out_sems.at[slot]).start()
    for slot in range(2):
        pltpu.make_async_copy(out_hbm.at[pl.ds(0, per)], staged.at[slot], out_sems.at[slot]).wait()


def run_weight_grads(x, saved, back, positions, edges, places, unit_rows):
    rows, width = x.shape
    bf = jnp.bfloat16
    ctx, hb, act = saved[5], saved[8], saved[9]
    _, df, du, da, dq, dk, dv, _ = back
    per = width // unit_rows
    anyw = pl.BlockSpec(memory_space=pl.ANY)
    return pl.pallas_call(
        functools.partial(weight_grad_kernel, edges),
        name="weight_grads",
        in_specs=[pl.BlockSpec(memory_space=pltpu.SMEM)] + [anyw] * 10,
        out_specs=anyw,
        scratch_shapes=[
            pltpu.VMEM((rows, width), bf), pltpu.VMEM((rows, width), bf), pltpu.VMEM((rows, FF), bf),
            pltpu.VMEM((rows, FF), bf), pltpu.VMEM((6, rows, width), bf),
            pltpu.VMEM((2, per, unit_rows, width), bf),
            pltpu.SemaphoreType.DMA((10,)), pltpu.SemaphoreType.DMA((2,)),
        ],
        out_shape=jax.ShapeDtypeStruct((places, unit_rows, width), bf),
        compiler_params=pltpu.CompilerParams(vmem_limit_bytes=VMEM_MOST),
    )(positions, x, ctx, du, act, dq, dk, dv, da, hb, df)


STEPS = 6
EARLY = 2
BAND = 16
HALF = 384


def step_units(edges):
    per = edges[1] - edges[0]
    firsts = [(edge + per * t, edge + per * (t + 1)) for edge in (edges[5], edges[4]) for t in (0, 2)]
    return firsts + [(edges[3], edges[0]), (edges[1], edges[2])]


def sum_places(edges):
    per = edges[1] - edges[0]
    table = [0] * edges[6]
    for t, firsts in enumerate(step_units(edges)):
        for m, first in enumerate(firsts):
            for k in range(per):
                table[first + k] = (k % 2) * (STEPS * per) + t * per + m * (per // 2) + k // 2
    return table


def backward_reduce_kernel(
    edges, tab_ref, scale_ref, small_ref, cls_ref, lang_row, lang_col, rs1_ref, rs2_ref, og_hbm, n2_hbm, slope_hbm, act_hbm, hb_hbm, n1_hbm, ctx_hbm,
    q_hbm, k_hbm, v_hbm, x_hbm, probs_hbm, units_hbm,
    dx_hbm, own_out, small_out, stats_ref,
    dh, nbuf, p0, p1, p2, p3, p4, p5, p6, p7, p8, wbuf, gbuf, c_in, xa, yb, ya, xb, ya_low, xb_low, zg, zd, zab, fbuf, a_out, a_in, x_in,
    gsm, t_acc, t_in, pooled, dlogits,
    l_sem, c_s, c_r, xa_s, xa_r, yb_s, yb_r, ya_s, ya_r, xb_s, xb_r, z_s, z_r, f_s, f_r, a_s, a_r, o_s, o_r,
    t_s, t_r, g_s, g_r, h_s, h_r, c_free,
):
    s, z, y, c = place()
    bf, f32 = jnp.bfloat16, jnp.float32
    rows_all, width = dh.shape
    count = rows_all // TILE
    inner_rows = FF // width
    per = edges[1] - edges[0]
    upper = gbuf.shape[5]
    unit_rows = 2 * upper
    slots = own_out.shape[0]
    sibling = (s, batch_of(z, y, 1 - c))
    across = (s, batch_of(z, 1 - y, c))
    other = (1 - s, batch_of(z, y, c))
    round_to = (sibling, across, other, (s, batch_of(z + 1 - 2 * (z % 2), y, c)), (s, batch_of((z + 2) % ZS, y, c)))

    barrier = pltpu.get_barrier_semaphore()

    def hello(target):
        pl.semaphore_signal(barrier, inc=1, device_id=target, device_id_type=MESH)

    hello(sibling)
    hello(other)
    turns = [(dz, dy) for dz in range(ZS) for dy in range(2) if dz or dy]
    for dz, dy in turns:
        hello((s, batch_of((z + dz) % ZS, (y + dy) % 2, c)))
    pl.semaphore_wait(barrier, 2 + len(turns))

    chunk = lambda ref, p: ref.at[:, pl.ds(p * width, width)]
    matrix = lambda first: units_hbm.at[pl.ds(first, per)]
    firsts = step_units(edges)
    acts, slopes = (p3, p5), (p4, p6, p3, p5)
    loads = {"og": (og_hbm, p0), "n2": (n2_hbm, nbuf), "hb": (hb_hbm, p2), "n1": (n1_hbm, nbuf), "probs": (probs_hbm, p0),
             "ctx": (ctx_hbm, p4), "q": (q_hbm, p6), "k": (k_hbm, p7), "v": (v_hbm, p8), "x": (x_hbm, p3)}
    for p in range(inner_rows):
        loads["act%d" % p] = (chunk(act_hbm, p), acts[p % 2])
        loads["slope%d" % p] = (chunk(slope_hbm, p), slopes[p])
        loads["wo%d" % p] = (matrix(edges[5] + p * per), wbuf.at[p % 2, 0])
        loads["wi%d" % p] = (matrix(edges[4] + p * per), wbuf.at[p % 2, 1])
    for t in (4, 5):
        for m in range(2):
            loads["w%d%d" % (t, m)] = (matrix(firsts[t][m]), wbuf.at[t % 2, m])
    copies = {
        name: pltpu.make_async_copy(src, dst, l_sem.at[n]) for n, (name, (src, dst)) in enumerate(loads.items())
    }

    def begin(*names):
        for name in names:
            copies[name].start()

    def ready(*names):
        for name in names:
            copies[name].wait()

    begin("og", "n2", "act0", "act1", "slope0", "wo0", "wi0", "hb", "slope1", "wo1", "wi1", "k", "v")

    row = lambda r: small_ref[r : r + 1, :]
    gsm[...] = jnp.zeros_like(gsm)

    def add_small(r, values):
        gsm[r : r + 1, :] += jnp.sum(values.astype(f32), axis=0, keepdims=True)

    def tile_rows(i):
        return pl.ds(pl.multiple_of(i * TILE, TILE), TILE)

    def weight(slot, m):
        return wbuf[slot, m].reshape(per * unit_rows, width)

    def remote(src, dst, send, recv, target):
        return pltpu.make_async_remote_copy(
            src_ref=src, dst_ref=dst, send_sem=send, recv_sem=recv, device_id=target, device_id_type=MESH
        )

    my_cols = pl.ds(pl.multiple_of(y * HALF, 128), HALF)
    its_cols = pl.ds(pl.multiple_of((1 - y) * HALF, 128), HALF)
    blocks = pl.ds(0, per // 2)
    both = pl.ds(0, 2)
    lines = pl.ds(0, upper)

    def band(zz):
        return pl.ds(pl.multiple_of(zz * BAND, BAND), BAND)

    def c_copy(t):
        return remote(gbuf.at[t, :, 1 - c], c_in.at[t % RING], c_s.at[t], c_r.at[t], sibling)

    def xa_copy(t):
        return remote(gbuf.at[t, 0, c, blocks, 1 - s], xa.at[t], xa_s.at[t], xa_r.at[t], other)

    def yb_copy(t):
        return remote(gbuf.at[t, 1, c, blocks, both, lines, its_cols], yb.at[t], yb_s.at[t], yb_r.at[t], across)

    def ya_view(t, cols):
        return gbuf.at[t, 0, c, blocks, s, band(z) if t < EARLY else lines, cols]

    def xb_view(t, ss):
        return gbuf.at[t, 1, c, blocks, ss, band(z) if t < EARLY else lines, my_cols]

    def ya_land(t):
        return ya_low.at[t] if t < EARLY else ya.at[t - EARLY]

    def xb_land(t):
        return xb_low.at[t] if t < EARLY else xb.at[t - EARLY]

    def ya_copy(t):
        return remote(ya_view(t, its_cols), ya_land(t), ya_s.at[t], ya_r.at[t], across)

    def xb_copy(t):
        return remote(xb_view(t, 1 - s), xb_land(t), xb_s.at[t], xb_r.at[t], other)

    def z_views(t, zz, dz):
        if t < EARLY:
            return [
                (gbuf.at[t, 0, c, blocks, s, band(zz)], zg.at[t, dz - 1]),
                (gbuf.at[t, 1, c, blocks, both, band(zz), my_cols], zd.at[t, dz - 1]),
            ]
        return [
            (gbuf.at[t, m, c, blocks, s, band(zz), my_cols], zab.at[t - EARLY, dz - 1, m]) for m in range(2)
        ]

    def z_copies(t, dz):
        zz = (z + dz) % ZS
        return [
            remote(view, land, z_s.at[n, t, dz - 1], z_r.at[n, t, dz - 1], (s, batch_of(zz, y, c)))
            for n, (view, land) in enumerate(z_views(t, zz, dz))
        ]

    def f_copy(t):
        mine = fbuf.at[pl.ds(c * (STEPS * per) + t * per, per)]
        return remote(mine, mine, f_s.at[t], f_r.at[t], sibling)

    def turn(r):
        return remote(t_acc.at[r], t_in.at[r], t_s.at[r], t_r.at[r], round_to[r])

    def add(view, got):
        @pl.loop(0, per // 2)
        def _(k):
            view.at[k][...] = (view.at[k][...].astype(f32) + got.at[k][...].astype(f32)).astype(bf)

    def ev_c_send(t):
        if t >= RING:
            pl.semaphore_wait(c_free, 1)
        c_copy(t).start()

    def ev_c_wait(t):
        c_copy(t).wait_recv()
        add(gbuf.at[t, 0, c], c_in.at[t % RING, 0])
        xa_copy(t).start()
        add(gbuf.at[t, 1, c], c_in.at[t % RING, 1])
        if t + RING < STEPS:
            pl.semaphore_signal(c_free, inc=1, device_id=sibling, device_id_type=MESH)
        yb_copy(t).start()

    def ev_first(t):
        xa_copy(t).wait_recv()
        add(gbuf.at[t, 0, c, blocks, s], xa.at[t])
        if t >= EARLY:
            ya_copy(t).start()
        yb_copy(t).wait_recv()
        add(gbuf.at[t, 1, c, blocks, both, lines, my_cols], yb.at[t])
        if t >= EARLY:
            xb_copy(t).start()

    def ev_second_start(t):
        ya_copy(t).start()
        xb_copy(t).start()

    def ev_second(t):
        ya_copy(t).wait_recv()
        add(ya_view(t, my_cols), ya_land(t))
        xb_copy(t).wait_recv()
        add(xb_view(t, s), xb_land(t))

    def ev_z_send(t):
        for dz in (2, 1, 3):
            for copy in z_copies(t, dz):
                copy.start()

    def ev_z_take(t):
        for dz in (1, 3, 2):
            for copy, (view, land) in zip(z_copies(t, dz), z_views(t, z, dz)):
                copy.wait_recv()
                add(view, land)

    def ev_fin(t):
        for m in range(2):

            @pl.loop(0, per // 2)
            def _(k):
                at = c * (STEPS * per) + t * per + m * (per // 2) + k
                fbuf[at] = gbuf[t, m, c, k, s, band(z), my_cols]

        f_copy(t).start()

    def ev_turn_start(r):
        if r == 0:
            t_acc[0] = gsm[...]
        turn(r).start()

    def ev_turn_wait(r):
        turn(r).wait()
        t_acc[r + 1] = t_acc[r] + t_in[r]

    sents = cls_ref.shape[0]
    pairs = lang_row.shape[1]
    cls = cls_ref[...]
    root = lax.rsqrt(jnp.sum(cls * cls, axis=-1, keepdims=True) + NORM_EPS)
    unit = cls * root
    pooled[s, z, y, c] = unit.astype(bf)
    all_z, low_z, high_z = pl.ds(0, ZS), pl.ds(0, ZS // 2), pl.ds(ZS // 2, ZS // 2)

    def g_copy(dz):
        mine = pooled.at[s, z, y, c]
        return remote(mine, mine, g_s.at[dz - 1], g_r.at[dz - 1], (s, batch_of((z + dz) % ZS, y, c)))

    def h_copy(n, view, target):
        return remote(view, view, h_s.at[n], h_r.at[n], target)

    swaps = [
        h_copy(0, pooled.at[s, all_z, y, c], across),
        h_copy(1, pooled.at[s, all_z, y, c], other),
        h_copy(2, pooled.at[1 - s, low_z, y, c], across),
        h_copy(3, pooled.at[s, high_z, 1 - y, c], other),
        h_copy(4, pooled.at[s, all_z, y, c], sibling),
        h_copy(5, pooled.at[s, all_z, 1 - y, c], sibling),
        h_copy(6, pooled.at[1 - s, all_z, y, c], sibling),
        h_copy(7, pooled.at[1 - s, all_z, 1 - y, c], sibling),
    ]
    for dz in (2, 1, 3):
        g_copy(dz).start()

    def tile_start(i):
        rows = slice(i * TILE, (i + 1) * TILE)
        later = lax.broadcasted_iota(jnp.int32, (TILE, 1), 0) % GROUP != 0
        dy = jnp.where(later, p0[rows, :].astype(f32), 0.0)
        n2 = nbuf[rows, :]
        add_small(6 + inner_rows, dy * n2)
        add_small(7 + inner_rows, dy)
        dr2 = norm_back(dy, n2, rs2_ref[rows, :], row(6 + inner_rows))
        dh[rows, :] = dr2
        df = dr2.astype(bf)
        p1[rows, :] = df
        add_small(3 + inner_rows, df)

    def rank_rows():
        scale = scale_ref[0]
        mix = (((1,), (0,)), ((), ()))
        e_zero = pooled[0].reshape(pairs, width)
        e_one = pooled[1].reshape(pairs, width)
        cosines = dot_nt(e_zero, e_one)
        own = lax.broadcasted_iota(jnp.int32, (pairs, pairs), 0) == lax.broadcasted_iota(jnp.int32, (pairs, pairs), 1)
        same = lang_col[...] == lang_row[...]
        diagonal = jnp.where(own, 1.0, 0.0)
        shifted = cosines - MARGIN * diagonal
        logits = scale * shifted
        masked = jnp.where(same, logits, -1e30)
        twice = -2.0 * diagonal
        total = -2.0 * jnp.sum(logits * diagonal)
        for axis in range(2):
            top = jnp.max(masked, axis=axis, keepdims=True)
            grown = jnp.where(same, jnp.exp(masked - top), 0.0)
            summed = jnp.sum(grown, axis=axis, keepdims=True)
            twice += grown / summed
            total += jnp.sum(jnp.log(summed) + top)
        line = lax.broadcasted_iota(jnp.int32, stats_ref.shape, 0)
        stats_ref[...] = jnp.where(line == 0, total, jnp.sum(twice * shifted))
        dlogits[0] = twice
        dlogits[1] = twice.T
        mine = dlogits[s, pl.ds(pl.multiple_of(batch_of(z, y, c) * sents, 16), sents), :]
        partners = pooled[1 - s].reshape(pairs, width)
        upper_part = mine.astype(bf)
        rest = (mine - upper_part.astype(f32)).astype(bf)
        de = lax.dot_general(upper_part, partners, mix, preferred_element_type=f32)
        de += lax.dot_general(rest, partners, mix, preferred_element_type=f32)
        de = scale * de
        return (de - unit * jnp.sum(unit * de, axis=-1, keepdims=True)) * root

    def sec_start():
        ready("og", "n2")
        tile_start(0)
        for dz in range(1, ZS):
            back = pooled.at[s, (z - dz) % ZS, y, c]
            remote(back, back, g_s.at[dz - 1], g_r.at[dz - 1], other).wait_recv()
        for n in (0, 1, 4):
            swaps[n].start()
        tile_start(1)
        tile_start(2)
        swaps[0].wait_recv()
        swaps[1].wait_recv()
        for n in (2, 3, 5, 6):
            swaps[n].start()
        for i in range(3, count):
            tile_start(i)
        swaps[2].wait_recv()
        swaps[3].wait_recv()
        swaps[7].start()
        for n in (4, 5, 6, 7):
            swaps[n].wait_recv()
        dc = rank_rows()
        head = [pl.ds(sent * GROUP, 1) for sent in range(sents)]
        og = jnp.concatenate([p0[sent * GROUP : sent * GROUP + 16, :].astype(f32)[:1] for sent in range(sents)], axis=0)
        n2 = jnp.concatenate([nbuf[at, :] for at in head], axis=0)
        rs2 = jnp.concatenate([rs2_ref[at, :] for at in head], axis=0)
        dy = og + dc
        add_small(6 + inner_rows, dy * n2)
        add_small(7 + inner_rows, dy)
        dr2 = norm_back(dy, n2, rs2, row(6 + inner_rows))
        add_small(3 + inner_rows, dr2.astype(bf))
        top = lax.broadcasted_iota(jnp.int32, (16, 1), 0) == 0
        for sent in range(sents):
            mine = dr2[sent : sent + 1, :]
            dh[head[sent], :] = mine
            block = slice(sent * GROUP, sent * GROUP + 16)
            p1[block, :] = jnp.where(top, mine, p1[block, :].astype(f32)).astype(bf)
        begin("n1", "probs")

    def store_grads(t, m, lhs, rhs):
        @pl.loop(0, 2)
        def _(piece):
            half = (per // 2) * unit_rows
            cols = pl.ds(pl.multiple_of(piece * half, 128), half)
            block = dot_tn(lhs[:, cols], rhs[...]).astype(bf)
            for i in range(per // 2):
                part = block[i * unit_rows : (i + 1) * unit_rows].reshape(2, upper, width)

                @pl.when(piece == 0)
                def _():
                    gbuf[t, m, i % 2, i // 2] = part

                @pl.when(piece == 1)
                def _():
                    k = per // 2 + i
                    gbuf[t, m, k % 2, k // 2] = part

    def sec_inner(p):
        def run():
            ready("slope%d" % p, "wo%d" % p, "wi%d" % p)
            slope = slopes[p]

            @pl.loop(0, count)
            def _(i):
                rows = tile_rows(i)
                da = dot_nt(p1[rows, :], weight(p % 2, 0))
                du = (da * slope[rows, :].astype(f32)).astype(bf)
                slope[rows, :] = du
                add_small(3 + p, du)
                dh[rows, :] += dot_nn(du, weight(p % 2, 1))

            if p == 2:
                begin("w40", "w41")
            if p == 3:
                begin("w50", "w51")
            if p + 2 < inner_rows:
                begin("wo%d" % (p + 2), "wi%d" % (p + 2))

        return run

    def sec_outer_grad(p):
        def run():
            ready("act%d" % p)
            store_grads(p // 2, p % 2, acts[p % 2], p1)
            if p + 2 < inner_rows:
                begin("act%d" % (p + 2))
            else:
                begin("slope%d" % p)

        return run

    def sec_inner_grad(p):
        def run():
            if p == 0:
                ready("hb")
            store_grads(2 + p // 2, p % 2, slopes[p], p2)
            if p < 3:
                begin(("ctx", "q", "x")[p])

        return run

    def sec_norm():
        ready("n1", "w40", "w41")

        @pl.loop(0, count)
        def _(i):
            rows = tile_rows(i)
            dh1 = dh[rows, :]
            n1 = nbuf[rows, :]
            add_small(4 + inner_rows, dh1 * n1)
            add_small(5 + inner_rows, dh1)
            dr1 = norm_back(dh1, n1, rs1_ref[rows, :], row(4 + inner_rows))
            dh[rows, :] = dr1
            dattn = dr1.astype(bf)
            p1[rows, :] = dattn
            add_small(2, dattn)
            p5[rows, :] = dot_nt(dattn, weight(0, 0)).astype(bf)

    def sec_out_grad():
        ready("ctx")
        store_grads(4, 0, p4, p1)

    first, second, is_first = lane_halves()
    every_pair = [slice(pair * 2 * HD, (pair + 1) * 2 * HD) for pair in range(H // 2)]

    def sec_heads(part):
        def run():
            if part == 0:
                ready("probs", "q", "k", "v")
            amount = rows_all // GROUP // 2

            @pl.loop(part * amount, (part + 1) * amount)
            def _(sent):
                rows = pl.ds(pl.multiple_of(sent * GROUP, GROUP), GROUP)
                dctx, q, k, v, low = p5[rows, :], p6[rows, :], p7[rows, :], p8[rows, :], p0[rows, :]
                dcc = [both_heads(dctx[:, lanes], first, second) for lanes in every_pair]
                dprobs = jnp.concatenate([dot_nt(v[:, lanes], wide) for lanes, wide in zip(every_pair, dcc)], axis=1)
                probs = low.astype(f32)
                dscores = probs * (dprobs - jnp.sum(dprobs * probs, axis=0, keepdims=True))
                dscores = (dscores * HD ** (-0.5)).astype(bf)
                dv = jnp.concatenate(
                    [dot_nn(low[:, lanes], wide) for lanes, wide in zip(every_pair, dcc)], axis=1
                ).astype(bf)
                p4[rows, :] = dv
                add_small(1, dv)
                qq = [both_heads(q[:, lanes], first, second) for lanes in every_pair]
                p2[rows, :] = jnp.concatenate(
                    [dot_nn(dscores[:, lanes], wide) for lanes, wide in zip(every_pair, qq)], axis=1
                ).astype(bf)
                mixed = [dot_tn(dscores[:, lanes], k[:, lanes]) for lanes in every_pair]
                dq = jnp.concatenate([jnp.where(is_first, m[:GROUP], m[GROUP:]) for m in mixed], axis=1).astype(bf)
                p1[rows, :] = dq
                add_small(0, dq)

        return run

    def sec_query_grad():
        ready("x")
        store_grads(4, 1, p3, p1)

    def sec_key_grad():
        store_grads(5, 0, p3, p2)

    def sec_value_grad():
        store_grads(5, 1, p3, p4)

    def sec_back(part):
        def run():
            if part == 0:
                ready("w50", "w51")

            @pl.loop(part * (count // 2), (part + 1) * (count // 2))
            def _(i):
                rows = tile_rows(i)
                dx = dh[rows, :] + dot_nt(p1[rows, :], weight(0, 1))
                dx += dot_nt(p2[rows, :], weight(1, 0)) + dot_nt(p4[rows, :], weight(1, 1))
                p6[rows, :] = dx.astype(bf)

        return run

    sections = [sec_start] + [sec_outer_grad(p) for p in range(inner_rows)]
    for p in range(inner_rows):
        sections += [sec_inner(p), sec_inner_grad(p)]
    sections += [sec_norm, sec_out_grad, sec_heads(0), sec_heads(1), sec_query_grad, sec_key_grad, sec_value_grad]
    sections += [sec_back(0), sec_back(1)]
    done = [2, 4, 8, 12, 17, 19]
    events = {}

    def at_tick(tick, order, action):
        events.setdefault(tick, []).append((order, action))

    for t in range(STEPS):
        at_tick(done[t], 0, functools.partial(ev_c_send, t))
        at_tick(PLACES[t][0], 1, functools.partial(ev_c_wait, t))
        at_tick(PLACES[t][1], 2, functools.partial(ev_first, t))
        if t < EARLY:
            at_tick(PLACES[t][1], 2.5, functools.partial(ev_z_send, t))
            at_tick(PLACES[t][2], 3, functools.partial(ev_z_take, t))
            at_tick(PLACES[t][2], 3.5, functools.partial(ev_second_start, t))
            at_tick(PLACES[t][3], 4, functools.partial(ev_second, t))
        else:
            at_tick(PLACES[t][2], 3, functools.partial(ev_second, t))
            at_tick(PLACES[t][2], 3.5, functools.partial(ev_z_send, t))
            at_tick(PLACES[t][3], 4, functools.partial(ev_z_take, t))
        at_tick(PLACES[t][3], 5, functools.partial(ev_fin, t))
    for r in range(5):
        at_tick(16 + r, 10, functools.partial(ev_turn_start, r))
        at_tick(17 + r, -1, functools.partial(ev_turn_wait, r))
    for tick in range(max(max(events) + 1, len(sections))):
        if tick < len(sections):
            sections[tick]()
        if tick == len(sections) - 1:
            dx_copy = pltpu.make_async_copy(p6, dx_hbm, l_sem.at[len(loads)])
            dx_copy.start()
        for _, action in sorted(events.get(tick, []), key=lambda item: item[0]):
            action()
    small_out[...] = t_acc[5]
    for t in range(STEPS):
        its = fbuf.at[pl.ds((1 - c) * (STEPS * per) + t * per, per)]
        remote(its, its, f_s.at[t], f_r.at[t], sibling).wait_recv()

    def a_copy(zz, yy):
        return remote(a_out.at[zz, yy], a_in.at[z, y], a_s.at[zz, yy], a_r.at[z, y], (s, batch_of(zz, yy, c)))

    def o_copy(zz, yy):
        return remote(a_in.at[zz, yy], x_in.at[zz, yy], o_s.at[zz, yy], o_r.at[zz, yy], other)

    for dz, dy in turns:
        zz, yy = (z + dz) % ZS, (y + dy) % 2
        for j in range(slots):
            a_out[zz, yy, j] = fbuf[tab_ref[batch_of(zz, yy, c) * slots + j]]
        a_copy(zz, yy).start()
    for j in range(slots):
        a_in[z, y, j] = fbuf[tab_ref[batch_of(z, y, c) * slots + j]]
    o_copy(z, y).start()

    def put(zz, yy, ss, got):
        rows = pl.ds(pl.multiple_of(ss * upper + zz * BAND, BAND), BAND)
        cols = pl.ds(pl.multiple_of(yy * HALF, 128), HALF)
        for j in range(slots):
            own_out[j, rows, cols] = got[zz, yy, j]

    put(z, y, s, a_in)
    for dz, dy in turns:
        zz, yy = (z + dz) % ZS, (y + dy) % 2
        remote(a_in.at[zz, yy], a_in.at[zz, yy], a_s.at[zz, yy], a_r.at[zz, yy], other).wait_recv()
        o_copy(zz, yy).start()
        put(zz, yy, s, a_in)
    for dz, dy in [(0, 0)] + turns:
        zz, yy = (z + dz) % ZS, (y + dy) % 2
        o_copy(zz, yy).wait_recv()
        put(zz, yy, 1 - s, x_in)
    for t in range(STEPS):
        for copy in (c_copy, xa_copy, yb_copy, ya_copy, xb_copy, f_copy):
            copy(t).wait_send()

        for dz in range(1, ZS):
            for copy in z_copies(t, dz):
                copy.wait_send()

    for dz in range(1, ZS):
        g_copy(dz).wait_send()
    for swap in swaps:
        swap.wait_send()
    for dz, dy in turns:
        a_copy((z + dz) % ZS, (y + dy) % 2).wait_send()
    for dz, dy in [(0, 0)] + turns:
        o_copy((z + dz) % ZS, (y + dy) % 2).wait_send()
    dx_copy.wait()


RING = 3
PLACES = ((5, 9, 36, 43), (8, 12, 22, 78), (10, 15, 19, 41), (13, 17, 21, 27), (18, 21, 35, 43), (20, 24, 41, 47))


def run_backward_reduce(og, cls, scale, langs, small, saved, x, units, table, edges, slots):
    rows, width = og.shape
    bf, f32 = jnp.bfloat16, jnp.float32
    _, q, k, v, probs, ctx, n1, rs1, hb, act, slope, n2, rs2, _ = saved[:14]
    unit_rows = units.shape[1]
    per = edges[1] - edges[0]
    half = per // 2
    pairs = langs.shape[0]
    dma = pltpu.SemaphoreType.DMA
    vm = pltpu.VMEM
    vmem = pl.BlockSpec(memory_space=pltpu.VMEM)
    anyw = pl.BlockSpec(memory_space=pl.ANY)
    upper = unit_rows // 2
    return pl.pallas_call(
        functools.partial(backward_reduce_kernel, edges),
        name="backward_reduce",
        out_shape=[
            jax.ShapeDtypeStruct((rows, width), bf),
            jax.ShapeDtypeStruct((slots, unit_rows, width), bf),
            jax.ShapeDtypeStruct(small.shape, f32),
            jax.ShapeDtypeStruct((8, 128), f32),
        ],
        in_specs=[pl.BlockSpec(memory_space=pltpu.SMEM)] * 2 + [vmem] * 6 + [anyw] * 13,
        out_specs=[anyw, vmem, vmem, vmem],
        scratch_shapes=[vm((rows, width), f32)] * 2
        + [vm((rows, width), bf)] * 9
        + [
            vm((2, 2, per, unit_rows, width), bf),
            vm((STEPS, 2, 2, half, 2, upper, width), bf),
            vm((RING, 2, half, 2, upper, width), bf),
            vm((STEPS, half, upper, width), bf),
            vm((STEPS, half, 2, upper, HALF), bf),
            vm((STEPS - EARLY, half, upper, HALF), bf),
            vm((STEPS - EARLY, half, upper, HALF), bf),
            vm((EARLY, half, BAND, HALF), bf),
            vm((EARLY, half, BAND, HALF), bf),
            vm((EARLY, ZS - 1, half, BAND, width), bf),
            vm((EARLY, ZS - 1, half, 2, BAND, HALF), bf),
            vm((STEPS - EARLY, ZS - 1, 2, half, BAND, HALF), bf),
            vm((2 * STEPS * per, BAND, HALF), bf),
            vm((ZS, 2, slots, BAND, HALF), bf),
            vm((ZS, 2, slots, BAND, HALF), bf),
            vm((ZS, 2, slots, BAND, HALF), bf),
            vm(small.shape, f32),
            vm((6,) + small.shape, f32),
            vm((5,) + small.shape, f32),
            vm((2, ZS, 2, 2) + cls.shape, bf),
            vm((2, pairs, pairs), f32),
        ]
        + [dma((32,))]
        + [dma((STEPS,))] * 10
        + [dma((2, STEPS, ZS - 1))] * 2
        + [dma((STEPS,))] * 2
        + [dma((ZS, 2))] * 4
        + [dma((5,))] * 2
        + [dma((ZS - 1,))] * 2
        + [dma((8,))] * 2
        + [pltpu.SemaphoreType.REGULAR],
        compiler_params=pltpu.CompilerParams(collective_id=3, has_side_effects=True, vmem_limit_bytes=63 << 20),
    )(table, scale, small, cls, langs.reshape(1, pairs), langs.reshape(pairs, 1), rs1, rs2, og, n2, slope, act, hb, n1, ctx, q, k, v, x, probs.reshape(rows, width), units)


def unit_positions(owner_list, slot_count):
    unit_total = owner_list.shape[0]
    same_owner = owner_list[:, None] == owner_list[None, :]
    ordinal = jnp.arange(unit_total, dtype=jnp.int32)
    earlier = ordinal[None, :] < ordinal[:, None]
    slot_number = jnp.sum(jnp.where(same_owner & earlier, 1, 0), axis=1).astype(jnp.int32)
    return owner_list * slot_count + slot_number


def adamw(weight_in, gradient, moment_one, moment_two, rate_value, decay_value, fix_one, fix_two):
    new_one = BETA_ONE * moment_one + (1.0 - BETA_ONE) * gradient
    new_two = BETA_TWO * moment_two + (1.0 - BETA_TWO) * gradient * gradient
    stepped = new_one / fix_one / (jnp.sqrt(new_two / fix_two) + ADAM_EPS)
    return (weight_in - rate_value * (stepped + decay_value * weight_in), new_one, new_two)


def adamw_kernel(fixes, filled_ref, weight_ref, grad_ref, first_ref, second_ref, new_ref, one_ref, two_ref, low_ref):
    weight, first, second = weight_ref[...], first_ref[...], second_ref[...]
    gradient = grad_ref[...].astype(jnp.float32)
    moved = adamw(weight, gradient, first, second, RATE_UNITS, DECAY, *fixes)
    used = filled_ref[pl.program_id(0)] > 0
    new = jnp.where(used, moved[0], weight)
    new_ref[...] = new
    one_ref[...] = jnp.where(used, moved[1], first)
    two_ref[...] = jnp.where(used, moved[2], second)
    low_ref[...] = new.astype(jnp.bfloat16)


def run_adamw(weight, gradient, first, second, filled, fixes):
    slots, rows, width = weight.shape
    block = pl.BlockSpec((1, rows // 2, width), lambda i, j, *_: (i, j, 0))
    kinds = [jnp.float32] * 3 + [jnp.bfloat16]
    return pl.pallas_call(
        functools.partial(adamw_kernel, fixes),
        name="adamw_units",
        grid_spec=pltpu.PrefetchScalarGridSpec(
            num_scalar_prefetch=1, grid=(slots, 2), in_specs=[block] * 4, out_specs=[block] * 4
        ),
        out_shape=[jax.ShapeDtypeStruct(weight.shape, kind) for kind in kinds],
        compiler_params=pltpu.CompilerParams(vmem_limit_bytes=VMEM_MOST),
    )(filled, weight, gradient, first, second)


def any_size_units(own, positions, owners):
    slots, rows, width = own.shape
    table = jnp.arange(owners * slots, dtype=jnp.int32)[:, None] == positions[None, :]
    bands = lax.all_to_all(
        own.transpose(1, 0, 2).astype(jnp.bfloat16), "batch", split_axis=0, concat_axis=1, tiled=True
    )
    ordered = jnp.einsum(
        "rpd,pu->rud", bands, table.astype(jnp.bfloat16), preferred_element_type=jnp.float32
    ).astype(jnp.bfloat16)
    return lax.all_gather(ordered, "batch", axis=0, tiled=True).transpose(1, 0, 2)


def any_size_sums(grads, positions, owners, slots):
    table = jnp.arange(owners * slots, dtype=jnp.int32)[:, None] == positions[None, :]
    pieces = lax.psum_scatter(grads.transpose(1, 0, 2).astype(jnp.float32), "batch", scatter_dimension=0, tiled=True)
    summed = lax.psum(pieces.astype(jnp.bfloat16), "stream").astype(jnp.float32)
    send_rows = jnp.einsum("rud,pu->rpd", summed, table.astype(jnp.float32), precision=HIGHEST)
    owned = lax.all_to_all(send_rows.astype(jnp.bfloat16), "batch", split_axis=1, concat_axis=0, tiled=True)
    return owned.astype(jnp.float32).transpose(1, 0, 2)


def any_size_rank(cls, scale, langs, owners):
    sents, width = cls.shape
    root = lax.rsqrt(jnp.sum(cls * cls, axis=-1, keepdims=True) + NORM_EPS)
    unit = cls * root
    every = lax.all_gather(unit.astype(jnp.bfloat16), "batch", axis=0, tiled=True)
    every = lax.all_gather(every, "stream", axis=0)
    cosines = jnp.dot(every[0], every[1].T, preferred_element_type=jnp.float32)
    diagonal = jnp.eye(cosines.shape[0], dtype=jnp.float32)
    same = langs[:, None] == langs[None, :]
    shifted = cosines - MARGIN * diagonal
    logits = scale[0] * shifted
    masked = jnp.where(same, logits, -1e30)
    both = -2.0 * diagonal
    total = -2.0 * jnp.sum(logits * diagonal)
    for axis in range(2):
        top = jnp.max(masked, axis=axis, keepdims=True)
        grown = jnp.where(same, jnp.exp(masked - top), 0.0)
        summed = jnp.sum(grown, axis=axis, keepdims=True)
        both += grown / summed
        total += jnp.sum(jnp.log(summed) + top)
    s = lax.axis_index("stream")
    turned = jnp.where(s == 0, both, both.T)
    rows = lax.dynamic_slice_in_dim(turned, lax.axis_index("batch") * sents, sents)
    partners = lax.dynamic_index_in_dim(every, 1 - s, keepdims=False).astype(jnp.float32)
    de = scale[0] * jnp.dot(rows, partners, precision=HIGHEST)
    dc = (de - unit * jnp.sum(unit * de, axis=-1, keepdims=True)) * root
    return dc, total, jnp.sum(both * shifted)


def per_device(
    tokens, out_grad, master, first_moment, second_moment, small_params, small_first, small_second, logit_scale,
    scale_first, scale_second, pair_lang, unit_owner,
):
    owners = lax.axis_size("batch")
    here_batch = lax.axis_index("batch")
    unit_rows, slot_count, width = master.shape
    query_blocks = width // unit_rows
    inner_blocks = FF // unit_rows
    edges = [query_blocks * n for n in range(5)]
    edges += [edges[4] + inner_blocks, edges[4] + 2 * inner_blocks]
    units_total = unit_owner.shape[0]
    positions = unit_positions(unit_owner, slot_count)
    on_block = owners == 4 * ZS
    own = master.transpose(1, 0, 2)
    if on_block:
        units, where, places = gather_units(own), positions, owners * slot_count
    else:
        units = any_size_units(own, positions, owners)
        where, places = jnp.arange(units_total, dtype=jnp.int32), units_total
    sentences, length = tokens.shape[1], tokens.shape[2]
    flat = tokens.reshape(sentences * length, width)
    saved = run_forward(flat, small_params, units, where, edges)
    cls = saved[13]
    grad_rows = out_grad.reshape(sentences * length, width)
    if on_block:
        slot_units = jnp.arange(places, dtype=jnp.int32)[:, None] == positions[None, :]
        sum_table = jnp.asarray(sum_places(edges), dtype=jnp.int32)
        table = jnp.sum(jnp.where(slot_units, sum_table[None, :], 0), axis=1, dtype=jnp.int32)
        d_tokens, owned_grad, small_total, stats = run_backward_reduce(
            grad_rows, cls.reshape(sentences, width), logit_scale, pair_lang, small_params, saved, flat, saved[14], table, edges,
            slot_count,
        )
        loss_total, grad_scale = stats[0, :1], stats[1, :1]
    else:
        dc, loss_total, grad_scale = any_size_rank(cls.reshape(sentences, width), logit_scale, pair_lang, owners)
        loss_total, grad_scale = loss_total.reshape(1), grad_scale.reshape(1)
        back = run_backward(grad_rows, dc.reshape(cls.shape), small_params, saved, units, where, edges)
        grads = run_weight_grads(flat, saved, back, where, edges, places, unit_rows)
        d_tokens = back[0]
        owned_grad = any_size_sums(grads, positions, owners, slot_count)
        small_total = lax.psum(back[7], ("stream", "batch"))
    step_value = float(STEP)
    fix_one = 1.0 - BETA_ONE**step_value
    fix_two = 1.0 - BETA_TWO**step_value
    my_places = here_batch * slot_count + jnp.arange(slot_count, dtype=jnp.int32)
    filled = jnp.any(my_places[:, None] == positions[None, :], axis=1).astype(jnp.int32)
    new_master, new_first, new_second, new_copy = run_adamw(
        own, owned_grad, first_moment.transpose(1, 0, 2), second_moment.transpose(1, 0, 2), filled, (fix_one, fix_two)
    )
    new_small, new_small_first, new_small_second = adamw(
        small_params, small_total, small_first, small_second, RATE_SMALL, 0.0, fix_one, fix_two
    )
    scale_new, scale_one, scale_two = adamw(
        logit_scale, grad_scale, scale_first, scale_second, RATE_SCALE, 0.0, fix_one, fix_two
    )
    loss_out = loss_total / (2 * owners * sentences)
    back_order = lambda a: a.transpose(1, 0, 2)
    return (
        saved[0].reshape(tokens.shape),
        d_tokens.reshape(tokens.shape),
        back_order(new_master),
        back_order(new_first),
        back_order(new_second),
        back_order(new_copy),
        new_small,
        new_small_first,
        new_small_second,
        scale_new,
        scale_one,
        scale_two,
        loss_out,
    )


def solution(mesh):
    rows = P("stream", "batch", None, None)
    blocks = P(None, "batch", None)
    return jax.shard_map(
        per_device,
        mesh=mesh,
        in_specs=(rows, rows, blocks, blocks, blocks) + (P(),) * 8,
        out_specs=(rows, rows, blocks, blocks, blocks, blocks) + (P(),) * 7,
        check_vma=False,
    )
```

```python
import functools

import jax
import jax.numpy as jnp
from jax import lax
from jax.experimental import pallas as pl
from jax.experimental.pallas import tpu as pltpu
from jax.sharding import PartitionSpec as P

H = 12
HD = 64
FF = 3072
STEP = 10
ZS = 4
UR_ROWS = 128
LEN_ROWS = 64
VMEM_MOST = 60 << 20
MESH = pl.DeviceIdType.MESH

HIGHEST = lax.Precision.HIGHEST
BETA_ONE = 0.9
BETA_TWO = 0.999
ADAM_EPS = 1e-06
RATE_UNITS = 0.02
RATE_SMALL = 0.1
RATE_SCALE = 2.0
DECAY = 0.01
MARGIN = 0.3
NORM_EPS = 1e-06


def place():
    s = lax.axis_index("stream")
    b = lax.axis_index("batch")
    return s, b // 4, (b // 2) % 2, b % 2


def batch_of(z, y, c):
    return (z * 2 + y) * 2 + c


def greet(s, z, y, c, others):
    barrier = pltpu.get_barrier_semaphore()

    def hello(target):
        pl.semaphore_signal(barrier, inc=1, device_id=target, device_id_type=MESH)

    hello((s, batch_of(z, y, 1 - c)))
    hello((s, batch_of(z, 1 - y, c)))
    hello((1 - s, batch_of(z, y, c)))
    if others == "line":
        for far in range(1, ZS):

            @pl.when(z >= far)
            def _():
                hello((s, batch_of(z - far, y, c)))

            @pl.when(z + far < ZS)
            def _():
                hello((s, batch_of(z + far, y, c)))

        pl.semaphore_wait(barrier, 3 + ZS - 1)
    else:

        @pl.when(z >= 1)
        def _():
            hello((s, batch_of(z - 1, y, c)))

        @pl.when(z + 1 < ZS)
        def _():
            hello((s, batch_of(z + 1, y, c)))

        pl.semaphore_wait(barrier, 3 + (z + 2) // 3 + (5 - z) // 3)


GR = 80
GX = UR_ROWS - GR


def gather_kernel(own_ref, out_ref, low, stage_sem, zl_s, zl_r, zr_s, zr_r, y_s, y_r, x_s, x_r, ca_s, ca_r, cb_s, cb_r):
    s, z, y, c = place()
    slots = own_ref.shape[0]
    steps = ZS * slots
    base = pl.multiple_of(s * GX, 16)
    only = pl.multiple_of(s * GR, 16)
    theirs = pl.multiple_of((1 - s) * GR, 16)

    def at(zz, yy, cc, j):
        return batch_of(zz, yy, cc) * slots + j

    greet(s, z, y, c, "next")

    def push(src, row, start, size, send, recv, target):
        return pltpu.make_async_remote_copy(
            src_ref=src,
            dst_ref=out_ref.at[row, pl.ds(start, size)],
            send_sem=send,
            recv_sem=recv,
            device_id=target,
            device_id_type=MESH,
        )

    left = (s, batch_of(z - 1, y, c))
    right = (s, batch_of(z + 1, y, c))
    across = (s, batch_of(z, 1 - y, c))
    other = (1 - s, batch_of(z, y, c))
    sibling = (s, batch_of(z, y, 1 - c))

    def to_left(src, zz, j):
        row = at(zz, y, c, j)
        return push(src(row), row, base, GR, zl_s.at[zz, j], zl_r.at[zz, j], left)

    def to_right(src, zz, j):
        row = at(zz, y, c, j)
        return push(src(row), row, base, GR, zr_s.at[zz, j], zr_r.at[zz, j], right)

    def to_across(src, zz, j):
        row = at(zz, y, c, j)
        return push(src(row), row, base, GR, y_s.at[zz, j], y_r.at[zz, j], across)

    def to_other(zz, yy, j):
        row = at(zz, yy, c, j)
        return push(out_ref.at[row, pl.ds(only, GX)], row, only, GX, x_s.at[zz, yy, j], x_r.at[zz, yy, j], other)

    def to_sibling(zz, yy, j):
        row = at(zz, yy, c, j)
        return push(out_ref.at[row, pl.ds(base, GR)], row, base, GR, ca_s.at[zz, yy, j], ca_r.at[zz, yy, j], sibling)

    def rest_to_sibling(zz, yy, j):
        row = at(zz, yy, c, j)
        return push(out_ref.at[row, pl.ds(theirs, GX)], row, theirs, GX, cb_s.at[zz, yy, j], cb_r.at[zz, yy, j], sibling)

    def landed(row):
        return out_ref.at[row, pl.ds(base, GR)]

    def from_left(zz, j):
        row = at(zz, y, c, j)
        return push(landed(row), row, base, GR, zr_s.at[zz, j], zr_r.at[zz, j], right)

    def arrived_line(zz, j, onward):
        onward.start()
        to_across(landed, zz, j).start()
        to_other(zz, y, j).start()
        to_sibling(zz, y, j).start()

    def stage(j):
        return pltpu.make_async_copy(low.at[j], out_ref.at[at(z, y, c, j)], stage_sem.at[j])

    for j in range(slots):
        low[j] = own_ref[j].astype(jnp.bfloat16)
        mine = lambda row: low.at[j, pl.ds(base, GR)]

        @pl.when(z > 0)
        def _():
            to_left(mine, z, j).start()

        @pl.when(z < ZS - 1)
        def _():
            to_right(mine, z, j).start()

        to_across(mine, z, j).start()
        row = at(z, y, c, j)
        push(low.at[j, pl.ds(base, GR)], row, base, GR, ca_s.at[z, y, j], ca_r.at[z, y, j], sibling).start()
        push(low.at[j, pl.ds(theirs, GX)], row, theirs, GX, cb_s.at[z, y, j], cb_r.at[z, y, j], sibling).start()
        stage(j).start()

    def line_step(t):
        d = t // slots
        j = t % slots

        @pl.when((d >= 1) & (z - d >= 0))
        def _():
            zz = z - d
            to_right(landed, zz, j).wait_recv()

            @pl.when(z < ZS - 1)
            def _():
                to_right(landed, zz, j).start()

            to_across(landed, zz, j).start()
            to_other(zz, y, j).start()
            to_sibling(zz, y, j).start()

        @pl.when((d >= 1) & (z + d < ZS))
        def _():
            zz = z + d
            to_left(landed, zz, j).wait_recv()

            @pl.when(z > 0)
            def _():
                to_left(landed, zz, j).start()

            to_across(landed, zz, j).start()
            to_other(zz, y, j).start()
            to_sibling(zz, y, j).start()

    def across_one(zz, j):
        row = at(zz, 1 - y, c, j)
        push(landed(row), row, base, GR, y_s.at[zz, j], y_r.at[zz, j], across).wait_recv()
        to_other(zz, 1 - y, j).start()
        to_sibling(zz, 1 - y, j).start()

    def across_step(t):
        d = t // slots
        j = t % slots

        @pl.when(z - d >= 0)
        def _():
            across_one(z - d, j)

        @pl.when((d >= 1) & (z + d < ZS))
        def _():
            across_one(z + d, j)

    def other_one(zz, yy, j):
        row = at(zz, yy, c, j)
        push(
            out_ref.at[row, pl.ds(theirs, GX)], row, theirs, GX, x_s.at[zz, yy, j], x_r.at[zz, yy, j], other
        ).wait_recv()
        rest_to_sibling(zz, yy, j).start()

    def other_step(t, yy, first):
        d = t // slots
        j = t % slots

        @pl.when((d >= first) & (z - d >= 0))
        def _():
            other_one(z - d, yy, j)

        @pl.when((d >= 1) & (z + d < ZS))
        def _():
            other_one(z + d, yy, j)

    @pl.loop(0, steps + 3)
    def _(t):
        @pl.when(t < steps)
        def _():
            line_step(t)

        @pl.when((t >= 1) & (t < steps + 1))
        def _():
            across_step(t - 1)

        @pl.when((t >= 2) & (t < steps + 2))
        def _():
            other_step(t - 2, y, 1)

        @pl.when(t >= 3)
        def _():
            other_step(t - 3, 1 - y, 0)

    for j in range(slots):
        stage(j).wait()

    @pl.loop(0, steps)
    def _(t):
        zz = t // slots
        j = t % slots

        @pl.when((z > 0) & (zz >= z))
        def _():
            to_left(landed, zz, j).wait_send()

        @pl.when((z < ZS - 1) & (zz <= z))
        def _():
            to_right(landed, zz, j).wait_send()

        to_across(landed, zz, j).wait_send()

        @pl.when(zz != z)
        def _():
            to_other(zz, y, j).wait_send()

        to_other(zz, 1 - y, j).wait_send()
        for yy in range(2):
            to_sibling(zz, yy, j).wait_send()
            rest_to_sibling(zz, yy, j).wait_send()
            row = at(zz, yy, 1 - c, j)
            push(landed(row), row, base, GR, ca_s.at[zz, yy, j], ca_r.at[zz, yy, j], sibling).wait_recv()
            push(
                out_ref.at[row, pl.ds(theirs, GX)], row, theirs, GX, cb_s.at[zz, yy, j], cb_r.at[zz, yy, j], sibling
            ).wait_recv()


def gather_units(own):
    slots, rows, width = own.shape
    owners = lax.axis_size("batch")
    line = [pltpu.SemaphoreType.DMA((ZS, slots))] * 6
    plane = [pltpu.SemaphoreType.DMA((ZS, 2, slots))] * 6
    return pl.pallas_call(
        gather_kernel,
        name="gather_units",
        out_shape=jax.ShapeDtypeStruct((owners * slots, rows, width), jnp.bfloat16),
        in_specs=[pl.BlockSpec(memory_space=pltpu.VMEM)],
        out_specs=pl.BlockSpec(memory_space=pl.ANY),
        scratch_shapes=[pltpu.VMEM((slots, rows, width), jnp.bfloat16), pltpu.SemaphoreType.DMA((slots,))] + line + plane,
        compiler_params=pltpu.CompilerParams(collective_id=0, has_side_effects=True, vmem_limit_bytes=VMEM_MOST),
    )(own)


TILE = 256
GROUP = LEN_ROWS


def dot_nn(a, b):
    return lax.dot_general(a, b, (((1,), (0,)), ((), ())), preferred_element_type=jnp.float32)


def dot_nt(a, b):
    return lax.dot_general(a, b, (((1,), (1,)), ((), ())), preferred_element_type=jnp.float32)


def dot_tn(a, b):
    return lax.dot_general(a, b, (((0,), (0,)), ((), ())), preferred_element_type=jnp.float32)


def gelu_parts(u):
    t = 1.0 / (1.0 + (0.3275911 * 0.7071067811865476) * jnp.abs(u))
    bell = jnp.exp(-0.5 * u * u)
    tail = t * (
        0.127414796 + t * (-0.142248368 + t * (0.7107068705 + t * (-0.7265760135 + t * 0.5307027145)))
    ) * bell
    phi_sum = jnp.where(u >= 0.0, 1.0 - tail, tail)
    return u * phi_sum, phi_sum + u * (0.3989422804014327 * bell)


def norm_parts(resid):
    centre = jnp.mean(resid, axis=-1, keepdims=True)
    centred = resid - centre
    rs = lax.rsqrt(jnp.mean(centred * centred, axis=-1, keepdims=True) + NORM_EPS)
    return centred * rs, rs


def norm_back(dy, unit, rs, gain):
    gd = gain * dy
    return rs * (gd - jnp.mean(gd, axis=-1, keepdims=True) - unit * jnp.mean(gd * unit, axis=-1, keepdims=True))


def lane_halves():
    lane = lax.broadcasted_iota(jnp.int32, (1, 2 * HD), 1)
    first = jnp.where(lane < HD, 1.0, 0.0)
    return first.astype(jnp.bfloat16), (1.0 - first).astype(jnp.bfloat16), lane < HD


def both_heads(rows, first, second):
    return jnp.concatenate([rows * first, rows * second], axis=0)


def fetch_all(pos_ref, units_hbm, held, sems, edges, order):
    for m in order:
        for u in range(edges[m], edges[m + 1]):
            pltpu.make_async_copy(units_hbm.at[pos_ref[u]], held.at[u], sems.at[m]).start()


def fetch_wait(units_hbm, held, sems, edges, m):
    lo, hi = edges[m], edges[m + 1]
    pltpu.make_async_copy(units_hbm.at[pl.ds(0, hi - lo)], held.at[pl.ds(lo, hi - lo)], sems.at[m]).wait()


def matrix_of(held, lo, hi):
    block = held[lo:hi]
    return block.reshape((hi - lo) * block.shape[1], block.shape[2])


def forward_kernel(
    edges, pos_ref, x_ref, small_ref, units_hbm,
    out_ref, q_ref, k_ref, v_ref, probs_ref, ctx_ref, n1_ref, rs1_ref, hb_ref, act_ref, slope_ref, n2_ref, rs2_ref,
    cls_ref, ordered_hbm, held, sems, keep_sem,
):
    first_tile = pl.program_id(0) == 0
    width = x_ref.shape[1]

    def need(m):
        @pl.when(first_tile)
        def _():
            fetch_wait(units_hbm, held, sems, edges, m)

    @pl.when(first_tile)
    def _():
        fetch_all(pos_ref, units_hbm, held, sems, edges, range(6))

    inner_rows = FF // width
    row = lambda r: small_ref[r : r + 1, :]
    x = x_ref[...]
    need(0)
    q = (dot_nn(x, matrix_of(held, edges[0], edges[1])) + row(0)).astype(jnp.bfloat16)
    q_ref[...] = q
    need(1)
    k = dot_nn(x, matrix_of(held, edges[1], edges[2])).astype(jnp.bfloat16)
    k_ref[...] = k
    need(2)
    v = (dot_nn(x, matrix_of(held, edges[2], edges[3])) + row(1)).astype(jnp.bfloat16)
    v_ref[...] = v
    first, second, is_first = lane_halves()
    every_pair = [slice(pair * 2 * HD, (pair + 1) * 2 * HD) for pair in range(H // 2)]
    every_sent = [slice(sent * GROUP, (sent + 1) * GROUP) for sent in range(TILE // GROUP)]
    for sent, rows in enumerate(every_sent):
        scores = jnp.concatenate(
            [dot_nt(k[rows, lanes], both_heads(q[rows, lanes], first, second)) for lanes in every_pair], axis=1
        )
        grown = jnp.exp((scores - jnp.max(scores, axis=0, keepdims=True)) * HD ** (-0.5))
        probs = (grown * (1.0 / jnp.sum(grown, axis=0, keepdims=True))).astype(jnp.bfloat16)
        probs_ref[sent] = probs
        mixed = [dot_tn(probs[:, lanes], v[rows, lanes]) for lanes in every_pair]
        ctx_ref[rows, :] = jnp.concatenate(
            [jnp.where(is_first, m[:GROUP], m[GROUP:]) for m in mixed], axis=1
        ).astype(jnp.bfloat16)
    need(3)
    attended = dot_nn(ctx_ref[...], matrix_of(held, edges[3], edges[4])) + row(2)
    n1, rs1 = norm_parts(x.astype(jnp.float32) + attended)
    n1_ref[...] = n1
    rs1_ref[...] = rs1
    h1 = n1 * row(4 + inner_rows) + row(5 + inner_rows)
    hb = h1.astype(jnp.bfloat16)
    hb_ref[...] = hb
    need(4)
    need(5)
    keep = pltpu.make_async_copy(held, ordered_hbm, keep_sem)

    @pl.when(first_tile)
    def _():
        keep.start()

    per = (edges[5] - edges[4]) // inner_rows
    total = h1 + row(3 + inner_rows)
    for part in range(inner_rows):
        cols = slice(part * width, (part + 1) * width)
        w_in = matrix_of(held, edges[4] + part * per, edges[4] + (part + 1) * per)
        u = dot_nt(hb, w_in) + row(3 + part)
        value, slope = gelu_parts(u)
        act = value.astype(jnp.bfloat16)
        act_ref[:, cols] = act
        slope_ref[:, cols] = slope.astype(jnp.bfloat16)
        total += dot_nn(act, matrix_of(held, edges[5] + part * per, edges[5] + (part + 1) * per))
    n2, rs2 = norm_parts(total)
    n2_ref[...] = n2
    rs2_ref[...] = rs2
    y = n2 * row(6 + inner_rows) + row(7 + inner_rows)
    out_ref[...] = y.astype(jnp.bfloat16)
    for sent in range(TILE // GROUP):
        here = pl.program_id(0) * (TILE // GROUP) + sent
        cls_ref[pl.ds(here, 1), :] = y[sent * GROUP : sent * GROUP + 1, :]

    @pl.when(pl.program_id(0) == pl.num_programs(0) - 1)
    def _():
        keep.wait()


def tiles(shape):
    rest = len(shape) - 1
    return pl.BlockSpec((TILE,) + tuple(shape[1:]), lambda i, *_: (i,) + (0,) * rest)


def whole(shape):
    return pl.BlockSpec(tuple(shape), lambda i, *_: (0,) * len(shape))


def run_forward(x, small, units, positions, edges):
    rows, width = x.shape
    count = rows // TILE
    sents = TILE // GROUP
    bf, f32 = jnp.bfloat16, jnp.float32
    probs_shape = (rows // GROUP, GROUP, width)
    outs = [
        ((rows, width), bf), ((rows, width), bf), ((rows, width), bf), ((rows, width), bf), (probs_shape, bf),
        ((rows, width), bf), ((rows, width), f32), ((rows, 1), f32), ((rows, width), bf), ((rows, FF), bf),
        ((rows, FF), bf), ((rows, width), f32), ((rows, 1), f32), ((rows // GROUP, width), f32),
        ((edges[6],) + units.shape[1:], bf),
    ]
    specs = [tiles(shape) for shape, _ in outs]
    specs[4] = pl.BlockSpec((sents,) + probs_shape[1:], lambda i, *_: (i, 0, 0))
    specs[13] = whole(outs[13][0])
    specs[14] = pl.BlockSpec(memory_space=pl.ANY)
    return pl.pallas_call(
        functools.partial(forward_kernel, edges),
        name="layer_forward",
        grid_spec=pltpu.PrefetchScalarGridSpec(
            num_scalar_prefetch=1,
            grid=(count,),
            in_specs=[tiles(x.shape), whole(small.shape), pl.BlockSpec(memory_space=pl.ANY)],
            out_specs=specs,
            scratch_shapes=[
                pltpu.VMEM((edges[6],) + units.shape[1:], bf), pltpu.SemaphoreType.DMA((6,)), pltpu.SemaphoreType.DMA,
            ],
        ),
        out_shape=[jax.ShapeDtypeStruct(shape, kind) for shape, kind in outs],
        compiler_params=pltpu.CompilerParams(vmem_limit_bytes=VMEM_MOST),
    )(positions, x, small, units)


def backward_kernel(
    edges, pos_ref, og_ref, dc_ref, small_ref, q_ref, k_ref, v_ref, probs_ref, n1_ref, rs1_ref, slope_ref, n2_ref,
    rs2_ref, units_hbm,
    dx_ref, df_ref, du_ref, da_ref, dq_ref, dk_ref, dv_ref, gsmall_ref, dy_ref, dctx_ref, held, sems,
):
    first_tile = pl.program_id(0) == 0
    width = og_ref.shape[1]
    inner_rows = FF // width

    def need(m):
        @pl.when(first_tile)
        def _():
            fetch_wait(units_hbm, held, sems, edges, m)

    @pl.when(first_tile)
    def _():
        fetch_all(pos_ref, units_hbm, held, sems, edges, (5, 4, 3, 0, 1, 2))
        gsmall_ref[...] = jnp.zeros_like(gsmall_ref)

    row = lambda r: small_ref[r : r + 1, :]

    def add_small(r, values):
        gsmall_ref[r : r + 1, :] += jnp.sum(values.astype(jnp.float32), axis=0, keepdims=True)

    dy_ref[...] = og_ref[...].astype(jnp.float32)
    for sent in range(TILE // GROUP):
        dy_ref[sent * GROUP : sent * GROUP + 1, :] += dc_ref[0, sent : sent + 1, :]
    dy = dy_ref[...]
    n2 = n2_ref[...]
    add_small(6 + inner_rows, dy * n2)
    add_small(7 + inner_rows, dy)
    dr2 = norm_back(dy, n2, rs2_ref[...], row(6 + inner_rows))
    df = dr2.astype(jnp.bfloat16)
    df_ref[...] = df
    add_small(3 + inner_rows, df)
    need(5)
    need(4)
    per = (edges[5] - edges[4]) // inner_rows
    dh1 = dr2
    for part in range(inner_rows):
        cols = slice(part * width, (part + 1) * width)
        da = dot_nt(df, matrix_of(held, edges[5] + part * per, edges[5] + (part + 1) * per))
        du = (da * slope_ref[:, cols].astype(jnp.float32)).astype(jnp.bfloat16)
        du_ref[:, cols] = du
        add_small(3 + part, du)
        dh1 += dot_nn(du, matrix_of(held, edges[4] + part * per, edges[4] + (part + 1) * per))
    n1 = n1_ref[...]
    add_small(4 + inner_rows, dh1 * n1)
    add_small(5 + inner_rows, dh1)
    dr1 = norm_back(dh1, n1, rs1_ref[...], row(4 + inner_rows))
    dattn = dr1.astype(jnp.bfloat16)
    da_ref[...] = dattn
    add_small(2, dattn)
    need(3)
    dctx_ref[...] = dot_nt(dattn, matrix_of(held, edges[3], edges[4])).astype(jnp.bfloat16)
    first, second, is_first = lane_halves()
    every_pair = [slice(pair * 2 * HD, (pair + 1) * 2 * HD) for pair in range(H // 2)]
    for sent in range(TILE // GROUP):
        rows = slice(sent * GROUP, (sent + 1) * GROUP)
        dcc = [both_heads(dctx_ref[rows, lanes], first, second) for lanes in every_pair]
        dprobs = jnp.concatenate(
            [dot_nt(v_ref[rows, lanes], wide) for lanes, wide in zip(every_pair, dcc)], axis=1
        )
        low = probs_ref[sent]
        probs = low.astype(jnp.float32)
        dscores = probs * (dprobs - jnp.sum(dprobs * probs, axis=0, keepdims=True))
        dscores = (dscores * HD ** (-0.5)).astype(jnp.bfloat16)
        dv_ref[rows, :] = jnp.concatenate(
            [dot_nn(low[:, lanes], wide) for lanes, wide in zip(every_pair, dcc)], axis=1
        ).astype(jnp.bfloat16)
        qq = [both_heads(q_ref[rows, lanes], first, second) for lanes in every_pair]
        dk_ref[rows, :] = jnp.concatenate(
            [dot_nn(dscores[:, lanes], wide) for lanes, wide in zip(every_pair, qq)], axis=1
        ).astype(jnp.bfloat16)
        mixed = [dot_tn(dscores[:, lanes], k_ref[rows, lanes]) for lanes in every_pair]
        dq_ref[rows, :] = jnp.concatenate(
            [jnp.where(is_first, m[:GROUP], m[GROUP:]) for m in mixed], axis=1
        ).astype(jnp.bfloat16)
    dx = dr1
    for m, (ref, r) in enumerate(((dq_ref, 0), (dk_ref, None), (dv_ref, 1))):
        need(m)
        rows = ref[...]
        if r is not None:
            add_small(r, rows)
        dx += dot_nt(rows, matrix_of(held, edges[m], edges[m + 1]))
    dx_ref[...] = dx.astype(jnp.bfloat16)


def run_backward(og, dc, small, saved, units, positions, edges):
    rows, width = og.shape
    count = rows // TILE
    sents = TILE // GROUP
    bf, f32 = jnp.bfloat16, jnp.float32
    _, q, k, v, probs, _, n1, rs1, _, _, slope, n2, rs2, _ = saved[:14]
    ins = [og, dc, small, q, k, v, probs, n1, rs1, slope, n2, rs2]
    in_specs = [tiles(a.shape) for a in ins]
    in_specs[1] = pl.BlockSpec((1, sents, width), lambda i, *_: (i, 0, 0))
    in_specs[2] = whole(small.shape)
    in_specs[6] = pl.BlockSpec((sents,) + probs.shape[1:], lambda i, *_: (i, 0, 0))
    outs = [((rows, width), bf)] * 2 + [((rows, FF), bf)] + [((rows, width), bf)] * 4 + [(small.shape, f32)]
    specs = [tiles(shape) for shape, _ in outs]
    specs[7] = whole(small.shape)
    return pl.pallas_call(
        functools.partial(backward_kernel, edges),
        name="layer_backward",
        grid_spec=pltpu.PrefetchScalarGridSpec(
            num_scalar_prefetch=1,
            grid=(count,),
            in_specs=in_specs + [pl.BlockSpec(memory_space=pl.ANY)],
            out_specs=specs,
            scratch_shapes=[
                pltpu.VMEM((TILE, width), f32),
                pltpu.VMEM((TILE, width), bf),
                pltpu.VMEM((edges[6],) + units.shape[1:], bf),
                pltpu.SemaphoreType.DMA((6,)),
            ],
        ),
        out_shape=[jax.ShapeDtypeStruct(shape, kind) for shape, kind in outs],
        compiler_params=pltpu.CompilerParams(vmem_limit_bytes=VMEM_MOST),
    )(positions, *ins, units)


def weight_grad_kernel(
    edges, pos_ref, x_hbm, ctx_hbm, du_hbm, act_hbm, dq_hbm, dk_hbm, dv_hbm, da_hbm, hb_hbm, df_hbm, out_hbm,
    x_v, ctx_v, du_v, act_v, right, staged, sems, out_sems,
):
    width = x_v.shape[1]
    unit_rows = out_hbm.shape[1]
    inner_rows = FF // width
    loads = [(act_hbm, act_v), (df_hbm, right.at[5]), (du_hbm, du_v), (hb_hbm, right.at[4]), (ctx_hbm, ctx_v),
             (da_hbm, right.at[3]), (x_hbm, x_v), (dq_hbm, right.at[0]), (dk_hbm, right.at[1]), (dv_hbm, right.at[2])]
    copies = [pltpu.make_async_copy(src, dst, sems.at[i]) for i, (src, dst) in enumerate(loads)]
    for copy in copies:
        copy.start()
    waited = set()
    per = width // unit_rows
    work = []
    for part in range(inner_rows):
        work.append((act_v, part, 5, edges[5] + part * per, (0, 1)))
    for part in range(inner_rows):
        work.append((du_v, part, 4, edges[4] + part * per, (2, 3)))
    work.append((ctx_v, 0, 3, edges[3], (4, 5)))
    work.append((x_v, 0, 0, edges[0], (6, 7)))
    work.append((x_v, 0, 1, edges[1], (6, 8)))
    work.append((x_v, 0, 2, edges[2], (6, 9)))
    for step, (left, part, m, unit, needs) in enumerate(work):
        slot = step % 2
        for n in needs:
            if n not in waited:
                copies[n].wait()
                waited.add(n)
        if step >= 2:
            pltpu.make_async_copy(out_hbm.at[pl.ds(0, per)], staged.at[slot], out_sems.at[slot]).wait()
        half = per // 2
        for piece in range(2):
            cols = slice(part * width + piece * half * unit_rows, part * width + (piece + 1) * half * unit_rows)
            block = dot_tn(left[:, cols], right[m]).astype(jnp.bfloat16)
            staged[slot, piece * half : (piece + 1) * half] = block.reshape(half, unit_rows, width)
        for n in range(per):
            pltpu.make_async_copy(staged.at[slot, n], out_hbm.at[pos_ref[unit + n]], out_sems.at[slot]).start()
    for slot in range(2):
        pltpu.make_async_copy(out_hbm.at[pl.ds(0, per)], staged.at[slot], out_sems.at[slot]).wait()


def run_weight_grads(x, saved, back, positions, edges, places, unit_rows):
    rows, width = x.shape
    bf = jnp.bfloat16
    ctx, hb, act = saved[5], saved[8], saved[9]
    _, df, du, da, dq, dk, dv, _ = back
    per = width // unit_rows
    anyw = pl.BlockSpec(memory_space=pl.ANY)
    return pl.pallas_call(
        functools.partial(weight_grad_kernel, edges),
        name="weight_grads",
        in_specs=[pl.BlockSpec(memory_space=pltpu.SMEM)] + [anyw] * 10,
        out_specs=anyw,
        scratch_shapes=[
            pltpu.VMEM((rows, width), bf), pltpu.VMEM((rows, width), bf), pltpu.VMEM((rows, FF), bf),
            pltpu.VMEM((rows, FF), bf), pltpu.VMEM((6, rows, width), bf),
            pltpu.VMEM((2, per, unit_rows, width), bf),
            pltpu.SemaphoreType.DMA((10,)), pltpu.SemaphoreType.DMA((2,)),
        ],
        out_shape=jax.ShapeDtypeStruct((places, unit_rows, width), bf),
        compiler_params=pltpu.CompilerParams(vmem_limit_bytes=VMEM_MOST),
    )(positions, x, ctx, du, act, dq, dk, dv, da, hb, df)


STEPS = 6
EARLY = 1
BAND = 16
HALF = 384


def step_units(edges):
    per = edges[1] - edges[0]
    firsts = [(edge + per * t, edge + per * (t + 1)) for edge in (edges[5], edges[4]) for t in (0, 2)]
    return firsts + [(edges[3], edges[0]), (edges[1], edges[2])]


def sum_places(edges):
    per = edges[1] - edges[0]
    table = [0] * edges[6]
    for t, firsts in enumerate(step_units(edges)):
        for m, first in enumerate(firsts):
            for k in range(per):
                table[first + k] = (k % 2) * (STEPS * per) + t * per + m * (per // 2) + k // 2
    return table


def backward_reduce_kernel(
    edges, tab_ref, scale_ref, small_ref, cls_ref, lang_row, rs1_ref, rs2_ref, og_hbm, n2_hbm, slope_hbm, act_hbm, hb_hbm, n1_hbm, ctx_hbm,
    q_hbm, k_hbm, v_hbm, x_hbm, probs_hbm, units_hbm,
    dx_hbm, own_out, small_out, loss_out, gscale_out,
    dh, nbuf, p0, p1, p2, p3, p4, p5, p6, p7, p8, wbuf, gbuf, c_in, xa, yb, ya, xb, ya_low, xb_low, zg, zd, zab, fbuf, a_out, a_in, x_in,
    gsm, t_acc, t_in, pooled, dlogits,
    l_sem, c_s, c_r, xa_s, xa_r, yb_s, yb_r, ya_s, ya_r, xb_s, xb_r, z_s, z_r, f_s, f_r, a_s, a_r, o_s, o_r,
    t_s, t_r, g_s, g_r, h_s, h_r, c_free,
):
    s, z, y, c = place()
    bf, f32 = jnp.bfloat16, jnp.float32
    rows_all, width = dh.shape
    count = rows_all // TILE
    inner_rows = FF // width
    per = edges[1] - edges[0]
    upper = gbuf.shape[5]
    unit_rows = 2 * upper
    slots = own_out.shape[0]
    sibling = (s, batch_of(z, y, 1 - c))
    across = (s, batch_of(z, 1 - y, c))
    other = (1 - s, batch_of(z, y, c))
    round_to = (sibling, across, other, (s, batch_of(z + 1 - 2 * (z % 2), y, c)), (s, batch_of((z + 2) % ZS, y, c)))

    barrier = pltpu.get_barrier_semaphore()

    def hello(target):
        pl.semaphore_signal(barrier, inc=1, device_id=target, device_id_type=MESH)

    hello(sibling)
    hello(other)
    turns = [(dz, dy) for dz in range(ZS) for dy in range(2) if dz or dy]
    for dz, dy in turns:
        hello((s, batch_of((z + dz) % ZS, (y + dy) % 2, c)))
    pl.semaphore_wait(barrier, 2 + len(turns))

    chunk = lambda ref, p: ref.at[:, pl.ds(p * width, width)]
    matrix = lambda first: units_hbm.at[pl.ds(first, per)]
    firsts = step_units(edges)
    acts, slopes = (p3, p5), (p4, p6, p3, p5)
    loads = {"og": (og_hbm, p0), "n2": (n2_hbm, nbuf), "hb": (hb_hbm, p2), "n1": (n1_hbm, nbuf), "probs": (probs_hbm, p0),
             "ctx": (ctx_hbm, p4), "q": (q_hbm, p6), "k": (k_hbm, p7), "v": (v_hbm, p8), "x": (x_hbm, p3)}
    for p in range(inner_rows):
        loads["act%d" % p] = (chunk(act_hbm, p), acts[p % 2])
        loads["slope%d" % p] = (chunk(slope_hbm, p), slopes[p])
        loads["wo%d" % p] = (matrix(edges[5] + p * per), wbuf.at[p % 2, 0])
        loads["wi%d" % p] = (matrix(edges[4] + p * per), wbuf.at[p % 2, 1])
    for t in (4, 5):
        for m in range(2):
            loads["w%d%d" % (t, m)] = (matrix(firsts[t][m]), wbuf.at[t % 2, m])
    copies = {
        name: pltpu.make_async_copy(src, dst, l_sem.at[n]) for n, (name, (src, dst)) in enumerate(loads.items())
    }

    def begin(*names):
        for name in names:
            copies[name].start()

    def ready(*names):
        for name in names:
            copies[name].wait()

    begin("og", "n2", "act0", "act1", "slope0", "wo0", "wi0", "hb", "slope1", "wo1", "wi1", "k", "v")

    row = lambda r: small_ref[r : r + 1, :]
    gsm[...] = jnp.zeros_like(gsm)

    def add_small(r, values):
        gsm[r : r + 1, :] += jnp.sum(values.astype(f32), axis=0, keepdims=True)

    def tile_rows(i):
        return pl.ds(pl.multiple_of(i * TILE, TILE), TILE)

    def weight(slot, m):
        return wbuf[slot, m].reshape(per * unit_rows, width)

    def remote(src, dst, send, recv, target):
        return pltpu.make_async_remote_copy(
            src_ref=src, dst_ref=dst, send_sem=send, recv_sem=recv, device_id=target, device_id_type=MESH
        )

    my_cols = pl.ds(pl.multiple_of(y * HALF, 128), HALF)
    its_cols = pl.ds(pl.multiple_of((1 - y) * HALF, 128), HALF)
    blocks = pl.ds(0, per // 2)
    both = pl.ds(0, 2)
    lines = pl.ds(0, upper)

    def band(zz):
        return pl.ds(pl.multiple_of(zz * BAND, BAND), BAND)

    def c_copy(t):
        return remote(gbuf.at[t, :, 1 - c], c_in.at[t % RING], c_s.at[t], c_r.at[t], sibling)

    def xa_copy(t):
        return remote(gbuf.at[t, 0, c, blocks, 1 - s], xa.at[t], xa_s.at[t], xa_r.at[t], other)

    def yb_copy(t):
        return remote(gbuf.at[t, 1, c, blocks, both, lines, its_cols], yb.at[t], yb_s.at[t], yb_r.at[t], across)

    def ya_view(t, cols):
        return gbuf.at[t, 0, c, blocks, s, band(z) if t < EARLY else lines, cols]

    def xb_view(t, ss):
        return gbuf.at[t, 1, c, blocks, ss, band(z) if t < EARLY else lines, my_cols]

    def ya_land(t):
        return ya_low.at[t] if t < EARLY else ya.at[t - EARLY]

    def xb_land(t):
        return xb_low.at[t] if t < EARLY else xb.at[t - EARLY]

    def ya_copy(t):
        return remote(ya_view(t, its_cols), ya_land(t), ya_s.at[t], ya_r.at[t], across)

    def xb_copy(t):
        return remote(xb_view(t, 1 - s), xb_land(t), xb_s.at[t], xb_r.at[t], other)

    def z_views(t, zz, dz):
        if t < EARLY:
            return [
                (gbuf.at[t, 0, c, blocks, s, band(zz)], zg.at[t, dz - 1]),
                (gbuf.at[t, 1, c, blocks, both, band(zz), my_cols], zd.at[t, dz - 1]),
            ]
        return [
            (gbuf.at[t, m, c, blocks, s, band(zz), my_cols], zab.at[t - EARLY, dz - 1, m]) for m in range(2)
        ]

    def z_copies(t, dz):
        zz = (z + dz) % ZS
        return [
            remote(view, land, z_s.at[n, t, dz - 1], z_r.at[n, t, dz - 1], (s, batch_of(zz, y, c)))
            for n, (view, land) in enumerate(z_views(t, zz, dz))
        ]

    def f_copy(t):
        mine = fbuf.at[pl.ds(c * (STEPS * per) + t * per, per)]
        return remote(mine, mine, f_s.at[t], f_r.at[t], sibling)

    def turn(r):
        return remote(t_acc.at[r], t_in.at[r], t_s.at[r], t_r.at[r], round_to[r])

    def add(view, got):
        @pl.loop(0, per // 2)
        def _(k):
            view.at[k][...] = (view.at[k][...].astype(f32) + got.at[k][...].astype(f32)).astype(bf)

    def ev_c_send(t):
        if t >= RING:
            pl.semaphore_wait(c_free, 1)
        c_copy(t).start()

    def ev_c_wait(t):
        c_copy(t).wait_recv()
        add(gbuf.at[t, 0, c], c_in.at[t % RING, 0])
        xa_copy(t).start()
        add(gbuf.at[t, 1, c], c_in.at[t % RING, 1])
        if t + RING < STEPS:
            pl.semaphore_signal(c_free, inc=1, device_id=sibling, device_id_type=MESH)
        yb_copy(t).start()

    def ev_first(t):
        xa_copy(t).wait_recv()
        add(gbuf.at[t, 0, c, blocks, s], xa.at[t])
        if t >= EARLY:
            ya_copy(t).start()
        yb_copy(t).wait_recv()
        add(gbuf.at[t, 1, c, blocks, both, lines, my_cols], yb.at[t])
        if t >= EARLY:
            xb_copy(t).start()

    def ev_second_start(t):
        ya_copy(t).start()
        xb_copy(t).start()

    def ev_second(t):
        ya_copy(t).wait_recv()
        add(ya_view(t, my_cols), ya_land(t))
        xb_copy(t).wait_recv()
        add(xb_view(t, s), xb_land(t))

    def ev_z_send(t):
        for dz in (2, 1, 3):
            for copy in z_copies(t, dz):
                copy.start()

    def ev_z_take(t):
        for dz in (1, 3, 2):
            for copy, (view, land) in zip(z_copies(t, dz), z_views(t, z, dz)):
                copy.wait_recv()
                add(view, land)

    def ev_fin(t):
        for m in range(2):

            @pl.loop(0, per // 2)
            def _(k):
                at = c * (STEPS * per) + t * per + m * (per // 2) + k
                fbuf[at] = gbuf[t, m, c, k, s, band(z), my_cols]

        f_copy(t).start()

    def ev_turn_start(r):
        if r == 0:
            t_acc[0] = gsm[...]
        turn(r).start()

    def ev_turn_wait(r):
        turn(r).wait()
        t_acc[r + 1] = t_acc[r] + t_in[r]

    sents = cls_ref.shape[0]
    pairs = lang_row.shape[1]
    cls = cls_ref[...]
    root = lax.rsqrt(jnp.sum(cls * cls, axis=-1, keepdims=True) + NORM_EPS)
    unit = cls * root
    pooled[s, z, y, c] = unit.astype(bf)
    all_z, low_z, high_z = pl.ds(0, ZS), pl.ds(0, ZS // 2), pl.ds(ZS // 2, ZS // 2)

    def g_copy(dz):
        mine = pooled.at[s, z, y, c]
        return remote(mine, mine, g_s.at[dz - 1], g_r.at[dz - 1], (s, batch_of((z + dz) % ZS, y, c)))

    def h_copy(n, view, target):
        return remote(view, view, h_s.at[n], h_r.at[n], target)

    swaps = [
        h_copy(0, pooled.at[s, all_z, y, c], across),
        h_copy(1, pooled.at[s, all_z, y, c], other),
        h_copy(2, pooled.at[1 - s, low_z, y, c], across),
        h_copy(3, pooled.at[s, high_z, 1 - y, c], other),
        h_copy(4, pooled.at[s, all_z, y, c], sibling),
        h_copy(5, pooled.at[s, all_z, 1 - y, c], sibling),
        h_copy(6, pooled.at[1 - s, all_z, y, c], sibling),
        h_copy(7, pooled.at[1 - s, all_z, 1 - y, c], sibling),
    ]
    for dz in (2, 1, 3):
        g_copy(dz).start()

    def tile_start(i):
        rows = slice(i * TILE, (i + 1) * TILE)
        later = lax.broadcasted_iota(jnp.int32, (TILE, 1), 0) % GROUP != 0
        dy = jnp.where(later, p0[rows, :].astype(f32), 0.0)
        n2 = nbuf[rows, :]
        add_small(6 + inner_rows, dy * n2)
        add_small(7 + inner_rows, dy)
        dr2 = norm_back(dy, n2, rs2_ref[rows, :], row(6 + inner_rows))
        dh[rows, :] = dr2
        df = dr2.astype(bf)
        p1[rows, :] = df
        add_small(3 + inner_rows, df)

    def rank_rows():
        scale = scale_ref[0]
        mix = (((1,), (0,)), ((), ()))
        e_zero = pooled[0].reshape(pairs, width)
        e_one = pooled[1].reshape(pairs, width)
        cosines = dot_nt(e_zero, e_one)
        own = lax.broadcasted_iota(jnp.int32, (pairs, pairs), 0) == lax.broadcasted_iota(jnp.int32, (pairs, pairs), 1)
        langs = jnp.broadcast_to(lang_row[...].astype(f32), (pairs, pairs))
        same = langs == langs.T
        diagonal = jnp.where(own, 1.0, 0.0)
        shifted = cosines - MARGIN * diagonal
        logits = scale * shifted
        masked = jnp.where(same, logits, -1e30)
        twice = -2.0 * diagonal
        total = -2.0 * jnp.sum(logits * diagonal)
        for axis in range(2):
            top = jnp.max(masked, axis=axis, keepdims=True)
            grown = jnp.where(same, jnp.exp(masked - top), 0.0)
            summed = jnp.sum(grown, axis=axis, keepdims=True)
            twice += grown / summed
            total += jnp.sum(jnp.log(summed) + top)
        loss_out[0] = total
        gscale_out[0] = jnp.sum(twice * shifted)
        dlogits[0] = twice
        dlogits[1] = twice.T
        mine = dlogits[s, pl.ds(pl.multiple_of(batch_of(z, y, c) * sents, 16), sents), :]
        partners = pooled[1 - s].reshape(pairs, width)
        upper_part = mine.astype(bf)
        rest = (mine - upper_part.astype(f32)).astype(bf)
        de = lax.dot_general(upper_part, partners, mix, preferred_element_type=f32)
        de += lax.dot_general(rest, partners, mix, preferred_element_type=f32)
        de = scale * de
        return (de - unit * jnp.sum(unit * de, axis=-1, keepdims=True)) * root

    def sec_start():
        ready("og", "n2")
        tile_start(0)
        for dz in range(1, ZS):
            back = pooled.at[s, (z - dz) % ZS, y, c]
            remote(back, back, g_s.at[dz - 1], g_r.at[dz - 1], other).wait_recv()
        for n in (0, 1, 4):
            swaps[n].start()
        tile_start(1)
        tile_start(2)
        swaps[0].wait_recv()
        swaps[1].wait_recv()
        for n in (2, 3, 5, 6):
            swaps[n].start()
        for i in range(3, count):
            tile_start(i)
        swaps[2].wait_recv()
        swaps[3].wait_recv()
        swaps[7].start()
        for n in (4, 5, 6, 7):
            swaps[n].wait_recv()
        dc = rank_rows()
        head = [pl.ds(sent * GROUP, 1) for sent in range(sents)]
        og = jnp.concatenate([p0[sent * GROUP : sent * GROUP + 16, :].astype(f32)[:1] for sent in range(sents)], axis=0)
        n2 = jnp.concatenate([nbuf[at, :] for at in head], axis=0)
        rs2 = jnp.concatenate([rs2_ref[at, :] for at in head], axis=0)
        dy = og + dc
        add_small(6 + inner_rows, dy * n2)
        add_small(7 + inner_rows, dy)
        dr2 = norm_back(dy, n2, rs2, row(6 + inner_rows))
        add_small(3 + inner_rows, dr2.astype(bf))
        top = lax.broadcasted_iota(jnp.int32, (16, 1), 0) == 0
        for sent in range(sents):
            mine = dr2[sent : sent + 1, :]
            dh[head[sent], :] = mine
            block = slice(sent * GROUP, sent * GROUP + 16)
            p1[block, :] = jnp.where(top, mine, p1[block, :].astype(f32)).astype(bf)
        begin("n1", "probs")

    def store_grads(t, m, lhs, rhs):
        @pl.loop(0, 2)
        def _(piece):
            half = (per // 2) * unit_rows
            cols = pl.ds(pl.multiple_of(piece * half, 128), half)
            block = dot_tn(lhs[:, cols], rhs[...]).astype(bf)
            for i in range(per // 2):
                part = block[i * unit_rows : (i + 1) * unit_rows].reshape(2, upper, width)

                @pl.when(piece == 0)
                def _():
                    gbuf[t, m, i % 2, i // 2] = part

                @pl.when(piece == 1)
                def _():
                    k = per // 2 + i
                    gbuf[t, m, k % 2, k // 2] = part

    def sec_inner(p):
        def run():
            ready("slope%d" % p, "wo%d" % p, "wi%d" % p)
            slope = slopes[p]

            @pl.loop(0, count)
            def _(i):
                rows = tile_rows(i)
                da = dot_nt(p1[rows, :], weight(p % 2, 0))
                du = (da * slope[rows, :].astype(f32)).astype(bf)
                slope[rows, :] = du
                add_small(3 + p, du)
                dh[rows, :] += dot_nn(du, weight(p % 2, 1))

            if p == 2:
                begin("w40", "w41")
            if p == 3:
                begin("w50", "w51")
            if p + 2 < inner_rows:
                begin("wo%d" % (p + 2), "wi%d" % (p + 2))

        return run

    def sec_outer_grad(p):
        def run():
            ready("act%d" % p)
            store_grads(p // 2, p % 2, acts[p % 2], p1)
            if p + 2 < inner_rows:
                begin("act%d" % (p + 2))
            else:
                begin("slope%d" % p)

        return run

    def sec_inner_grad(p):
        def run():
            if p == 0:
                ready("hb")
            store_grads(2 + p // 2, p % 2, slopes[p], p2)
            if p < 3:
                begin(("ctx", "q", "x")[p])

        return run

    def sec_norm():
        ready("n1", "w40", "w41")

        @pl.loop(0, count)
        def _(i):
            rows = tile_rows(i)
            dh1 = dh[rows, :]
            n1 = nbuf[rows, :]
            add_small(4 + inner_rows, dh1 * n1)
            add_small(5 + inner_rows, dh1)
            dr1 = norm_back(dh1, n1, rs1_ref[rows, :], row(4 + inner_rows))
            dh[rows, :] = dr1
            dattn = dr1.astype(bf)
            p1[rows, :] = dattn
            add_small(2, dattn)
            p5[rows, :] = dot_nt(dattn, weight(0, 0)).astype(bf)

    def sec_out_grad():
        ready("ctx")
        store_grads(4, 0, p4, p1)

    first, second, is_first = lane_halves()
    every_pair = [slice(pair * 2 * HD, (pair + 1) * 2 * HD) for pair in range(H // 2)]

    def sec_heads(part):
        def run():
            if part == 0:
                ready("probs", "q", "k", "v")
            amount = rows_all // GROUP // 2

            @pl.loop(part * amount, (part + 1) * amount)
            def _(sent):
                rows = pl.ds(pl.multiple_of(sent * GROUP, GROUP), GROUP)
                dctx, q, k, v, low = p5[rows, :], p6[rows, :], p7[rows, :], p8[rows, :], p0[rows, :]
                dcc = [both_heads(dctx[:, lanes], first, second) for lanes in every_pair]
                dprobs = jnp.concatenate([dot_nt(v[:, lanes], wide) for lanes, wide in zip(every_pair, dcc)], axis=1)
                probs = low.astype(f32)
                dscores = probs * (dprobs - jnp.sum(dprobs * probs, axis=0, keepdims=True))
                dscores = (dscores * HD ** (-0.5)).astype(bf)
                dv = jnp.concatenate(
                    [dot_nn(low[:, lanes], wide) for lanes, wide in zip(every_pair, dcc)], axis=1
                ).astype(bf)
                p4[rows, :] = dv
                add_small(1, dv)
                qq = [both_heads(q[:, lanes], first, second) for lanes in every_pair]
                p2[rows, :] = jnp.concatenate(
                    [dot_nn(dscores[:, lanes], wide) for lanes, wide in zip(every_pair, qq)], axis=1
                ).astype(bf)
                mixed = [dot_tn(dscores[:, lanes], k[:, lanes]) for lanes in every_pair]
                dq = jnp.concatenate([jnp.where(is_first, m[:GROUP], m[GROUP:]) for m in mixed], axis=1).astype(bf)
                p1[rows, :] = dq
                add_small(0, dq)

        return run

    def sec_query_grad():
        ready("x")
        store_grads(4, 1, p3, p1)

    def sec_key_grad():
        store_grads(5, 0, p3, p2)

    def sec_value_grad():
        store_grads(5, 1, p3, p4)

    def sec_back(part):
        def run():
            if part == 0:
                ready("w50", "w51")

            @pl.loop(part * (count // 2), (part + 1) * (count // 2))
            def _(i):
                rows = tile_rows(i)
                dx = dh[rows, :] + dot_nt(p1[rows, :], weight(0, 1))
                dx += dot_nt(p2[rows, :], weight(1, 0)) + dot_nt(p4[rows, :], weight(1, 1))
                p6[rows, :] = dx.astype(bf)

        return run

    sections = [sec_start] + [sec_outer_grad(p) for p in range(inner_rows)]
    for p in range(inner_rows):
        sections += [sec_inner(p), sec_inner_grad(p)]
    sections += [sec_norm, sec_out_grad, sec_heads(0), sec_heads(1), sec_query_grad, sec_key_grad, sec_value_grad]
    sections += [sec_back(0), sec_back(1)]
    done = [2, 4, 8, 12, 17, 19]
    events = {}

    def at_tick(tick, order, action):
        events.setdefault(tick, []).append((order, action))

    for t in range(STEPS):
        at_tick(done[t], 0, functools.partial(ev_c_send, t))
        at_tick(PLACES[t][0], 1, functools.partial(ev_c_wait, t))
        at_tick(PLACES[t][1], 2, functools.partial(ev_first, t))
        if t < EARLY:
            at_tick(PLACES[t][1], 2.5, functools.partial(ev_z_send, t))
            at_tick(PLACES[t][2], 3, functools.partial(ev_z_take, t))
            at_tick(PLACES[t][2], 3.5, functools.partial(ev_second_start, t))
            at_tick(PLACES[t][3], 4, functools.partial(ev_second, t))
        else:
            at_tick(PLACES[t][2], 3, functools.partial(ev_second, t))
            at_tick(PLACES[t][2], 3.5, functools.partial(ev_z_send, t))
            at_tick(PLACES[t][3], 4, functools.partial(ev_z_take, t))
        at_tick(PLACES[t][3], 5, functools.partial(ev_fin, t))
    for r in range(5):
        at_tick(16 + r, 10, functools.partial(ev_turn_start, r))
        at_tick(17 + r, -1, functools.partial(ev_turn_wait, r))
    for tick in range(max(max(events) + 1, len(sections))):
        if tick < len(sections):
            sections[tick]()
        if tick == len(sections) - 1:
            dx_copy = pltpu.make_async_copy(p6, dx_hbm, l_sem.at[len(loads)])
            dx_copy.start()
        for _, action in sorted(events.get(tick, []), key=lambda item: item[0]):
            action()
    small_out[...] = t_acc[5]
    for t in range(STEPS):
        its = fbuf.at[pl.ds((1 - c) * (STEPS * per) + t * per, per)]
        remote(its, its, f_s.at[t], f_r.at[t], sibling).wait_recv()

    def a_copy(zz, yy):
        return remote(a_out.at[zz, yy], a_in.at[z, y], a_s.at[zz, yy], a_r.at[z, y], (s, batch_of(zz, yy, c)))

    def o_copy(zz, yy):
        return remote(a_in.at[zz, yy], x_in.at[zz, yy], o_s.at[zz, yy], o_r.at[zz, yy], other)

    for dz, dy in turns:
        zz, yy = (z + dz) % ZS, (y + dy) % 2
        for j in range(slots):
            a_out[zz, yy, j] = fbuf[tab_ref[batch_of(zz, yy, c) * slots + j]]
        a_copy(zz, yy).start()
    for j in range(slots):
        a_in[z, y, j] = fbuf[tab_ref[batch_of(z, y, c) * slots + j]]
    o_copy(z, y).start()

    def put(zz, yy, ss, got):
        rows = pl.ds(pl.multiple_of(ss * upper + zz * BAND, BAND), BAND)
        cols = pl.ds(pl.multiple_of(yy * HALF, 128), HALF)
        for j in range(slots):
            own_out[j, rows, cols] = got[zz, yy, j]

    put(z, y, s, a_in)
    for dz, dy in turns:
        zz, yy = (z + dz) % ZS, (y + dy) % 2
        remote(a_in.at[zz, yy], a_in.at[zz, yy], a_s.at[zz, yy], a_r.at[zz, yy], other).wait_recv()
        o_copy(zz, yy).start()
        put(zz, yy, s, a_in)
    for dz, dy in [(0, 0)] + turns:
        zz, yy = (z + dz) % ZS, (y + dy) % 2
        o_copy(zz, yy).wait_recv()
        put(zz, yy, 1 - s, x_in)
    for t in range(STEPS):
        for copy in (c_copy, xa_copy, yb_copy, ya_copy, xb_copy, f_copy):
            copy(t).wait_send()

        for dz in range(1, ZS):
            for copy in z_copies(t, dz):
                copy.wait_send()

    for dz in range(1, ZS):
        g_copy(dz).wait_send()
    for swap in swaps:
        swap.wait_send()
    for dz, dy in turns:
        a_copy((z + dz) % ZS, (y + dy) % 2).wait_send()
    for dz, dy in [(0, 0)] + turns:
        o_copy((z + dz) % ZS, (y + dy) % 2).wait_send()
    dx_copy.wait()


RING = 3
PLACES = ((5, 12, 18, 22), (8, 12, 15, 20), (10, 14, 18, 24), (15, 19, 22, 26), (19, 22, 25, 26), (24, 26, 32, 42))


def run_backward_reduce(og, cls, scale, langs, small, saved, x, units, table, edges, slots):
    rows, width = og.shape
    bf, f32 = jnp.bfloat16, jnp.float32
    _, q, k, v, probs, ctx, n1, rs1, hb, act, slope, n2, rs2, _ = saved[:14]
    unit_rows = units.shape[1]
    per = edges[1] - edges[0]
    half = per // 2
    pairs = langs.shape[0]
    dma = pltpu.SemaphoreType.DMA
    vm = pltpu.VMEM
    vmem = pl.BlockSpec(memory_space=pltpu.VMEM)
    anyw = pl.BlockSpec(memory_space=pl.ANY)
    upper = unit_rows // 2
    return pl.pallas_call(
        functools.partial(backward_reduce_kernel, edges),
        name="backward_reduce",
        out_shape=[
            jax.ShapeDtypeStruct((rows, width), bf),
            jax.ShapeDtypeStruct((slots, unit_rows, width), bf),
            jax.ShapeDtypeStruct(small.shape, f32),
            jax.ShapeDtypeStruct((1,), f32),
            jax.ShapeDtypeStruct((1,), f32),
        ],
        in_specs=[pl.BlockSpec(memory_space=pltpu.SMEM)] * 2 + [vmem] * 5 + [anyw] * 13,
        out_specs=[anyw, vmem, vmem] + [pl.BlockSpec(memory_space=pltpu.SMEM)] * 2,
        scratch_shapes=[vm((rows, width), f32)] * 2
        + [vm((rows, width), bf)] * 9
        + [
            vm((2, 2, per, unit_rows, width), bf),
            vm((STEPS, 2, 2, half, 2, upper, width), bf),
            vm((RING, 2, half, 2, upper, width), bf),
            vm((STEPS, half, upper, width), bf),
            vm((STEPS, half, 2, upper, HALF), bf),
            vm((STEPS - EARLY, half, upper, HALF), bf),
            vm((STEPS - EARLY, half, upper, HALF), bf),
            vm((EARLY, half, BAND, HALF), bf),
            vm((EARLY, half, BAND, HALF), bf),
            vm((EARLY, ZS - 1, half, BAND, width), bf),
            vm((EARLY, ZS - 1, half, 2, BAND, HALF), bf),
            vm((STEPS - EARLY, ZS - 1, 2, half, BAND, HALF), bf),
            vm((2 * STEPS * per, BAND, HALF), bf),
            vm((ZS, 2, slots, BAND, HALF), bf),
            vm((ZS, 2, slots, BAND, HALF), bf),
            vm((ZS, 2, slots, BAND, HALF), bf),
            vm(small.shape, f32),
            vm((6,) + small.shape, f32),
            vm((5,) + small.shape, f32),
            vm((2, ZS, 2, 2) + cls.shape, bf),
            vm((2, pairs, pairs), f32),
        ]
        + [dma((32,))]
        + [dma((STEPS,))] * 10
        + [dma((2, STEPS, ZS - 1))] * 2
        + [dma((STEPS,))] * 2
        + [dma((ZS, 2))] * 4
        + [dma((5,))] * 2
        + [dma((ZS - 1,))] * 2
        + [dma((8,))] * 2
        + [pltpu.SemaphoreType.REGULAR],
        compiler_params=pltpu.CompilerParams(collective_id=3, has_side_effects=True, vmem_limit_bytes=63 << 20),
    )(table, scale, small, cls, langs.reshape(1, pairs), rs1, rs2, og, n2, slope, act, hb, n1, ctx, q, k, v, x, probs.reshape(rows, width), units)


def unit_positions(owner_list, slot_count):
    unit_total = owner_list.shape[0]
    same_owner = owner_list[:, None] == owner_list[None, :]
    ordinal = jnp.arange(unit_total, dtype=jnp.int32)
    earlier = ordinal[None, :] < ordinal[:, None]
    slot_number = jnp.sum(jnp.where(same_owner & earlier, 1, 0), axis=1).astype(jnp.int32)
    return owner_list * slot_count + slot_number


def adamw(weight_in, gradient, moment_one, moment_two, rate_value, decay_value, fix_one, fix_two):
    new_one = BETA_ONE * moment_one + (1.0 - BETA_ONE) * gradient
    new_two = BETA_TWO * moment_two + (1.0 - BETA_TWO) * gradient * gradient
    stepped = new_one * (1.0 / fix_one) / (jnp.sqrt(new_two * (1.0 / fix_two)) + ADAM_EPS)
    return (weight_in - rate_value * (stepped + decay_value * weight_in), new_one, new_two)


def adamw_kernel(
    fixes, mean_by, filled_ref, weight_hbm, grad_hbm, first_hbm, second_hbm, small_ref, small_grad, small_one, small_two,
    scale_ref, scale_grad, scale_one, scale_two, loss_ref, pass_hbm,
    new_hbm, one_hbm, two_hbm, low_hbm, new_small, new_small_one, new_small_two, new_scale, new_scale_one, new_scale_two,
    new_loss, passed_hbm,
    weight_v, grad_v, first_v, second_v, low_v, pass_v, in_sem, out_sem, pass_sem,
):
    slots = weight_v.shape[0]

    def copy(src, dst, sem):
        return pltpu.make_async_copy(src, dst, sem)

    ins = [
        [
            copy(hbm.at[j], held.at[j], in_sem.at[n, j])
            for n, (hbm, held) in enumerate(
                ((weight_hbm, weight_v), (grad_hbm, grad_v), (first_hbm, first_v), (second_hbm, second_v))
            )
        ]
        for j in range(slots)
    ]
    outs = [
        [
            copy(held.at[j], hbm.at[j], out_sem.at[n, j])
            for n, (hbm, held) in enumerate(
                ((new_hbm, weight_v), (one_hbm, first_v), (two_hbm, second_v), (low_hbm, low_v))
            )
        ]
        for j in range(slots)
    ]
    for group in ins:
        for item in group:
            item.start()
    pass_in, pass_out = copy(pass_hbm, pass_v, pass_sem.at[0]), copy(pass_v, passed_hbm, pass_sem.at[1])
    pass_in.start()
    new_small[...], new_small_one[...], new_small_two[...] = adamw(
        small_ref[...], small_grad[...], small_one[...], small_two[...], RATE_SMALL, 0.0, *fixes
    )
    spread = lambda ref: jnp.full((8, 128), ref[0], dtype=jnp.float32)
    turned = adamw(spread(scale_ref), spread(scale_grad), spread(scale_one), spread(scale_two), RATE_SCALE, 0.0, *fixes)
    for ref, value in zip((new_scale, new_scale_one, new_scale_two), turned):
        ref[0] = jnp.max(value)
    new_loss[0] = loss_ref[0] * mean_by
    for j in range(slots):
        for item in ins[j]:
            item.wait()
        weight, first, second = weight_v[j], first_v[j], second_v[j]
        moved = adamw(weight, grad_v[j].astype(jnp.float32), first, second, RATE_UNITS, DECAY, *fixes)
        used = filled_ref[j] > 0
        new = jnp.where(used, moved[0], weight)
        weight_v[j] = new
        first_v[j] = jnp.where(used, moved[1], first)
        second_v[j] = jnp.where(used, moved[2], second)
        low_v[j] = new.astype(jnp.bfloat16)
        for item in outs[j]:
            item.start()
        if j == 0:
            pass_in.wait()
            pass_out.start()
    for group in outs:
        for item in group:
            item.wait()
    pass_out.wait()


def run_adamw(units, small, scale, loss, filled, fixes, mean_by, passed):
    weight, gradient = units[:2]
    f32, bf = jnp.float32, jnp.bfloat16
    slots = weight.shape[0]
    anyw = pl.BlockSpec(memory_space=pl.ANY)
    flat = pl.BlockSpec(memory_space=pltpu.VMEM)
    single = pl.BlockSpec(memory_space=pltpu.SMEM)
    outs = [(weight.shape, f32)] * 3 + [(weight.shape, bf)] + [(small[0].shape, f32)] * 3 + [((1,), f32)] * 4
    outs += [(passed.shape, passed.dtype)]
    dma = pltpu.SemaphoreType.DMA
    return pl.pallas_call(
        functools.partial(adamw_kernel, fixes, mean_by),
        name="adamw_all",
        in_specs=[single] + [anyw] * 4 + [flat] * 4 + [single] * 5 + [anyw],
        out_specs=[anyw] * 4 + [flat] * 3 + [single] * 4 + [anyw],
        scratch_shapes=[
            pltpu.VMEM(weight.shape, f32), pltpu.VMEM(weight.shape, gradient.dtype), pltpu.VMEM(weight.shape, f32),
            pltpu.VMEM(weight.shape, f32), pltpu.VMEM(weight.shape, bf), pltpu.VMEM(passed.shape, passed.dtype),
            dma((4, slots)), dma((4, slots)), dma((2,)),
        ],
        out_shape=[jax.ShapeDtypeStruct(shape, kind) for shape, kind in outs],
        compiler_params=pltpu.CompilerParams(vmem_limit_bytes=VMEM_MOST),
    )(filled, *units, *small, *scale, loss, passed)


def any_size_units(own, positions, owners):
    slots, rows, width = own.shape
    table = jnp.arange(owners * slots, dtype=jnp.int32)[:, None] == positions[None, :]
    bands = lax.all_to_all(
        own.transpose(1, 0, 2).astype(jnp.bfloat16), "batch", split_axis=0, concat_axis=1, tiled=True
    )
    ordered = jnp.einsum(
        "rpd,pu->rud", bands, table.astype(jnp.bfloat16), preferred_element_type=jnp.float32
    ).astype(jnp.bfloat16)
    return lax.all_gather(ordered, "batch", axis=0, tiled=True).transpose(1, 0, 2)


def any_size_sums(grads, positions, owners, slots):
    table = jnp.arange(owners * slots, dtype=jnp.int32)[:, None] == positions[None, :]
    pieces = lax.psum_scatter(grads.transpose(1, 0, 2).astype(jnp.float32), "batch", scatter_dimension=0, tiled=True)
    summed = lax.psum(pieces.astype(jnp.bfloat16), "stream").astype(jnp.float32)
    send_rows = jnp.einsum("rud,pu->rpd", summed, table.astype(jnp.float32), precision=HIGHEST)
    owned = lax.all_to_all(send_rows.astype(jnp.bfloat16), "batch", split_axis=1, concat_axis=0, tiled=True)
    return owned.astype(jnp.float32).transpose(1, 0, 2)


def any_size_rank(cls, scale, langs, owners):
    sents, width = cls.shape
    root = lax.rsqrt(jnp.sum(cls * cls, axis=-1, keepdims=True) + NORM_EPS)
    unit = cls * root
    every = lax.all_gather(unit.astype(jnp.bfloat16), "batch", axis=0, tiled=True)
    every = lax.all_gather(every, "stream", axis=0)
    cosines = jnp.dot(every[0], every[1].T, preferred_element_type=jnp.float32)
    diagonal = jnp.eye(cosines.shape[0], dtype=jnp.float32)
    same = langs[:, None] == langs[None, :]
    shifted = cosines - MARGIN * diagonal
    logits = scale[0] * shifted
    masked = jnp.where(same, logits, -1e30)
    both = -2.0 * diagonal
    total = -2.0 * jnp.sum(logits * diagonal)
    for axis in range(2):
        top = jnp.max(masked, axis=axis, keepdims=True)
        grown = jnp.where(same, jnp.exp(masked - top), 0.0)
        summed = jnp.sum(grown, axis=axis, keepdims=True)
        both += grown / summed
        total += jnp.sum(jnp.log(summed) + top)
    s = lax.axis_index("stream")
    turned = jnp.where(s == 0, both, both.T)
    rows = lax.dynamic_slice_in_dim(turned, lax.axis_index("batch") * sents, sents)
    partners = lax.dynamic_index_in_dim(every, 1 - s, keepdims=False).astype(jnp.float32)
    de = scale[0] * jnp.dot(rows, partners, precision=HIGHEST)
    dc = (de - unit * jnp.sum(unit * de, axis=-1, keepdims=True)) * root
    return dc, total, jnp.sum(both * shifted)


def per_device(
    tokens, out_grad, master, first_moment, second_moment, small_params, small_first, small_second, logit_scale,
    scale_first, scale_second, pair_lang, unit_owner,
):
    owners = lax.axis_size("batch")
    here_batch = lax.axis_index("batch")
    unit_rows, slot_count, width = master.shape
    query_blocks = width // unit_rows
    inner_blocks = FF // unit_rows
    edges = [query_blocks * n for n in range(5)]
    edges += [edges[4] + inner_blocks, edges[4] + 2 * inner_blocks]
    units_total = unit_owner.shape[0]
    positions = unit_positions(unit_owner, slot_count)
    on_block = owners == 4 * ZS
    own = master.transpose(1, 0, 2)
    if on_block:
        units, where, places = gather_units(own), positions, owners * slot_count
    else:
        units = any_size_units(own, positions, owners)
        where, places = jnp.arange(units_total, dtype=jnp.int32), units_total
    sentences, length = tokens.shape[1], tokens.shape[2]
    flat = tokens.reshape(sentences * length, width)
    saved = run_forward(flat, small_params, units, where, edges)
    cls = saved[13]
    grad_rows = out_grad.reshape(sentences * length, width)
    if on_block:
        slot_units = jnp.arange(places, dtype=jnp.int32)[:, None] == positions[None, :]
        sum_table = jnp.asarray(sum_places(edges), dtype=jnp.int32)
        table = jnp.sum(jnp.where(slot_units, sum_table[None, :], 0), axis=1, dtype=jnp.int32)
        d_tokens, owned_grad, small_total, loss_total, grad_scale = run_backward_reduce(
            grad_rows, cls, logit_scale, pair_lang, small_params, saved, flat, saved[14], table, edges,
            slot_count,
        )
    else:
        dc, loss_total, grad_scale = any_size_rank(cls, logit_scale, pair_lang, owners)
        loss_total, grad_scale = loss_total.reshape(1), grad_scale.reshape(1)
        back = run_backward(grad_rows, dc.reshape(-1, TILE // GROUP, width), small_params, saved, units, where, edges)
        grads = run_weight_grads(flat, saved, back, where, edges, places, unit_rows)
        d_tokens = back[0]
        owned_grad = any_size_sums(grads, positions, owners, slot_count)
        small_total = lax.psum(back[7], ("stream", "batch"))
    step_value = float(STEP)
    fix_one = 1.0 - BETA_ONE**step_value
    fix_two = 1.0 - BETA_TWO**step_value
    my_places = here_batch * slot_count + jnp.arange(slot_count, dtype=jnp.int32)
    filled = jnp.any(my_places[:, None] == positions[None, :], axis=1).astype(jnp.int32)
    (
        new_master, new_first, new_second, new_copy, new_small, new_small_first, new_small_second, scale_new, scale_one,
        scale_two, loss_out, d_tokens,
    ) = run_adamw(
        (own, owned_grad, first_moment.transpose(1, 0, 2), second_moment.transpose(1, 0, 2)),
        (small_params, small_total, small_first, small_second),
        (logit_scale, grad_scale, scale_first, scale_second),
        loss_total,
        filled,
        (fix_one, fix_two),
        1.0 / (2 * owners * sentences),
        d_tokens,
    )
    back_order = lambda a: a.transpose(1, 0, 2)
    return (
        saved[0].reshape(tokens.shape),
        d_tokens.reshape(tokens.shape),
        back_order(new_master),
        back_order(new_first),
        back_order(new_second),
        back_order(new_copy),
        new_small,
        new_small_first,
        new_small_second,
        scale_new,
        scale_one,
        scale_two,
        loss_out,
    )


def solution(mesh):
    rows = P("stream", "batch", None, None)
    blocks = P(None, "batch", None)
    return jax.shard_map(
        per_device,
        mesh=mesh,
        in_specs=(rows, rows, blocks, blocks, blocks) + (P(),) * 8,
        out_specs=(rows, rows, blocks, blocks, blocks, blocks) + (P(),) * 7,
        check_vma=False,
    )
```

```python
import functools

import jax
import jax.numpy as jnp
from jax import lax
from jax.experimental import pallas as pl
from jax.experimental.pallas import tpu as pltpu
from jax.sharding import PartitionSpec as P

H = 12
HD = 64
FF = 3072
STEP = 10
ZS = 4
UR_ROWS = 128
LEN_ROWS = 64
VMEM_MOST = 60 << 20
MESH = pl.DeviceIdType.MESH

HIGHEST = lax.Precision.HIGHEST
BETA_ONE = 0.9
BETA_TWO = 0.999
ADAM_EPS = 1e-06
RATE_UNITS = 0.02
RATE_SMALL = 0.1
RATE_SCALE = 2.0
DECAY = 0.01
MARGIN = 0.3
NORM_EPS = 1e-06


def place():
    s = lax.axis_index("stream")
    b = lax.axis_index("batch")
    return s, b // 4, (b // 2) % 2, b % 2


def batch_of(z, y, c):
    return (z * 2 + y) * 2 + c


def greet(s, z, y, c, others):
    barrier = pltpu.get_barrier_semaphore()

    def hello(target):
        pl.semaphore_signal(barrier, inc=1, device_id=target, device_id_type=MESH)

    hello((s, batch_of(z, y, 1 - c)))
    hello((s, batch_of(z, 1 - y, c)))
    hello((1 - s, batch_of(z, y, c)))
    if others == "line":
        for far in range(1, ZS):

            @pl.when(z >= far)
            def _():
                hello((s, batch_of(z - far, y, c)))

            @pl.when(z + far < ZS)
            def _():
                hello((s, batch_of(z + far, y, c)))

        pl.semaphore_wait(barrier, 3 + ZS - 1)
    else:

        @pl.when(z >= 1)
        def _():
            hello((s, batch_of(z - 1, y, c)))

        @pl.when(z + 1 < ZS)
        def _():
            hello((s, batch_of(z + 1, y, c)))

        pl.semaphore_wait(barrier, 3 + (z + 2) // 3 + (5 - z) // 3)


GR = 80
GX = UR_ROWS - GR


def gather_kernel(own_ref, out_ref, low, stage_sem, zl_s, zl_r, zr_s, zr_r, y_s, y_r, x_s, x_r, ca_s, ca_r, cb_s, cb_r):
    s, z, y, c = place()
    slots = own_ref.shape[0]
    steps = ZS * slots
    base = pl.multiple_of(s * GX, 16)
    only = pl.multiple_of(s * GR, 16)
    theirs = pl.multiple_of((1 - s) * GR, 16)

    def at(zz, yy, cc, j):
        return batch_of(zz, yy, cc) * slots + j

    greet(s, z, y, c, "next")

    def push(src, row, start, size, send, recv, target):
        return pltpu.make_async_remote_copy(
            src_ref=src,
            dst_ref=out_ref.at[row, pl.ds(start, size)],
            send_sem=send,
            recv_sem=recv,
            device_id=target,
            device_id_type=MESH,
        )

    left = (s, batch_of(z - 1, y, c))
    right = (s, batch_of(z + 1, y, c))
    across = (s, batch_of(z, 1 - y, c))
    other = (1 - s, batch_of(z, y, c))
    sibling = (s, batch_of(z, y, 1 - c))

    def to_left(src, zz, j):
        row = at(zz, y, c, j)
        return push(src(row), row, base, GR, zl_s.at[zz, j], zl_r.at[zz, j], left)

    def to_right(src, zz, j):
        row = at(zz, y, c, j)
        return push(src(row), row, base, GR, zr_s.at[zz, j], zr_r.at[zz, j], right)

    def to_across(src, zz, j):
        row = at(zz, y, c, j)
        return push(src(row), row, base, GR, y_s.at[zz, j], y_r.at[zz, j], across)

    def to_other(zz, yy, j):
        row = at(zz, yy, c, j)
        return push(out_ref.at[row, pl.ds(only, GX)], row, only, GX, x_s.at[zz, yy, j], x_r.at[zz, yy, j], other)

    def to_sibling(zz, yy, j):
        row = at(zz, yy, c, j)
        return push(out_ref.at[row, pl.ds(base, GR)], row, base, GR, ca_s.at[zz, yy, j], ca_r.at[zz, yy, j], sibling)

    def rest_to_sibling(zz, yy, j):
        row = at(zz, yy, c, j)
        return push(out_ref.at[row, pl.ds(theirs, GX)], row, theirs, GX, cb_s.at[zz, yy, j], cb_r.at[zz, yy, j], sibling)

    def landed(row):
        return out_ref.at[row, pl.ds(base, GR)]

    def from_left(zz, j):
        row = at(zz, y, c, j)
        return push(landed(row), row, base, GR, zr_s.at[zz, j], zr_r.at[zz, j], right)

    def arrived_line(zz, j, onward):
        onward.start()
        to_across(landed, zz, j).start()
        to_other(zz, y, j).start()
        to_sibling(zz, y, j).start()

    def stage(j):
        return pltpu.make_async_copy(low.at[j], out_ref.at[at(z, y, c, j)], stage_sem.at[j])

    for j in range(slots):
        low[j] = own_ref[j].astype(jnp.bfloat16)
        mine = lambda row: low.at[j, pl.ds(base, GR)]

        @pl.when(z > 0)
        def _():
            to_left(mine, z, j).start()

        @pl.when(z < ZS - 1)
        def _():
            to_right(mine, z, j).start()

        to_across(mine, z, j).start()
        row = at(z, y, c, j)
        push(low.at[j, pl.ds(base, GR)], row, base, GR, ca_s.at[z, y, j], ca_r.at[z, y, j], sibling).start()
        push(low.at[j, pl.ds(theirs, GX)], row, theirs, GX, cb_s.at[z, y, j], cb_r.at[z, y, j], sibling).start()
        stage(j).start()

    def line_step(t):
        d = t // slots
        j = t % slots

        @pl.when((d >= 1) & (z - d >= 0))
        def _():
            zz = z - d
            to_right(landed, zz, j).wait_recv()

            @pl.when(z < ZS - 1)
            def _():
                to_right(landed, zz, j).start()

            to_across(landed, zz, j).start()
            to_other(zz, y, j).start()
            to_sibling(zz, y, j).start()

        @pl.when((d >= 1) & (z + d < ZS))
        def _():
            zz = z + d
            to_left(landed, zz, j).wait_recv()

            @pl.when(z > 0)
            def _():
                to_left(landed, zz, j).start()

            to_across(landed, zz, j).start()
            to_other(zz, y, j).start()
            to_sibling(zz, y, j).start()

    def across_one(zz, j):
        row = at(zz, 1 - y, c, j)
        push(landed(row), row, base, GR, y_s.at[zz, j], y_r.at[zz, j], across).wait_recv()
        to_other(zz, 1 - y, j).start()
        to_sibling(zz, 1 - y, j).start()

    def across_step(t):
        d = t // slots
        j = t % slots

        @pl.when(z - d >= 0)
        def _():
            across_one(z - d, j)

        @pl.when((d >= 1) & (z + d < ZS))
        def _():
            across_one(z + d, j)

    def other_one(zz, yy, j):
        row = at(zz, yy, c, j)
        push(
            out_ref.at[row, pl.ds(theirs, GX)], row, theirs, GX, x_s.at[zz, yy, j], x_r.at[zz, yy, j], other
        ).wait_recv()
        rest_to_sibling(zz, yy, j).start()

    def other_step(t, yy, first):
        d = t // slots
        j = t % slots

        @pl.when((d >= first) & (z - d >= 0))
        def _():
            other_one(z - d, yy, j)

        @pl.when((d >= 1) & (z + d < ZS))
        def _():
            other_one(z + d, yy, j)

    @pl.loop(0, steps + 3)
    def _(t):
        @pl.when(t < steps)
        def _():
            line_step(t)

        @pl.when((t >= 1) & (t < steps + 1))
        def _():
            across_step(t - 1)

        @pl.when((t >= 2) & (t < steps + 2))
        def _():
            other_step(t - 2, y, 1)

        @pl.when(t >= 3)
        def _():
            other_step(t - 3, 1 - y, 0)

    for j in range(slots):
        stage(j).wait()

    @pl.loop(0, steps)
    def _(t):
        zz = t // slots
        j = t % slots

        @pl.when((z > 0) & (zz >= z))
        def _():
            to_left(landed, zz, j).wait_send()

        @pl.when((z < ZS - 1) & (zz <= z))
        def _():
            to_right(landed, zz, j).wait_send()

        to_across(landed, zz, j).wait_send()

        @pl.when(zz != z)
        def _():
            to_other(zz, y, j).wait_send()

        to_other(zz, 1 - y, j).wait_send()
        for yy in range(2):
            to_sibling(zz, yy, j).wait_send()
            rest_to_sibling(zz, yy, j).wait_send()
            row = at(zz, yy, 1 - c, j)
            push(landed(row), row, base, GR, ca_s.at[zz, yy, j], ca_r.at[zz, yy, j], sibling).wait_recv()
            push(
                out_ref.at[row, pl.ds(theirs, GX)], row, theirs, GX, cb_s.at[zz, yy, j], cb_r.at[zz, yy, j], sibling
            ).wait_recv()


def gather_units(own):
    slots, rows, width = own.shape
    owners = lax.axis_size("batch")
    line = [pltpu.SemaphoreType.DMA((ZS, slots))] * 6
    plane = [pltpu.SemaphoreType.DMA((ZS, 2, slots))] * 6
    return pl.pallas_call(
        gather_kernel,
        name="gather_units",
        out_shape=jax.ShapeDtypeStruct((owners * slots, rows, width), jnp.bfloat16),
        in_specs=[pl.BlockSpec(memory_space=pltpu.VMEM)],
        out_specs=pl.BlockSpec(memory_space=pl.ANY),
        scratch_shapes=[pltpu.VMEM((slots, rows, width), jnp.bfloat16), pltpu.SemaphoreType.DMA((slots,))] + line + plane,
        compiler_params=pltpu.CompilerParams(collective_id=0, has_side_effects=True, vmem_limit_bytes=VMEM_MOST),
    )(own)


TILE = 256
PART = 6
GROUP = LEN_ROWS


def dot_nn(a, b):
    return lax.dot_general(a, b, (((1,), (0,)), ((), ())), preferred_element_type=jnp.float32)


def dot_nt(a, b):
    return lax.dot_general(a, b, (((1,), (1,)), ((), ())), preferred_element_type=jnp.float32)


def dot_tn(a, b):
    return lax.dot_general(a, b, (((0,), (0,)), ((), ())), preferred_element_type=jnp.float32)


def gelu_parts(u):
    t = 1.0 / (1.0 + (0.3275911 * 0.7071067811865476) * jnp.abs(u))
    bell = jnp.exp(-0.5 * u * u)
    tail = t * (
        0.127414796 + t * (-0.142248368 + t * (0.7107068705 + t * (-0.7265760135 + t * 0.5307027145)))
    ) * bell
    phi_sum = jnp.where(u >= 0.0, 1.0 - tail, tail)
    return u * phi_sum, phi_sum + u * (0.3989422804014327 * bell)


def norm_parts(resid):
    centre = jnp.mean(resid, axis=-1, keepdims=True)
    centred = resid - centre
    rs = lax.rsqrt(jnp.mean(centred * centred, axis=-1, keepdims=True) + NORM_EPS)
    return centred * rs, rs


def norm_back(dy, unit, rs, gain):
    gd = gain * dy
    return rs * (gd - jnp.mean(gd, axis=-1, keepdims=True) - unit * jnp.mean(gd * unit, axis=-1, keepdims=True))


def lane_halves():
    lane = lax.broadcasted_iota(jnp.int32, (1, 2 * HD), 1)
    first = jnp.where(lane < HD, 1.0, 0.0)
    return first.astype(jnp.bfloat16), (1.0 - first).astype(jnp.bfloat16), lane < HD


def both_heads(rows, first, second):
    return jnp.concatenate([rows * first, rows * second], axis=0)


def fetch_all(pos_ref, units_hbm, held, sems, edges, order):
    for m in order:
        for u in range(edges[m], edges[m + 1]):
            pltpu.make_async_copy(units_hbm.at[pos_ref[u]], held.at[u], sems.at[m]).start()


def fetch_wait(units_hbm, held, sems, edges, m):
    lo, hi = edges[m], edges[m + 1]
    pltpu.make_async_copy(units_hbm.at[pl.ds(0, hi - lo)], held.at[pl.ds(lo, hi - lo)], sems.at[m]).wait()


def matrix_of(held, lo, hi):
    block = held[lo:hi]
    return block.reshape((hi - lo) * block.shape[1], block.shape[2])


def forward_kernel(
    edges, pos_ref, x_ref, small_ref, units_hbm,
    out_ref, q_ref, k_ref, v_ref, probs_ref, ctx_ref, n1_ref, rs1_ref, hb_ref, act_ref, slope_ref, n2_ref, rs2_ref,
    cls_ref, ordered_hbm, held, sems, keep_sem,
):
    first_tile = pl.program_id(0) == 0
    width = x_ref.shape[1]

    def need(m):
        @pl.when(first_tile)
        def _():
            fetch_wait(units_hbm, held, sems, edges, m)

    @pl.when(first_tile)
    def _():
        fetch_all(pos_ref, units_hbm, held, sems, edges, range(6))

    inner_rows = FF // width
    row = lambda r: small_ref[r : r + 1, :]
    x = x_ref[...]
    need(0)
    q = (dot_nn(x, matrix_of(held, edges[0], edges[1])) + row(0)).astype(jnp.bfloat16)
    q_ref[...] = q
    need(1)
    k = dot_nn(x, matrix_of(held, edges[1], edges[2])).astype(jnp.bfloat16)
    k_ref[...] = k
    need(2)
    v = (dot_nn(x, matrix_of(held, edges[2], edges[3])) + row(1)).astype(jnp.bfloat16)
    v_ref[...] = v
    first, second, is_first = lane_halves()
    every_pair = [slice(pair * 2 * HD, (pair + 1) * 2 * HD) for pair in range(H // 2)]
    every_sent = [slice(sent * GROUP, (sent + 1) * GROUP) for sent in range(TILE // GROUP)]
    for sent, rows in enumerate(every_sent):
        scores = jnp.concatenate(
            [dot_nt(k[rows, lanes], both_heads(q[rows, lanes], first, second)) for lanes in every_pair], axis=1
        )
        grown = jnp.exp((scores - jnp.max(scores, axis=0, keepdims=True)) * HD ** (-0.5))
        probs = (grown * (1.0 / jnp.sum(grown, axis=0, keepdims=True))).astype(jnp.bfloat16)
        probs_ref[sent] = probs
        mixed = [dot_tn(probs[:, lanes], v[rows, lanes]) for lanes in every_pair]
        ctx_ref[rows, :] = jnp.concatenate(
            [jnp.where(is_first, m[:GROUP], m[GROUP:]) for m in mixed], axis=1
        ).astype(jnp.bfloat16)
    need(3)
    attended = dot_nn(ctx_ref[...], matrix_of(held, edges[3], edges[4])) + row(2)
    n1, rs1 = norm_parts(x.astype(jnp.float32) + attended)
    n1_ref[...] = n1
    rs1_ref[...] = rs1
    h1 = n1 * row(4 + inner_rows) + row(5 + inner_rows)
    hb = h1.astype(jnp.bfloat16)
    hb_ref[...] = hb
    need(4)
    need(5)
    keep = pltpu.make_async_copy(held, ordered_hbm, keep_sem)

    @pl.when(first_tile)
    def _():
        keep.start()

    unit_rows = units_hbm.shape[1]
    total = h1 + row(3 + inner_rows)
    parts = FF // (PART * unit_rows)

    def inner_part(part):
        at = part * PART * unit_rows
        bias = small_ref[3 + at // width : 4 + at // width, at % width : at % width + PART * unit_rows]
        return dot_nt(hb, matrix_of(held, edges[4] + part * PART, edges[4] + (part + 1) * PART)) + bias

    ahead = inner_part(0)
    for part in range(parts):
        u = ahead
        if part + 1 < parts:
            ahead = inner_part(part + 1)
        cols = slice(part * PART * unit_rows, (part + 1) * PART * unit_rows)
        value, slope = gelu_parts(u)
        act = value.astype(jnp.bfloat16)
        act_ref[:, cols] = act
        slope_ref[:, cols] = slope.astype(jnp.bfloat16)
        total += dot_nn(act, matrix_of(held, edges[5] + part * PART, edges[5] + (part + 1) * PART))
    n2, rs2 = norm_parts(total)
    n2_ref[...] = n2
    rs2_ref[...] = rs2
    y = n2 * row(6 + inner_rows) + row(7 + inner_rows)
    out_ref[...] = y.astype(jnp.bfloat16)
    for sent in range(TILE // GROUP):
        here = pl.program_id(0) * (TILE // GROUP) + sent
        cls_ref[pl.ds(here, 1), :] = y[sent * GROUP : sent * GROUP + 1, :]

    @pl.when(pl.program_id(0) == pl.num_programs(0) - 1)
    def _():
        keep.wait()


def tiles(shape):
    rest = len(shape) - 1
    return pl.BlockSpec((TILE,) + tuple(shape[1:]), lambda i, *_: (i,) + (0,) * rest)


def whole(shape):
    return pl.BlockSpec(tuple(shape), lambda i, *_: (0,) * len(shape))


def run_forward(x, small, units, positions, edges):
    rows, width = x.shape
    count = rows // TILE
    sents = TILE // GROUP
    bf, f32 = jnp.bfloat16, jnp.float32
    probs_shape = (rows // GROUP, GROUP, width)
    outs = [
        ((rows, width), bf), ((rows, width), bf), ((rows, width), bf), ((rows, width), bf), (probs_shape, bf),
        ((rows, width), bf), ((rows, width), f32), ((rows, 1), f32), ((rows, width), bf), ((rows, FF), bf),
        ((rows, FF), bf), ((rows, width), f32), ((rows, 1), f32), ((rows // GROUP, width), f32),
        ((edges[6],) + units.shape[1:], bf),
    ]
    specs = [tiles(shape) for shape, _ in outs]
    specs[4] = pl.BlockSpec((sents,) + probs_shape[1:], lambda i, *_: (i, 0, 0))
    specs[13] = whole(outs[13][0])
    specs[14] = pl.BlockSpec(memory_space=pl.ANY)
    return pl.pallas_call(
        functools.partial(forward_kernel, edges),
        name="layer_forward",
        grid_spec=pltpu.PrefetchScalarGridSpec(
            num_scalar_prefetch=1,
            grid=(count,),
            in_specs=[tiles(x.shape), whole(small.shape), pl.BlockSpec(memory_space=pl.ANY)],
            out_specs=specs,
            scratch_shapes=[
                pltpu.VMEM((edges[6],) + units.shape[1:], bf), pltpu.SemaphoreType.DMA((6,)), pltpu.SemaphoreType.DMA,
            ],
        ),
        out_shape=[jax.ShapeDtypeStruct(shape, kind) for shape, kind in outs],
        compiler_params=pltpu.CompilerParams(vmem_limit_bytes=VMEM_MOST),
    )(positions, x, small, units)


def backward_kernel(
    edges, pos_ref, og_ref, dc_ref, small_ref, q_ref, k_ref, v_ref, probs_ref, n1_ref, rs1_ref, slope_ref, n2_ref,
    rs2_ref, units_hbm,
    dx_ref, df_ref, du_ref, da_ref, dq_ref, dk_ref, dv_ref, gsmall_ref, dy_ref, dctx_ref, held, sems,
):
    first_tile = pl.program_id(0) == 0
    width = og_ref.shape[1]
    inner_rows = FF // width

    def need(m):
        @pl.when(first_tile)
        def _():
            fetch_wait(units_hbm, held, sems, edges, m)

    @pl.when(first_tile)
    def _():
        fetch_all(pos_ref, units_hbm, held, sems, edges, (5, 4, 3, 0, 1, 2))
        gsmall_ref[...] = jnp.zeros_like(gsmall_ref)

    row = lambda r: small_ref[r : r + 1, :]

    def add_small(r, values):
        gsmall_ref[r : r + 1, :] += jnp.sum(values.astype(jnp.float32), axis=0, keepdims=True)

    dy_ref[...] = og_ref[...].astype(jnp.float32)
    for sent in range(TILE // GROUP):
        dy_ref[sent * GROUP : sent * GROUP + 1, :] += dc_ref[0, sent : sent + 1, :]
    dy = dy_ref[...]
    n2 = n2_ref[...]
    add_small(6 + inner_rows, dy * n2)
    add_small(7 + inner_rows, dy)
    dr2 = norm_back(dy, n2, rs2_ref[...], row(6 + inner_rows))
    df = dr2.astype(jnp.bfloat16)
    df_ref[...] = df
    add_small(3 + inner_rows, df)
    need(5)
    need(4)
    per = (edges[5] - edges[4]) // inner_rows
    dh1 = dr2
    for part in range(inner_rows):
        cols = slice(part * width, (part + 1) * width)
        da = dot_nt(df, matrix_of(held, edges[5] + part * per, edges[5] + (part + 1) * per))
        du = (da * slope_ref[:, cols].astype(jnp.float32)).astype(jnp.bfloat16)
        du_ref[:, cols] = du
        add_small(3 + part, du)
        dh1 += dot_nn(du, matrix_of(held, edges[4] + part * per, edges[4] + (part + 1) * per))
    n1 = n1_ref[...]
    add_small(4 + inner_rows, dh1 * n1)
    add_small(5 + inner_rows, dh1)
    dr1 = norm_back(dh1, n1, rs1_ref[...], row(4 + inner_rows))
    dattn = dr1.astype(jnp.bfloat16)
    da_ref[...] = dattn
    add_small(2, dattn)
    need(3)
    dctx_ref[...] = dot_nt(dattn, matrix_of(held, edges[3], edges[4])).astype(jnp.bfloat16)
    first, second, is_first = lane_halves()
    every_pair = [slice(pair * 2 * HD, (pair + 1) * 2 * HD) for pair in range(H // 2)]
    for sent in range(TILE // GROUP):
        rows = slice(sent * GROUP, (sent + 1) * GROUP)
        dcc = [both_heads(dctx_ref[rows, lanes], first, second) for lanes in every_pair]
        dprobs = jnp.concatenate(
            [dot_nt(v_ref[rows, lanes], wide) for lanes, wide in zip(every_pair, dcc)], axis=1
        )
        low = probs_ref[sent]
        probs = low.astype(jnp.float32)
        dscores = probs * (dprobs - jnp.sum(dprobs * probs, axis=0, keepdims=True))
        dscores = (dscores * HD ** (-0.5)).astype(jnp.bfloat16)
        dv_ref[rows, :] = jnp.concatenate(
            [dot_nn(low[:, lanes], wide) for lanes, wide in zip(every_pair, dcc)], axis=1
        ).astype(jnp.bfloat16)
        qq = [both_heads(q_ref[rows, lanes], first, second) for lanes in every_pair]
        dk_ref[rows, :] = jnp.concatenate(
            [dot_nn(dscores[:, lanes], wide) for lanes, wide in zip(every_pair, qq)], axis=1
        ).astype(jnp.bfloat16)
        mixed = [dot_tn(dscores[:, lanes], k_ref[rows, lanes]) for lanes in every_pair]
        dq_ref[rows, :] = jnp.concatenate(
            [jnp.where(is_first, m[:GROUP], m[GROUP:]) for m in mixed], axis=1
        ).astype(jnp.bfloat16)
    dx = dr1
    for m, (ref, r) in enumerate(((dq_ref, 0), (dk_ref, None), (dv_ref, 1))):
        need(m)
        rows = ref[...]
        if r is not None:
            add_small(r, rows)
        dx += dot_nt(rows, matrix_of(held, edges[m], edges[m + 1]))
    dx_ref[...] = dx.astype(jnp.bfloat16)


def run_backward(og, dc, small, saved, units, positions, edges):
    rows, width = og.shape
    count = rows // TILE
    sents = TILE // GROUP
    bf, f32 = jnp.bfloat16, jnp.float32
    _, q, k, v, probs, _, n1, rs1, _, _, slope, n2, rs2, _ = saved[:14]
    ins = [og, dc, small, q, k, v, probs, n1, rs1, slope, n2, rs2]
    in_specs = [tiles(a.shape) for a in ins]
    in_specs[1] = pl.BlockSpec((1, sents, width), lambda i, *_: (i, 0, 0))
    in_specs[2] = whole(small.shape)
    in_specs[6] = pl.BlockSpec((sents,) + probs.shape[1:], lambda i, *_: (i, 0, 0))
    outs = [((rows, width), bf)] * 2 + [((rows, FF), bf)] + [((rows, width), bf)] * 4 + [(small.shape, f32)]
    specs = [tiles(shape) for shape, _ in outs]
    specs[7] = whole(small.shape)
    return pl.pallas_call(
        functools.partial(backward_kernel, edges),
        name="layer_backward",
        grid_spec=pltpu.PrefetchScalarGridSpec(
            num_scalar_prefetch=1,
            grid=(count,),
            in_specs=in_specs + [pl.BlockSpec(memory_space=pl.ANY)],
            out_specs=specs,
            scratch_shapes=[
                pltpu.VMEM((TILE, width), f32),
                pltpu.VMEM((TILE, width), bf),
                pltpu.VMEM((edges[6],) + units.shape[1:], bf),
                pltpu.SemaphoreType.DMA((6,)),
            ],
        ),
        out_shape=[jax.ShapeDtypeStruct(shape, kind) for shape, kind in outs],
        compiler_params=pltpu.CompilerParams(vmem_limit_bytes=VMEM_MOST),
    )(positions, *ins, units)


def weight_grad_kernel(
    edges, pos_ref, x_hbm, ctx_hbm, du_hbm, act_hbm, dq_hbm, dk_hbm, dv_hbm, da_hbm, hb_hbm, df_hbm, out_hbm,
    x_v, ctx_v, du_v, act_v, right, staged, sems, out_sems,
):
    width = x_v.shape[1]
    unit_rows = out_hbm.shape[1]
    inner_rows = FF // width
    loads = [(act_hbm, act_v), (df_hbm, right.at[5]), (du_hbm, du_v), (hb_hbm, right.at[4]), (ctx_hbm, ctx_v),
             (da_hbm, right.at[3]), (x_hbm, x_v), (dq_hbm, right.at[0]), (dk_hbm, right.at[1]), (dv_hbm, right.at[2])]
    copies = [pltpu.make_async_copy(src, dst, sems.at[i]) for i, (src, dst) in enumerate(loads)]
    for copy in copies:
        copy.start()
    waited = set()
    per = width // unit_rows
    work = []
    for part in range(inner_rows):
        work.append((act_v, part, 5, edges[5] + part * per, (0, 1)))
    for part in range(inner_rows):
        work.append((du_v, part, 4, edges[4] + part * per, (2, 3)))
    work.append((ctx_v, 0, 3, edges[3], (4, 5)))
    work.append((x_v, 0, 0, edges[0], (6, 7)))
    work.append((x_v, 0, 1, edges[1], (6, 8)))
    work.append((x_v, 0, 2, edges[2], (6, 9)))
    for step, (left, part, m, unit, needs) in enumerate(work):
        slot = step % 2
        for n in needs:
            if n not in waited:
                copies[n].wait()
                waited.add(n)
        if step >= 2:
            pltpu.make_async_copy(out_hbm.at[pl.ds(0, per)], staged.at[slot], out_sems.at[slot]).wait()
        half = per // 2
        for piece in range(2):
            cols = slice(part * width + piece * half * unit_rows, part * width + (piece + 1) * half * unit_rows)
            block = dot_tn(left[:, cols], right[m]).astype(jnp.bfloat16)
            staged[slot, piece * half : (piece + 1) * half] = block.reshape(half, unit_rows, width)
        for n in range(per):
            pltpu.make_async_copy(staged.at[slot, n], out_hbm.at[pos_ref[unit + n]], out_sems.at[slot]).start()
    for slot in range(2):
        pltpu.make_async_copy(out_hbm.at[pl.ds(0, per)], staged.at[slot], out_sems.at[slot]).wait()


def run_weight_grads(x, saved, back, positions, edges, places, unit_rows):
    rows, width = x.shape
    bf = jnp.bfloat16
    ctx, hb, act = saved[5], saved[8], saved[9]
    _, df, du, da, dq, dk, dv, _ = back
    per = width // unit_rows
    anyw = pl.BlockSpec(memory_space=pl.ANY)
    return pl.pallas_call(
        functools.partial(weight_grad_kernel, edges),
        name="weight_grads",
        in_specs=[pl.BlockSpec(memory_space=pltpu.SMEM)] + [anyw] * 10,
        out_specs=anyw,
        scratch_shapes=[
            pltpu.VMEM((rows, width), bf), pltpu.VMEM((rows, width), bf), pltpu.VMEM((rows, FF), bf),
            pltpu.VMEM((rows, FF), bf), pltpu.VMEM((6, rows, width), bf),
            pltpu.VMEM((2, per, unit_rows, width), bf),
            pltpu.SemaphoreType.DMA((10,)), pltpu.SemaphoreType.DMA((2,)),
        ],
        out_shape=jax.ShapeDtypeStruct((places, unit_rows, width), bf),
        compiler_params=pltpu.CompilerParams(vmem_limit_bytes=VMEM_MOST),
    )(positions, x, ctx, du, act, dq, dk, dv, da, hb, df)


STEPS = 6
EARLY = 1
BAND = 16
HALF = 384


def step_units(edges):
    per = edges[1] - edges[0]
    firsts = [(edge + per * t, edge + per * (t + 1)) for edge in (edges[5], edges[4]) for t in (0, 2)]
    return firsts + [(edges[3], edges[0]), (edges[1], edges[2])]


def sum_places(edges):
    per = edges[1] - edges[0]
    table = [0] * edges[6]
    for t, firsts in enumerate(step_units(edges)):
        for m, first in enumerate(firsts):
            for k in range(per):
                table[first + k] = (k % 2) * (STEPS * per) + t * per + m * (per // 2) + k // 2
    return table


def backward_reduce_kernel(
    edges, tab_ref, scale_ref, small_ref, cls_ref, lang_row, rs1_ref, rs2_ref, og_hbm, n2_hbm, slope_hbm, act_hbm, hb_hbm, n1_hbm, ctx_hbm,
    q_hbm, k_hbm, v_hbm, x_hbm, probs_hbm, units_hbm,
    dx_hbm, own_out, small_out, loss_out, gscale_out,
    dh, nbuf, p0, p1, p2, p3, p4, p5, p6, p7, p8, wbuf, gbuf, c_in, xa, yb, ya, xb, ya_low, xb_low, zg, zd, zab, fbuf, a_out, a_in, x_in,
    gsm, t_acc, t_in, pooled, dlogits,
    l_sem, c_s, c_r, xa_s, xa_r, yb_s, yb_r, ya_s, ya_r, xb_s, xb_r, z_s, z_r, f_s, f_r, a_s, a_r, o_s, o_r,
    t_s, t_r, g_s, g_r, h_s, h_r, c_free,
):
    s, z, y, c = place()
    bf, f32 = jnp.bfloat16, jnp.float32
    rows_all, width = dh.shape
    count = rows_all // TILE
    inner_rows = FF // width
    per = edges[1] - edges[0]
    upper = gbuf.shape[5]
    unit_rows = 2 * upper
    slots = own_out.shape[0]
    sibling = (s, batch_of(z, y, 1 - c))
    across = (s, batch_of(z, 1 - y, c))
    other = (1 - s, batch_of(z, y, c))
    round_to = (sibling, across, other, (s, batch_of(z + 1 - 2 * (z % 2), y, c)), (s, batch_of((z + 2) % ZS, y, c)))

    barrier = pltpu.get_barrier_semaphore()

    def hello(target):
        pl.semaphore_signal(barrier, inc=1, device_id=target, device_id_type=MESH)

    hello(sibling)
    hello(other)
    turns = [(dz, dy) for dz in range(ZS) for dy in range(2) if dz or dy]
    for dz, dy in turns:
        hello((s, batch_of((z + dz) % ZS, (y + dy) % 2, c)))
    pl.semaphore_wait(barrier, 2 + len(turns))

    chunk = lambda ref, p: ref.at[:, pl.ds(p * width, width)]
    matrix = lambda first: units_hbm.at[pl.ds(first, per)]
    firsts = step_units(edges)
    acts, slopes = (p3, p5), (p4, p6, p3, p5)
    loads = {"og": (og_hbm, p0), "n2": (n2_hbm, nbuf), "hb": (hb_hbm, p2), "n1": (n1_hbm, nbuf), "probs": (probs_hbm, p0),
             "ctx": (ctx_hbm, p4), "q": (q_hbm, p6), "k": (k_hbm, p7), "v": (v_hbm, p8), "x": (x_hbm, p3)}
    for p in range(inner_rows):
        loads["act%d" % p] = (chunk(act_hbm, p), acts[p % 2])
        loads["slope%d" % p] = (chunk(slope_hbm, p), slopes[p])
        loads["wo%d" % p] = (matrix(edges[5] + p * per), wbuf.at[p % 2, 0])
        loads["wi%d" % p] = (matrix(edges[4] + p * per), wbuf.at[p % 2, 1])
    for t in (4, 5):
        for m in range(2):
            loads["w%d%d" % (t, m)] = (matrix(firsts[t][m]), wbuf.at[t % 2, m])
    copies = {
        name: pltpu.make_async_copy(src, dst, l_sem.at[n]) for n, (name, (src, dst)) in enumerate(loads.items())
    }

    def begin(*names):
        for name in names:
            copies[name].start()

    def ready(*names):
        for name in names:
            copies[name].wait()

    begin("og", "n2", "act0", "act1", "slope0", "wo0", "wi0", "hb", "slope1", "wo1", "wi1", "k", "v")

    row = lambda r: small_ref[r : r + 1, :]
    gsm[...] = jnp.zeros_like(gsm)

    def add_small(r, values):
        gsm[r : r + 1, :] += jnp.sum(values.astype(f32), axis=0, keepdims=True)

    def tile_rows(i):
        return pl.ds(pl.multiple_of(i * TILE, TILE), TILE)

    def weight(slot, m):
        return wbuf[slot, m].reshape(per * unit_rows, width)

    def remote(src, dst, send, recv, target):
        return pltpu.make_async_remote_copy(
            src_ref=src, dst_ref=dst, send_sem=send, recv_sem=recv, device_id=target, device_id_type=MESH
        )

    my_cols = pl.ds(pl.multiple_of(y * HALF, 128), HALF)
    its_cols = pl.ds(pl.multiple_of((1 - y) * HALF, 128), HALF)
    blocks = pl.ds(0, per // 2)
    both = pl.ds(0, 2)
    lines = pl.ds(0, upper)

    def band(zz):
        return pl.ds(pl.multiple_of(zz * BAND, BAND), BAND)

    def c_copy(t):
        return remote(gbuf.at[t, :, 1 - c], c_in.at[t % RING], c_s.at[t], c_r.at[t], sibling)

    def xa_copy(t):
        return remote(gbuf.at[t, 0, c, blocks, 1 - s], xa.at[t], xa_s.at[t], xa_r.at[t], other)

    def yb_copy(t):
        return remote(gbuf.at[t, 1, c, blocks, both, lines, its_cols], yb.at[t], yb_s.at[t], yb_r.at[t], across)

    def ya_view(t, cols):
        return gbuf.at[t, 0, c, blocks, s, band(z) if t < EARLY else lines, cols]

    def xb_view(t, ss):
        return gbuf.at[t, 1, c, blocks, ss, band(z) if t < EARLY else lines, my_cols]

    def ya_land(t):
        return ya_low.at[t] if t < EARLY else ya.at[t - EARLY]

    def xb_land(t):
        return xb_low.at[t] if t < EARLY else xb.at[t - EARLY]

    def ya_copy(t):
        return remote(ya_view(t, its_cols), ya_land(t), ya_s.at[t], ya_r.at[t], across)

    def xb_copy(t):
        return remote(xb_view(t, 1 - s), xb_land(t), xb_s.at[t], xb_r.at[t], other)

    def z_views(t, zz, dz):
        if t < EARLY:
            return [
                (gbuf.at[t, 0, c, blocks, s, band(zz)], zg.at[t, dz - 1]),
                (gbuf.at[t, 1, c, blocks, both, band(zz), my_cols], zd.at[t, dz - 1]),
            ]
        return [
            (gbuf.at[t, m, c, blocks, s, band(zz), my_cols], zab.at[t - EARLY, dz - 1, m]) for m in range(2)
        ]

    def z_copies(t, dz):
        zz = (z + dz) % ZS
        return [
            remote(view, land, z_s.at[n, t, dz - 1], z_r.at[n, t, dz - 1], (s, batch_of(zz, y, c)))
            for n, (view, land) in enumerate(z_views(t, zz, dz))
        ]

    def f_copy(t):
        mine = fbuf.at[pl.ds(c * (STEPS * per) + t * per, per)]
        return remote(mine, mine, f_s.at[t], f_r.at[t], sibling)

    def turn(r):
        return remote(t_acc.at[r], t_in.at[r], t_s.at[r], t_r.at[r], round_to[r])

    def add(view, got):
        @pl.loop(0, per // 2)
        def _(k):
            view.at[k][...] = (view.at[k][...].astype(f32) + got.at[k][...].astype(f32)).astype(bf)

    def ev_c_send(t):
        if t >= RING:
            pl.semaphore_wait(c_free, 1)
        c_copy(t).start()

    def ev_c_wait(t):
        c_copy(t).wait_recv()
        add(gbuf.at[t, 0, c], c_in.at[t % RING, 0])
        xa_copy(t).start()
        add(gbuf.at[t, 1, c], c_in.at[t % RING, 1])
        if t + RING < STEPS:
            pl.semaphore_signal(c_free, inc=1, device_id=sibling, device_id_type=MESH)
        yb_copy(t).start()

    def ev_first(t):
        xa_copy(t).wait_recv()
        add(gbuf.at[t, 0, c, blocks, s], xa.at[t])
        if t >= EARLY:
            ya_copy(t).start()
        yb_copy(t).wait_recv()
        add(gbuf.at[t, 1, c, blocks, both, lines, my_cols], yb.at[t])
        if t >= EARLY:
            xb_copy(t).start()

    def ev_second_start(t):
        ya_copy(t).start()
        xb_copy(t).start()

    def ev_second(t):
        ya_copy(t).wait_recv()
        add(ya_view(t, my_cols), ya_land(t))
        xb_copy(t).wait_recv()
        add(xb_view(t, s), xb_land(t))

    def ev_z_send(t):
        for dz in (2, 1, 3):
            for copy in z_copies(t, dz):
                copy.start()

    def ev_z_take(t):
        for dz in (1, 3, 2):
            for copy, (view, land) in zip(z_copies(t, dz), z_views(t, z, dz)):
                copy.wait_recv()
                add(view, land)

    def ev_fin(t):
        for m in range(2):

            @pl.loop(0, per // 2)
            def _(k):
                at = c * (STEPS * per) + t * per + m * (per // 2) + k
                fbuf[at] = gbuf[t, m, c, k, s, band(z), my_cols]

        f_copy(t).start()

    def ev_turn_start(r):
        if r == 0:
            t_acc[0] = gsm[...]
        turn(r).start()

    def ev_turn_wait(r):
        turn(r).wait()
        t_acc[r + 1] = t_acc[r] + t_in[r]

    sents = cls_ref.shape[0]
    pairs = lang_row.shape[1]
    cls = cls_ref[...]
    root = lax.rsqrt(jnp.sum(cls * cls, axis=-1, keepdims=True) + NORM_EPS)
    unit = cls * root
    pooled[s, z, y, c] = unit.astype(bf)
    all_z, low_z, high_z = pl.ds(0, ZS), pl.ds(0, ZS // 2), pl.ds(ZS // 2, ZS // 2)

    def g_copy(dz):
        mine = pooled.at[s, z, y, c]
        return remote(mine, mine, g_s.at[dz - 1], g_r.at[dz - 1], (s, batch_of((z + dz) % ZS, y, c)))

    def h_copy(n, view, target):
        return remote(view, view, h_s.at[n], h_r.at[n], target)

    swaps = [
        h_copy(0, pooled.at[s, all_z, y, c], across),
        h_copy(1, pooled.at[s, all_z, y, c], other),
        h_copy(2, pooled.at[1 - s, low_z, y, c], across),
        h_copy(3, pooled.at[s, high_z, 1 - y, c], other),
        h_copy(4, pooled.at[s, all_z, y, c], sibling),
        h_copy(5, pooled.at[s, all_z, 1 - y, c], sibling),
        h_copy(6, pooled.at[1 - s, all_z, y, c], sibling),
        h_copy(7, pooled.at[1 - s, all_z, 1 - y, c], sibling),
    ]
    for dz in (2, 1, 3):
        g_copy(dz).start()

    def tile_start(i):
        rows = slice(i * TILE, (i + 1) * TILE)
        later = lax.broadcasted_iota(jnp.int32, (TILE, 1), 0) % GROUP != 0
        dy = jnp.where(later, p0[rows, :].astype(f32), 0.0)
        n2 = nbuf[rows, :]
        add_small(6 + inner_rows, dy * n2)
        add_small(7 + inner_rows, dy)
        dr2 = norm_back(dy, n2, rs2_ref[rows, :], row(6 + inner_rows))
        dh[rows, :] = dr2
        df = dr2.astype(bf)
        p1[rows, :] = df
        add_small(3 + inner_rows, df)

    def rank_rows():
        scale = scale_ref[0]
        mix = (((1,), (0,)), ((), ()))
        e_zero = pooled[0].reshape(pairs, width)
        e_one = pooled[1].reshape(pairs, width)
        cosines = dot_nt(e_zero, e_one)
        own = lax.broadcasted_iota(jnp.int32, (pairs, pairs), 0) == lax.broadcasted_iota(jnp.int32, (pairs, pairs), 1)
        langs = jnp.broadcast_to(lang_row[...].astype(f32), (pairs, pairs))
        same = langs == langs.T
        diagonal = jnp.where(own, 1.0, 0.0)
        shifted = cosines - MARGIN * diagonal
        logits = scale * shifted
        masked = jnp.where(same, logits, -1e30)
        twice = -2.0 * diagonal
        total = -2.0 * jnp.sum(logits * diagonal)
        for axis in range(2):
            top = jnp.max(masked, axis=axis, keepdims=True)
            grown = jnp.where(same, jnp.exp(masked - top), 0.0)
            summed = jnp.sum(grown, axis=axis, keepdims=True)
            twice += grown / summed
            total += jnp.sum(jnp.log(summed) + top)
        loss_out[0] = total
        gscale_out[0] = jnp.sum(twice * shifted)
        dlogits[0] = twice
        dlogits[1] = twice.T
        mine = dlogits[s, pl.ds(pl.multiple_of(batch_of(z, y, c) * sents, 16), sents), :]
        partners = pooled[1 - s].reshape(pairs, width)
        upper_part = mine.astype(bf)
        rest = (mine - upper_part.astype(f32)).astype(bf)
        de = lax.dot_general(upper_part, partners, mix, preferred_element_type=f32)
        de += lax.dot_general(rest, partners, mix, preferred_element_type=f32)
        de = scale * de
        return (de - unit * jnp.sum(unit * de, axis=-1, keepdims=True)) * root

    def sec_start():
        ready("og", "n2")
        tile_start(0)
        for dz in range(1, ZS):
            back = pooled.at[s, (z - dz) % ZS, y, c]
            remote(back, back, g_s.at[dz - 1], g_r.at[dz - 1], other).wait_recv()
        for n in (0, 1, 4):
            swaps[n].start()
        tile_start(1)
        tile_start(2)
        swaps[0].wait_recv()
        swaps[1].wait_recv()
        for n in (2, 3, 5, 6):
            swaps[n].start()
        for i in range(3, count):
            tile_start(i)
        swaps[2].wait_recv()
        swaps[3].wait_recv()
        swaps[7].start()
        for n in (4, 5, 6, 7):
            swaps[n].wait_recv()
        dc = rank_rows()
        head = [pl.ds(sent * GROUP, 1) for sent in range(sents)]
        og = jnp.concatenate([p0[sent * GROUP : sent * GROUP + 16, :].astype(f32)[:1] for sent in range(sents)], axis=0)
        n2 = jnp.concatenate([nbuf[at, :] for at in head], axis=0)
        rs2 = jnp.concatenate([rs2_ref[at, :] for at in head], axis=0)
        dy = og + dc
        add_small(6 + inner_rows, dy * n2)
        add_small(7 + inner_rows, dy)
        dr2 = norm_back(dy, n2, rs2, row(6 + inner_rows))
        add_small(3 + inner_rows, dr2.astype(bf))
        top = lax.broadcasted_iota(jnp.int32, (16, 1), 0) == 0
        for sent in range(sents):
            mine = dr2[sent : sent + 1, :]
            dh[head[sent], :] = mine
            block = slice(sent * GROUP, sent * GROUP + 16)
            p1[block, :] = jnp.where(top, mine, p1[block, :].astype(f32)).astype(bf)
        begin("n1", "probs")

    def store_grads(t, m, lhs, rhs):
        @pl.loop(0, 2)
        def _(piece):
            half = (per // 2) * unit_rows
            cols = pl.ds(pl.multiple_of(piece * half, 128), half)
            block = dot_tn(lhs[:, cols], rhs[...]).astype(bf)
            for i in range(per // 2):
                part = block[i * unit_rows : (i + 1) * unit_rows].reshape(2, upper, width)

                @pl.when(piece == 0)
                def _():
                    gbuf[t, m, i % 2, i // 2] = part

                @pl.when(piece == 1)
                def _():
                    k = per // 2 + i
                    gbuf[t, m, k % 2, k // 2] = part

    def sec_inner(p):
        def run():
            ready("slope%d" % p, "wo%d" % p, "wi%d" % p)
            slope = slopes[p]

            @pl.loop(0, count)
            def _(i):
                rows = tile_rows(i)
                da = dot_nt(p1[rows, :], weight(p % 2, 0))
                du = (da * slope[rows, :].astype(f32)).astype(bf)
                slope[rows, :] = du
                add_small(3 + p, du)
                dh[rows, :] += dot_nn(du, weight(p % 2, 1))

            if p == 2:
                begin("w40", "w41")
            if p == 3:
                begin("w50", "w51")
            if p + 2 < inner_rows:
                begin("wo%d" % (p + 2), "wi%d" % (p + 2))

        return run

    def sec_outer_grad(p):
        def run():
            ready("act%d" % p)
            store_grads(p // 2, p % 2, acts[p % 2], p1)
            if p + 2 < inner_rows:
                begin("act%d" % (p + 2))
            else:
                begin("slope%d" % p)

        return run

    def sec_inner_grad(p):
        def run():
            if p == 0:
                ready("hb")
            store_grads(2 + p // 2, p % 2, slopes[p], p2)
            if p < 3:
                begin(("ctx", "q", "x")[p])

        return run

    def sec_norm():
        ready("n1", "w40", "w41")

        @pl.loop(0, count)
        def _(i):
            rows = tile_rows(i)
            dh1 = dh[rows, :]
            n1 = nbuf[rows, :]
            add_small(4 + inner_rows, dh1 * n1)
            add_small(5 + inner_rows, dh1)
            dr1 = norm_back(dh1, n1, rs1_ref[rows, :], row(4 + inner_rows))
            dh[rows, :] = dr1
            dattn = dr1.astype(bf)
            p1[rows, :] = dattn
            add_small(2, dattn)
            p5[rows, :] = dot_nt(dattn, weight(0, 0)).astype(bf)

    def sec_out_grad():
        ready("ctx")
        store_grads(4, 0, p4, p1)

    first, second, is_first = lane_halves()
    every_pair = [slice(pair * 2 * HD, (pair + 1) * 2 * HD) for pair in range(H // 2)]

    def sec_heads(part):
        def run():
            if part == 0:
                ready("probs", "q", "k", "v")
            amount = rows_all // GROUP // 2

            @pl.loop(part * amount, (part + 1) * amount)
            def _(sent):
                rows = pl.ds(pl.multiple_of(sent * GROUP, GROUP), GROUP)
                dctx, q, k, v, low = p5[rows, :], p6[rows, :], p7[rows, :], p8[rows, :], p0[rows, :]
                dcc = [both_heads(dctx[:, lanes], first, second) for lanes in every_pair]
                dprobs = jnp.concatenate([dot_nt(v[:, lanes], wide) for lanes, wide in zip(every_pair, dcc)], axis=1)
                probs = low.astype(f32)
                dscores = probs * (dprobs - jnp.sum(dprobs * probs, axis=0, keepdims=True))
                dscores = (dscores * HD ** (-0.5)).astype(bf)
                dv = jnp.concatenate(
                    [dot_nn(low[:, lanes], wide) for lanes, wide in zip(every_pair, dcc)], axis=1
                ).astype(bf)
                p4[rows, :] = dv
                add_small(1, dv)
                qq = [both_heads(q[:, lanes], first, second) for lanes in every_pair]
                p2[rows, :] = jnp.concatenate(
                    [dot_nn(dscores[:, lanes], wide) for lanes, wide in zip(every_pair, qq)], axis=1
                ).astype(bf)
                mixed = [dot_tn(dscores[:, lanes], k[:, lanes]) for lanes in every_pair]
                dq = jnp.concatenate([jnp.where(is_first, m[:GROUP], m[GROUP:]) for m in mixed], axis=1).astype(bf)
                p1[rows, :] = dq
                add_small(0, dq)

        return run

    def sec_query_grad():
        ready("x")
        store_grads(4, 1, p3, p1)

    def sec_key_grad():
        store_grads(5, 0, p3, p2)

    def sec_value_grad():
        store_grads(5, 1, p3, p4)

    def sec_back(part):
        def run():
            if part == 0:
                ready("w50", "w51")

            @pl.loop(part * (count // 2), (part + 1) * (count // 2))
            def _(i):
                rows = tile_rows(i)
                dx = dh[rows, :] + dot_nt(p1[rows, :], weight(0, 1))
                dx += dot_nt(p2[rows, :], weight(1, 0)) + dot_nt(p4[rows, :], weight(1, 1))
                p6[rows, :] = dx.astype(bf)

        return run

    sections = [sec_start] + [sec_outer_grad(p) for p in range(inner_rows)]
    for p in range(inner_rows):
        sections += [sec_inner(p), sec_inner_grad(p)]
    sections += [sec_norm, sec_out_grad, sec_heads(0), sec_heads(1), sec_query_grad, sec_key_grad, sec_value_grad]
    sections += [sec_back(0), sec_back(1)]
    done = [2, 4, 8, 12, 17, 19]
    events = {}

    def at_tick(tick, order, action):
        events.setdefault(tick, []).append((order, action))

    for t in range(STEPS):
        at_tick(done[t], 0, functools.partial(ev_c_send, t))
        at_tick(PLACES[t][0], 1, functools.partial(ev_c_wait, t))
        at_tick(PLACES[t][1], 2, functools.partial(ev_first, t))
        if t < EARLY:
            at_tick(PLACES[t][1], 2.5, functools.partial(ev_z_send, t))
            at_tick(PLACES[t][2], 3, functools.partial(ev_z_take, t))
            at_tick(PLACES[t][2], 3.5, functools.partial(ev_second_start, t))
            at_tick(PLACES[t][3], 4, functools.partial(ev_second, t))
        else:
            at_tick(PLACES[t][2], 3, functools.partial(ev_second, t))
            at_tick(PLACES[t][2], 3.5, functools.partial(ev_z_send, t))
            at_tick(PLACES[t][3], 4, functools.partial(ev_z_take, t))
        at_tick(PLACES[t][3], 5, functools.partial(ev_fin, t))
    for r in range(5):
        at_tick(16 + r, 10, functools.partial(ev_turn_start, r))
        at_tick(17 + r, -1, functools.partial(ev_turn_wait, r))
    for tick in range(max(max(events) + 1, len(sections))):
        if tick < len(sections):
            sections[tick]()
        if tick == len(sections) - 1:
            dx_copy = pltpu.make_async_copy(p6, dx_hbm, l_sem.at[len(loads)])
            dx_copy.start()
        for _, action in sorted(events.get(tick, []), key=lambda item: item[0]):
            action()
    small_out[...] = t_acc[5]
    for t in range(STEPS):
        its = fbuf.at[pl.ds((1 - c) * (STEPS * per) + t * per, per)]
        remote(its, its, f_s.at[t], f_r.at[t], sibling).wait_recv()

    def a_copy(zz, yy):
        return remote(a_out.at[zz, yy], a_in.at[z, y], a_s.at[zz, yy], a_r.at[z, y], (s, batch_of(zz, yy, c)))

    def o_copy(zz, yy):
        return remote(a_in.at[zz, yy], x_in.at[zz, yy], o_s.at[zz, yy], o_r.at[zz, yy], other)

    for dz, dy in turns:
        zz, yy = (z + dz) % ZS, (y + dy) % 2
        for j in range(slots):
            a_out[zz, yy, j] = fbuf[tab_ref[batch_of(zz, yy, c) * slots + j]]
        a_copy(zz, yy).start()
    for j in range(slots):
        a_in[z, y, j] = fbuf[tab_ref[batch_of(z, y, c) * slots + j]]
    o_copy(z, y).start()

    def put(zz, yy, ss, got):
        rows = pl.ds(pl.multiple_of(ss * upper + zz * BAND, BAND), BAND)
        cols = pl.ds(pl.multiple_of(yy * HALF, 128), HALF)
        for j in range(slots):
            own_out[j, rows, cols] = got[zz, yy, j]

    put(z, y, s, a_in)
    for dz, dy in turns:
        zz, yy = (z + dz) % ZS, (y + dy) % 2
        remote(a_in.at[zz, yy], a_in.at[zz, yy], a_s.at[zz, yy], a_r.at[zz, yy], other).wait_recv()
        o_copy(zz, yy).start()
        put(zz, yy, s, a_in)
    for dz, dy in [(0, 0)] + turns:
        zz, yy = (z + dz) % ZS, (y + dy) % 2
        o_copy(zz, yy).wait_recv()
        put(zz, yy, 1 - s, x_in)
    for t in range(STEPS):
        for copy in (c_copy, xa_copy, yb_copy, ya_copy, xb_copy, f_copy):
            copy(t).wait_send()

        for dz in range(1, ZS):
            for copy in z_copies(t, dz):
                copy.wait_send()

    for dz in range(1, ZS):
        g_copy(dz).wait_send()
    for swap in swaps:
        swap.wait_send()
    for dz, dy in turns:
        a_copy((z + dz) % ZS, (y + dy) % 2).wait_send()
    for dz, dy in [(0, 0)] + turns:
        o_copy((z + dz) % ZS, (y + dy) % 2).wait_send()
    dx_copy.wait()


RING = 3
PLACES = ((5, 12, 18, 22), (8, 12, 15, 20), (10, 14, 18, 24), (15, 19, 22, 26), (19, 22, 25, 26), (24, 26, 32, 42))


def run_backward_reduce(og, cls, scale, langs, small, saved, x, units, table, edges, slots):
    rows, width = og.shape
    bf, f32 = jnp.bfloat16, jnp.float32
    _, q, k, v, probs, ctx, n1, rs1, hb, act, slope, n2, rs2, _ = saved[:14]
    unit_rows = units.shape[1]
    per = edges[1] - edges[0]
    half = per // 2
    pairs = langs.shape[0]
    dma = pltpu.SemaphoreType.DMA
    vm = pltpu.VMEM
    vmem = pl.BlockSpec(memory_space=pltpu.VMEM)
    anyw = pl.BlockSpec(memory_space=pl.ANY)
    upper = unit_rows // 2
    return pl.pallas_call(
        functools.partial(backward_reduce_kernel, edges),
        name="backward_reduce",
        out_shape=[
            jax.ShapeDtypeStruct((rows, width), bf),
            jax.ShapeDtypeStruct((slots, unit_rows, width), bf),
            jax.ShapeDtypeStruct(small.shape, f32),
            jax.ShapeDtypeStruct((1,), f32),
            jax.ShapeDtypeStruct((1,), f32),
        ],
        in_specs=[pl.BlockSpec(memory_space=pltpu.SMEM)] * 2 + [vmem] * 5 + [anyw] * 13,
        out_specs=[anyw, vmem, vmem] + [pl.BlockSpec(memory_space=pltpu.SMEM)] * 2,
        scratch_shapes=[vm((rows, width), f32)] * 2
        + [vm((rows, width), bf)] * 9
        + [
            vm((2, 2, per, unit_rows, width), bf),
            vm((STEPS, 2, 2, half, 2, upper, width), bf),
            vm((RING, 2, half, 2, upper, width), bf),
            vm((STEPS, half, upper, width), bf),
            vm((STEPS, half, 2, upper, HALF), bf),
            vm((STEPS - EARLY, half, upper, HALF), bf),
            vm((STEPS - EARLY, half, upper, HALF), bf),
            vm((EARLY, half, BAND, HALF), bf),
            vm((EARLY, half, BAND, HALF), bf),
            vm((EARLY, ZS - 1, half, BAND, width), bf),
            vm((EARLY, ZS - 1, half, 2, BAND, HALF), bf),
            vm((STEPS - EARLY, ZS - 1, 2, half, BAND, HALF), bf),
            vm((2 * STEPS * per, BAND, HALF), bf),
            vm((ZS, 2, slots, BAND, HALF), bf),
            vm((ZS, 2, slots, BAND, HALF), bf),
            vm((ZS, 2, slots, BAND, HALF), bf),
            vm(small.shape, f32),
            vm((6,) + small.shape, f32),
            vm((5,) + small.shape, f32),
            vm((2, ZS, 2, 2) + cls.shape, bf),
            vm((2, pairs, pairs), f32),
        ]
        + [dma((32,))]
        + [dma((STEPS,))] * 10
        + [dma((2, STEPS, ZS - 1))] * 2
        + [dma((STEPS,))] * 2
        + [dma((ZS, 2))] * 4
        + [dma((5,))] * 2
        + [dma((ZS - 1,))] * 2
        + [dma((8,))] * 2
        + [pltpu.SemaphoreType.REGULAR],
        compiler_params=pltpu.CompilerParams(collective_id=3, has_side_effects=True, vmem_limit_bytes=63 << 20),
    )(table, scale, small, cls, langs.reshape(1, pairs), rs1, rs2, og, n2, slope, act, hb, n1, ctx, q, k, v, x, probs.reshape(rows, width), units)


def unit_positions(owner_list, slot_count):
    unit_total = owner_list.shape[0]
    same_owner = owner_list[:, None] == owner_list[None, :]
    ordinal = jnp.arange(unit_total, dtype=jnp.int32)
    earlier = ordinal[None, :] < ordinal[:, None]
    slot_number = jnp.sum(jnp.where(same_owner & earlier, 1, 0), axis=1).astype(jnp.int32)
    return owner_list * slot_count + slot_number


def adamw(weight_in, gradient, moment_one, moment_two, rate_value, decay_value, fix_one, fix_two):
    new_one = BETA_ONE * moment_one + (1.0 - BETA_ONE) * gradient
    new_two = BETA_TWO * moment_two + (1.0 - BETA_TWO) * gradient * gradient
    stepped = new_one * (1.0 / fix_one) / (jnp.sqrt(new_two * (1.0 / fix_two)) + ADAM_EPS)
    return (weight_in - rate_value * (stepped + decay_value * weight_in), new_one, new_two)


def adamw_kernel(
    fixes, mean_by, filled_ref, weight_hbm, grad_hbm, first_hbm, second_hbm, small_ref, small_grad, small_one, small_two,
    scale_ref, scale_grad, scale_one, scale_two, loss_ref, pass_hbm,
    new_hbm, one_hbm, two_hbm, low_hbm, new_small, new_small_one, new_small_two, new_scale, new_scale_one, new_scale_two,
    new_loss, passed_hbm,
    weight_v, grad_v, first_v, second_v, low_v, pass_v, in_sem, out_sem, pass_sem,
):
    slots = weight_v.shape[0]

    def copy(src, dst, sem):
        return pltpu.make_async_copy(src, dst, sem)

    ins = [
        [
            copy(hbm.at[j], held.at[j], in_sem.at[n, j])
            for n, (hbm, held) in enumerate(
                ((weight_hbm, weight_v), (grad_hbm, grad_v), (first_hbm, first_v), (second_hbm, second_v))
            )
        ]
        for j in range(slots)
    ]
    outs = [
        [
            copy(held.at[j], hbm.at[j], out_sem.at[n, j])
            for n, (hbm, held) in enumerate(
                ((new_hbm, weight_v), (one_hbm, first_v), (two_hbm, second_v), (low_hbm, low_v))
            )
        ]
        for j in range(slots)
    ]
    for group in ins:
        for item in group:
            item.start()
    pass_in, pass_out = copy(pass_hbm, pass_v, pass_sem.at[0]), copy(pass_v, passed_hbm, pass_sem.at[1])
    pass_in.start()
    new_small[...], new_small_one[...], new_small_two[...] = adamw(
        small_ref[...], small_grad[...], small_one[...], small_two[...], RATE_SMALL, 0.0, *fixes
    )
    spread = lambda ref: jnp.full((8, 128), ref[0], dtype=jnp.float32)
    turned = adamw(spread(scale_ref), spread(scale_grad), spread(scale_one), spread(scale_two), RATE_SCALE, 0.0, *fixes)
    for ref, value in zip((new_scale, new_scale_one, new_scale_two), turned):
        ref[0] = jnp.max(value)
    new_loss[0] = loss_ref[0] * mean_by
    for j in range(slots):
        for item in ins[j]:
            item.wait()
        weight, first, second = weight_v[j], first_v[j], second_v[j]
        moved = adamw(weight, grad_v[j].astype(jnp.float32), first, second, RATE_UNITS, DECAY, *fixes)
        used = filled_ref[j] > 0
        new = jnp.where(used, moved[0], weight)
        weight_v[j] = new
        first_v[j] = jnp.where(used, moved[1], first)
        second_v[j] = jnp.where(used, moved[2], second)
        low_v[j] = new.astype(jnp.bfloat16)
        for item in outs[j]:
            item.start()
        if j == 0:
            pass_in.wait()
            pass_out.start()
    for group in outs:
        for item in group:
            item.wait()
    pass_out.wait()


def run_adamw(units, small, scale, loss, filled, fixes, mean_by, passed):
    weight, gradient = units[:2]
    f32, bf = jnp.float32, jnp.bfloat16
    slots = weight.shape[0]
    anyw = pl.BlockSpec(memory_space=pl.ANY)
    flat = pl.BlockSpec(memory_space=pltpu.VMEM)
    single = pl.BlockSpec(memory_space=pltpu.SMEM)
    outs = [(weight.shape, f32)] * 3 + [(weight.shape, bf)] + [(small[0].shape, f32)] * 3 + [((1,), f32)] * 4
    outs += [(passed.shape, passed.dtype)]
    dma = pltpu.SemaphoreType.DMA
    return pl.pallas_call(
        functools.partial(adamw_kernel, fixes, mean_by),
        name="adamw_all",
        in_specs=[single] + [anyw] * 4 + [flat] * 4 + [single] * 5 + [anyw],
        out_specs=[anyw] * 4 + [flat] * 3 + [single] * 4 + [anyw],
        scratch_shapes=[
            pltpu.VMEM(weight.shape, f32), pltpu.VMEM(weight.shape, gradient.dtype), pltpu.VMEM(weight.shape, f32),
            pltpu.VMEM(weight.shape, f32), pltpu.VMEM(weight.shape, bf), pltpu.VMEM(passed.shape, passed.dtype),
            dma((4, slots)), dma((4, slots)), dma((2,)),
        ],
        out_shape=[jax.ShapeDtypeStruct(shape, kind) for shape, kind in outs],
        compiler_params=pltpu.CompilerParams(vmem_limit_bytes=VMEM_MOST),
    )(filled, *units, *small, *scale, loss, passed)


def any_size_units(own, positions, owners):
    slots, rows, width = own.shape
    table = jnp.arange(owners * slots, dtype=jnp.int32)[:, None] == positions[None, :]
    bands = lax.all_to_all(
        own.transpose(1, 0, 2).astype(jnp.bfloat16), "batch", split_axis=0, concat_axis=1, tiled=True
    )
    ordered = jnp.einsum(
        "rpd,pu->rud", bands, table.astype(jnp.bfloat16), preferred_element_type=jnp.float32
    ).astype(jnp.bfloat16)
    return lax.all_gather(ordered, "batch", axis=0, tiled=True).transpose(1, 0, 2)


def any_size_sums(grads, positions, owners, slots):
    table = jnp.arange(owners * slots, dtype=jnp.int32)[:, None] == positions[None, :]
    pieces = lax.psum_scatter(grads.transpose(1, 0, 2).astype(jnp.float32), "batch", scatter_dimension=0, tiled=True)
    summed = lax.psum(pieces.astype(jnp.bfloat16), "stream").astype(jnp.float32)
    send_rows = jnp.einsum("rud,pu->rpd", summed, table.astype(jnp.float32), precision=HIGHEST)
    owned = lax.all_to_all(send_rows.astype(jnp.bfloat16), "batch", split_axis=1, concat_axis=0, tiled=True)
    return owned.astype(jnp.float32).transpose(1, 0, 2)


def any_size_rank(cls, scale, langs, owners):
    sents, width = cls.shape
    root = lax.rsqrt(jnp.sum(cls * cls, axis=-1, keepdims=True) + NORM_EPS)
    unit = cls * root
    every = lax.all_gather(unit.astype(jnp.bfloat16), "batch", axis=0, tiled=True)
    every = lax.all_gather(every, "stream", axis=0)
    cosines = jnp.dot(every[0], every[1].T, preferred_element_type=jnp.float32)
    diagonal = jnp.eye(cosines.shape[0], dtype=jnp.float32)
    same = langs[:, None] == langs[None, :]
    shifted = cosines - MARGIN * diagonal
    logits = scale[0] * shifted
    masked = jnp.where(same, logits, -1e30)
    both = -2.0 * diagonal
    total = -2.0 * jnp.sum(logits * diagonal)
    for axis in range(2):
        top = jnp.max(masked, axis=axis, keepdims=True)
        grown = jnp.where(same, jnp.exp(masked - top), 0.0)
        summed = jnp.sum(grown, axis=axis, keepdims=True)
        both += grown / summed
        total += jnp.sum(jnp.log(summed) + top)
    s = lax.axis_index("stream")
    turned = jnp.where(s == 0, both, both.T)
    rows = lax.dynamic_slice_in_dim(turned, lax.axis_index("batch") * sents, sents)
    partners = lax.dynamic_index_in_dim(every, 1 - s, keepdims=False).astype(jnp.float32)
    de = scale[0] * jnp.dot(rows, partners, precision=HIGHEST)
    dc = (de - unit * jnp.sum(unit * de, axis=-1, keepdims=True)) * root
    return dc, total, jnp.sum(both * shifted)


def per_device(
    tokens, out_grad, master, first_moment, second_moment, small_params, small_first, small_second, logit_scale,
    scale_first, scale_second, pair_lang, unit_owner,
):
    owners = lax.axis_size("batch")
    here_batch = lax.axis_index("batch")
    unit_rows, slot_count, width = master.shape
    query_blocks = width // unit_rows
    inner_blocks = FF // unit_rows
    edges = [query_blocks * n for n in range(5)]
    edges += [edges[4] + inner_blocks, edges[4] + 2 * inner_blocks]
    units_total = unit_owner.shape[0]
    positions = unit_positions(unit_owner, slot_count)
    on_block = owners == 4 * ZS
    own = master.transpose(1, 0, 2)
    if on_block:
        units, where, places = gather_units(own), positions, owners * slot_count
    else:
        units = any_size_units(own, positions, owners)
        where, places = jnp.arange(units_total, dtype=jnp.int32), units_total
    sentences, length = tokens.shape[1], tokens.shape[2]
    flat = tokens.reshape(sentences * length, width)
    saved = run_forward(flat, small_params, units, where, edges)
    cls = saved[13]
    grad_rows = out_grad.reshape(sentences * length, width)
    if on_block:
        slot_units = jnp.arange(places, dtype=jnp.int32)[:, None] == positions[None, :]
        sum_table = jnp.asarray(sum_places(edges), dtype=jnp.int32)
        table = jnp.sum(jnp.where(slot_units, sum_table[None, :], 0), axis=1, dtype=jnp.int32)
        d_tokens, owned_grad, small_total, loss_total, grad_scale = run_backward_reduce(
            grad_rows, cls, logit_scale, pair_lang, small_params, saved, flat, saved[14], table, edges,
            slot_count,
        )
    else:
        dc, loss_total, grad_scale = any_size_rank(cls, logit_scale, pair_lang, owners)
        loss_total, grad_scale = loss_total.reshape(1), grad_scale.reshape(1)
        back = run_backward(grad_rows, dc.reshape(-1, TILE // GROUP, width), small_params, saved, units, where, edges)
        grads = run_weight_grads(flat, saved, back, where, edges, places, unit_rows)
        d_tokens = back[0]
        owned_grad = any_size_sums(grads, positions, owners, slot_count)
        small_total = lax.psum(back[7], ("stream", "batch"))
    step_value = float(STEP)
    fix_one = 1.0 - BETA_ONE**step_value
    fix_two = 1.0 - BETA_TWO**step_value
    my_places = here_batch * slot_count + jnp.arange(slot_count, dtype=jnp.int32)
    filled = jnp.any(my_places[:, None] == positions[None, :], axis=1).astype(jnp.int32)
    (
        new_master, new_first, new_second, new_copy, new_small, new_small_first, new_small_second, scale_new, scale_one,
        scale_two, loss_out, d_tokens,
    ) = run_adamw(
        (own, owned_grad, first_moment.transpose(1, 0, 2), second_moment.transpose(1, 0, 2)),
        (small_params, small_total, small_first, small_second),
        (logit_scale, grad_scale, scale_first, scale_second),
        loss_total,
        filled,
        (fix_one, fix_two),
        1.0 / (2 * owners * sentences),
        d_tokens,
    )
    back_order = lambda a: a.transpose(1, 0, 2)
    return (
        saved[0].reshape(tokens.shape),
        d_tokens.reshape(tokens.shape),
        back_order(new_master),
        back_order(new_first),
        back_order(new_second),
        back_order(new_copy),
        new_small,
        new_small_first,
        new_small_second,
        scale_new,
        scale_one,
        scale_two,
        loss_out,
    )


def solution(mesh):
    rows = P("stream", "batch", None, None)
    blocks = P(None, "batch", None)
    return jax.shard_map(
        per_device,
        mesh=mesh,
        in_specs=(rows, rows, blocks, blocks, blocks) + (P(),) * 8,
        out_specs=(rows, rows, blocks, blocks, blocks, blocks) + (P(),) * 7,
        check_vma=False,
    )
```
